32 devices in a mesh: dp: 8 (over z, x), mp: 4 (over y, core).
Axes of the slice: x: 2, y: 2, z: 4, core: 2. Of those that a mesh axis runs over, the one named last changes fastest.
Arguments:
- inputs: bfloat16 [16, 512, 512], P('dp'), may hold values from -6 to 6
- memory: bfloat16 [16, 512, 512], P(None, 'dp'), may hold values from -6 to 6
- segment_ids: int32 [16, 512], P('dp'), may hold values from 0 to 7, never falling along the last dimension, each value on 1 to 128 neighbouring positions
- mem_lengths: int32 [16, 8], P('dp'), may hold values from 1 to 128, 512 in all within a row
- bucket_group: int32 [8], replicated, may hold values from 0 to 5
- group_tokens: int32 [6], replicated, may hold values from 64 to 1023
- norm_gain: bfloat16 [3, 512], replicated, may hold values from 0.5 to 1.5
- norm_bias: bfloat16 [3, 512], replicated, may hold values from -3 to 3
- self_qkv: bfloat16 [3, 512, 512], P(None, None, 'mp'), may hold values from -0.25 to 0.25
- self_bias: bfloat16 [2, 512], P(None, 'mp'), may hold values from -3 to 3
- self_out: bfloat16 [512, 512], P('mp'), may hold values from -0.75 to 0.75
- cross_q: bfloat16 [512, 512], P(None, 'mp'), may hold values from -0.25 to 0.25
- cross_kv: bfloat16 [2, 512, 512], P(None, None, 'mp'), may hold values from -0.25 to 0.25
- cross_bias: bfloat16 [2, 512], P(None, 'mp'), may hold values from -3 to 3
- cross_out: bfloat16 [512, 512], P('mp'), may hold values from -0.75 to 0.75
- ffn_in: bfloat16 [512, 2048], P(None, 'mp'), may hold values from -0.25 to 0.25
- ffn_bias: bfloat16 [2048], P('mp'), may hold values from -3 to 3
- ffn_out: bfloat16 [2048, 512], P('mp'), may hold values from -0.125 to 0.125
- out_bias: bfloat16 [3, 512], replicated, may hold values from -3 to 3
- cotangent: bfloat16 [16, 512, 512], P('dp'), may hold values from -6 to 6
Outputs:
- mixed: bfloat16 [16, 512, 512], P('dp')
- grad_inputs: float32 [16, 512, 512], P('dp')
- grad_memory: float32 [16, 512, 512], P(None, 'dp', 'mp')
- grad_norm_gain: float32 [3, 512], replicated
- grad_norm_bias: float32 [3, 512], replicated
- grad_self_qkv: float32 [3, 512, 512], P(None, None, 'mp')
- grad_self_bias: float32 [2, 512], P(None, 'mp')
- grad_self_out: float32 [512, 512], P('mp')
- grad_cross_q: float32 [512, 512], P(None, 'mp')
- grad_cross_kv: float32 [2, 512, 512], P(None, None, 'mp')
- grad_cross_bias: float32 [2, 512], P(None, 'mp')
- grad_cross_out: float32 [512, 512], P('mp')
- grad_ffn_in: float32 [512, 2048], P(None, 'mp')
- grad_ffn_bias: float32 [2048], P('mp')
- grad_ffn_out: float32 [2048, 512], P('mp')
- grad_out_bias: float32 [3, 512], replicated
The draws below stay inside these ranges and needn't reach their ends.
Inputs may be any that keep to these rules, and one draw needn't show every extreme that they name: `segment_ids`: each row holds 8 target molecules, numbered 0 to 7 in order, each of 1 to 128 tokens, one of exactly 128. `mem_lengths`: the token counts of a row's 8 source molecules in its memory, in order, summing to 512; target molecule k reads source molecule k; the longest is exactly 128.
All inputs are finite; a program needn't handle non-finite values.
Results may differ from the reference program's by a relative error of at most 0.02.
Values may be sent and summed in bfloat16 or wider, within the bound.
No kernel may reach another device: no remote copies, remote signals or barrier semaphores. Data moves between devices by JAX's collectives and lax.ppermute only.
A program may use at most 64 MiB of HBM per device.

```python
import math
import jax
import jax.numpy as jnp
import numpy as np
from jax import lax

D = 512
HEADS = 8
HDIM = 64
FF = 2048
SEQ = 512
MLEN = 512
MOLS = 8
MOST = 128
GROUPS = 6
ROWS_DEV = 2
ROWS = 16
N_DP = 8


def plant(values, rng, smallest, high):
    longest = values.shape.index(max(values.shape))
    spots = []
    for shift in (0, 1):
        where = [jax.random.randint(jax.random.fold_in(rng, axis), (), 0, length) for axis, length in enumerate(values.shape)]
        where[longest] = (where[longest] + shift) % values.shape[longest]
        spots.append(tuple(where))
    return values.at[spots[0]].set(smallest).at[spots[1]].set(high)


def block_levels(own_key, shape, split, smallest, top_value):
    loudness = 1.0
    for dim, blocks in split:
        heights = jax.random.uniform(jax.random.fold_in(jax.random.fold_in(own_key, 6), dim), (blocks,), jnp.float32, smallest / len(split), top_value / len(split))
        loudness = loudness * jnp.repeat(jnp.exp(heights), shape[dim] // blocks).reshape((-1,) + (1,) * (len(shape) - 1 - dim))
    return loudness


def profile(number_of, total, reach, skew):
    portions = [(1 << 20) // math.isqrt(rank ** skew) + 1 for rank in range(2, number_of + 1)]
    surplus, given = total - reach - (number_of - 1), [1] * (number_of - 1)
    while surplus > 0:
        movable = [i for i in range(number_of - 1) if given[i] < reach]
        whole, left = sum([portions[i] for i in movable]), surplus
        for i in movable:
            more = min(reach - given[i], max(1, left * portions[i] // whole), surplus)
            given[i] = given[i] + more
            surplus = surplus - more
    return np.array([reach] + given)


def ragged(key, number_of, total, reach, lean):
    if number_of == 2:
        one = jax.random.randint(key, (), max(1, total - reach), min(reach, total - 1) + 1)
        return jnp.stack([one, total - one])
    sizes = jnp.asarray(profile(number_of, total, reach, lean), jnp.int32)
    pairs = (number_of - 1) // 2
    giver, sink = sizes[1:1 + 2 * pairs:2], sizes[2:2 + 2 * pairs:2]
    room = jnp.minimum(giver - 1, reach - sink)
    moved = jax.random.randint(jax.random.fold_in(key, 1), (pairs,), 0, 1 << 20) % (room + 1)
    sizes = sizes.at[1:1 + 2 * pairs:2].set(giver - moved).at[2:2 + 2 * pairs:2].set(sink + moved)
    return sizes[jax.random.permutation(jax.random.fold_in(key, 2), number_of)]


def centred(stream_key, shape, scale, bound, cuts=(), held_as=jnp.bfloat16):
    gain = block_levels(stream_key, shape, cuts, -0.22, 0.18) if cuts else 1.0
    values = jax.random.normal(stream_key, shape, jnp.float32) * scale * gain
    return jnp.minimum(jnp.maximum(values, -bound), bound).astype(held_as)


def setup_inputs(seed: int = 0) -> dict:
    streams_of = jax.random.split(jax.random.key(seed), 21)
    return {
        "inputs": centred(streams_of[0], (ROWS, SEQ, D), 1.0, 6.0, ((0, 8),)),
        "memory": centred(streams_of[1], (ROWS, MLEN, D), 1.0, 6.0, ((1, 8),)),
        "segment_ids": jax.vmap(lambda own: jnp.searchsorted(jnp.cumsum(ragged(own, MOLS, SEQ, MOST, 1)), jnp.arange(SEQ), side="right"))(jax.random.split(streams_of[2], ROWS)).reshape((ROWS, SEQ)).astype(jnp.int32),
        "mem_lengths": jax.vmap(lambda own: ragged(own, MOLS, MLEN, MOST, 1))(jax.random.split(streams_of[3], ROWS)).reshape((ROWS, MOLS)).astype(jnp.int32),
        "bucket_group": plant(jax.random.randint(streams_of[4], (N_DP,), 0, GROUPS), jax.random.fold_in(streams_of[4], 1), 0, GROUPS - 1).astype(jnp.int32),
        "group_tokens": plant(jax.random.randint(streams_of[5], (GROUPS,), 64, 1024), jax.random.fold_in(streams_of[5], 1), 64, 1023).astype(jnp.int32),
        "norm_gain": jnp.clip(1.0 + 0.1 * jax.random.normal(streams_of[6], (3, D), jnp.float32), 0.5, 1.5).astype(jnp.bfloat16),
        "norm_bias": centred(streams_of[7], (3, D), 0.3, 3.0),
        "self_qkv": centred(streams_of[8], (3, D, D), D ** -0.5, 0.25, ((2, 4),)),
        "self_bias": centred(streams_of[9], (2, D), 0.5, 3.0, ((1, 4),)),
        "self_out": centred(streams_of[10], (D, D), (D // 8) ** -0.5, 0.75, ((0, 4),)),
        "cross_q": centred(streams_of[11], (D, D), D ** -0.5, 0.25, ((1, 4),)),
        "cross_kv": centred(streams_of[12], (2, D, D), D ** -0.5, 0.25, ((2, 4),)),
        "cross_bias": centred(streams_of[13], (2, D), 0.5, 3.0, ((1, 4),)),
        "cross_out": centred(streams_of[14], (D, D), (D // 8) ** -0.5, 0.75, ((0, 4),)),
        "ffn_in": centred(streams_of[15], (D, FF), D ** -0.5, 0.25, ((1, 4),)),
        "ffn_bias": centred(streams_of[16], (FF,), 0.5, 3.0, ((0, 4),)),
        "ffn_out": centred(streams_of[17], (FF, D), FF ** -0.5, 0.125, ((0, 4),)),
        "out_bias": centred(streams_of[18], (3, D), 0.3, 3.0),
        "cotangent": centred(streams_of[19], (ROWS, SEQ, D), 1.0, 6.0, ((0, 8),)),
    }


EPSILON = 1e-05
HIGHEST = lax.Precision.HIGHEST

@jax.custom_vjp
def low(v):
    return lax.optimization_barrier(v.astype(jnp.bfloat16)).astype(jnp.float32)

@jax.custom_vjp
def low_back(v):
    return v

def low_keep(v):
    return (low(v), None)

def low_pass(kept, grad):
    return (grad,)

def back_keep(v):
    return (v, None)

def back_low(kept, grad):
    return (low(grad),)
low.defvjp(low_keep, low_pass)
low_back.defvjp(back_keep, back_low)

def both_ways(value):
    return low_back(low(value))

def layer_norm(value, gains, shifts):
    centre = value - lax.optimization_barrier(jnp.mean(value, axis=-1, keepdims=True))
    spread = lax.optimization_barrier(jnp.mean(centre * centre, axis=-1, keepdims=True))
    return centre * lax.rsqrt(spread + EPSILON) * gains + shifts

def project(value, matrix):
    return jnp.einsum('rsd,df->rsf', value, matrix, precision=HIGHEST)

def split_heads(value):
    return value.reshape(value.shape[0], value.shape[1], HEADS, HDIM)

def attend(queries, keyset, values, allowed):
    scores = jnp.einsum('rshe,rkhe->rhsk', split_heads(queries), split_heads(keyset), precision=HIGHEST)
    scores = low_back(scores * 0.125)
    scores = jnp.where(allowed[:, None], scores, -1e+30)
    maxima = lax.optimization_barrier(jnp.max(scores, axis=-1, keepdims=True))
    raised = jnp.exp(scores - maxima)
    chances = low(raised / lax.optimization_barrier(jnp.sum(raised, axis=-1, keepdims=True)))
    mixed_heads = jnp.einsum('rhsk,rkhe->rshe', chances, split_heads(values), precision=HIGHEST)
    return both_ways(mixed_heads.reshape(queries.shape))

def decoder_layer(inputs, memory, segments, lengths, layer_params):
    gains, shifts, self_qkv, self_bias, self_out, cross_q, cross_kv, cross_bias, cross_out, ffn_in, ffn_bias, ffn_out, out_bias = layer_params
    places = jnp.arange(SEQ)
    mem_places = jnp.arange(MLEN)
    ends = jnp.cumsum(lengths, axis=-1, dtype=jnp.int32)
    mem_segments = lax.optimization_barrier(jnp.sum((ends[:, None, :] <= mem_places[None, :, None]).astype(jnp.int32), axis=-1))
    causal = places[:, None] >= places[None, :]
    self_mask = (segments[:, :, None] == segments[:, None, :]) & causal[None]
    cross_mask = segments[:, :, None] == mem_segments[:, None, :]
    normed = low(layer_norm(inputs, gains[0], shifts[0]))
    queries = both_ways(project(normed, self_qkv[0]) + self_bias[0])
    keyset = both_ways(project(normed, self_qkv[1]))
    values = both_ways(project(normed, self_qkv[2]) + self_bias[1])
    attended = attend(queries, keyset, values, self_mask)
    after_self = inputs + low_back(project(attended, self_out)) + out_bias[0]
    normed = low(layer_norm(after_self, gains[1], shifts[1]))
    cross_queries = both_ways(project(normed, cross_q) + cross_bias[0])
    cross_keys = both_ways(project(memory, cross_kv[0]))
    cross_values = both_ways(project(memory, cross_kv[1]) + cross_bias[1])
    attended = attend(cross_queries, cross_keys, cross_values, cross_mask)
    after_cross = after_self + low_back(project(attended, cross_out)) + out_bias[1]
    normed = low(layer_norm(after_cross, gains[2], shifts[2]))
    hidden = low_back(project(normed, ffn_in) + ffn_bias)
    active = low(jax.nn.gelu(hidden, approximate=False))
    return after_cross + low_back(project(active, ffn_out)) + out_bias[2]

def reference(inputs, memory, segment_ids, mem_lengths, bucket_group, group_tokens, norm_gain, norm_bias, self_qkv, self_bias, self_out, cross_q, cross_kv, cross_bias, cross_out, ffn_in, ffn_bias, ffn_out, out_bias, cotangent):
    weights = (norm_gain, norm_bias, self_qkv, self_bias, self_out, cross_q, cross_kv, cross_bias, cross_out, ffn_in, ffn_bias, ffn_out, out_bias)
    layer_params = tuple((item.astype(jnp.float32) for item in weights))
    counts = group_tokens[bucket_group].astype(jnp.float32)
    row_scale = jnp.repeat(N_DP * counts / jnp.sum(counts), ROWS_DEV)
    block_rows = 8
    blocks = ROWS_DEV * N_DP // block_rows

    def forward(activations, memory_all, params_all):

        def one_block(carry, pieces):
            part_in, part_mem, part_seg, part_len = pieces
            result = jax.checkpoint(decoder_layer)(part_in, part_mem, part_seg, part_len, params_all)
            return (carry, result)
        _, outputs = lax.scan(one_block, None, (activations.reshape(blocks, block_rows, SEQ, D), memory_all.reshape(blocks, block_rows, MLEN, D), segment_ids.reshape(blocks, block_rows, SEQ), mem_lengths.reshape(blocks, block_rows, MOLS)))
        return outputs.reshape(blocks * block_rows, SEQ, D)
    result, pullback = jax.vjp(forward, inputs.astype(jnp.float32), memory.astype(jnp.float32), layer_params)
    grad_in, grad_mem, grads = pullback(cotangent.astype(jnp.float32) * row_scale[:, None, None])
    return (result.astype(jnp.bfloat16), grad_in, grad_mem, grads[0], grads[1], grads[2], grads[3], grads[4], grads[5], grads[6], grads[7], grads[8], grads[9], grads[10], grads[11], grads[12])
```

```python
import jax
import jax.numpy as jnp
from jax import lax
from jax.sharding import PartitionSpec as P

HDIM = 64
EPSILON = 1e-05
F32 = jnp.float32
BF16 = jnp.bfloat16


def norm_parts(value):
    centre = value - jnp.mean(value, axis=-1, keepdims=True)
    spread = jnp.mean(centre * centre, axis=-1, keepdims=True)
    scale = lax.rsqrt(spread + EPSILON)
    return centre * scale, scale


def norm_backward(value, gain, incoming):
    xhat, scale = norm_parts(value)
    weighted = incoming * gain
    grad = scale * (
        weighted
        - jnp.mean(weighted, axis=-1, keepdims=True)
        - xhat * jnp.mean(weighted * xhat, axis=-1, keepdims=True)
    )
    return grad, jnp.sum(incoming * xhat, axis=0), jnp.sum(incoming, axis=0)


def dot(left, right):
    return lax.dot_general(left, right, (((1,), (0,)), ((), ())), preferred_element_type=F32)


def dot_right(left, right):
    return lax.dot_general(left, right, (((1,), (1,)), ((), ())), preferred_element_type=F32)


def dot_left(left, right):
    return lax.dot_general(left, right, (((0,), (0,)), ((), ())), preferred_element_type=F32)


def split_heads(value):
    return value.reshape(value.shape[0], value.shape[1] // HDIM, HDIM)


def masked_scores(queries, keyset, allowed):
    scores = jnp.einsum("she,khe->hsk", queries, keyset, preferred_element_type=F32) * 0.125
    return jnp.where(allowed[None], scores, -1e30)


def attend_forward(queries, keyset, values, allowed):
    shape = queries.shape
    queries, keyset, values = split_heads(queries), split_heads(keyset), split_heads(values)
    scores = masked_scores(queries, keyset, allowed)
    maxima = jnp.max(scores, axis=-1, keepdims=True)
    raised = jnp.exp(scores - maxima)
    totals = jnp.sum(raised, axis=-1, keepdims=True)
    chances = (raised / totals).astype(BF16)
    heads = jnp.einsum("hsk,khe->she", chances, values, preferred_element_type=F32)
    return heads.astype(BF16).reshape(shape), (maxima + jnp.log(totals))[..., 0]


def attend_backward(queries, keyset, values, allowed, log_total, grad_heads):
    shape = queries.shape
    queries, keyset, values = split_heads(queries), split_heads(keyset), split_heads(values)
    grad_heads = split_heads(grad_heads)
    scores = masked_scores(queries, keyset, allowed)
    chances = jnp.exp(scores - log_total[..., None])
    grad_values = jnp.einsum("hsk,she->khe", chances.astype(BF16), grad_heads, preferred_element_type=F32)
    grad_chances = jnp.einsum("she,khe->hsk", grad_heads, values, preferred_element_type=F32)
    grad_scores = chances * (grad_chances - jnp.sum(chances * grad_chances, axis=-1, keepdims=True))
    grad_scores = grad_scores.astype(BF16)
    grad_queries = jnp.einsum("hsk,khe->she", grad_scores, keyset, preferred_element_type=F32) * 0.125
    grad_keys = jnp.einsum("hsk,she->khe", grad_scores, queries, preferred_element_type=F32) * 0.125
    return tuple(g.astype(BF16).reshape(shape) for g in (grad_queries, grad_keys, grad_values))


def shards(
    inputs,
    memory,
    segment_ids,
    mem_lengths,
    bucket_group,
    group_tokens,
    norm_gain,
    norm_bias,
    self_qkv,
    self_bias,
    self_out,
    cross_q,
    cross_kv,
    cross_bias,
    cross_out,
    ffn_in,
    ffn_bias,
    ffn_out,
    out_bias,
    cotangent,
):
    dp, mp = lax.axis_size("dp"), lax.axis_size("mp")
    rows, seq, width = inputs.shape
    team = mp // rows
    data, place = lax.axis_index("dp"), lax.axis_index("mp")
    row, seat = place // team, place % team
    across = [(i, (i + team) % mp) for i in range(mp)]

    def own_row(value):
        return lax.dynamic_index_in_dim(value, row, 0, keepdims=False)

    def other(value):
        return lax.ppermute(value, "mp", across)

    def seat_swap(value, step):
        return lax.ppermute(value, "mp", [(i, i ^ step) for i in range(mp)])

    def data_swap(value, step):
        return lax.ppermute(value, "dp", [(i, i ^ step) for i in range(dp)])

    def team_sum(value):
        step = 1
        while step < team:
            low = value.astype(BF16)
            value = low.astype(F32) + seat_swap(low, step).astype(F32)
            step *= 2
        return value

    def team_scatter(value, axis):
        step = team // 2
        while step:
            half = value.shape[axis] // 2
            bit = (seat // step) % 2
            mine = lax.dynamic_slice_in_dim(value, bit * half, half, axis)
            rest = lax.dynamic_slice_in_dim(value, (1 - bit) * half, half, axis)
            value = mine.astype(F32) + seat_swap(rest.astype(BF16), step).astype(F32)
            step //= 2
        return value

    def team_gather(value):
        step = 1
        while step < team:
            got = seat_swap(value, step)
            bit = (seat // step) % 2
            value = jnp.where(bit == 0, jnp.concatenate([value, got]), jnp.concatenate([got, value]))
            step *= 2
        return value

    def both_rows(value):
        part = value.shape[0] // team
        got = team_gather(other(lax.dynamic_slice_in_dim(value, seat * part, part, 0)))
        return jnp.where(row == 0, jnp.stack([value, got]), jnp.stack([got, value]))

    def data_sum(value):
        step = 1
        while step < dp:
            half = value.shape[0] // 2
            bit = (data // step) % 2
            mine = lax.dynamic_slice_in_dim(value, bit * half, half, 0)
            rest = lax.dynamic_slice_in_dim(value, (1 - bit) * half, half, 0)
            value = mine + data_swap(rest.astype(BF16), step).astype(F32)
            step *= 2
        value = value.astype(BF16)
        while step > 1:
            step //= 2
            got = data_swap(value, step)
            bit = (data // step) % 2
            value = jnp.where(bit == 0, jnp.concatenate([value, got]), jnp.concatenate([got, value]))
        return value.astype(F32)

    def reduce_group(pieces):
        own = jnp.concatenate([p[: p.shape[0] // 2] for p in pieces])
        rest = jnp.concatenate([p[p.shape[0] // 2 :] for p in pieces]).astype(BF16)
        return data_sum(own.astype(BF16).astype(F32) + other(rest).astype(F32))

    def columns(value):
        return jnp.concatenate([value, other(value)], axis=-1)

    def stacked(value):
        return jnp.concatenate([value, other(value)], axis=0)

    group_count = group_tokens.shape[0]
    picked = bucket_group[:, None] == jnp.arange(group_count)[None, :]
    bucket_tokens = jnp.sum(jnp.where(picked, group_tokens[None, :], 0), axis=1).astype(F32)
    own_tokens = jnp.sum(jnp.where(jnp.arange(dp) == data, bucket_tokens, 0.0))
    row_scale = dp * own_tokens / jnp.sum(bucket_tokens)
    gains = norm_gain.astype(F32)
    shifts = norm_bias.astype(F32)
    biases = out_bias.astype(F32)

    segments = own_row(segment_ids)
    lengths = own_row(mem_lengths)
    mem_len = memory.shape[1] * dp
    places = jnp.arange(seq)
    self_mask = (segments[:, None] == segments[None, :]) & (places[:, None] >= places[None, :])
    ends = jnp.cumsum(lengths, dtype=jnp.int32)
    mem_segments = jnp.sum((ends[None, :] <= jnp.arange(mem_len)[:, None]).astype(jnp.int32), axis=-1)
    cross_mask = segments[:, None] == mem_segments[None, :]

    w_qkv = columns(self_qkv)
    b_self = columns(self_bias).astype(F32)
    w_self_out = stacked(self_out)
    memory_part = lax.dynamic_index_in_dim(memory.reshape((dp, rows) + memory.shape[1:]), row, 1, keepdims=False)
    memory_row = lax.all_to_all(memory_part, "dp", split_axis=0, concat_axis=0, tiled=True).reshape(mem_len, width)
    w_cross_q = columns(cross_q)
    w_cross_kv = columns(cross_kv)
    b_cross = columns(cross_bias).astype(F32)
    w_cross_out = stacked(cross_out)
    w_in = columns(ffn_in)
    b_in = columns(ffn_bias).astype(F32)
    w_out = stacked(ffn_out)

    resid = own_row(inputs).astype(F32)
    normed_self = (norm_parts(resid)[0] * gains[0] + shifts[0]).astype(BF16)
    queries = (dot(normed_self, w_qkv[0]) + b_self[0]).astype(BF16)
    keyset = dot(normed_self, w_qkv[1]).astype(BF16)
    values = (dot(normed_self, w_qkv[2]) + b_self[1]).astype(BF16)
    self_heads, self_total = attend_forward(queries, keyset, values, self_mask)
    after_self = resid + team_sum(dot(self_heads, w_self_out)) + biases[0]

    cross_keys = dot(memory_row, w_cross_kv[0]).astype(BF16)
    cross_values = (dot(memory_row, w_cross_kv[1]) + b_cross[1]).astype(BF16)
    normed_cross = (norm_parts(after_self)[0] * gains[1] + shifts[1]).astype(BF16)
    cross_queries = (dot(normed_cross, w_cross_q) + b_cross[0]).astype(BF16)
    cross_heads, cross_total = attend_forward(cross_queries, cross_keys, cross_values, cross_mask)
    after_cross = after_self + team_sum(dot(cross_heads, w_cross_out)) + biases[1]

    normed_ffn = (norm_parts(after_cross)[0] * gains[2] + shifts[2]).astype(BF16)
    hidden = dot(normed_ffn, w_in) + b_in
    cdf = 0.5 * (1.0 + lax.erf(hidden * 0.7071067811865476))
    active = (hidden * cdf).astype(BF16)
    grad_result = own_row(cotangent).astype(F32) * row_scale
    low_ffn = grad_result.astype(BF16)
    slope = cdf + hidden * (0.3989422804014327 * jnp.exp(-0.5 * hidden * hidden))
    grad_hidden = (slope * dot_right(low_ffn, w_out)).astype(BF16)
    grad_normed = team_sum(dot_right(grad_hidden, w_in))
    result = after_cross + team_sum(dot(active, w_out)) + biases[2]
    mixed = both_rows(result.astype(BF16))
    ffn_group = [dot_left(grad_hidden, normed_ffn), dot_left(active, low_ffn)]
    grad_ffn_bias = jnp.sum(grad_hidden.astype(F32), axis=0)
    back, gain_ffn, shift_ffn = norm_backward(after_cross, gains[2], grad_normed)
    grad_cross = grad_result + back
    ffn_sum = reduce_group(ffn_group)

    low_cross = grad_cross.astype(BF16)
    grad_heads = dot_right(low_cross, w_cross_out).astype(BF16)
    grad_cq, grad_ck, grad_cv = attend_backward(
        cross_queries, cross_keys, cross_values, cross_mask, cross_total, grad_heads
    )
    grad_normed = team_sum(dot_right(grad_cq, w_cross_q))
    cross_group = [
        dot_left(grad_cq, normed_cross),
        dot_left(grad_ck, memory_row),
        dot_left(grad_cv, memory_row),
        dot_left(cross_heads, low_cross),
    ]
    grad_cross_bias = jnp.stack([jnp.sum(g.astype(F32), axis=0) for g in (grad_cq, grad_cv)])
    back, gain_cross, shift_cross = norm_backward(after_self, gains[1], grad_normed)
    grad_self = grad_cross + back
    cross_sum = reduce_group(cross_group)

    low_self = grad_self.astype(BF16)
    grad_heads = dot_right(low_self, w_self_out).astype(BF16)
    grad_q, grad_k, grad_v = attend_backward(queries, keyset, values, self_mask, self_total, grad_heads)
    grad_normed = team_sum(dot_right(grad_q, w_qkv[0]) + dot_right(grad_k, w_qkv[1]) + dot_right(grad_v, w_qkv[2]))
    self_group = [
        dot_left(grad_q, normed_self),
        dot_left(grad_k, normed_self),
        dot_left(grad_v, normed_self),
        dot_left(self_heads, low_self),
    ]
    grad_self_bias = jnp.stack([jnp.sum(g.astype(F32), axis=0) for g in (grad_q, grad_v)])
    self_sum = reduce_group(self_group)
    back, gain_self, shift_self = norm_backward(resid, gains[0], grad_normed)
    grad_inputs = both_rows((grad_self + back).astype(BF16)).astype(F32)

    memory_terms = dot_right(grad_ck, w_cross_kv[0]) + dot_right(grad_cv, w_cross_kv[1])
    part = width // mp
    by_row = memory_terms.reshape(mem_len, rows, team * part)
    by_seat = team_scatter(by_row, 2).astype(BF16)
    kept = lax.dynamic_index_in_dim(by_seat, row, 1, keepdims=False)
    sent = lax.dynamic_index_in_dim(by_seat, 1 - row, 1, keepdims=False)
    got = other(sent)
    pair = jnp.where(row == 0, jnp.stack([kept, got]), jnp.stack([got, kept]))
    pair = pair.reshape(rows, dp, mem_len // dp, part).swapaxes(0, 1)
    grad_memory = lax.all_to_all(pair, "dp", split_axis=0, concat_axis=0, tiled=True)
    grad_memory = grad_memory.reshape(dp * rows, mem_len // dp, part).astype(F32)

    common = jnp.concatenate(
        [
            gain_self, gain_cross, gain_ffn,
            shift_self, shift_cross, shift_ffn,
            jnp.sum(grad_self, axis=0), jnp.sum(grad_cross, axis=0), jnp.sum(grad_result, axis=0),
        ]
    )
    head, unit = self_bias.shape[1], ffn_bias.shape[0]
    shard_small = [
        jnp.concatenate([grad_self_bias[:, k * head : (k + 1) * head].reshape(-1),
                         grad_cross_bias[:, k * head : (k + 1) * head].reshape(-1),
                         grad_ffn_bias[k * unit : (k + 1) * unit]])
        for k in (0, 1)
    ]
    got = other(jnp.concatenate([common, shard_small[1]]))
    small = lax.psum(jnp.concatenate([common, shard_small[0]]) + got, "dp")
    common, own_small = small[: common.shape[0]].reshape(3, 3, width), small[common.shape[0] :]

    grad_self_bias = own_small[: 2 * head].reshape(2, head)
    grad_cross_bias = own_small[2 * head : 4 * head].reshape(2, head)
    grad_ffn_bias = own_small[4 * head :]
    self_parts = self_sum.reshape(4, head, width)
    cross_parts = cross_sum.reshape(4, head, width)
    ffn_parts = ffn_sum.reshape(2, unit, width)
    return (
        mixed,
        grad_inputs,
        grad_memory,
        common[0],
        common[1],
        self_parts[:3].swapaxes(1, 2),
        grad_self_bias,
        self_parts[3],
        cross_parts[0].T,
        cross_parts[1:3].swapaxes(1, 2),
        grad_cross_bias,
        cross_parts[3],
        ffn_parts[0].T,
        grad_ffn_bias,
        ffn_parts[1],
        common[2],
    )


def solution(mesh):
    placed = (
        P("dp", None, None),
        P(None, "dp", None),
        P("dp", None),
        P("dp", None),
        P(),
        P(),
        P(),
        P(),
        P(None, None, "mp"),
        P(None, "mp"),
        P("mp", None),
        P(None, "mp"),
        P(None, None, "mp"),
        P(None, "mp"),
        P("mp", None),
        P(None, "mp"),
        P("mp"),
        P("mp", None),
        P(),
        P("dp", None, None),
    )
    return jax.shard_map(
        shards,
        mesh=mesh,
        in_specs=placed,
        out_specs=(
            P("dp", None, None),
            P("dp", None, None),
            P(None, "dp", "mp"),
            P(),
            P(),
            P(None, None, "mp"),
            P(None, "mp"),
            P("mp", None),
            P(None, "mp"),
            P(None, None, "mp"),
            P(None, "mp"),
            P("mp", None),
            P(None, "mp"),
            P("mp"),
            P("mp", None),
            P(),
        ),
        check_vma=False,
    )
```

```python
import functools

import jax
import jax.numpy as jnp
from jax import lax
from jax.experimental import pallas as pl
from jax.experimental.pallas import tpu as pltpu
from jax.sharding import PartitionSpec as P

HDIM = 64
LANES = 128
BLOCK = 128
SMALL = 16
EPSILON = 1e-05
F32 = jnp.float32
BF16 = jnp.bfloat16


def dot(left, right):
    return lax.dot_general(left, right, (((1,), (0,)), ((), ())), preferred_element_type=F32)


def dot_right(left, right):
    return lax.dot_general(left, right, (((1,), (1,)), ((), ())), preferred_element_type=F32)


def dot_left(left, right):
    return lax.dot_general(left, right, (((0,), (0,)), ((), ())), preferred_element_type=F32)


class Far:
    def __init__(self, value, pick=False):
        self.value, self.pick = value, pick


class Scalars:
    def __init__(self, value):
        self.value = value


class Flow:
    def __init__(self):
        self.loads, self.stores, self.sent = {}, {}, []

    def need(self, *refs):
        for ref in refs:
            copy = self.loads.pop(id(ref), None)
            if copy is not None:
                copy.wait()

    def send(self, *refs):
        for ref in refs:
            copy = self.stores.pop(id(ref), None)
            if copy is not None:
                copy.start()
                self.sent.append(copy)


class Steps:
    def __init__(self, where):
        self.where, self.token = where, None

    def __call__(self, kernel, ins, outs, scratch=(), name=None):
        near = pl.BlockSpec(memory_space=pltpu.VMEM)
        far = pl.BlockSpec(memory_space=pltpu.HBM)
        words = pl.BlockSpec(memory_space=pltpu.SMEM)
        values, specs, stages = [], [], []
        for v in ins:
            if isinstance(v, Scalars):
                values.append(v.value)
                specs.append(words)
            elif isinstance(v, Far):
                values.append(pltpu.with_memory_space_constraint(v.value, pltpu.HBM))
                specs.append(far)
                stages.append(pltpu.VMEM(v.value.shape[1:] if v.pick else v.value.shape, v.value.dtype))
            else:
                values.append(pltpu.with_memory_space_constraint(v, pltpu.VMEM))
                specs.append(near)
        after = [] if self.token is None else [pltpu.with_memory_space_constraint(self.token, pltpu.HBM)]
        for v in outs:
            if isinstance(v, Far):
                stages.append(pltpu.VMEM(*v.value))
        shapes = [pltpu.HBM(*v.value) if isinstance(v, Far) else pltpu.VMEM(*v) for v in outs]
        count, n_in, n_out, n_after = len(stages), len(ins), len(outs), len(after)

        def body(where_ref, *refs):
            refs = list(refs)
            in_refs, refs = refs[:n_in], refs[n_in + n_after :]
            out_refs, refs = refs[:n_out], refs[n_out + 1 :]
            stage_refs, refs = refs[:count], refs[count:]
            flow = Flow()
            if count:
                sems, refs = refs[0], refs[1:]
            given, k = [], 0
            for v, ref in zip(ins, in_refs):
                if isinstance(v, Far):
                    source = ref.at[where_ref[0]] if v.pick else ref
                    copy = pltpu.make_async_copy(source, stage_refs[k], sems.at[k])
                    copy.start()
                    flow.loads[id(stage_refs[k])] = copy
                    ref, k = stage_refs[k], k + 1
                given.append(ref)
            for v, ref in zip(outs, out_refs):
                if isinstance(v, Far):
                    flow.stores[id(stage_refs[k])] = pltpu.make_async_copy(stage_refs[k], ref, sems.at[k])
                    ref, k = stage_refs[k], k + 1
                given.append(ref)
            kernel(flow, where_ref, *given, *refs)
            for copy in flow.loads.values():
                copy.wait()
            for copy in flow.stores.values():
                copy.start()
            for copy in [*flow.sent, *flow.stores.values()]:
                copy.wait()

        results = pl.pallas_call(
            body,
            in_specs=[words] + specs + [far] * n_after,
            out_specs=[far if isinstance(v, Far) else near for v in outs] + [far],
            out_shape=shapes + [pltpu.HBM((8, LANES), F32)],
            scratch_shapes=stages + ([pltpu.SemaphoreType.DMA((count,))] if count else []) + list(scratch),
            compiler_params=pltpu.CompilerParams(vmem_limit_bytes=24 * 1024 * 1024),
            cost_estimate=pl.CostEstimate(flops=10**6, bytes_accessed=10**5, transcendentals=0),
            name=name,
        )(self.where, *values, *after)
        self.token = results[-1]
        return list(results[:-1])


def row_blocks(seq):
    return [slice(start, start + BLOCK) for start in range(0, seq, BLOCK)]


def row_of(ref, i):
    return ref[i : i + 1, :].astype(F32)


GAIN, SHIFT, OUT, SCALE, VECTORS = 0, 3, 6, 9, 16


def norm_parts(value):
    centre = value - jnp.mean(value, axis=-1, keepdims=True)
    spread = jnp.mean(centre * centre, axis=-1, keepdims=True)
    scale = lax.rsqrt(spread + EPSILON)
    return centre * scale, scale


def norm_backward(value, gain, incoming):
    xhat, scale = norm_parts(value)
    weighted = incoming * gain
    grad = scale * (
        weighted
        - jnp.mean(weighted, axis=-1, keepdims=True)
        - xhat * jnp.mean(weighted * xhat, axis=-1, keepdims=True)
    )
    return grad, jnp.sum(incoming * xhat, axis=0, keepdims=True), jnp.sum(incoming, axis=0, keepdims=True)


def head_lanes(value, j):
    lane = lax.broadcasted_iota(jnp.int32, value.shape, 1)
    return jnp.where((lane >= HDIM) == bool(j), value, jnp.zeros_like(value))


def span_of(block, seq, banded):
    if not banded:
        return slice(0, seq)
    return slice(max(block.start - BLOCK, 0), block.stop)


def setup_kernel(flow, where, group_tokens, bucket_group, lengths, segments, gains, shifts, biases, vectors, molecules):
    flow.need(segments, gains, shifts, biases)
    width = vectors.shape[1]
    total, own = 0, 0
    for b in range(bucket_group.shape[0]):
        tokens = group_tokens[bucket_group[b]]
        total = total + tokens
        own = own + jnp.where(where[2] == b, tokens, 0)
    scaled = jnp.full((1, width), bucket_group.shape[0] * own, jnp.int32).astype(F32)
    scale = scaled / jnp.full((1, width), total, jnp.int32).astype(F32)
    rows = [r[...].astype(F32) for r in (gains, shifts, biases)] + [scale]
    vectors[...] = jnp.concatenate(rows + [jnp.zeros((VECTORS - 10, width), F32)], axis=0)
    size = molecules.shape[1]
    place = lax.broadcasted_iota(jnp.int32, (1, size), 1)
    count, end = jnp.zeros((1, size), jnp.int32), 0
    for k in range(lengths.shape[1]):
        end = end + lengths[where[0], k]
        count = count + (end <= place).astype(jnp.int32)
    molecules[0:1, :] = segments[pl.ds(where[0], 1), :]
    molecules[1:2, :] = count


def allowed_of(own, keys, block, span, banded):
    column = jnp.broadcast_to(own[:, block], (LANES, BLOCK)).T
    wide = span.stop - span.start
    allowed = jnp.concatenate([column] * (wide // LANES), axis=1) == keys[:, span]
    if banded:
        query = lax.broadcasted_iota(jnp.int32, (BLOCK, wide), 0) + block.start
        key = lax.broadcasted_iota(jnp.int32, (BLOCK, wide), 1) + span.start
        allowed = allowed & (key <= query)
    return allowed


def attend_forward(q, k, v, own, keys, heads, totals, banded):
    seq, wide = q.shape
    for block in row_blocks(seq):
        span = span_of(block, k.shape[0], banded)
        allowed = allowed_of(own, keys, block, span, banded)
        lane = lax.broadcasted_iota(jnp.int32, (BLOCK, LANES), 1)
        kept = jnp.zeros((BLOCK, LANES), F32)
        for pair in range(wide // LANES):
            lanes = slice(pair * LANES, (pair + 1) * LANES)
            query, keyset, values = q[block, lanes] * 0.125, k[span, lanes], v[span, lanes]
            mixed = None
            for j in (0, 1):
                scores = jnp.where(allowed, dot_right(head_lanes(query, j), keyset), -1e30)
                maxima = jnp.max(scores, axis=-1, keepdims=True)
                raised = jnp.exp(scores - maxima)
                total = jnp.sum(raised, axis=-1, keepdims=True)
                chances = (raised * (1.0 / total)).astype(BF16)
                term = dot(chances, head_lanes(values, j))
                mixed = term if mixed is None else mixed + term
                kept = jnp.where(lane == 2 * pair + j, maxima + jnp.log(total), kept)
            heads[block, lanes] = mixed.astype(BF16)
        totals[block, :] = kept


def attend_backward(q, k, v, own, keys, totals, grad_heads, dq, dk, dv, sum_k, sum_v, banded):
    seq, wide = q.shape
    sum_k[...] = jnp.zeros_like(sum_k)
    sum_v[...] = jnp.zeros_like(sum_v)
    for block in row_blocks(seq):
        span = span_of(block, k.shape[0], banded)
        allowed = allowed_of(own, keys, block, span, banded)
        for pair in range(wide // LANES):
            lanes = slice(pair * LANES, (pair + 1) * LANES)
            query, keyset, values = q[block, lanes], k[span, lanes], v[span, lanes]
            grad = grad_heads[block, lanes]
            grad_query = grad_key = grad_value = 0.0
            for j in (0, 1):
                head = 2 * pair + j
                part = head_lanes(query, j) * 0.125
                scores = jnp.where(allowed, dot_right(part, keyset), -1e30)
                chances = jnp.exp(scores - totals[block, head : head + 1])
                own_grad = head_lanes(grad, j)
                grad_value += dot_left(chances.astype(BF16), own_grad)
                weighted = chances * dot_right(own_grad, values)
                mean = jnp.sum(weighted, axis=-1, keepdims=True)
                grad_scores = (weighted - chances * mean).astype(BF16)
                grad_query += dot(grad_scores, head_lanes(keyset, j))
                grad_key += dot_left(grad_scores, part)
            dq[block, lanes] = (grad_query * 0.125).astype(BF16)
            sum_k[span, lanes] += grad_key
            sum_v[span, lanes] += grad_value
    dk[...] = sum_k[...].astype(BF16)
    dv[...] = sum_v[...].astype(BF16)


def self_forward_kernel(n, i, flow, where, *refs):
    last = i == n - 1
    first, vectors, molecules, w, bias, refs = *refs[:5], refs[5:]
    if last:
        w_out, done, refs = refs[:n], refs[n : 2 * n - 1], refs[2 * n - 1 :]
    if i == 0:
        normed, refs = refs[0], refs[1:]
        flow.need(first)
        for block in row_blocks(first.shape[0]):
            norm = norm_parts(first[block, :].astype(F32))[0]
            normed[block, :] = (norm * row_of(vectors, GAIN) + row_of(vectors, SHIFT)).astype(BF16)
    else:
        normed = first
    q, k, v, heads, totals = refs[:5]
    flow.need(w)
    q[...] = (dot(normed[...], w[0]) + row_of(bias, 0)).astype(BF16)
    k[...] = dot(normed[...], w[1]).astype(BF16)
    v[...] = (dot(normed[...], w[2]) + row_of(bias, 1)).astype(BF16)
    own = molecules[0:1, :]
    attend_forward(q, k, v, own, own, heads, totals, True)
    if last:
        project_out(flow, [*done, heads], w_out, refs[5])


def project_out(flow, heads, w_out, part):
    flow.need(*w_out)
    for block in row_blocks(part.shape[0]):
        part[block, :] = sum(dot(h[block, :], w[...]) for h, w in zip(heads, w_out)).astype(BF16)


def memory_kernel(flow, where, memory, w, bias, k, v):
    flow.need(w)
    k[...] = dot(memory[...], w[0]).astype(BF16)
    v[...] = (dot(memory[...], w[1]) + row_of(bias, 3)).astype(BF16)


def cross_forward_kernel(n, i, flow, where, *refs):
    last = i == n - 1
    if i == 0:
        x, mine, theirs, refs = *refs[:3], refs[3:]
    else:
        normed, refs = refs[0], refs[1:]
    vectors, molecules, w, bias, k, v, refs = *refs[:6], refs[6:]
    if last:
        w_out, done, refs = refs[:n], refs[n : 2 * n - 1], refs[2 * n - 1 :]
    if i == 0:
        after_self, normed, refs = refs[0], refs[1], refs[2:]
    q, heads, totals = refs[:3]
    if i == 0:
        flow.need(x)
        for block in row_blocks(x.shape[0]):
            both = mine[block, :].astype(F32) + theirs[block, :].astype(F32)
            value = x[block, :].astype(F32) + both + row_of(vectors, OUT)
            after_self[block, :] = value
            norm = norm_parts(value)[0]
            normed[block, :] = (norm * row_of(vectors, GAIN + 1) + row_of(vectors, SHIFT + 1)).astype(BF16)
    flow.need(w)
    q[...] = (dot(normed[...], w[...]) + row_of(bias, 2)).astype(BF16)
    attend_forward(q, k, v, molecules[0:1, :], molecules[1:2, :], heads, totals, False)
    if last:
        project_out(flow, [*done, heads], w_out, refs[3])


def ffn_kernel(i, flow, where, *refs):
    if i == 0:
        after_self, mine, theirs, cotangent, vectors, w_in, bias, w_out, refs = *refs[:8], refs[8:]
        after_cross, normed, low, active, grad_hidden, part, part_grad = refs
        flow.need(cotangent)
    else:
        normed, low, begun, begun_grad, w_in, bias, w_out, refs = *refs[:7], refs[7:]
        active, grad_hidden, part, part_grad = refs
    flow.need(w_in, w_out)
    if bias.shape[0] == 1:
        row = row_of(bias, 0)
    else:
        row = jnp.concatenate([row_of(bias, k) for k in range(4, bias.shape[0])], axis=1)
    for block in row_blocks(normed.shape[0]):
        if i == 0:
            both = mine[block, :].astype(F32) + theirs[block, :].astype(F32)
            value = after_self[block, :] + both + row_of(vectors, OUT + 1)
            after_cross[block, :] = value
            norm = norm_parts(value)[0]
            norm = (norm * row_of(vectors, GAIN + 2) + row_of(vectors, SHIFT + 2)).astype(BF16)
            normed[block, :] = norm
            grad = (cotangent[block, :].astype(F32) * row_of(vectors, SCALE)).astype(BF16)
            low[block, :] = grad
        else:
            norm, grad = normed[block, :], low[block, :]
        hidden = dot(norm, w_in[...]) + row
        cdf = 0.5 * (1.0 + lax.erf(hidden * 0.7071067811865476))
        act = (hidden * cdf).astype(BF16)
        active[block, :] = act
        slope = cdf + hidden * (0.3989422804014327 * jnp.exp(-0.5 * hidden * hidden))
        back = (slope * dot_right(grad, w_out[...])).astype(BF16)
        grad_hidden[block, :] = back
        out, out_grad = dot(act, w_out[...]), dot_right(back, w_in[...])
        if i == 0:
            part[block, :], part_grad[block, :] = out, out_grad
        else:
            part[block, :] = (begun[block, :] + out).astype(BF16)
            part_grad[block, :] = (begun_grad[block, :] + out_grad).astype(BF16)


def ffn_weights_kernel(flow, where, *refs):
    hidden, active, normed, low, sums = refs[:2], refs[2:4], refs[4], refs[5], refs[6]
    keep_out, send_out, keep_in, send_in = refs[7:]
    half = keep_in.shape[1]
    for i in (0, 1):
        for target, bit in ((keep_in, where[3]), (send_in, 1 - where[3])):
            lanes = pl.ds(pl.multiple_of(bit * half, half), half)
            target[i] = dot_left(hidden[i][:, lanes], normed[...]).astype(target.dtype)
        sums[i : i + 1, :] = jnp.sum(hidden[i][...].astype(F32), axis=0, keepdims=True)
    keep_out[0] = dot_left(active[0][...], low[...])
    send_out[0] = dot_left(active[1][...], low[...]).astype(BF16)


def spread_grad_heads(low, w_out, grad_heads):
    for piece, target in zip(w_out, grad_heads):
        target[...] = dot_right(low[...], piece[...]).astype(BF16)


def column_sums(sums, values):
    for i, value in enumerate(values):
        sums[i : i + 1, :] = jnp.sum(value[...].astype(F32), axis=0, keepdims=True)


def cross_backward_kernel(n, flow, where, *refs):
    after_cross, mine, theirs, cotangent, vectors, molecules, refs = *refs[:6], refs[6:]
    (q, k, v, totals, w_out, w), refs = [refs[i * n : (i + 1) * n] for i in range(6)], refs[6 * n :]
    grad_cross, low, refs = refs[0], refs[1], refs[2:]
    (dq, dk, dv, bias_sums), refs = [refs[i * n : (i + 1) * n] for i in range(4)], refs[4 * n :]
    part, sums, refs = refs[0], refs[1], refs[2:]
    grad_heads, sum_k, sum_v = refs[:n], refs[n], refs[n + 1]
    seq, width = after_cross.shape
    rows = [jnp.zeros((1, width), F32)] * 3
    flow.need(cotangent)
    for block in row_blocks(seq):
        incoming = mine[block, :].astype(F32) + theirs[block, :].astype(F32)
        grad_result = cotangent[block, :].astype(F32) * row_of(vectors, SCALE)
        back, by_gain, by_shift = norm_backward(after_cross[block, :], row_of(vectors, GAIN + 2), incoming)
        value = grad_result + back
        grad_cross[block, :] = value
        low[block, :] = value.astype(BF16)
        parts = (by_gain, by_shift, jnp.sum(grad_result, axis=0, keepdims=True))
        rows = [a + b for a, b in zip(rows, parts)]
    for i, row in enumerate(rows):
        sums[i : i + 1, :] = row
    flow.need(*w_out)
    spread_grad_heads(low, w_out, grad_heads)
    own, keys = molecules[0:1, :], molecules[1:2, :]
    for i in range(n):
        attend_backward(
            q[i], k[i], v[i], own, keys, totals[i], grad_heads[i], dq[i], dk[i], dv[i], sum_k, sum_v, False
        )
        column_sums(bias_sums[i], (dq[i], dv[i]))
    flow.need(*w)
    for block in row_blocks(seq):
        part[block, :] = sum(dot_right(d[block, :], m[...]) for d, m in zip(dq, w)).astype(BF16)


def shard_grads(kinds):
    grads = ([], [])
    for kind in kinds:
        if len(kind) == 2:
            for i in (0, 1):
                grads[i].append(dot_left(kind[i][0][...], kind[i][1][...]))
        else:
            left, right = kind[0]
            both, half = dot_left(left[...], right[...]), left.shape[1] // 2
            grads[0].append(both[:half])
            grads[1].append(both[half:])
    return grads


def cross_weights_kernel(n, flow, where, *refs):
    (dq, dk, dv, heads, w), refs = [refs[i * n : (i + 1) * n] for i in range(5)], refs[5 * n :]
    normed, memory, low, after_cross, mine, theirs, vectors, refs = *refs[:7], refs[7:]
    keep, send, terms, result, result_part = refs
    flow.need(*w)
    pairs = [[(a, b) for a in left] for left, b in ((dq, normed), (dk, memory), (dv, memory), (heads, low))]
    first = where[4] == 0
    for i, grads in enumerate(shard_grads(pairs)):
        upper, lower = jnp.concatenate(grads[:2], axis=0), jnp.concatenate(grads[2:], axis=0)
        keep[i] = jnp.where(first, upper, lower)
        send[i] = jnp.where(first, lower, upper).astype(BF16)
    for block in row_blocks(memory.shape[0]):
        total = sum(
            dot_right(a[block, :], m[0]) + dot_right(b[block, :], m[1]) for a, b, m in zip(dk, dv, w)
        )
        terms[block, :] = total.astype(BF16)
    for block in row_blocks(after_cross.shape[0]):
        both = mine[block, :].astype(F32) + theirs[block, :].astype(F32)
        result[block, :] = (after_cross[block, :] + both + row_of(vectors, OUT + 2)).astype(BF16)
    size = result_part.shape[0]
    result_part[...] = result[pl.ds(pl.multiple_of(where[1] * size, size), size), :]


def self_backward_kernel(n, flow, where, *refs):
    after_self, mine, theirs, grad_cross, vectors, molecules, refs = *refs[:6], refs[6:]
    (q, k, v, totals, w_out, w), refs = [refs[i * n : (i + 1) * n] for i in range(6)], refs[6 * n :]
    grad_self, low, refs = refs[0], refs[1], refs[2:]
    (dq, dk, dv, bias_sums), refs = [refs[i * n : (i + 1) * n] for i in range(4)], refs[4 * n :]
    part, sums, refs = refs[0], refs[1], refs[2:]
    grad_heads, sum_k, sum_v = refs[:n], refs[n], refs[n + 1]
    seq, width = after_self.shape
    rows = [jnp.zeros((1, width), F32)] * 3
    for block in row_blocks(seq):
        incoming = mine[block, :].astype(F32) + theirs[block, :].astype(F32)
        back, by_gain, by_shift = norm_backward(after_self[block, :], row_of(vectors, GAIN + 1), incoming)
        upper = grad_cross[block, :]
        value = upper + back
        grad_self[block, :] = value
        low[block, :] = value.astype(BF16)
        parts = (by_gain, by_shift, jnp.sum(upper, axis=0, keepdims=True))
        rows = [a + b for a, b in zip(rows, parts)]
    for i, row in enumerate(rows):
        sums[i : i + 1, :] = row
    flow.need(*w_out)
    spread_grad_heads(low, w_out, grad_heads)
    own = molecules[0:1, :]
    for i in range(n):
        attend_backward(
            q[i], k[i], v[i], own, own, totals[i], grad_heads[i], dq[i], dk[i], dv[i], sum_k, sum_v, True
        )
        column_sums(bias_sums[i], (dq[i], dv[i]))
    flow.need(*w)
    for block in row_blocks(seq):
        total = 0.0
        for i in range(n):
            for which, d in enumerate((dq[i], dk[i], dv[i])):
                total += dot_right(d[block, :], w[i][which])
        part[block, :] = total.astype(BF16)


def input_backward_kernel(flow, where, x, mine, theirs, grad_self, vectors, grad_inputs, inputs_part, sums):
    rows = [jnp.zeros((1, x.shape[1]), F32)] * 3
    flow.need(x)
    for block in row_blocks(x.shape[0]):
        incoming = mine[block, :].astype(F32) + theirs[block, :].astype(F32)
        back, by_gain, by_shift = norm_backward(x[block, :].astype(F32), row_of(vectors, GAIN), incoming)
        upper = grad_self[block, :]
        grad_inputs[block, :] = (upper + back).astype(BF16)
        parts = (by_gain, by_shift, jnp.sum(upper, axis=0, keepdims=True))
        rows = [a + b for a, b in zip(rows, parts)]
    for i, row in enumerate(rows):
        sums[i : i + 1, :] = row
    size = inputs_part.shape[0]
    inputs_part[...] = grad_inputs[pl.ds(pl.multiple_of(where[1] * size, size), size), :]


def self_weights_kernel(n, flow, where, *refs):
    (dq, dk, dv, heads), refs = [refs[i * n : (i + 1) * n] for i in range(4)], refs[4 * n :]
    normed, low, by_self, by_cross, by_ffn, refs = *refs[:5], refs[5:]
    shard_rows, (keep, send) = refs[:-2], refs[-2:]
    width = normed.shape[1]
    common = [r[k : k + 1, :] for k in range(3) for r in (by_self, by_cross, by_ffn)]
    if len(shard_rows) == 1:
        lines = [shard_rows[0][i] for i in (0, 1)]
    else:
        sums_self, sums_cross, sums_ffn = shard_rows[:n], shard_rows[n : 2 * n], shard_rows[2 * n]
        lines = []
        for i in (0, 1):
            pieces = [r[k : k + 1, :] for r in (sums_self[i], sums_cross[i]) for k in (0, 1)]
            lines.append(jnp.concatenate([jnp.concatenate(pieces, axis=1), sums_ffn[i : i + 1, :]], axis=0))
    rest = jnp.zeros((SMALL - 9 - lines[0].shape[0], width), F32)
    pairs = [[(a, b) for a in left] for left, b in ((dq, normed), (dk, normed), (dv, normed), (heads, low))]
    for target, grads, line in zip((keep, send), shard_grads(pairs), lines):
        small = jnp.concatenate([*common, line, rest], axis=0).astype(BF16).astype(F32)
        target[0] = jnp.concatenate([*grads, small], axis=0).astype(target.dtype)


def fold_kernel(count, small, mode, bit, flow, where, *refs):
    keeps, gots, outs = refs[:count], refs[count : 2 * count], refs[2 * count :]

    def part(k, p, rows):
        return keeps[k][p, rows, :].astype(F32) + gots[k][p, rows, :].astype(F32)

    planes = [(k, p) for k in range(count) for p in range(keeps[k].shape[0])]
    size = keeps[0].shape[1]
    main = size - small
    if mode == "half":
        keep, send = outs
        half = main // 2
        for at, (k, p) in enumerate(planes):
            for target, side in ((keep, where[3 + bit]), (send, 1 - where[3 + bit])):
                rows = pl.ds(pl.multiple_of(side * half, half), half)
                value = part(k, p, rows)
                if small:
                    tail = part(k, p, slice(main, size)).astype(BF16).astype(F32)
                    value = jnp.concatenate([value, tail], axis=0)
                target[at] = value.astype(target.dtype)
    elif mode == "shard":
        keep, send = outs
        for target, (k, p) in zip((keep, send), planes):
            target[0] = part(k, p, slice(0, size)).astype(target.dtype)
    else:
        for at, (k, p) in enumerate(planes):
            outs[0][at] = part(k, p, slice(0, main if mode == "last" else size)).astype(outs[0].dtype)
        if mode == "last" and small:
            outs[1][...] = part(*planes[0], slice(main, size))


def join_kernel(bit, flow, where, near, got, out):
    half = near.shape[1]
    for value, side in ((near, where[3 + bit]), (got, 1 - where[3 + bit])):
        rows = pl.ds(pl.multiple_of(side * half, half), half)
        for p in range(near.shape[0]):
            out[p, rows, :] = value[p]


def joined(where, bit, near, got, p):
    first = where[3 + bit] == 0
    a, b = near[p], got[p]
    rows = [jnp.where(first, a, b), jnp.where(first, b, a)]
    return jnp.concatenate(rows, axis=0).astype(F32)


def self_grads_kernel(bit, flow, where, near, got, qkv, out):
    value = joined(where, bit, near, got, 0)
    size = out.shape[0]
    for k in range(3):
        qkv[k] = value[k * size : (k + 1) * size].T
    out[...] = value[3 * size :]


def cross_grads_kernel(bit, flow, where, near, got, query, kv, out):
    value = joined(where, bit, near, got, 0)
    size = out.shape[0]
    query[...] = value[:size].T
    for k in (0, 1):
        kv[k] = value[(k + 1) * size : (k + 2) * size].T
    out[...] = value[3 * size :]


def ffn_grads_kernel(bit, flow, where, near, got, grad_in, grad_out):
    grad_out[...] = joined(where, bit, near, got, 0)
    flow.send(grad_out)
    grad_in[...] = joined(where, bit, near, got, 1).T


def place_rows_kernel(flow, where, own, near, got, out):
    kind = out.dtype
    out[where[0]] = own[...].astype(kind)
    size = near.shape[0]
    mine, theirs = near[...].astype(kind), got[...].astype(kind)
    first = where[1] == 0
    out[1 - where[0], :size, :] = jnp.where(first, mine, theirs)
    out[1 - where[0], size:, :] = jnp.where(first, theirs, mine)


def memory_blocks_kernel(flow, where, mine, theirs, out):
    dp, rows, tokens, share = out.shape
    team = mine.shape[1] // (rows * share)
    for r in range(rows):
        lanes = pl.ds(pl.multiple_of((r * team + where[1]) * share, share), share)
        total = (mine[:, lanes].astype(F32) + theirs[:, lanes].astype(F32)).astype(BF16)
        for d in range(dp):
            out[d, r] = total[d * tokens : (d + 1) * tokens]


def pack_ffn_kernel(flow, where, w_in, w_out, half_in, half_out):
    flow.need(w_in, w_out)
    for source, target in ((w_in, half_in), (w_out, half_out)):
        half = target.shape[0]
        target[...] = source[pl.ds(pl.multiple_of(where[3] * half, half), half), :]


def join_weights_kernel(flow, where, *refs):
    count = len(refs) // 3
    for near, got, out in zip(refs[:count], refs[count : 2 * count], refs[2 * count :]):
        half = near.shape[0]
        for value, bit in ((near, where[3]), (got, 1 - where[3])):
            out[pl.ds(pl.multiple_of(bit * half, half), half), :] = value[...]


def shards(
    inputs,
    memory,
    segment_ids,
    mem_lengths,
    bucket_group,
    group_tokens,
    norm_gain,
    norm_bias,
    self_qkv,
    self_bias,
    self_out,
    cross_q,
    cross_kv,
    cross_bias,
    cross_out,
    ffn_in,
    ffn_bias,
    ffn_out,
    out_bias,
    cotangent,
):
    dp, mp = lax.axis_size("dp"), lax.axis_size("mp")
    rows, seq, width = inputs.shape
    team = mp // rows
    data, place = lax.axis_index("dp"), lax.axis_index("mp")
    row, seat = place // team, place % team
    bits = dp.bit_length() - 1
    where = jnp.stack([row, seat, data] + [(data >> k) & 1 for k in range(bits)]).astype(jnp.int32)
    run, far = Steps(where), Far

    across = [(i, (i + team) % mp) for i in range(mp)]

    def other(value):
        return lax.ppermute(value, "mp", across)

    def seat_swap(value, step):
        return lax.ppermute(value, "mp", [(i, i ^ step) for i in range(mp)])

    def data_swap(value, k):
        return lax.ppermute(value, "dp", [(i, i ^ (1 << k)) for i in range(dp)])

    def swap(value, axis):
        return other(value) if axis == "row" else data_swap(value, axis)

    def later(value, *after):
        return lax.optimization_barrier((value, *after))[0]

    def team_parts(value):
        step = 1
        while 2 * step < team:
            value = (value.astype(F32) + seat_swap(value, step).astype(F32)).astype(BF16)
            step *= 2
        return value, seat_swap(value, step)

    def team_gather(value):
        step = 1
        while 2 * step < team:
            got = seat_swap(value, step)
            low = (seat // step) % 2 == 0
            value = jnp.where(low, jnp.concatenate([value, got]), jnp.concatenate([got, value]))
            step *= 2
        return value, seat_swap(value, step)

    head, unit = self_bias.shape[1], ffn_bias.shape[0]
    mem_len = memory.shape[1] * dp
    apart = head % LANES == 0
    n = 2 if apart else 1
    wide = head if apart else 2 * head

    other_qkv = other(self_qkv)
    memory_part = lax.dynamic_index_in_dim(memory.reshape((dp, rows) + memory.shape[1:]), row, 1, keepdims=False)
    memory_row = lax.all_to_all(memory_part, "dp", split_axis=0, concat_axis=0, tiled=True).reshape(mem_len, width)
    other_self_out = other(self_out)
    bias_own = jnp.concatenate([self_bias, cross_bias, ffn_bias.reshape(-1, head)])
    bias_other = other(bias_own)
    other_cross_q = other(later(cross_q, other_qkv))
    other_cross_kv = other(later(cross_kv, other_qkv))
    other_cross_out = other(later(cross_out, other_qkv))

    def pieces(own, theirs, axis):
        return [far(own), theirs] if apart else [jnp.concatenate([own, theirs], axis=axis)]

    w_qkv = pieces(self_qkv, other_qkv, 2)
    w_self_out = pieces(self_out, other_self_out, 0)
    w_cross_q = pieces(cross_q, other_cross_q, 1)
    w_cross_kv = pieces(cross_kv, other_cross_kv, 2)
    w_cross_out = pieces(cross_out, other_cross_out, 0)
    b_heads = [bias_own, bias_other] if apart else [jnp.concatenate([bias_own, bias_other], axis=1)]
    b_in = b_heads if apart else [b[4:].reshape(1, unit) for b in (bias_own, bias_other)]

    whole, full = ((seq, width), BF16), ((seq, width), F32)
    local, totals = ((seq, wide), BF16), ((seq, LANES), F32)
    units = ((seq, unit), BF16)

    vectors, molecules = run(
        setup_kernel,
        [Scalars(group_tokens), Scalars(bucket_group), Scalars(mem_lengths)]
        + [far(segment_ids), far(norm_gain), far(norm_bias), far(out_bias)],
        [((VECTORS, width), F32), ((2, seq), jnp.int32)],
        name="setup",
    )

    heads_self, saved_self, part = [], [], None
    for i in range(n):
        last = i == n - 1
        ins = [far(inputs, True) if i == 0 else normed_self, vectors, molecules, w_qkv[i], b_heads[i]]
        outs = ([whole] if i == 0 else []) + [local] * 4 + [totals]
        if last:
            ins += [*w_self_out, *heads_self]
            outs += [whole]
        got = run(functools.partial(self_forward_kernel, n, i), ins, outs, name=f"self_forward_{i}")
        if i == 0:
            normed_self, got = got[0], got[1:]
        saved_self.append((got[0], got[1], got[2], got[4]))
        heads_self.append(got[3])
    mine, theirs = team_parts(got[5])

    heads_cross, saved_cross = [], []
    for i in range(n):
        last = i == n - 1
        kv = run(memory_kernel, [memory_row, w_cross_kv[i], b_heads[i]], [((mem_len, wide), BF16)] * 2, name=f"memory_{i}")
        if i == 0:
            half_in, half_out = run(
                pack_ffn_kernel,
                [far(ffn_in), far(ffn_out)],
                [((width // 2, unit), BF16), ((unit // 2, width), BF16)],
                name="pack_ffn",
            )
        first = [far(inputs, True), mine, theirs] if i == 0 else [normed_cross]
        ins = first + [vectors, molecules, w_cross_q[i], b_heads[i], *kv]
        outs = ([full, whole] if i == 0 else []) + [local] * 2 + [totals]
        if last:
            ins += [*w_cross_out, *heads_cross]
            outs += [whole]
        got = run(functools.partial(cross_forward_kernel, n, i), ins, outs, name=f"cross_forward_{i}")
        if i == 0:
            after_self, normed_cross, got = got[0], got[1], got[2:]
            near_in = other(later(half_in, other_cross_kv))
            near_out = other(later(half_out, other_cross_kv))
        saved_cross.append((got[0], *kv, got[2]))
        heads_cross.append(got[1])
    mine, theirs = team_parts(got[3])

    far_in, far_out = data_swap(near_in, 0), data_swap(near_out, 0)
    after_cross, normed_ffn, low_ffn, act_own, hid_own, part, part_grad = run(
        functools.partial(ffn_kernel, 0),
        [after_self, mine, theirs, far(cotangent, True), vectors, far(ffn_in), b_in[0], far(ffn_out)],
        [full, whole, whole, units, units, full, full],
        name="ffn_0",
    )
    other_in, other_out = run(
        join_weights_kernel,
        [near_in, near_out, far_in, far_out],
        [(ffn_in.shape, BF16), (ffn_out.shape, BF16)],
        name="join_ffn",
    )
    act_other, hid_other, part, part_grad = run(
        functools.partial(ffn_kernel, 1),
        [normed_ffn, low_ffn, part, part_grad, other_in, b_in[1], other_out],
        [units, units, whole, whole],
        name="ffn_1",
    )
    mine, theirs = team_parts(part_grad)
    out_mine, out_theirs = team_parts(part)

    class Reduction:
        def __init__(self, name, keeps, sends, axes, small=0):
            self.name, self.keeps, self.small = name, keeps, small
            self.axes = axes
            self.gots = [swap(s, a) for s, a in zip(sends, axes[0])]
            self.halved = [b for b in axes[0] if b != "row"][:1]
            self.chunk = None

        def fold(self):
            axes, small, keeps = self.axes, self.small, self.keeps
            planes = sum(k.shape[0] for k in keeps)
            size = keeps[0].shape[1]
            bit = 0
            if len(axes) == 1:
                mode, outs = "last", [((planes, size - small, width), BF16)]
                if small:
                    outs.append(((small, width), F32))
            elif len(keeps) > 1 and len(axes[1]) > 1:
                mode = None
            elif axes[1][0] == "row":
                mode, shape = "shard", (1, size, width)
                outs = [(shape, F32), (shape, BF16)]
            elif len(axes) == 2:
                mode, outs = "full", [((planes, size, width), BF16)]
            else:
                mode, bit, shape = "half", axes[1][0], (planes, (size - small) // 2 + small, width)
                outs = [(shape, F32), (shape, BF16)]
                self.halved.append(bit)
            got = run(
                functools.partial(fold_kernel, len(keeps), small, mode, bit),
                [*keeps, *self.gots],
                outs,
                name=f"{self.name}_{mode}_{len(axes)}",
            )
            self.axes = axes[1:]
            if mode == "last":
                self.chunk = got[0]
                self.rest = got[1] if small else None
                self.keeps = None
                self.got = swap(self.chunk, self.halved[-1])
            else:
                self.keeps = [got[0]]
                self.gots = [swap(got[-1], axes[1][0])]

        def join(self):
            bit = self.halved.pop()
            planes, size, _ = self.chunk.shape
            (self.chunk,) = run(
                functools.partial(join_kernel, bit),
                [self.chunk, self.got],
                [((planes, 2 * size, width), BF16)],
                name=f"{self.name}_join_{bit}",
            )
            self.got = swap(self.chunk, self.halved[-1])

        def ready(self):
            return self.chunk is not None and len(self.halved) == 1

        def step(self):
            if self.chunk is None:
                self.fold()
            elif not self.ready():
                self.join()

    ffn_sums, keep_out, send_out, keep_in, send_in = run(
        ffn_weights_kernel,
        [hid_own, hid_other, act_own, act_other, normed_ffn, low_ffn],
        [((2, unit), F32), ((1, unit, width), F32), ((1, unit, width), BF16)]
        + [((2, unit // 2, width), F32), ((2, unit // 2, width), BF16)],
        name="ffn_weights",
    )
    by_out = Reduction("ffn_out", [keep_out], [send_out], [["row"], [0], [1]])
    by_in = Reduction("ffn_in", [keep_in], [send_in], [[0], ["row"], [1]])

    scratch = [pltpu.VMEM((seq, wide), BF16)] * n + [pltpu.VMEM((seq, wide), F32)] * 2
    bias_sum = ((2, wide), F32)

    def saved_of(saved):
        return [s[k] for k in range(4) for s in saved]

    got = run(
        functools.partial(cross_backward_kernel, n),
        [after_cross, mine, theirs, far(cotangent, True), vectors, molecules]
        + saved_of(saved_cross) + [*w_cross_out, *w_cross_q],
        [full, whole] + [local] * (3 * n) + [bias_sum] * n + [whole, ((3, width), F32)],
        scratch=scratch,
        name="cross_backward",
    )
    grad_cross, low_cross, got = got[0], got[1], got[2:]
    cross_grads, cross_bias_sums, got = got[: 3 * n], got[3 * n : 4 * n], got[4 * n :]
    part, small_ffn = got
    mine, theirs = team_parts(part)
    part_rows = seq // team
    keep, send, memory_terms, result, result_part = run(
        functools.partial(cross_weights_kernel, n),
        [*cross_grads, *heads_cross, *w_cross_kv]
        + [normed_cross, memory_row, low_cross, after_cross, out_mine, out_theirs, vectors],
        [((2, 2 * head, width), F32), ((2, 2 * head, width), BF16), whole, whole, ((part_rows, width), BF16)],
        name="cross_weights",
    )
    by_cross = Reduction("cross", [keep], [send], [[1], [0], ["row"]] + [[k] for k in range(2, bits)])
    by_out.fold()
    by_in.fold()

    got = run(
        functools.partial(self_backward_kernel, n),
        [after_self, mine, theirs, grad_cross, vectors, molecules] + saved_of(saved_self) + [*w_self_out, *w_qkv],
        [full, whole] + [local] * (3 * n) + [bias_sum] * n + [whole, ((3, width), F32)],
        scratch=scratch,
        name="self_backward",
    )
    grad_self, low_self, got = got[0], got[1], got[2:]
    self_grads, self_bias_sums, got = got[: 3 * n], got[3 * n : 4 * n], got[4 * n :]
    part, small_cross = got
    mine, theirs = team_parts(part)
    by_ffn = by_out
    by_ffn.name, by_ffn.keeps, by_ffn.gots = "ffn", by_out.keeps + by_in.keeps, by_out.gots + by_in.gots
    by_ffn.axes = [[0]] + [[k] for k in range(1, bits)]
    by_ffn.fold()
    grad_row, grad_part, small_self = run(
        input_backward_kernel,
        [far(inputs, True), mine, theirs, grad_self, vectors],
        [whole, ((part_rows, width), BF16), ((3, width), F32)],
        name="input_backward",
    )
    if apart and 4 * head == width and unit == width:
        shard_rows = [*self_bias_sums, *cross_bias_sums, ffn_sums]
        lines = 2
    else:
        def by_shard(sums):
            return sums if n == 2 else [sums[0][:, :head], sums[0][:, head:]]

        shard_rows = [
            jnp.stack(
                [
                    jnp.concatenate([a.reshape(-1), b.reshape(-1), ffn_sums[i]]).reshape(-1, width)
                    for i, (a, b) in enumerate(zip(by_shard(self_bias_sums), by_shard(cross_bias_sums)))
                ]
            )
        ]
        lines = shard_rows[0].shape[1]
    size = 4 * head + SMALL
    keep, send = run(
        functools.partial(self_weights_kernel, n),
        [*self_grads, *heads_self, normed_self, low_self, small_self, small_cross, small_ffn, *shard_rows],
        [((1, size, width), F32), ((1, size, width), BF16)],
        name="self_weights",
    )
    by_self = Reduction("self", [keep], [send], [["row"]] + [[k] for k in range(bits)], SMALL)

    by_cross.fold()
    by_ffn.fold()
    by_cross.fold()
    by_self.fold()
    groups = [by_ffn, by_cross, by_self]
    while not all(g.ready() for g in groups):
        for g in groups:
            g.step()

    grad_ffn_out, grad_ffn_in = ffn_result = [None, None]
    grad_ffn_in, grad_ffn_out = run(
        functools.partial(ffn_grads_kernel, by_ffn.halved[0]),
        [by_ffn.chunk, by_ffn.got],
        [far(((width, unit), F32)), far(((unit, width), F32))],
        name="ffn_grads",
    )
    grad_cross_q, grad_cross_kv, grad_cross_out = run(
        functools.partial(cross_grads_kernel, by_cross.halved[0]),
        [by_cross.chunk, by_cross.got],
        [far(((width, head), F32)), far(((2, width, head), F32)), far(((head, width), F32))],
        name="cross_grads",
    )

    mem_mine, mem_theirs = team_parts(memory_terms)
    share = width // mp
    if share % LANES == 0 and team == 2:
        (blocks,) = run(
            memory_blocks_kernel,
            [mem_mine, mem_theirs],
            [((dp, rows, mem_len // dp, share), BF16)],
            name="memory_blocks",
        )
    else:
        total = (mem_mine.astype(F32) + mem_theirs.astype(F32)).astype(BF16)
        total = total.reshape(dp, mem_len // dp, rows, team, share)
        blocks = lax.dynamic_index_in_dim(total, seat, 3, keepdims=False).swapaxes(1, 2)
    blocks = blocks.reshape(dp * rows, mem_len // dp, share)
    same_seat = [[d * mp + m for d in range(dp) for m in range(mp) if m % team == s] for s in range(team)]
    grad_memory = lax.all_to_all(
        blocks, ("dp", "mp"), split_axis=0, concat_axis=0, tiled=True, axis_index_groups=same_seat
    ).astype(F32)

    def both_rows(own, part, kind, name):
        near, got = team_gather(other(part))
        top = where if team == 2 else jnp.stack([row, seat // (team // 2)]).astype(jnp.int32)
        run.where = top
        (out,) = run(place_rows_kernel, [own, near, got], [far(((rows, seq, width), kind))], name=name)
        run.where = where
        return out

    mixed = both_rows(result, result_part, BF16, "place_mixed")
    grad_inputs = both_rows(grad_row, grad_part, F32, "place_grad_inputs")
    grad_self_qkv, grad_self_out = run(
        functools.partial(self_grads_kernel, by_self.halved[0]),
        [by_self.chunk, by_self.got],
        [far(((3, width, head), F32)), far(((head, width), F32))],
        name="self_grads",
    )
    small = by_self.rest
    own_small = small[9 : 9 + lines].reshape(-1)
    grad_self_bias = own_small[: 2 * head].reshape(2, head)
    grad_cross_bias = own_small[2 * head : 4 * head].reshape(2, head)
    grad_ffn_bias = own_small[4 * head :]
    return (
        mixed,
        grad_inputs,
        grad_memory,
        small[0:3],
        small[3:6],
        grad_self_qkv,
        grad_self_bias,
        grad_self_out,
        grad_cross_q,
        grad_cross_kv,
        grad_cross_bias,
        grad_cross_out,
        grad_ffn_in,
        grad_ffn_bias,
        grad_ffn_out,
        small[6:9],
    )


def solution(mesh):
    placed = (
        P("dp", None, None),
        P(None, "dp", None),
        P("dp", None),
        P("dp", None),
        P(),
        P(),
        P(),
        P(),
        P(None, None, "mp"),
        P(None, "mp"),
        P("mp", None),
        P(None, "mp"),
        P(None, None, "mp"),
        P(None, "mp"),
        P("mp", None),
        P(None, "mp"),
        P("mp"),
        P("mp", None),
        P(),
        P("dp", None, None),
    )
    return jax.shard_map(
        shards,
        mesh=mesh,
        in_specs=placed,
        out_specs=(
            P("dp", None, None),
            P("dp", None, None),
            P(None, "dp", "mp"),
            P(),
            P(),
            P(None, None, "mp"),
            P(None, "mp"),
            P("mp", None),
            P(None, "mp"),
            P(None, None, "mp"),
            P(None, "mp"),
            P("mp", None),
            P(None, "mp"),
            P("mp"),
            P("mp", None),
            P(),
        ),
        check_vma=False,
    )
```

```python
import functools

import jax
import jax.numpy as jnp
from jax import lax
from jax.experimental import pallas as pl
from jax.experimental.pallas import tpu as pltpu
from jax.sharding import PartitionSpec as P

HDIM = 64
LANES = 128
BLOCK = 128
SMALL = 16
FRONT = 2
BACK = 2
EPSILON = 1e-05
F32 = jnp.float32
BF16 = jnp.bfloat16


def dot(left, right):
    return lax.dot_general(left, right, (((1,), (0,)), ((), ())), preferred_element_type=F32)


def dot_right(left, right):
    return lax.dot_general(left, right, (((1,), (1,)), ((), ())), preferred_element_type=F32)


def dot_left(left, right):
    return lax.dot_general(left, right, (((0,), (0,)), ((), ())), preferred_element_type=F32)


class Far:
    def __init__(self, value, pick=False):
        self.value, self.pick = value, pick


class Raw:
    def __init__(self, value):
        self.value = value


class Scalars:
    def __init__(self, value):
        self.value = value


class Flow:
    def __init__(self):
        self.loads, self.stores, self.sent = {}, {}, []

    def need(self, *refs):
        for ref in refs:
            copy = self.loads.pop(id(ref), None)
            if copy is not None:
                copy.wait()

    def send(self, *refs):
        for ref in refs:
            copy = self.stores.pop(id(ref), None)
            if copy is not None:
                copy.start()
                self.sent.append(copy)


class Steps:
    def __init__(self, where):
        self.where, self.token = where, None

    def batch(self, parts, name=None, cost=0.1):
        def kernel(flow, where, *refs):
            at, to = 0, sum(len(ins) for _, ins, _ in parts)
            for part, ins, outs in parts:
                part(flow, where, *refs[at : at + len(ins)], *refs[to : to + len(outs)])
                at, to = at + len(ins), to + len(outs)

        got = self(
            kernel, [v for _, ins, _ in parts for v in ins], [v for _, _, outs in parts for v in outs], name=name, cost=cost
        )
        results = []
        for _, _, outs in parts:
            results.append(got[: len(outs)])
            got = got[len(outs) :]
        return results

    def __call__(self, kernel, ins, outs, scratch=(), name=None, cost=0.1, hold=()):
        near = pl.BlockSpec(memory_space=pltpu.VMEM)
        far = pl.BlockSpec(memory_space=pltpu.HBM)
        words = pl.BlockSpec(memory_space=pltpu.SMEM)
        values, specs, stages = [], [], []
        for v in ins:
            if isinstance(v, Scalars):
                values.append(v.value)
                specs.append(words)
            elif isinstance(v, Raw):
                values.append(pltpu.with_memory_space_constraint(v.value, pltpu.HBM))
                specs.append(far)
            elif isinstance(v, Far):
                values.append(pltpu.with_memory_space_constraint(v.value, pltpu.HBM))
                specs.append(far)
                stages.append(pltpu.VMEM(v.value.shape[1:] if v.pick else v.value.shape, v.value.dtype))
            else:
                values.append(pltpu.with_memory_space_constraint(v, pltpu.VMEM))
                specs.append(near)
        after = [pltpu.with_memory_space_constraint(v, pltpu.VMEM) for v in hold]
        after_specs = [near] * len(after)
        if self.token is not None:
            after.append(pltpu.with_memory_space_constraint(self.token, pltpu.HBM))
            after_specs.append(far)
        for v in outs:
            if isinstance(v, Far):
                stages.append(pltpu.VMEM(*v.value))
        shapes = [pltpu.HBM(*v.value) if isinstance(v, (Far, Raw)) else pltpu.VMEM(*v) for v in outs]
        count, n_in, n_out, n_after = len(stages), len(ins), len(outs), len(after)

        def body(where_ref, *refs):
            refs = list(refs)
            in_refs, refs = refs[:n_in], refs[n_in + n_after :]
            out_refs, refs = refs[:n_out], refs[n_out + 1 :]
            stage_refs, refs = refs[:count], refs[count:]
            flow = Flow()
            if count:
                sems, refs = refs[0], refs[1:]
            given, k = [], 0
            for v, ref in zip(ins, in_refs):
                if isinstance(v, Far):
                    source = ref.at[where_ref[0]] if v.pick else ref
                    copy = pltpu.make_async_copy(source, stage_refs[k], sems.at[k])
                    copy.start()
                    flow.loads[id(stage_refs[k])] = copy
                    ref, k = stage_refs[k], k + 1
                given.append(ref)
            for v, ref in zip(outs, out_refs):
                if isinstance(v, Far):
                    flow.stores[id(stage_refs[k])] = pltpu.make_async_copy(stage_refs[k], ref, sems.at[k])
                    ref, k = stage_refs[k], k + 1
                given.append(ref)
            kernel(flow, where_ref, *given, *refs)
            for copy in flow.loads.values():
                copy.wait()
            for copy in flow.stores.values():
                copy.start()
            for copy in [*flow.sent, *flow.stores.values()]:
                copy.wait()

        results = pl.pallas_call(
            body,
            in_specs=[words] + specs + after_specs,
            out_specs=[far if isinstance(v, (Far, Raw)) else near for v in outs] + [far],
            out_shape=shapes + [pltpu.HBM((8, LANES), F32)],
            scratch_shapes=stages + ([pltpu.SemaphoreType.DMA((count,))] if count else []) + list(scratch),
            compiler_params=pltpu.CompilerParams(vmem_limit_bytes=24 * 1024 * 1024),
            cost_estimate=pl.CostEstimate(flops=10**6, bytes_accessed=int(cost * 3 * 10**6), transcendentals=0),
            name=name,
        )(self.where, *values, *after)
        self.token = results[-1]
        return list(results[:-1])


def row_blocks(seq):
    return [slice(start, start + BLOCK) for start in range(0, seq, BLOCK)]


def row_of(ref, i):
    return ref[i : i + 1, :].astype(F32)


GAIN, SHIFT, OUT, SCALE, VECTORS = 0, 3, 6, 9, 16


def norm_parts(value):
    centre = value - jnp.mean(value, axis=-1, keepdims=True)
    spread = jnp.mean(centre * centre, axis=-1, keepdims=True)
    scale = lax.rsqrt(spread + EPSILON)
    return centre * scale, scale


def norm_backward(value, gain, incoming):
    xhat, scale = norm_parts(value)
    weighted = incoming * gain
    grad = scale * (
        weighted
        - jnp.mean(weighted, axis=-1, keepdims=True)
        - xhat * jnp.mean(weighted * xhat, axis=-1, keepdims=True)
    )
    return grad, jnp.sum(incoming * xhat, axis=0, keepdims=True), jnp.sum(incoming, axis=0, keepdims=True)


def head_lanes(value, j):
    lane = lax.broadcasted_iota(jnp.int32, value.shape, 1)
    return jnp.where((lane >= HDIM) == bool(j), value, jnp.zeros_like(value))


def span_of(block, seq, banded):
    if not banded:
        return slice(0, seq)
    return slice(max(block.start - BLOCK, 0), block.stop)


def start_all(moves, sems):
    copies = [pltpu.make_async_copy(a, b, sems.at[i]) for i, (a, b) in enumerate(moves)]
    for copy in copies:
        copy.start()
    return copies


def setup_kernel(packing, flow, where, *refs):
    group_tokens, bucket_group, lengths, inputs, cotangent, memory, segments, gains, shifts, biases, refs = *refs[:10], refs[10:]
    if packing:
        query, kv, out, cross, refs = *refs[:4], refs[4:]
    x, cot, memory_part, vectors, molecules, tokens_now, group_now, lengths_now, word_sems, sems = refs
    words = start_all([(group_tokens, tokens_now), (bucket_group, group_now), (lengths, lengths_now)], word_sems)
    moves = [(memory.at[:, where[0]], memory_part), (inputs.at[where[0]], x), (cotangent.at[where[0]], cot)]
    if packing:
        full, wide = query.shape
        half = full // 2
        rows = pl.ds(pl.multiple_of(where[3] * half, half), half)
        moves += [
            (query.at[rows, :], cross.at[0:half, :]),
            (kv.at[0, rows, :], cross.at[half : 2 * half, :]),
            (kv.at[1, rows, :], cross.at[2 * half : 3 * half, :]),
        ]
        count, size = out.shape[1] // wide // 2, out.shape[0]
        for k in range(count):
            lanes = pl.ds(pl.multiple_of((where[3] * count + k) * wide, wide), wide)
            moves.append((out.at[:, lanes], cross.at[3 * half + k * size : 3 * half + (k + 1) * size, :]))
    copies = start_all(moves, sems)
    for copy in words:
        copy.wait()
    width = vectors.shape[1]
    total, own = 0, 0
    for b in range(bucket_group.shape[0]):
        tokens = tokens_now[group_now[b]]
        total = total + tokens
        own = own + jnp.where(where[2] == b, tokens, 0)
    scaled = jnp.full((1, width), bucket_group.shape[0] * own, jnp.int32).astype(F32)
    scale = scaled / jnp.full((1, width), total, jnp.int32).astype(F32)
    size = molecules.shape[1]
    place = lax.broadcasted_iota(jnp.int32, (1, size), 1)
    count, end = jnp.zeros((1, size), jnp.int32), 0
    for k in range(lengths.shape[1]):
        end = end + lengths_now[where[0], k]
        count = count + (end <= place).astype(jnp.int32)
    molecules[1:2, :] = count
    flow.need(segments, gains, shifts, biases)
    molecules[0:1, :] = segments[pl.ds(where[0], 1), :]
    rows = [r[...].astype(F32) for r in (gains, shifts, biases)] + [scale]
    vectors[...] = jnp.concatenate(rows + [jnp.zeros((VECTORS - 10, width), F32)], axis=0)
    for copy in copies:
        copy.wait()


def key_columns(keys):
    size = keys.shape[1]
    tiles = [jnp.broadcast_to(keys[:, at : at + BLOCK], (LANES, BLOCK)).T for at in range(0, size, BLOCK)]
    return jnp.concatenate(tiles, axis=0)


def allowed_of(own, columns, block, span, banded):
    allowed = columns[span] == own[:, block]
    if banded:
        query = lax.broadcasted_iota(jnp.int32, allowed.shape, 1) + block.start
        key = lax.broadcasted_iota(jnp.int32, allowed.shape, 0) + span.start
        allowed = allowed & (key <= query)
    return allowed


def head_rows(value, j):
    row = lax.broadcasted_iota(jnp.int32, value.shape, 0)
    return jnp.where((row >= HDIM) == bool(j), value, jnp.zeros_like(value))


def attend_forward(q, k, v, own, keys, heads, totals, banded):
    seq, wide = q.shape
    columns = key_columns(keys)
    for pair in range(wide // LANES):
        lanes = slice(pair * LANES, (pair + 1) * LANES)
        turned = [head_rows(v[:, lanes].T, j) for j in (0, 1)]
        for block in row_blocks(seq):
            span = span_of(block, k.shape[0], banded)
            allowed = allowed_of(own, columns, block, span, banded)
            query, keyset = q[block, lanes] * 0.125, k[span, lanes]
            mixed = None
            for j in (0, 1):
                scores = jnp.where(allowed, dot_right(keyset, head_lanes(query, j)), -1e30)
                maxima = jnp.max(scores, axis=0, keepdims=True)
                raised = jnp.exp(scores - maxima)
                total = jnp.sum(raised, axis=0, keepdims=True)
                chances = (raised * (1.0 / total)).astype(BF16)
                term = dot(turned[j][:, span], chances)
                mixed = term if mixed is None else mixed + term
                totals[2 * pair + j : 2 * pair + j + 1, block] = maxima + jnp.log(total)
            heads[block, lanes] = mixed.T.astype(BF16)


def attend_backward(q, k, v, own, keys, totals, grad_heads, dq, dk, dv, sum_k, sum_v, banded):
    seq, wide = q.shape
    columns = key_columns(keys)
    for pair in range(wide // LANES):
        lanes = slice(pair * LANES, (pair + 1) * LANES)
        turned = [head_rows(k[:, lanes].T, j) for j in (0, 1)]
        for at, block in enumerate(row_blocks(seq)):
            span = span_of(block, k.shape[0], banded)
            allowed = allowed_of(own, columns, block, span, banded)
            query, keyset, values = q[block, lanes] * 0.125, k[span, lanes], v[span, lanes]
            grad = grad_heads[block, lanes]
            grad_query = grad_key = grad_value = None
            for j in (0, 1):
                head = 2 * pair + j
                part, own_grad = head_lanes(query, j), head_lanes(grad, j)
                scores = jnp.where(allowed, dot_right(keyset, part), -1e30)
                chances = jnp.exp(scores - totals[head : head + 1, block])
                by_value = dot(chances.astype(BF16), own_grad)
                weighted = chances * dot_right(values, own_grad)
                mean = jnp.sum(weighted, axis=0, keepdims=True)
                grad_scores = (weighted - chances * mean).astype(BF16)
                by_query, by_key = dot(turned[j][:, span], grad_scores), dot(grad_scores, part)
                if j == 0:
                    grad_query, grad_key, grad_value = by_query, by_key, by_value
                else:
                    grad_query, grad_key, grad_value = grad_query + by_query, grad_key + by_key, grad_value + by_value
            dq[block, lanes] = (grad_query.T * 0.125).astype(BF16)
            if banded:
                early = block.start - span.start
                sum_k[block, lanes] = grad_key[early:]
                sum_v[block, lanes] = grad_value[early:]
                if early:
                    sum_k[span.start : block.start, lanes] += grad_key[:early]
                    sum_v[span.start : block.start, lanes] += grad_value[:early]
            elif at == 0:
                sum_k[:, lanes] = grad_key
                sum_v[:, lanes] = grad_value
            else:
                sum_k[:, lanes] += grad_key
                sum_v[:, lanes] += grad_value
    dk[...] = sum_k[...].astype(BF16)
    dv[...] = sum_v[...].astype(BF16)


def team_total(mine, theirs, block):
    half = mine[0].shape[0]
    k, rows = block.start // half, slice(block.start % half, block.start % half + BLOCK)
    return mine[k][rows, :].astype(F32) + theirs[k][rows, :].astype(F32)


def put_half(parts, block, value):
    half = parts[0].shape[0]
    start = block.start % half
    parts[block.start // half][start : start + BLOCK, :] = value.astype(parts[0].dtype)


def self_forward_kernel(n, i, flow, where, *refs):
    last = i == n - 1
    first, vectors, molecules, w, bias, refs = *refs[:5], refs[5:]
    if last:
        w_out, done, refs = refs[:n], refs[n : 2 * n - 1], refs[2 * n - 1 :]
    if i == 0:
        normed, refs = refs[0], refs[1:]
        for block in row_blocks(first.shape[0]):
            norm = norm_parts(first[block, :].astype(F32))[0]
            normed[block, :] = (norm * row_of(vectors, GAIN) + row_of(vectors, SHIFT)).astype(BF16)
    else:
        normed = first
    q, k, v, heads, totals = refs[:5]
    flow.need(w)
    q[...] = (dot(normed[...], w[0]) + row_of(bias, 0)).astype(BF16)
    k[...] = dot(normed[...], w[1]).astype(BF16)
    v[...] = (dot(normed[...], w[2]) + row_of(bias, 1)).astype(BF16)
    own = molecules[0:1, :]
    flow.send(q, k, v)
    attend_forward(q, k, v, own, own, heads, totals, True)
    flow.send(totals)
    if last:
        project_out(flow, [*done, heads], w_out, refs[5 : 5 + FRONT])


def project_out(flow, heads, w_out, parts):
    flow.need(*w_out)
    for block in row_blocks(heads[0].shape[0]):
        put_half(parts, block, sum(dot(h[block, :], w[...]) for h, w in zip(heads, w_out)))


def memory_kernel(flow, where, memory, w, bias, k, v):
    flow.need(w)
    k[...] = dot(memory[...], w[0]).astype(BF16)
    v[...] = (dot(memory[...], w[1]) + row_of(bias, 3)).astype(BF16)


def unpack_memory_kernel(flow, where, near, got, memory, bias, query, kv, out, k, v):
    full, wide = query.shape
    half, size = full // 2, out.shape[0]
    count = out.shape[1] // wide // 2
    for packed, bit in ((near, where[3]), (got, 1 - where[3])):
        rows = pl.ds(pl.multiple_of(bit * half, half), half)
        query[rows, :] = packed[:half]
        for i in (0, 1):
            kv[i, rows, :] = packed[(i + 1) * half : (i + 2) * half]
        for i in range(count):
            lanes = pl.ds(pl.multiple_of((bit * count + i) * wide, wide), wide)
            out[:, lanes] = packed[3 * half + i * size : 3 * half + (i + 1) * size]
    memory_kernel(flow, where, memory, kv, bias, k, v)


def cross_forward_kernel(n, i, flow, where, *refs):
    last = i == n - 1
    if i == 0:
        x, mine, theirs, refs = refs[0], refs[1 : 1 + FRONT], refs[1 + FRONT : 1 + 2 * FRONT], refs[1 + 2 * FRONT :]
    else:
        normed, refs = refs[0], refs[1:]
    vectors, molecules, w, bias, k, v, refs = *refs[:6], refs[6:]
    if last:
        w_out, done, refs = refs[:n], refs[n : 2 * n - 1], refs[2 * n - 1 :]
    if i == 0:
        after_self, normed, refs = refs[0], refs[1], refs[2:]
    q, heads, totals = refs[:3]
    if i == 0:
        for block in row_blocks(x.shape[0]):
            value = x[block, :].astype(F32) + team_total(mine, theirs, block) + row_of(vectors, OUT)
            after_self[block, :] = value
            norm = norm_parts(value)[0]
            normed[block, :] = (norm * row_of(vectors, GAIN + 1) + row_of(vectors, SHIFT + 1)).astype(BF16)
    flow.need(w)
    q[...] = (dot(normed[...], w[...]) + row_of(bias, 2)).astype(BF16)
    attend_forward(q, k, v, molecules[0:1, :], molecules[1:2, :], heads, totals, False)
    if last:
        project_out(flow, [*done, heads], w_out, refs[3 : 3 + FRONT])


def ffn_kernel(i, flow, where, *refs):
    if i == 0:
        after_self, mine, theirs, refs = refs[0], refs[1 : 1 + FRONT], refs[1 + FRONT : 1 + 2 * FRONT], refs[1 + 2 * FRONT :]
        cotangent, vectors, w_in, bias, w_out, refs = *refs[:5], refs[5:]
        after_cross, normed, low, active, grad_hidden, part, part_grad = refs
    else:
        normed, low, begun, begun_grad, w_in, w_out, bias, refs = *refs[:7], refs[7:]
        active, grad_hidden, parts, parts_grad = refs[0], refs[1], refs[2 : 2 + BACK], refs[2 + BACK :]
    if bias.shape[0] == 1:
        row = row_of(bias, 0)
    else:
        row = jnp.concatenate([row_of(bias, k) for k in range(4, bias.shape[0])], axis=1)
    if i == 0:
        for block in row_blocks(normed.shape[0]):
            value = after_self[block, :] + team_total(mine, theirs, block) + row_of(vectors, OUT + 1)
            after_cross[block, :] = value
            norm = norm_parts(value)[0]
            normed[block, :] = (norm * row_of(vectors, GAIN + 2) + row_of(vectors, SHIFT + 2)).astype(BF16)
            low[block, :] = (cotangent[block, :].astype(F32) * row_of(vectors, SCALE)).astype(BF16)
    flow.need(w_in, w_out)
    for block in row_blocks(normed.shape[0]):
        hidden = dot(normed[block, :], w_in[...]) + row
        cdf = 0.5 * (1.0 + lax.erf(hidden * 0.7071067811865476))
        act = (hidden * cdf).astype(BF16)
        active[block, :] = act
        slope = cdf + hidden * (0.3989422804014327 * jnp.exp(-0.5 * hidden * hidden))
        back = (slope * dot_right(low[block, :], w_out[...])).astype(BF16)
        grad_hidden[block, :] = back
        out, out_grad = dot(act, w_out[...]), dot_right(back, w_in[...])
        if i == 0:
            part[block, :], part_grad[block, :] = out, out_grad
        else:
            put_half(parts, block, begun[block, :] + out)
            put_half(parts_grad, block, begun_grad[block, :] + out_grad)


def ffn_weights_kernel(flow, where, *refs):
    hidden, active, normed, low, sums = refs[:2], refs[2:4], refs[4], refs[5], refs[6]
    keep_out, send_out, keep_in, send_in = refs[7:]
    half = keep_in.shape[1]
    for i in (0, 1):
        for target, bit in ((keep_in, where[3]), (send_in, 1 - where[3])):
            lanes = pl.ds(pl.multiple_of(bit * half, half), half)
            target[i] = dot_left(hidden[i][:, lanes], normed[...]).astype(target.dtype)
        sums[i : i + 1, :] = jnp.sum(hidden[i][...].astype(F32), axis=0, keepdims=True)
    keep_out[0] = dot_left(active[0][...], low[...])
    send_out[0] = dot_left(active[1][...], low[...]).astype(BF16)


def spread_grad_heads(low, w_out, grad_heads):
    for piece, target in zip(w_out, grad_heads):
        target[...] = dot_right(low[...], piece[...]).astype(BF16)


def column_sums(sums, values):
    for i, value in enumerate(values):
        sums[i : i + 1, :] = jnp.sum(value[...].astype(F32), axis=0, keepdims=True)


def cross_backward_kernel(n, flow, where, *refs):
    after_cross, mine, theirs, refs = refs[0], refs[1 : 1 + BACK], refs[1 + BACK : 1 + 2 * BACK], refs[1 + 2 * BACK :]
    cotangent, vectors, molecules, refs = *refs[:3], refs[3:]
    (q, k, v, totals, w_out, w), refs = [refs[i * n : (i + 1) * n] for i in range(6)], refs[6 * n :]
    grad_cross, low, refs = refs[0], refs[1], refs[2:]
    (dq, dk, dv, bias_sums), refs = [refs[i * n : (i + 1) * n] for i in range(4)], refs[4 * n :]
    parts_out, sums, refs = refs[:BACK], refs[BACK], refs[BACK + 1 :]
    grad_heads, sum_k, sum_v = refs[:n], refs[n], refs[n + 1]
    seq, width = after_cross.shape
    rows = [jnp.zeros((1, width), F32)] * 3
    for block in row_blocks(seq):
        incoming = team_total(mine, theirs, block)
        grad_result = cotangent[block, :].astype(F32) * row_of(vectors, SCALE)
        back, by_gain, by_shift = norm_backward(after_cross[block, :], row_of(vectors, GAIN + 2), incoming)
        value = grad_result + back
        grad_cross[block, :] = value
        low[block, :] = value.astype(BF16)
        parts = (by_gain, by_shift, jnp.sum(grad_result, axis=0, keepdims=True))
        rows = [a + b for a, b in zip(rows, parts)]
    for i, row in enumerate(rows):
        sums[i : i + 1, :] = row
    flow.need(*w_out)
    spread_grad_heads(low, w_out, grad_heads)
    own, keys = molecules[0:1, :], molecules[1:2, :]
    for i in range(n):
        attend_backward(
            q[i], k[i], v[i], own, keys, totals[i], grad_heads[i], dq[i], dk[i], dv[i], sum_k, sum_v, False
        )
        column_sums(bias_sums[i], (dq[i], dv[i]))
    flow.need(*w)
    for block in row_blocks(seq):
        put_half(parts_out, block, sum(dot_right(d[block, :], m[...]) for d, m in zip(dq, w)))


def shard_grads(kinds):
    grads = ([], [])
    for kind in kinds:
        if len(kind) == 2:
            for i in (0, 1):
                grads[i].append(dot_left(kind[i][0][...], kind[i][1][...]))
        else:
            left, right = kind[0]
            both, half = dot_left(left[...], right[...]), left.shape[1] // 2
            grads[0].append(both[:half])
            grads[1].append(both[half:])
    return grads


def cross_weights_kernel(n, flow, where, *refs):
    (dq, dk, dv, heads, w), refs = [refs[i * n : (i + 1) * n] for i in range(5)], refs[5 * n :]
    normed, memory, low, after_cross, refs = *refs[:4], refs[4:]
    mine, theirs, vectors, refs = refs[:BACK], refs[BACK : 2 * BACK], refs[2 * BACK], refs[2 * BACK + 1 :]
    keep, send, terms, result = refs[0], refs[1], refs[2 : 2 + BACK], refs[-1]
    flow.need(*w)
    pairs = [[(a, b) for a in left] for left, b in ((dq, normed), (dk, memory), (dv, memory), (heads, low))]
    first = where[4] == 0
    for i, grads in enumerate(shard_grads(pairs)):
        upper, lower = jnp.concatenate(grads[:2], axis=0), jnp.concatenate(grads[2:], axis=0)
        keep[i] = jnp.where(first, upper, lower)
        send[i] = jnp.where(first, lower, upper).astype(BF16)
    for block in row_blocks(memory.shape[0]):
        total = sum(
            dot_right(a[block, :], m[0]) + dot_right(b[block, :], m[1]) for a, b, m in zip(dk, dv, w)
        )
        put_half(terms, block, total)
    for block in row_blocks(after_cross.shape[0]):
        both = team_total(mine, theirs, block)
        result[block, :] = (after_cross[block, :] + both + row_of(vectors, OUT + 2)).astype(BF16)


def self_backward_kernel(n, flow, where, *refs):
    after_self, mine, theirs, refs = refs[0], refs[1 : 1 + BACK], refs[1 + BACK : 1 + 2 * BACK], refs[1 + 2 * BACK :]
    grad_cross, vectors, molecules, refs = *refs[:3], refs[3:]
    (q, k, v, totals, w_out), refs = [refs[i * n : (i + 1) * n] for i in range(5)], refs[5 * n :]
    grad_self, low, refs = refs[0], refs[1], refs[2:]
    (dq, dk, dv, bias_sums), refs = [refs[i * n : (i + 1) * n] for i in range(4)], refs[4 * n :]
    sums, refs = refs[0], refs[1:]
    grad_heads, sum_k, sum_v = refs[:n], refs[n], refs[n + 1]
    seq, width = after_self.shape
    rows = [jnp.zeros((1, width), F32)] * 3
    for block in row_blocks(seq):
        incoming = team_total(mine, theirs, block)
        back, by_gain, by_shift = norm_backward(after_self[block, :], row_of(vectors, GAIN + 1), incoming)
        upper = grad_cross[block, :]
        value = upper + back
        grad_self[block, :] = value
        low[block, :] = value.astype(BF16)
        parts = (by_gain, by_shift, jnp.sum(upper, axis=0, keepdims=True))
        rows = [a + b for a, b in zip(rows, parts)]
    for i, row in enumerate(rows):
        sums[i : i + 1, :] = row
    flow.need(*w_out)
    spread_grad_heads(low, w_out, grad_heads)
    own = molecules[0:1, :]
    flow.need(*q, *k, *v, *totals)
    for i in range(n):
        attend_backward(
            q[i], k[i], v[i], own, own, totals[i], grad_heads[i], dq[i], dk[i], dv[i], sum_k, sum_v, True
        )
        column_sums(bias_sums[i], (dq[i], dv[i]))


def input_backward_kernel(n, flow, where, x, *refs):
    mine, theirs, refs = refs[:BACK], refs[BACK : 2 * BACK], refs[2 * BACK :]
    grad_self, vectors, result, by_cross, by_ffn, refs = *refs[:5], refs[5:]
    shard_rows, (both, small_own, small_other) = refs[:-3], refs[-3:]
    seq = x.shape[0]
    both[:seq, :] = result[...]
    width = x.shape[1]
    rows = [jnp.zeros((1, width), F32)] * 3
    for block in row_blocks(x.shape[0]):
        incoming = team_total(mine, theirs, block)
        back, by_gain, by_shift = norm_backward(x[block, :].astype(F32), row_of(vectors, GAIN), incoming)
        upper = grad_self[block, :]
        both[seq + block.start : seq + block.stop, :] = (upper + back).astype(BF16)
        parts = (by_gain, by_shift, jnp.sum(upper, axis=0, keepdims=True))
        rows = [a + b for a, b in zip(rows, parts)]
    common = [r for k in range(3) for r in (rows[k], by_cross[k : k + 1, :], by_ffn[k : k + 1, :])]
    if len(shard_rows) == 1:
        lines = [shard_rows[0][i] for i in (0, 1)]
    else:
        sums_self, sums_cross, sums_ffn = shard_rows[:n], shard_rows[n : 2 * n], shard_rows[2 * n]
        lines = []
        for i in (0, 1):
            pieces = [r[k : k + 1, :] for r in (sums_self[i], sums_cross[i]) for k in (0, 1)]
            lines.append(jnp.concatenate([jnp.concatenate(pieces, axis=1), sums_ffn[i : i + 1, :]], axis=0))
    rest = jnp.zeros((SMALL - 9 - lines[0].shape[0], width), F32)
    small = [jnp.concatenate([*common, line, rest], axis=0).astype(BF16) for line in lines]
    small_own[...] = small[0]
    small_other[...] = small[1]


def self_weights_kernel(n, flow, where, *refs):
    (dq, dk, dv, heads, w), refs = [refs[i * n : (i + 1) * n] for i in range(5)], refs[5 * n :]
    normed, low, parts_out, keep, send = refs[0], refs[1], refs[2 : 2 + BACK], refs[-2], refs[-1]
    pairs = [[(a, b) for a in left] for left, b in ((dq, normed), (dk, normed), (dv, normed), (heads, low))]
    for target, grads in zip((keep, send), shard_grads(pairs)):
        size = grads[0].shape[0]
        for k, grad in enumerate(grads):
            target[0, k * size : (k + 1) * size, :] = grad.astype(target.dtype)
    flow.need(*w)
    for block in row_blocks(normed.shape[0]):
        total = 0.0
        for i in range(n):
            for which, d in enumerate((dq[i], dk[i], dv[i])):
                total += dot_right(d[block, :], w[i][which])
        put_half(parts_out, block, total)


def fold_kernel(count, ride, mode, bit, flow, where, *refs):
    keeps, gots, refs = refs[:count], refs[count : 2 * count], refs[2 * count :]
    planes = [(k, p) for k in range(count) for p in range(keeps[k].shape[0])]
    size = keeps[0].shape[1]

    def part(at, rows):
        k, p = planes[at]
        return keeps[k][p, rows, :].astype(F32) + gots[k][p, rows, :].astype(F32)

    if mode == "half":
        keep, send = refs
        half = size // 2
        for at in range(len(planes)):
            for target, side in ((keep, where[3 + bit]), (send, 1 - where[3 + bit])):
                rows = pl.ds(pl.multiple_of(side * half, half), half)
                target[at] = part(at, rows).astype(target.dtype)
    elif mode == "shard":
        if ride:
            refs[2][0, size:, :] = refs[0][...]
        for at, target in enumerate(refs[-2:]):
            target[0, :size, :] = part(at, slice(0, size)).astype(target.dtype)
    else:
        out = refs[-1]
        for at in range(len(planes)):
            value = part(at, slice(0, size))
            if ride and mode == "full":
                own, came = refs[:2]
                last = came.shape[1]
                small = own[...].astype(F32) + came[0, last - SMALL : last, :].astype(F32)
                value = jnp.concatenate([value, small], axis=0)
            out[at] = value.astype(out.dtype)


def join_kernel(ride, bit, flow, where, near, got, out):
    half = near.shape[1] - (SMALL if ride else 0)
    for value, side in ((near, where[3 + bit]), (got, 1 - where[3 + bit])):
        rows = pl.ds(pl.multiple_of(side * half, half), half)
        for p in range(near.shape[0]):
            out[p, rows, :] = value[p, :half]
    if ride:
        out[0, 2 * half :, :] = (near[0, half:].astype(F32) + got[0, half:].astype(F32)).astype(BF16)


def joined(where, bit, near, got, p, ride=0):
    first = where[3 + bit] == 0
    size = near.shape[1] - ride
    a, b = near[p, :size], got[p, :size]
    rows = [jnp.where(first, a, b), jnp.where(first, b, a)]
    return jnp.concatenate(rows, axis=0).astype(F32)


def self_grads_kernel(bit, flow, where, near, got, qkv, out, gains, shifts, biases, *rest):
    size = near.shape[1] - SMALL
    small = near[0, size:].astype(F32) + got[0, size:].astype(F32)
    for k, target in enumerate((gains, shifts, biases)):
        target[...] = small[3 * k : 3 * k + 3]
    if len(rest) == 1:
        rest[0][...] = small[9 : 9 + rest[0].shape[0]]
    else:
        for k, target in enumerate(rest[:2]):
            wide = target.shape[1]
            for i in (0, 1):
                at = (2 * k + i) * wide
                target[i : i + 1, :] = small[9:10, at : at + wide]
        rest[2][...] = small[10:11]
    flow.send(gains, shifts, biases, *rest)
    value = joined(where, bit, near, got, 0, SMALL)
    size = out.shape[0]
    for k in range(3):
        qkv[k] = value[k * size : (k + 1) * size].T
    out[...] = value[3 * size :]


def cross_grads_kernel(bit, flow, where, near, got, query, kv, out):
    half = near.shape[1] // 2
    value = [joined(where, bit, near[:, k * half : (k + 1) * half], got[:, k * half : (k + 1) * half], 0) for k in (0, 1)]
    value = jnp.concatenate(value, axis=0)
    size = out.shape[0]
    query[...] = value[:size].T
    for k in (0, 1):
        kv[k] = value[(k + 1) * size : (k + 2) * size].T
    out[...] = value[3 * size :]


def widen_kernel(flow, where, value, out):
    out[...] = value[...].astype(out.dtype)


def ffn_grads_kernel(bit, flow, where, near, got, grad_in, grad_out):
    grad_out[...] = joined(where, bit, near, got, 0)
    flow.send(grad_out)
    grad_in[...] = joined(where, bit, near, got, 1).T


def place_rows_kernel(flow, where, own, got, mixed, grad):
    seq = own.shape[0] // 2
    for k, out in enumerate((mixed, grad)):
        for row, value in ((where[0], own), (1 - where[0], got)):
            out[row] = value[k * seq : (k + 1) * seq, :].astype(out.dtype)
        flow.send(out)


def memory_blocks_kernel(flow, where, *refs):
    mine, theirs, out = refs[:BACK], refs[BACK : 2 * BACK], refs[2 * BACK]
    dp, rows, tokens, share = out.shape
    half, width = mine[0].shape
    team = width // (rows * share)
    for r in range(rows):
        lanes = pl.ds(pl.multiple_of((r * team + where[1]) * share, share), share)
        for k in range(BACK):
            total = (mine[k][:, lanes].astype(F32) + theirs[k][:, lanes].astype(F32)).astype(BF16)
            for d in range(half // tokens):
                out[k * half // tokens + d, r] = total[d * tokens : (d + 1) * tokens]


def shards(
    inputs,
    memory,
    segment_ids,
    mem_lengths,
    bucket_group,
    group_tokens,
    norm_gain,
    norm_bias,
    self_qkv,
    self_bias,
    self_out,
    cross_q,
    cross_kv,
    cross_bias,
    cross_out,
    ffn_in,
    ffn_bias,
    ffn_out,
    out_bias,
    cotangent,
):
    dp, mp = lax.axis_size("dp"), lax.axis_size("mp")
    rows, seq, width = inputs.shape
    team = mp // rows
    data, place = lax.axis_index("dp"), lax.axis_index("mp")
    row, seat = place // team, place % team
    bits = dp.bit_length() - 1
    where = jnp.stack([row, seat, data] + [(data >> k) & 1 for k in range(bits)]).astype(jnp.int32)
    run, far = Steps(where), Far

    across = [(i, (i + team) % mp) for i in range(mp)]

    def other(value):
        return lax.ppermute(value, "mp", across)

    def seat_swap(value, step):
        return lax.ppermute(value, "mp", [(i, i ^ step) for i in range(mp)])

    def data_swap(value, k):
        return lax.ppermute(value, "dp", [(i, i ^ (1 << k)) for i in range(dp)])

    def swap(value, axis):
        return other(value) if axis == "row" else data_swap(value, axis)

    def later(value, *after):
        return lax.optimization_barrier((value, *after))[0]

    def team_parts(values):
        step = 1
        while 2 * step < team:
            values = [(v.astype(F32) + seat_swap(v, step).astype(F32)).astype(BF16) for v in values]
            step *= 2
        return [*values, *(seat_swap(v, step) for v in values)]

    head, unit = self_bias.shape[1], ffn_bias.shape[0]
    mem_len = memory.shape[1] * dp
    apart = head % LANES == 0
    n = 2 if apart else 1
    wide = head if apart else 2 * head

    front = [((seq // FRONT, width), BF16)] * FRONT
    back = [((seq // BACK, width), BF16)] * BACK
    whole, full = ((seq, width), BF16), ((seq, width), F32)
    local, totals = ((seq, wide), BF16), ((2 * wide // LANES, seq), F32)
    units = ((seq, unit), BF16)

    other_qkv = other(self_qkv)
    bias_own = jnp.concatenate([self_bias, cross_bias, ffn_bias.reshape(-1, head)])
    bias_other = other(bias_own)
    other_self_out = other(self_out)
    memory_rows = memory.reshape((dp, rows) + memory.shape[1:])
    packing = apart and width % (2 * head) == 0
    ins = [Raw(group_tokens), Raw(bucket_group), Raw(mem_lengths), Raw(inputs), Raw(cotangent), Raw(memory_rows)]
    ins += [far(segment_ids), far(norm_gain), far(norm_bias), far(out_bias)]
    outs = [whole, whole, ((dp,) + memory.shape[1:], BF16), ((VECTORS, width), F32), ((2, seq), jnp.int32)]
    if packing:
        ins += [Raw(v) for v in (cross_q, cross_kv, cross_out)]
        outs = [((3 * width // 2 + cross_out.size // head // 2, head), BF16)] + outs
    *packed, x, cot, memory_part, vectors, molecules = run(
        functools.partial(setup_kernel, packing),
        ins,
        outs,
        scratch=[pltpu.SMEM(v.shape, jnp.int32) for v in (group_tokens, bucket_group, mem_lengths)]
        + [pltpu.SemaphoreType.DMA((3,)), pltpu.SemaphoreType.DMA((6 + width // head // 2,))],
        name="setup",
    )
    memory_row = lax.all_to_all(memory_part, "dp", split_axis=0, concat_axis=0, tiled=True).reshape(mem_len, width)
    def pieces(own, theirs, axis):
        return [far(own), theirs] if apart else [jnp.concatenate([own, theirs], axis=axis)]

    w_qkv = pieces(self_qkv, other_qkv, 2)
    w_self_out = pieces(self_out, other_self_out, 0)
    b_heads = [bias_own, bias_other] if apart else [jnp.concatenate([bias_own, bias_other], axis=1)]
    b_in = b_heads if apart else [b[4:].reshape(1, unit) for b in (bias_own, bias_other)]

    heads_self, saved_self = [], []
    for i in range(n):
        last = i == n - 1
        ins = [x if i == 0 else normed_self, vectors, molecules, w_qkv[i], b_heads[i]]
        outs = ([whole] if i == 0 else []) + [far(local)] * 3 + [local, far(totals)]
        if last:
            ins += [*w_self_out, *heads_self]
            outs += front
        hold = [near_cross] if packing and i == 1 else []
        got = run(functools.partial(self_forward_kernel, n, i), ins, outs, name=f"self_forward_{i}", hold=hold)
        if i == 0:
            normed_self, got = got[0], got[1:]
            early = (normed_self, other_qkv, bias_other, other_self_out)
            if packing:
                near_cross = other(later(packed[0], *early))
                got_cross = data_swap(near_cross, 0)
                other_in, other_out = [other(later(w, near_cross)) for w in (ffn_in, ffn_out)]
            else:
                other_cross = [other(later(w, *early)) for w in (cross_q, cross_kv, cross_out)]
                other_in, other_out = [other(later(w, *other_cross)) for w in (ffn_in, ffn_out)]
        saved_self.append((got[0], got[1], got[2], got[4]))
        heads_self.append(got[3])
    terms = team_parts(got[5:])

    heads_cross, saved_cross = [], []
    if apart:
        w_cross_q, w_cross_kv, w_cross_out = [far(cross_q)], [far(cross_kv)], [far(cross_out)]
    else:
        w_cross_q = pieces(cross_q, other_cross[0], 1)
        w_cross_kv = pieces(cross_kv, other_cross[1], 2)
        w_cross_out = pieces(cross_out, other_cross[2], 0)
    projected = ((mem_len, wide), BF16)
    for i in range(n):
        last = i == n - 1
        if i == 1 and packing:
            query, both, out, *kv = run(
                unpack_memory_kernel,
                [near_cross, got_cross, memory_row, b_heads[1]],
                [(v.shape, BF16) for v in (cross_q, cross_kv, cross_out)] + [projected] * 2,
                name="memory_1",
            )
            for pieces_of, w in ((w_cross_q, query), (w_cross_kv, both), (w_cross_out, out)):
                pieces_of.append(w)
        else:
            if i == 1:
                for pieces_of, w in zip((w_cross_q, w_cross_kv, w_cross_out), other_cross):
                    pieces_of.append(w)
            kv = run(memory_kernel, [memory_row, w_cross_kv[i], b_heads[i]], [projected] * 2, name=f"memory_{i}")
        first = [x, *terms] if i == 0 else [normed_cross]
        ins = first + [vectors, molecules, w_cross_q[i], b_heads[i], *kv]
        outs = ([full, whole] if i == 0 else []) + [local] * 2 + [totals]
        if last:
            ins += [*w_cross_out, *heads_cross]
            outs += front
        got = run(functools.partial(cross_forward_kernel, n, i), ins, outs, name=f"cross_forward_{i}")
        if i == 0:
            after_self, normed_cross, got = got[0], got[1], got[2:]
        saved_cross.append((got[0], *kv, got[2]))
        heads_cross.append(got[1])
    terms = team_parts(got[3:])

    after_cross, normed_ffn, low_ffn, act_own, hid_own, begun, begun_grad = run(
        functools.partial(ffn_kernel, 0),
        [after_self, *terms, cot, vectors, far(ffn_in), b_in[0], far(ffn_out)],
        [full, whole, whole, units, units, full, full],
        name="ffn_0",
    )
    ins = [other_in, other_out, b_in[1]]
    act_other, hid_other, *parts = run(
        functools.partial(ffn_kernel, 1),
        [normed_ffn, low_ffn, begun, begun_grad, *ins],
        [units, units] + back + back,
        name="ffn_1",
    )
    terms = team_parts(parts[BACK:])
    out_terms = team_parts(parts[:BACK])

    class Reduction:
        def __init__(self, keeps, sends, axes):
            self.keeps, self.axes, self.ride, self.carry, self.turned = keeps, axes, [], [], False
            self.gots = [swap(s, a) for s, a in zip(sends, axes[0])]
            self.halved = [b for b in axes[0] if b != "row"][:1]
            self.chunk = None

        def plan(self):
            extra = SMALL if self.ride else 0
            if self.chunk is not None:
                bit = self.halved.pop()
                planes, size, _ = self.chunk.shape
                outs = [((planes, 2 * size - extra, width), BF16)]
                return functools.partial(join_kernel, bool(extra), bit), [self.chunk, self.got], outs
            axes, keeps, ride = self.axes, self.keeps, []
            planes = sum(k.shape[0] for k in keeps)
            size = keeps[0].shape[1]
            bit = 0
            if len(axes) == 1:
                mode, outs = "last", [((planes, size, width), BF16)]
            elif axes[1][0] == "row":
                mode, ride = "shard", self.carry
                outs = [((1, size, width), F32), ((1, size + (SMALL if ride else 0), width), BF16)]
            elif len(axes) == 2:
                mode, ride, outs = "full", self.ride, [((planes, size + extra, width), BF16)]
            else:
                mode, bit, shape = "half", axes[1][0], (planes, size // 2, width)
                outs = [(shape, F32), (shape, BF16)]
                self.halved.append(bit)
            return functools.partial(fold_kernel, len(keeps), bool(ride), mode, bit), [*keeps, *self.gots, *ride], outs

        def take(self, got):
            if self.chunk is not None or len(self.axes) == 1:
                if self.chunk is None and self.turned:
                    self.halved[:2] = self.halved[1::-1]
                self.chunk = got[0]
                self.got = swap(self.chunk, self.halved[-1])
            else:
                self.axes = self.axes[1:]
                self.keeps = [got[0]]
                self.gots = [swap(got[-1], self.axes[0][0])]

        def ready(self):
            return self.chunk is not None and len(self.halved) == 1

    def advance(name, *groups, cost=0.1):
        groups = [g for g in groups if not g.ready()]
        if groups:
            for g, got in zip(groups, run.batch([g.plan() for g in groups], name=name, cost=cost)):
                g.take(got)

    ffn_sums, keep_out, send_out, keep_in, send_in = run(
        ffn_weights_kernel,
        [hid_own, hid_other, act_own, act_other, normed_ffn, low_ffn],
        [((2, unit), F32), ((1, unit, width), F32), ((1, unit, width), BF16)]
        + [((2, unit // 2, width), F32), ((2, unit // 2, width), BF16)],
        name="ffn_weights",
    )
    by_out = Reduction([keep_out], [send_out], [["row"], [0], [1]])
    by_in = Reduction([keep_in], [send_in], [[0], ["row"], [1]])

    scratch = [pltpu.VMEM((seq, wide), BF16)] * n + [pltpu.VMEM((seq, wide), F32)] * 2
    bias_sum = ((2, wide), F32)

    def saved_of(saved):
        return [s[k] for k in range(4) for s in saved]

    got = run(
        functools.partial(cross_backward_kernel, n),
        [after_cross, *terms, cot, vectors, molecules]
        + saved_of(saved_cross) + [*w_cross_out, *w_cross_q],
        [full, whole] + [local] * (3 * n) + [bias_sum] * n + back + [((3, width), F32)],
        scratch=scratch,
        name="cross_backward",
    )
    grad_cross, low_cross, got = got[0], got[1], got[2:]
    cross_grads, cross_bias_sums, got = got[: 3 * n], got[3 * n : 4 * n], got[4 * n :]
    terms, small_ffn = team_parts(got[:BACK]), got[BACK]
    keep, send, *memory_terms, result = run(
        functools.partial(cross_weights_kernel, n),
        [*cross_grads, *heads_cross, *w_cross_kv]
        + [normed_cross, memory_row, low_cross, after_cross, *out_terms, vectors],
        [((2, 2 * head, width), F32), ((2, 2 * head, width), BF16)] + back + [whole],
        name="cross_weights",
    )
    by_cross = Reduction([keep], [send], [[1], [0], ["row"]] + [[k] for k in range(2, bits)])
    by_cross.turned = True
    advance("fold_ffn", by_out, by_in)

    got = run(
        functools.partial(self_backward_kernel, n),
        [after_self, *terms, grad_cross, vectors, molecules] + [far(v) for v in saved_of(saved_self)] + [*w_self_out],
        [full, whole] + [local] * (3 * n) + [bias_sum] * n + [((3, width), F32)],
        scratch=scratch,
        name="self_backward",
    )
    grad_self, low_self, got = got[0], got[1], got[2:]
    self_grads, self_bias_sums, small_cross = got[: 3 * n], got[3 * n : 4 * n], got[4 * n]
    by_ffn = by_out
    by_ffn.keeps, by_ffn.gots = by_out.keeps + by_in.keeps, by_out.gots + by_in.gots
    by_ffn.axes = [[0]] + [[k] for k in range(1, bits)]
    advance("ffn_1", by_ffn)
    *parts, keep, send = run(
        functools.partial(self_weights_kernel, n),
        [*self_grads, *heads_self, *w_qkv, normed_self, low_self],
        back + [((1, 4 * head, width), F32), ((1, 4 * head, width), BF16)],
        name="self_weights",
    )
    by_self = Reduction([keep], [send], [["row"]] + [[k] for k in range(bits)])
    terms = team_parts(parts)
    advance("cross_1", by_cross)
    advance("ffn_2", by_ffn)
    mem_terms = team_parts(memory_terms)
    share = width // mp
    if share % LANES == 0 and team == 2:
        (blocks,) = run(
            memory_blocks_kernel, mem_terms, [((dp, rows, mem_len // dp, share), BF16)], name="memory_blocks"
        )
    else:
        mine, theirs = jnp.concatenate(mem_terms[:BACK]), jnp.concatenate(mem_terms[BACK:])
        total = (mine.astype(F32) + theirs.astype(F32)).astype(BF16)
        total = total.reshape(dp, mem_len // dp, rows, team, share)
        blocks = lax.dynamic_index_in_dim(total, seat, 3, keepdims=False).swapaxes(1, 2)
    blocks = blocks.reshape(dp * rows, mem_len // dp, share)
    same_seat = [[d * mp + m for d in range(dp) for m in range(mp) if m % team == s] for s in range(team)]
    memory_got = lax.all_to_all(
        blocks, ("dp", "mp"), split_axis=0, concat_axis=0, tiled=True, axis_index_groups=same_seat
    )


    fits = apart and 4 * head == width and unit == width
    if fits:
        shard_rows = [*self_bias_sums, *cross_bias_sums, ffn_sums]
        lines = 2
    else:

        def by_shard(sums):
            return sums if n == 2 else [sums[0][:, :head], sums[0][:, head:]]

        shard_rows = [
            jnp.stack(
                [
                    jnp.concatenate([a.reshape(-1), b.reshape(-1), ffn_sums[i]]).reshape(-1, width)
                    for i, (a, b) in enumerate(zip(by_shard(self_bias_sums), by_shard(cross_bias_sums)))
                ]
            )
        ]
        lines = shard_rows[0].shape[1]
    both, small_own, small_other = run(
        functools.partial(input_backward_kernel, n),
        [x, *terms, grad_self, vectors, result, small_cross, small_ffn, *shard_rows],
        [((2 * seq, width), BF16)] + [((SMALL, width), BF16)] * 2,
        name="input_backward",
    )

    by_cross.carry = [small_other]

    advance("cross_2", by_cross)
    by_self.ride = [small_own, by_cross.gots[0]]
    advance("self_1", by_self)
    advance("all_1", by_self, by_ffn, by_cross)
    got_both = other(later(both, by_self.keeps[0]))
    (grad_memory,) = run(widen_kernel, [memory_got], [far((memory_got.shape, F32))], name="widen_memory")
    advance("all_2", by_self, by_ffn, by_cross)
    advance("self_cross_3", by_self, by_cross)
    while not (by_self.ready() and by_cross.ready() and by_ffn.ready()):
        advance("rest", by_self, by_cross, by_ffn)
    mixed, grad_inputs = run(
        place_rows_kernel,
        [both, got_both],
        [far(((rows, seq, width), BF16)), far(((rows, seq, width), F32))],
        name="place_rows",
    )
    grad_ffn_in, grad_ffn_out = run(
        functools.partial(ffn_grads_kernel, by_ffn.halved[0]),
        [by_ffn.chunk, by_ffn.got],
        [far(((width, unit), F32)), far(((unit, width), F32))],
        name="ffn_grads",
    )
    grad_cross_q, grad_cross_kv, grad_cross_out = run(
        functools.partial(cross_grads_kernel, by_cross.halved[0]),
        [by_cross.chunk, by_cross.got],
        [far(((width, head), F32)), far(((2, width, head), F32)), far(((head, width), F32))],
        name="cross_grads",
    )
    if fits:
        outs = [((2, head), F32), ((2, head), F32), ((1, unit), F32)]
    else:
        outs = [((lines, width), F32)]
    grad_self_qkv, grad_self_out, grad_gain, grad_shift, grad_out_bias, *rest = run(
        functools.partial(self_grads_kernel, by_self.halved[0]),
        [by_self.chunk, by_self.got],
        [far(((3, width, head), F32)), far(((head, width), F32))] + [far(((3, width), F32))] * 3 + [far(v) for v in outs],
        name="self_grads",
    )
    if fits:
        grad_self_bias, grad_cross_bias, grad_ffn_bias = rest[0], rest[1], rest[2].reshape(-1)
    else:
        own_small = rest[0].reshape(-1)
        grad_self_bias = own_small[: 2 * head].reshape(2, head)
        grad_cross_bias = own_small[2 * head : 4 * head].reshape(2, head)
        grad_ffn_bias = own_small[4 * head :]
    return (
        mixed,
        grad_inputs,
        grad_memory,
        grad_gain,
        grad_shift,
        grad_self_qkv,
        grad_self_bias,
        grad_self_out,
        grad_cross_q,
        grad_cross_kv,
        grad_cross_bias,
        grad_cross_out,
        grad_ffn_in,
        grad_ffn_bias,
        grad_ffn_out,
        grad_out_bias,
    )


def solution(mesh):
    placed = (
        P("dp", None, None),
        P(None, "dp", None),
        P("dp", None),
        P("dp", None),
        P(),
        P(),
        P(),
        P(),
        P(None, None, "mp"),
        P(None, "mp"),
        P("mp", None),
        P(None, "mp"),
        P(None, None, "mp"),
        P(None, "mp"),
        P("mp", None),
        P(None, "mp"),
        P("mp"),
        P("mp", None),
        P(),
        P("dp", None, None),
    )
    return jax.shard_map(
        shards,
        mesh=mesh,
        in_specs=placed,
        out_specs=(
            P("dp", None, None),
            P("dp", None, None),
            P(None, "dp", "mp"),
            P(),
            P(),
            P(None, None, "mp"),
            P(None, "mp"),
            P("mp", None),
            P(None, "mp"),
            P(None, None, "mp"),
            P(None, "mp"),
            P("mp", None),
            P(None, "mp"),
            P("mp"),
            P("mp", None),
            P(),
        ),
        check_vma=False,
    )
```

```python
import functools

import jax
import jax.numpy as jnp
from jax import lax
from jax.experimental import pallas as pl
from jax.experimental.pallas import tpu as pltpu
from jax.sharding import PartitionSpec as P

HDIM = 64
LANES = 128
BLOCK = 128
SMALL = 16
FRONT = 2
BACK = 2
EPSILON = 1e-05
F32 = jnp.float32
BF16 = jnp.bfloat16


def dot(left, right):
    return lax.dot_general(left, right, (((1,), (0,)), ((), ())), preferred_element_type=F32)


def dot_right(left, right):
    return lax.dot_general(left, right, (((1,), (1,)), ((), ())), preferred_element_type=F32)


def dot_left(left, right):
    return lax.dot_general(left, right, (((0,), (0,)), ((), ())), preferred_element_type=F32)


class Far:
    def __init__(self, value, pick=False):
        self.value, self.pick = value, pick


class Raw:
    def __init__(self, value):
        self.value = value


class Scalars:
    def __init__(self, value):
        self.value = value


class Flow:
    def __init__(self):
        self.loads, self.stores, self.sent = {}, {}, []

    def need(self, *refs):
        for ref in refs:
            copy = self.loads.pop(id(ref), None)
            if copy is not None:
                copy.wait()

    def send(self, *refs):
        for ref in refs:
            copy = self.stores.pop(id(ref), None)
            if copy is not None:
                copy.start()
                self.sent.append(copy)


class Steps:
    def __init__(self, where):
        self.where, self.token = where, None

    def batch(self, parts, name=None, cost=0.1):
        def kernel(flow, where, *refs):
            at, to = 0, sum(len(ins) for _, ins, _ in parts)
            for part, ins, outs in parts:
                part(flow, where, *refs[at : at + len(ins)], *refs[to : to + len(outs)])
                at, to = at + len(ins), to + len(outs)

        got = self(
            kernel, [v for _, ins, _ in parts for v in ins], [v for _, _, outs in parts for v in outs], name=name, cost=cost
        )
        results = []
        for _, _, outs in parts:
            results.append(got[: len(outs)])
            got = got[len(outs) :]
        return results

    def __call__(self, kernel, ins, outs, scratch=(), name=None, cost=0.1, hold=()):
        near = pl.BlockSpec(memory_space=pltpu.VMEM)
        far = pl.BlockSpec(memory_space=pltpu.HBM)
        words = pl.BlockSpec(memory_space=pltpu.SMEM)
        values, specs, stages = [], [], []
        for v in ins:
            if isinstance(v, Scalars):
                values.append(v.value)
                specs.append(words)
            elif isinstance(v, Raw):
                values.append(pltpu.with_memory_space_constraint(v.value, pltpu.HBM))
                specs.append(far)
            elif isinstance(v, Far):
                values.append(pltpu.with_memory_space_constraint(v.value, pltpu.HBM))
                specs.append(far)
                stages.append(pltpu.VMEM(v.value.shape[1:] if v.pick else v.value.shape, v.value.dtype))
            else:
                values.append(pltpu.with_memory_space_constraint(v, pltpu.VMEM))
                specs.append(near)
        after = [pltpu.with_memory_space_constraint(v, pltpu.VMEM) for v in hold]
        after_specs = [near] * len(after)
        if self.token is not None:
            after.append(pltpu.with_memory_space_constraint(self.token, pltpu.HBM))
            after_specs.append(far)
        for v in outs:
            if isinstance(v, Far):
                stages.append(pltpu.VMEM(*v.value))
        shapes = [pltpu.HBM(*v.value) if isinstance(v, (Far, Raw)) else pltpu.VMEM(*v) for v in outs]
        count, n_in, n_out, n_after = len(stages), len(ins), len(outs), len(after)

        def body(where_ref, *refs):
            refs = list(refs)
            in_refs, refs = refs[:n_in], refs[n_in + n_after :]
            out_refs, refs = refs[:n_out], refs[n_out + 1 :]
            stage_refs, refs = refs[:count], refs[count:]
            flow = Flow()
            if count:
                sems, refs = refs[0], refs[1:]
            given, k = [], 0
            for v, ref in zip(ins, in_refs):
                if isinstance(v, Far):
                    source = ref.at[where_ref[0]] if v.pick else ref
                    copy = pltpu.make_async_copy(source, stage_refs[k], sems.at[k])
                    copy.start()
                    flow.loads[id(stage_refs[k])] = copy
                    ref, k = stage_refs[k], k + 1
                given.append(ref)
            for v, ref in zip(outs, out_refs):
                if isinstance(v, Far):
                    flow.stores[id(stage_refs[k])] = pltpu.make_async_copy(stage_refs[k], ref, sems.at[k])
                    ref, k = stage_refs[k], k + 1
                given.append(ref)
            kernel(flow, where_ref, *given, *refs)
            for copy in flow.loads.values():
                copy.wait()
            for copy in flow.stores.values():
                copy.start()
            for copy in [*flow.sent, *flow.stores.values()]:
                copy.wait()

        results = pl.pallas_call(
            body,
            in_specs=[words] + specs + after_specs,
            out_specs=[far if isinstance(v, (Far, Raw)) else near for v in outs] + [far],
            out_shape=shapes + [pltpu.HBM((8, LANES), F32)],
            scratch_shapes=stages + ([pltpu.SemaphoreType.DMA((count,))] if count else []) + list(scratch),
            compiler_params=pltpu.CompilerParams(vmem_limit_bytes=24 * 1024 * 1024),
            cost_estimate=pl.CostEstimate(flops=10**6, bytes_accessed=int(cost * 3 * 10**6), transcendentals=0),
            name=name,
        )(self.where, *values, *after)
        self.token = results[-1]
        return list(results[:-1])


def row_blocks(seq):
    return [slice(start, start + BLOCK) for start in range(0, seq, BLOCK)]


def row_of(ref, i):
    return ref[i : i + 1, :].astype(F32)


GAIN, SHIFT, OUT, SCALE, VECTORS = 0, 3, 6, 9, 16


def norm_parts(value):
    centre = value - jnp.mean(value, axis=-1, keepdims=True)
    spread = jnp.mean(centre * centre, axis=-1, keepdims=True)
    scale = lax.rsqrt(spread + EPSILON)
    return centre * scale, scale


def norm_backward(value, gain, incoming):
    xhat, scale = norm_parts(value)
    weighted = incoming * gain
    grad = scale * (
        weighted
        - jnp.mean(weighted, axis=-1, keepdims=True)
        - xhat * jnp.mean(weighted * xhat, axis=-1, keepdims=True)
    )
    return grad, jnp.sum(incoming * xhat, axis=0, keepdims=True), jnp.sum(incoming, axis=0, keepdims=True)


def head_lanes(value, j):
    lane = lax.broadcasted_iota(jnp.int32, value.shape, 1)
    return jnp.where((lane >= HDIM) == bool(j), value, jnp.zeros_like(value))


def span_of(block, seq, banded):
    if not banded:
        return slice(0, seq)
    return slice(max(block.start - BLOCK, 0), block.stop)


def start_all(moves, sems):
    copies = [pltpu.make_async_copy(a, b, sems.at[i]) for i, (a, b) in enumerate(moves)]
    for copy in copies:
        copy.start()
    return copies


def setup_kernel(packing, flow, where, *refs):
    group_tokens, bucket_group, lengths, inputs, cotangent, memory, segments, gains, shifts, biases, refs = *refs[:10], refs[10:]
    if packing:
        query, kv, out, w_in, w_out, cross, ffn, refs = *refs[:7], refs[7:]
    x, cot, memory_part, vectors, molecules, tokens_now, group_now, lengths_now, word_sems, sems = refs
    words = start_all([(group_tokens, tokens_now), (bucket_group, group_now), (lengths, lengths_now)], word_sems)
    moves = [(memory.at[:, where[0]], memory_part), (inputs.at[where[0]], x), (cotangent.at[where[0]], cot)]
    if packing:
        full, wide = query.shape
        half = full // 2
        rows = pl.ds(pl.multiple_of(where[3] * half, half), half)
        moves += [
            (query.at[rows, :], cross.at[0:half, :]),
            (kv.at[0, rows, :], cross.at[half : 2 * half, :]),
            (kv.at[1, rows, :], cross.at[2 * half : 3 * half, :]),
        ]
        count, size = out.shape[1] // wide // 2, out.shape[0]
        for k in range(count):
            lanes = pl.ds(pl.multiple_of((where[3] * count + k) * wide, wide), wide)
            moves.append((out.at[:, lanes], cross.at[3 * half + k * size : 3 * half + (k + 1) * size, :]))
        moves += [(w_in, ffn.at[0]), (w_out, ffn.at[1])]
    copies = start_all(moves, sems)
    for copy in words:
        copy.wait()
    width = vectors.shape[1]
    total, own = 0, 0
    for b in range(bucket_group.shape[0]):
        tokens = tokens_now[group_now[b]]
        total = total + tokens
        own = own + jnp.where(where[2] == b, tokens, 0)
    scaled = jnp.full((1, width), bucket_group.shape[0] * own, jnp.int32).astype(F32)
    scale = scaled / jnp.full((1, width), total, jnp.int32).astype(F32)
    size = molecules.shape[1]
    place = lax.broadcasted_iota(jnp.int32, (1, size), 1)
    count, end = jnp.zeros((1, size), jnp.int32), 0
    for k in range(lengths.shape[1]):
        end = end + lengths_now[where[0], k]
        count = count + (end <= place).astype(jnp.int32)
    molecules[1:2, :] = count
    flow.need(segments, gains, shifts, biases)
    molecules[0:1, :] = segments[pl.ds(where[0], 1), :]
    rows = [r[...].astype(F32) for r in (gains, shifts, biases)] + [scale]
    vectors[...] = jnp.concatenate(rows + [jnp.zeros((VECTORS - 10, width), F32)], axis=0)
    for copy in copies:
        copy.wait()


def key_columns(keys):
    size = keys.shape[1]
    tiles = [jnp.broadcast_to(keys[:, at : at + BLOCK], (LANES, BLOCK)).T for at in range(0, size, BLOCK)]
    return jnp.concatenate(tiles, axis=0)


def allowed_of(own, columns, block, span, banded):
    allowed = columns[span] == own[:, block]
    if banded:
        query = lax.broadcasted_iota(jnp.int32, allowed.shape, 1) + block.start
        key = lax.broadcasted_iota(jnp.int32, allowed.shape, 0) + span.start
        allowed = allowed & (key <= query)
    return allowed


def head_rows(value, j):
    row = lax.broadcasted_iota(jnp.int32, value.shape, 0)
    return jnp.where((row >= HDIM) == bool(j), value, jnp.zeros_like(value))


def attend_forward(q, k, v, own, keys, heads, totals, banded):
    seq, wide = q.shape
    columns = key_columns(keys)
    for pair in range(wide // LANES):
        lanes = slice(pair * LANES, (pair + 1) * LANES)
        turned = [head_rows(v[:, lanes].T, j) for j in (0, 1)]
        for block in row_blocks(seq):
            span = span_of(block, k.shape[0], banded)
            allowed = allowed_of(own, columns, block, span, banded)
            query, keyset = q[block, lanes] * 0.125, k[span, lanes]
            mixed = None
            for j in (0, 1):
                scores = jnp.where(allowed, dot_right(keyset, head_lanes(query, j)), -1e30)
                maxima = jnp.max(scores, axis=0, keepdims=True)
                raised = jnp.exp(scores - maxima)
                total = jnp.sum(raised, axis=0, keepdims=True)
                chances = (raised * (1.0 / total)).astype(BF16)
                term = dot(turned[j][:, span], chances)
                mixed = term if mixed is None else mixed + term
                totals[2 * pair + j : 2 * pair + j + 1, block] = maxima + jnp.log(total)
            heads[block, lanes] = mixed.T.astype(BF16)


def attend_backward(q, k, v, own, keys, totals, grad_heads, dq, dk, dv, sum_k, sum_v, banded):
    seq, wide = q.shape
    columns = key_columns(keys)
    for pair in range(wide // LANES):
        lanes = slice(pair * LANES, (pair + 1) * LANES)
        turned = [head_rows(k[:, lanes].T, j) for j in (0, 1)]
        for at, block in enumerate(row_blocks(seq)):
            span = span_of(block, k.shape[0], banded)
            allowed = allowed_of(own, columns, block, span, banded)
            query, keyset, values = q[block, lanes] * 0.125, k[span, lanes], v[span, lanes]
            grad = grad_heads[block, lanes]
            grad_query = grad_key = grad_value = None
            for j in (0, 1):
                head = 2 * pair + j
                part, own_grad = head_lanes(query, j), head_lanes(grad, j)
                scores = jnp.where(allowed, dot_right(keyset, part), -1e30)
                chances = jnp.exp(scores - totals[head : head + 1, block])
                by_value = dot(chances.astype(BF16), own_grad)
                weighted = chances * dot_right(values, own_grad)
                mean = jnp.sum(weighted, axis=0, keepdims=True)
                grad_scores = (weighted - chances * mean).astype(BF16)
                by_query, by_key = dot(turned[j][:, span], grad_scores), dot(grad_scores, part)
                if j == 0:
                    grad_query, grad_key, grad_value = by_query, by_key, by_value
                else:
                    grad_query, grad_key, grad_value = grad_query + by_query, grad_key + by_key, grad_value + by_value
            dq[block, lanes] = (grad_query.T * 0.125).astype(BF16)
            if banded:
                early = block.start - span.start
                sum_k[block, lanes] = grad_key[early:]
                sum_v[block, lanes] = grad_value[early:]
                if early:
                    sum_k[span.start : block.start, lanes] += grad_key[:early]
                    sum_v[span.start : block.start, lanes] += grad_value[:early]
            elif at == 0:
                sum_k[:, lanes] = grad_key
                sum_v[:, lanes] = grad_value
            else:
                sum_k[:, lanes] += grad_key
                sum_v[:, lanes] += grad_value
    dk[...] = sum_k[...].astype(BF16)
    dv[...] = sum_v[...].astype(BF16)


def team_total(mine, theirs, block):
    half = mine[0].shape[0]
    k, rows = block.start // half, slice(block.start % half, block.start % half + BLOCK)
    return mine[k][rows, :].astype(F32) + theirs[k][rows, :].astype(F32)


def put_half(parts, block, value):
    half = parts[0].shape[0]
    start = block.start % half
    parts[block.start // half][start : start + BLOCK, :] = value.astype(parts[0].dtype)


def self_forward_kernel(n, i, flow, where, *refs):
    last = i == n - 1
    first, vectors, molecules, w, bias, refs = *refs[:5], refs[5:]
    if last:
        w_out, done, refs = refs[:n], refs[n : 2 * n - 1], refs[2 * n - 1 :]
    if i == 0:
        normed, refs = refs[0], refs[1:]
        for block in row_blocks(first.shape[0]):
            norm = norm_parts(first[block, :].astype(F32))[0]
            normed[block, :] = (norm * row_of(vectors, GAIN) + row_of(vectors, SHIFT)).astype(BF16)
    else:
        normed = first
    q, k, v, heads, totals = refs[:5]
    flow.need(w)
    q[...] = (dot(normed[...], w[0]) + row_of(bias, 0)).astype(BF16)
    k[...] = dot(normed[...], w[1]).astype(BF16)
    v[...] = (dot(normed[...], w[2]) + row_of(bias, 1)).astype(BF16)
    own = molecules[0:1, :]
    flow.send(q, k, v)
    attend_forward(q, k, v, own, own, heads, totals, True)
    flow.send(totals)
    if last:
        project_out(flow, [*done, heads], w_out, refs[5 : 5 + FRONT])


def project_out(flow, heads, w_out, parts):
    flow.need(*w_out)
    for block in row_blocks(heads[0].shape[0]):
        put_half(parts, block, sum(dot(h[block, :], w[...]) for h, w in zip(heads, w_out)))


def memory_kernel(flow, where, memory, w, bias, k, v):
    flow.need(w)
    k[...] = dot(memory[...], w[0]).astype(BF16)
    v[...] = (dot(memory[...], w[1]) + row_of(bias, 3)).astype(BF16)


def unpack_memory_kernel(flow, where, near, got, memory, bias, query, kv, out, k, v):
    full, wide = query.shape
    half, size = full // 2, out.shape[0]
    count = out.shape[1] // wide // 2
    for packed, bit in ((near, where[3]), (got, 1 - where[3])):
        rows = pl.ds(pl.multiple_of(bit * half, half), half)
        query[rows, :] = packed[:half]
        for i in (0, 1):
            kv[i, rows, :] = packed[(i + 1) * half : (i + 2) * half]
        for i in range(count):
            lanes = pl.ds(pl.multiple_of((bit * count + i) * wide, wide), wide)
            out[:, lanes] = packed[3 * half + i * size : 3 * half + (i + 1) * size]
    memory_kernel(flow, where, memory, kv, bias, k, v)


def cross_forward_kernel(n, i, flow, where, *refs):
    last = i == n - 1
    if i == 0:
        x, mine, theirs, refs = refs[0], refs[1 : 1 + FRONT], refs[1 + FRONT : 1 + 2 * FRONT], refs[1 + 2 * FRONT :]
    else:
        normed, refs = refs[0], refs[1:]
    vectors, molecules, w, bias, k, v, refs = *refs[:6], refs[6:]
    if last:
        w_out, done, refs = refs[:n], refs[n : 2 * n - 1], refs[2 * n - 1 :]
    if i == 0:
        after_self, normed, refs = refs[0], refs[1], refs[2:]
    q, heads, totals = refs[:3]
    if i == 0:
        for block in row_blocks(x.shape[0]):
            value = x[block, :].astype(F32) + team_total(mine, theirs, block) + row_of(vectors, OUT)
            after_self[block, :] = value
            norm = norm_parts(value)[0]
            normed[block, :] = (norm * row_of(vectors, GAIN + 1) + row_of(vectors, SHIFT + 1)).astype(BF16)
    flow.need(w)
    q[...] = (dot(normed[...], w[...]) + row_of(bias, 2)).astype(BF16)
    attend_forward(q, k, v, molecules[0:1, :], molecules[1:2, :], heads, totals, False)
    if last:
        project_out(flow, [*done, heads], w_out, refs[3 : 3 + FRONT])


def ffn_kernel(i, flow, where, *refs):
    if i == 0:
        after_self, mine, theirs, refs = refs[0], refs[1 : 1 + FRONT], refs[1 + FRONT : 1 + 2 * FRONT], refs[1 + 2 * FRONT :]
        cotangent, vectors, w_in, bias, w_out, refs = *refs[:5], refs[5:]
        after_cross, normed, low, active, grad_hidden, part, part_grad = refs
    else:
        normed, low, begun, begun_grad, w_in, bias, refs = *refs[:6], refs[6:]
        if len(w_in.shape) == 3:
            w_in, w_out = w_in.at[0], w_in.at[1]
        else:
            w_out, refs = refs[0], refs[1:]
        active, grad_hidden, parts, parts_grad = refs[0], refs[1], refs[2 : 2 + BACK], refs[2 + BACK :]
    if bias.shape[0] == 1:
        row = row_of(bias, 0)
    else:
        row = jnp.concatenate([row_of(bias, k) for k in range(4, bias.shape[0])], axis=1)
    if i == 0:
        for block in row_blocks(normed.shape[0]):
            value = after_self[block, :] + team_total(mine, theirs, block) + row_of(vectors, OUT + 1)
            after_cross[block, :] = value
            norm = norm_parts(value)[0]
            normed[block, :] = (norm * row_of(vectors, GAIN + 2) + row_of(vectors, SHIFT + 2)).astype(BF16)
            low[block, :] = (cotangent[block, :].astype(F32) * row_of(vectors, SCALE)).astype(BF16)
    flow.need(w_in, w_out)
    for block in row_blocks(normed.shape[0]):
        hidden = dot(normed[block, :], w_in[...]) + row
        cdf = 0.5 * (1.0 + lax.erf(hidden * 0.7071067811865476))
        act = (hidden * cdf).astype(BF16)
        active[block, :] = act
        slope = cdf + hidden * (0.3989422804014327 * jnp.exp(-0.5 * hidden * hidden))
        back = (slope * dot_right(low[block, :], w_out[...])).astype(BF16)
        grad_hidden[block, :] = back
        out, out_grad = dot(act, w_out[...]), dot_right(back, w_in[...])
        if i == 0:
            part[block, :], part_grad[block, :] = out, out_grad
        else:
            put_half(parts, block, begun[block, :] + out)
            put_half(parts_grad, block, begun_grad[block, :] + out_grad)


def ffn_weights_kernel(flow, where, *refs):
    hidden, active, normed, low, sums = refs[:2], refs[2:4], refs[4], refs[5], refs[6]
    keep_out, send_out, keep_in, send_in = refs[7:]
    half = keep_in.shape[1]
    for i in (0, 1):
        for target, bit in ((keep_in, where[3]), (send_in, 1 - where[3])):
            lanes = pl.ds(pl.multiple_of(bit * half, half), half)
            target[i] = dot_left(hidden[i][:, lanes], normed[...]).astype(target.dtype)
        sums[i : i + 1, :] = jnp.sum(hidden[i][...].astype(F32), axis=0, keepdims=True)
    keep_out[0] = dot_left(active[0][...], low[...])
    send_out[0] = dot_left(active[1][...], low[...]).astype(BF16)


def spread_grad_heads(low, w_out, grad_heads):
    for piece, target in zip(w_out, grad_heads):
        target[...] = dot_right(low[...], piece[...]).astype(BF16)


def column_sums(sums, values):
    for i, value in enumerate(values):
        sums[i : i + 1, :] = jnp.sum(value[...].astype(F32), axis=0, keepdims=True)


def cross_backward_kernel(n, flow, where, *refs):
    after_cross, mine, theirs, refs = refs[0], refs[1 : 1 + BACK], refs[1 + BACK : 1 + 2 * BACK], refs[1 + 2 * BACK :]
    cotangent, vectors, molecules, refs = *refs[:3], refs[3:]
    (q, k, v, totals, w_out, w), refs = [refs[i * n : (i + 1) * n] for i in range(6)], refs[6 * n :]
    grad_cross, low, refs = refs[0], refs[1], refs[2:]
    (dq, dk, dv, bias_sums), refs = [refs[i * n : (i + 1) * n] for i in range(4)], refs[4 * n :]
    parts_out, sums, refs = refs[:BACK], refs[BACK], refs[BACK + 1 :]
    grad_heads, sum_k, sum_v = refs[:n], refs[n], refs[n + 1]
    seq, width = after_cross.shape
    rows = [jnp.zeros((1, width), F32)] * 3
    for block in row_blocks(seq):
        incoming = team_total(mine, theirs, block)
        grad_result = cotangent[block, :].astype(F32) * row_of(vectors, SCALE)
        back, by_gain, by_shift = norm_backward(after_cross[block, :], row_of(vectors, GAIN + 2), incoming)
        value = grad_result + back
        grad_cross[block, :] = value
        low[block, :] = value.astype(BF16)
        parts = (by_gain, by_shift, jnp.sum(grad_result, axis=0, keepdims=True))
        rows = [a + b for a, b in zip(rows, parts)]
    for i, row in enumerate(rows):
        sums[i : i + 1, :] = row
    flow.need(*w_out)
    spread_grad_heads(low, w_out, grad_heads)
    own, keys = molecules[0:1, :], molecules[1:2, :]
    for i in range(n):
        attend_backward(
            q[i], k[i], v[i], own, keys, totals[i], grad_heads[i], dq[i], dk[i], dv[i], sum_k, sum_v, False
        )
        column_sums(bias_sums[i], (dq[i], dv[i]))
    flow.need(*w)
    for block in row_blocks(seq):
        put_half(parts_out, block, sum(dot_right(d[block, :], m[...]) for d, m in zip(dq, w)))


def shard_grads(kinds):
    grads = ([], [])
    for kind in kinds:
        if len(kind) == 2:
            for i in (0, 1):
                grads[i].append(dot_left(kind[i][0][...], kind[i][1][...]))
        else:
            left, right = kind[0]
            both, half = dot_left(left[...], right[...]), left.shape[1] // 2
            grads[0].append(both[:half])
            grads[1].append(both[half:])
    return grads


def cross_weights_kernel(n, flow, where, *refs):
    (dq, dk, dv, heads, w), refs = [refs[i * n : (i + 1) * n] for i in range(5)], refs[5 * n :]
    normed, memory, low, after_cross, refs = *refs[:4], refs[4:]
    mine, theirs, vectors, refs = refs[:BACK], refs[BACK : 2 * BACK], refs[2 * BACK], refs[2 * BACK + 1 :]
    keep, send, terms, result = refs[0], refs[1], refs[2 : 2 + BACK], refs[-1]
    flow.need(*w)
    pairs = [[(a, b) for a in left] for left, b in ((dq, normed), (dk, memory), (dv, memory), (heads, low))]
    first = where[3] == 0
    for i, grads in enumerate(shard_grads(pairs)):
        upper, lower = jnp.concatenate(grads[:2], axis=0), jnp.concatenate(grads[2:], axis=0)
        keep[i] = jnp.where(first, upper, lower)
        send[i] = jnp.where(first, lower, upper).astype(BF16)
    for block in row_blocks(memory.shape[0]):
        total = sum(
            dot_right(a[block, :], m[0]) + dot_right(b[block, :], m[1]) for a, b, m in zip(dk, dv, w)
        )
        put_half(terms, block, total)
    for block in row_blocks(after_cross.shape[0]):
        both = team_total(mine, theirs, block)
        result[block, :] = (after_cross[block, :] + both + row_of(vectors, OUT + 2)).astype(BF16)


def put_grads(target, grads):
    size = grads[0].shape[0]
    for k, grad in enumerate(grads):
        target[0, k * size : (k + 1) * size, :] = grad.astype(target.dtype)


def self_backward_kernel(n, flow, where, *refs):
    after_self, mine, theirs, refs = refs[0], refs[1 : 1 + BACK], refs[1 + BACK : 1 + 2 * BACK], refs[1 + 2 * BACK :]
    grad_cross, vectors, molecules, q, k, v, totals, refs = *refs[:7], refs[7:]
    w_out, refs = refs[:n], refs[n:]
    normed, heads, grad_self, low, dq, dk, dv, bias_sums, sums, refs = *refs[:9], refs[9:]
    first, send, grad_heads, sum_k, sum_v = refs
    seq, width = after_self.shape
    rows = [jnp.zeros((1, width), F32)] * 3
    for block in row_blocks(seq):
        incoming = team_total(mine, theirs, block)
        back, by_gain, by_shift = norm_backward(after_self[block, :], row_of(vectors, GAIN + 1), incoming)
        upper = grad_cross[block, :]
        value = upper + back
        grad_self[block, :] = value
        low[block, :] = value.astype(BF16)
        parts = (by_gain, by_shift, jnp.sum(upper, axis=0, keepdims=True))
        rows = [a + b for a, b in zip(rows, parts)]
    for i, row in enumerate(rows):
        sums[i : i + 1, :] = row
    flow.need(*w_out)
    spread_grad_heads(low, w_out, [first, grad_heads] if n == 2 else [grad_heads])
    own = molecules[0:1, :]
    flow.need(q, k, v, totals)
    attend_backward(q, k, v, own, own, totals, grad_heads, dq, dk, dv, sum_k, sum_v, True)
    column_sums(bias_sums, (dq, dv))
    grads = [dot_left(a[...], b[...]) for a, b in ((dq, normed), (dk, normed), (dv, normed), (heads, low))]
    if n == 2:
        put_grads(send, grads)
    else:
        half = grads[0].shape[0] // 2
        put_grads(first, [g[:half] for g in grads])
        put_grads(send, [g[half:] for g in grads])


def self_backward_rest_kernel(n, flow, where, *refs):
    w, grads_last, refs = refs[:n], refs[n : n + 3], refs[n + 3 :]
    pieces = [grads_last]
    if n == 2:
        molecules, q, k, v, totals, grad_heads, normed, heads, low, refs = *refs[:9], refs[9:]
        bias_sums, keep, parts_out, refs = refs[0], refs[1], refs[2 : 2 + BACK], refs[2 + BACK :]
        dq, dk, dv, sum_k, sum_v = refs
        own = molecules[0:1, :]
        flow.need(q, k, v, totals)
        attend_backward(q, k, v, own, own, totals, grad_heads, dq, dk, dv, sum_k, sum_v, True)
        column_sums(bias_sums, (dq, dv))
        put_grads(keep, [dot_left(a[...], b[...]) for a, b in ((dq, normed), (dk, normed), (dv, normed), (heads, low))])
        pieces = [(dq, dk, dv), grads_last]
    else:
        parts_out = refs[:BACK]
    flow.need(*w)
    for block in row_blocks(grads_last[0].shape[0]):
        total = 0.0
        for matrices, grads in zip(w, pieces):
            for which, d in enumerate(grads):
                total += dot_right(d[block, :], matrices[which])
        put_half(parts_out, block, total)


def input_backward_kernel(n, flow, where, x, *refs):
    mine, theirs, refs = refs[:BACK], refs[BACK : 2 * BACK], refs[2 * BACK :]
    grad_self, vectors, result, by_cross, by_ffn, refs = *refs[:5], refs[5:]
    shard_rows, (both, small_own, small_other) = refs[:-3], refs[-3:]
    seq = x.shape[0]
    both[:seq, :] = result[...]
    width = x.shape[1]
    rows = [jnp.zeros((1, width), F32)] * 3
    for block in row_blocks(x.shape[0]):
        incoming = team_total(mine, theirs, block)
        back, by_gain, by_shift = norm_backward(x[block, :].astype(F32), row_of(vectors, GAIN), incoming)
        upper = grad_self[block, :]
        both[seq + block.start : seq + block.stop, :] = (upper + back).astype(BF16)
        parts = (by_gain, by_shift, jnp.sum(upper, axis=0, keepdims=True))
        rows = [a + b for a, b in zip(rows, parts)]
    common = [r for k in range(3) for r in (rows[k], by_cross[k : k + 1, :], by_ffn[k : k + 1, :])]
    if len(shard_rows) == 1:
        lines = [shard_rows[0][i] for i in (0, 1)]
    else:
        sums_self, sums_cross, sums_ffn = shard_rows[:n], shard_rows[n : 2 * n], shard_rows[2 * n]
        lines = []
        for i in (0, 1):
            pieces = [r[k : k + 1, :] for r in (sums_self[i], sums_cross[i]) for k in (0, 1)]
            lines.append(jnp.concatenate([jnp.concatenate(pieces, axis=1), sums_ffn[i : i + 1, :]], axis=0))
    rest = jnp.zeros((SMALL - 9 - lines[0].shape[0], width), F32)
    small = [jnp.concatenate([*common, line, rest], axis=0).astype(BF16) for line in lines]
    small_own[...] = small[0]
    small_other[...] = small[1]


def fold_kernel(count, size, ride, mode, bit, flow, where, *refs):
    keeps, gots, refs = refs[:count], refs[count : 2 * count], refs[2 * count :]
    planes = [(k, p) for k in range(count) for p in range(keeps[k].shape[0])]

    def part(at, rows):
        k, p = planes[at]
        return keeps[k][p, rows, :].astype(F32) + gots[k][p, rows, :].astype(F32)

    if mode == "half":
        keep, send = refs
        half = size // 2
        for at in range(len(planes)):
            for target, side in ((keep, where[3 + bit]), (send, 1 - where[3 + bit])):
                rows = pl.ds(pl.multiple_of(side * half, half), half)
                target[at, :half, :] = part(at, rows).astype(target.dtype)
    elif mode == "shard":
        if ride is not None:
            refs[-1][0, size : size + SMALL, :] = refs[0][...]
        for at, target in enumerate(refs[-2:]):
            target[0, :size, :] = part(at, slice(0, size)).astype(target.dtype)
    else:
        out = refs[-1]
        for at in range(len(planes)):
            out[at, :size, :] = part(at, slice(0, size)).astype(out.dtype)
        if ride is not None:
            own, came = refs[:2]
            small = own[...].astype(F32) + came[0, ride : ride + SMALL, :].astype(F32)
            out[0, size : size + SMALL, :] = small.astype(out.dtype)


def memory_pairs(axis):
    step = 1 if axis == "row" else 2 << axis
    return [(k, k | step) for k in range(16) if not k & step]


def memory_bit(where, axis):
    return where[0] if axis == "row" else where[3 + axis]


def send_blocks(where, axis, blocks, send, offset):
    low = memory_bit(where, axis) == 0
    per = 8 // send.shape[0]
    for k, (a, b) in enumerate(memory_pairs(axis)):
        at = offset + k % per * SMALL
        send[k // per, at : at + SMALL, :] = jnp.where(low, blocks[b], blocks[a])


def take_blocks(where, axis, kept, got, offset):
    low = memory_bit(where, axis) == 0
    per = 8 // got.shape[0]
    blocks = {}
    for k, (a, b) in enumerate(memory_pairs(axis)):
        at = offset + k % per * SMALL
        came = got[k // per, at : at + SMALL, :]
        blocks[a] = jnp.where(low, kept[a], came)
        blocks[b] = jnp.where(low, came, kept[b])
    return blocks


def memory_start_kernel(axis, flow, where, *refs, send, offset):
    mine, theirs, kept = refs[:BACK], refs[BACK : 2 * BACK], refs[2 * BACK]
    half, width = mine[0].shape
    tokens = half * BACK // 8
    share = LANES
    blocks = {}
    for r in (0, 1):
        lanes = pl.ds(pl.multiple_of((2 * r + where[1]) * share, share), share)
        for k in range(BACK):
            total = (mine[k][:, lanes].astype(F32) + theirs[k][:, lanes].astype(F32)).astype(BF16)
            for d in range(half // tokens):
                block = total[d * tokens : (d + 1) * tokens]
                parts = [block[q : q + SMALL] for q in range(0, tokens, SMALL)]
                at = 2 * (k * half // tokens + d) + r
                blocks[at] = jnp.concatenate(parts, axis=1)
                kept[at] = blocks[at]
    send_blocks(where, axis, blocks, send, offset)


def memory_send_kernel(before, at, axis, flow, where, old, got, kept, send):
    blocks = take_blocks(where, before, old, got, at)
    for k, block in blocks.items():
        kept[k] = block
    send_blocks(where, axis, blocks, send, 0)


def memory_end_kernel(before, at, flow, where, old, got, out):
    for k, block in take_blocks(where, before, old, got, at).items():
        parts = [block[:, q : q + LANES] for q in range(0, block.shape[1], LANES)]
        out[k] = jnp.concatenate(parts, axis=0).astype(out.dtype)


def join_kernel(ride, bit, flow, where, near, got, out):
    half = near.shape[1] - (SMALL if ride else 0)
    for value, side in ((near, where[3 + bit]), (got, 1 - where[3 + bit])):
        rows = pl.ds(pl.multiple_of(side * half, half), half)
        for p in range(near.shape[0]):
            out[p, rows, :] = value[p, :half]
    if ride:
        out[0, 2 * half :, :] = (near[0, half:].astype(F32) + got[0, half:].astype(F32)).astype(BF16)


def joined(where, bit, near, got, p, ride=0):
    first = where[3 + bit] == 0
    size = near.shape[1] - ride
    a, b = near[p, :size], got[p, :size]
    rows = [jnp.where(first, a, b), jnp.where(first, b, a)]
    return jnp.concatenate(rows, axis=0).astype(F32)


def self_grads_kernel(bit, flow, where, near, got, qkv, out, gains, shifts, biases, *rest):
    size = near.shape[1] - SMALL
    small = near[0, size:].astype(F32) + got[0, size:].astype(F32)
    for k, target in enumerate((gains, shifts, biases)):
        target[...] = small[3 * k : 3 * k + 3]
    if len(rest) == 1:
        rest[0][...] = small[9 : 9 + rest[0].shape[0]]
    else:
        for k, target in enumerate(rest[:2]):
            wide = target.shape[1]
            for i in (0, 1):
                at = (2 * k + i) * wide
                target[i : i + 1, :] = small[9:10, at : at + wide]
        rest[2][...] = small[10:11]
    flow.send(gains, shifts, biases, *rest)
    value = joined(where, bit, near, got, 0, SMALL)
    size = out.shape[0]
    for k in range(3):
        qkv[k] = value[k * size : (k + 1) * size].T
    out[...] = value[3 * size :]


def cross_grads_kernel(bit, flow, where, near, got, query, kv, out):
    value = joined(where, bit, near, got, 0)
    size = out.shape[0]
    query[...] = value[:size].T
    for k in (0, 1):
        kv[k] = value[(k + 1) * size : (k + 2) * size].T
    out[...] = value[3 * size :]


def ffn_grads_kernel(bit, flow, where, near, got, grad_in, grad_out):
    grad_out[...] = joined(where, bit, near, got, 0)
    flow.send(grad_out)
    grad_in[...] = joined(where, bit, near, got, 1).T


def place_rows_kernel(flow, where, own, got, mixed, grad):
    seq = own.shape[0] // 2
    for k, out in enumerate((mixed, grad)):
        for row, value in ((where[0], own), (1 - where[0], got)):
            out[row] = value[k * seq : (k + 1) * seq, :].astype(out.dtype)
        flow.send(out)


def shards(
    inputs,
    memory,
    segment_ids,
    mem_lengths,
    bucket_group,
    group_tokens,
    norm_gain,
    norm_bias,
    self_qkv,
    self_bias,
    self_out,
    cross_q,
    cross_kv,
    cross_bias,
    cross_out,
    ffn_in,
    ffn_bias,
    ffn_out,
    out_bias,
    cotangent,
):
    dp, mp = lax.axis_size("dp"), lax.axis_size("mp")
    rows, seq, width = inputs.shape
    team = mp // rows
    data, place = lax.axis_index("dp"), lax.axis_index("mp")
    row, seat = place // team, place % team
    bits = dp.bit_length() - 1
    where = jnp.stack([row, seat, data] + [(data >> k) & 1 for k in range(bits)]).astype(jnp.int32)
    run, far = Steps(where), Far

    across = [(i, (i + team) % mp) for i in range(mp)]

    def other(value):
        return lax.ppermute(value, "mp", across)

    def seat_swap(value, step):
        return lax.ppermute(value, "mp", [(i, i ^ step) for i in range(mp)])

    def data_swap(value, k):
        return lax.ppermute(value, "dp", [(i, i ^ (1 << k)) for i in range(dp)])

    def swap(value, axis):
        return other(value) if axis == "row" else data_swap(value, axis)

    def later(value, *after):
        return lax.optimization_barrier((value, *after))[0]

    def team_parts(values):
        step = 1
        while 2 * step < team:
            values = [(v.astype(F32) + seat_swap(v, step).astype(F32)).astype(BF16) for v in values]
            step *= 2
        return [*values, *(seat_swap(v, step) for v in values)]

    head, unit = self_bias.shape[1], ffn_bias.shape[0]
    mem_len = memory.shape[1] * dp
    apart = head % LANES == 0
    n = 2 if apart else 1
    wide = head if apart else 2 * head

    front = [((seq // FRONT, width), BF16)] * FRONT
    back = [((seq // BACK, width), BF16)] * BACK
    whole, full = ((seq, width), BF16), ((seq, width), F32)
    local, totals = ((seq, wide), BF16), ((2 * wide // LANES, seq), F32)
    units = ((seq, unit), BF16)

    other_qkv = other(self_qkv)
    bias_own = jnp.concatenate([self_bias, cross_bias, ffn_bias.reshape(-1, head)])
    bias_other = other(bias_own)
    other_self_out = other(self_out)
    memory_rows = memory.reshape((dp, rows) + memory.shape[1:])
    packing = apart and width % (2 * head) == 0 and ffn_in.shape == ffn_out.shape
    ins = [Raw(group_tokens), Raw(bucket_group), Raw(mem_lengths), Raw(inputs), Raw(cotangent), Raw(memory_rows)]
    ins += [far(segment_ids), far(norm_gain), far(norm_bias), far(out_bias)]
    outs = [whole, whole, ((dp,) + memory.shape[1:], BF16), ((VECTORS, width), F32), ((2, seq), jnp.int32)]
    if packing:
        ins += [Raw(v) for v in (cross_q, cross_kv, cross_out, ffn_in, ffn_out)]
        outs = [((3 * width // 2 + cross_out.size // head // 2, head), BF16), ((2,) + ffn_in.shape, BF16)] + outs
    *packed, x, cot, memory_part, vectors, molecules = run(
        functools.partial(setup_kernel, packing),
        ins,
        outs,
        scratch=[pltpu.SMEM(v.shape, jnp.int32) for v in (group_tokens, bucket_group, mem_lengths)]
        + [pltpu.SemaphoreType.DMA((3,)), pltpu.SemaphoreType.DMA((8 + width // head // 2,))],
        name="setup",
    )
    if packing:
        near_cross = other(packed[0])
        got_cross = data_swap(near_cross, 0)
    memory_row = lax.all_to_all(memory_part, "dp", split_axis=0, concat_axis=0, tiled=True).reshape(mem_len, width)
    def pieces(own, theirs, axis):
        return [far(own), theirs] if apart else [jnp.concatenate([own, theirs], axis=axis)]

    w_qkv = pieces(self_qkv, other_qkv, 2)
    w_self_out = pieces(self_out, other_self_out, 0)
    b_heads = [bias_own, bias_other] if apart else [jnp.concatenate([bias_own, bias_other], axis=1)]
    b_in = b_heads if apart else [b[4:].reshape(1, unit) for b in (bias_own, bias_other)]

    heads_self, saved_self = [], []
    for i in range(n):
        last = i == n - 1
        ins = [x if i == 0 else normed_self, vectors, molecules, w_qkv[i], b_heads[i]]
        outs = ([whole] if i == 0 else []) + [far(local)] * 3 + [local, far(totals)]
        if last:
            ins += [*w_self_out, *heads_self]
            outs += front
        got = run(functools.partial(self_forward_kernel, n, i), ins, outs, name=f"self_forward_{i}")
        if i == 0:
            normed_self, got = got[0], got[1:]
            early = (normed_self, other_qkv, bias_other, other_self_out)
            if packing:
                other_ffn = other(later(packed[1], *early, near_cross))
            else:
                other_cross = [other(later(w, *early)) for w in (cross_q, cross_kv, cross_out)]
                other_in, other_out = [other(later(w, *other_cross)) for w in (ffn_in, ffn_out)]
        saved_self.append((got[0], got[1], got[2], got[4]))
        heads_self.append(got[3])
    terms = team_parts(got[5:])

    heads_cross, saved_cross = [], []
    if apart:
        w_cross_q, w_cross_kv, w_cross_out = [far(cross_q)], [far(cross_kv)], [far(cross_out)]
    else:
        w_cross_q = pieces(cross_q, other_cross[0], 1)
        w_cross_kv = pieces(cross_kv, other_cross[1], 2)
        w_cross_out = pieces(cross_out, other_cross[2], 0)
    projected = ((mem_len, wide), BF16)
    for i in range(n):
        last = i == n - 1
        if i == 1 and packing:
            query, both, out, *kv = run(
                unpack_memory_kernel,
                [near_cross, got_cross, memory_row, b_heads[1]],
                [(v.shape, BF16) for v in (cross_q, cross_kv, cross_out)] + [projected] * 2,
                name="memory_1",
            )
            for pieces_of, w in ((w_cross_q, query), (w_cross_kv, both), (w_cross_out, out)):
                pieces_of.append(w)
        else:
            if i == 1:
                for pieces_of, w in zip((w_cross_q, w_cross_kv, w_cross_out), other_cross):
                    pieces_of.append(w)
            kv = run(memory_kernel, [memory_row, w_cross_kv[i], b_heads[i]], [projected] * 2, name=f"memory_{i}")
        first = [x, *terms] if i == 0 else [normed_cross]
        ins = first + [vectors, molecules, w_cross_q[i], b_heads[i], *kv]
        outs = ([full, whole] if i == 0 else []) + [local] * 2 + [totals]
        if last:
            ins += [*w_cross_out, *heads_cross]
            outs += front
        got = run(functools.partial(cross_forward_kernel, n, i), ins, outs, name=f"cross_forward_{i}")
        if i == 0:
            after_self, normed_cross, got = got[0], got[1], got[2:]
        saved_cross.append((got[0], *kv, got[2]))
        heads_cross.append(got[1])
    terms = team_parts(got[3:])

    after_cross, normed_ffn, low_ffn, act_own, hid_own, begun, begun_grad = run(
        functools.partial(ffn_kernel, 0),
        [after_self, *terms, cot, vectors, far(ffn_in), b_in[0], far(ffn_out)],
        [full, whole, whole, units, units, full, full],
        name="ffn_0",
    )
    ins = [other_ffn if packing else other_in, b_in[1]] + ([] if packing else [other_out])
    act_other, hid_other, *parts = run(
        functools.partial(ffn_kernel, 1),
        [normed_ffn, low_ffn, begun, begun_grad, *ins],
        [units, units] + back + back,
        name="ffn_1",
    )
    terms = team_parts(parts[BACK:])
    out_terms = team_parts(parts[:BACK])

    class Reduction:
        def __init__(self, keeps, sends, axes):
            self.keeps, self.axes, self.ride, self.carry = keeps, axes, [], []
            self.gots = [swap(s, a) for s, a in zip(sends, axes[0])]
            self.halved = [b for b in axes[0] if b != "row"][:1]
            self.size = sends[0].shape[1]
            self.chunk = None

        def plan(self, extra=None):
            if self.chunk is not None:
                bit, small = self.halved.pop(), SMALL if self.ride else 0
                planes, size, _ = self.chunk.shape
                outs = [((planes, 2 * size - small, width), BF16)]
                return functools.partial(join_kernel, bool(small), bit), [self.chunk, self.got], outs
            axes, keeps, size = self.axes, self.keeps, self.size
            planes = sum(k.shape[0] for k in keeps)
            bit, ride, at, rows = 0, [], None, size
            if len(axes) == 1:
                mode = "last"
            elif axes[1][0] == "row":
                mode, planes = "shard", 1
                if self.carry:
                    ride, at, rows = self.carry, size, size + SMALL
            elif len(axes) == 2:
                mode = "full"
                if self.ride:
                    ride, at, rows = self.ride, self.ride_at, size + SMALL
                    self.size += SMALL
            else:
                mode, bit, rows = "half", axes[1][0], size // 2
                self.size = rows
                self.halved.append(bit)
            more = 8 // planes * SMALL if extra else 0
            outs = [((planes, rows + more, width), BF16)]
            if mode in ("half", "shard"):
                outs = [((planes, self.size, width), F32)] + outs
            ins = [*keeps, *self.gots, *ride]
            kernel = functools.partial(fold_kernel, len(keeps), size, at, mode, bit)
            if not extra:
                return kernel, ins, outs
            second, second_ins, second_outs = extra
            self.extra_at = rows

            def both(flow, where, *refs):
                a, b = len(ins), len(ins) + len(second_ins)
                c = b + len(second_outs)
                kernel(flow, where, *refs[:a], *refs[c:])
                second(flow, where, *refs[a:c], send=refs[-1], offset=rows)

            return both, ins + second_ins, second_outs + outs

        def take(self, got):
            if self.chunk is not None or len(self.axes) == 1:
                self.chunk = got[0]
                self.got = swap(self.chunk, self.halved[-1])
            else:
                self.axes = self.axes[1:]
                self.keeps = [got[0]]
                self.gots = [swap(got[-1], self.axes[0][0])]

        def ready(self):
            return self.chunk is not None and len(self.halved) == 1

    def advance(name, *groups, extra=None, more=None):
        groups = [g for g in groups if not g.ready()]
        parts = [g.plan(extra if i == 0 else None) for i, g in enumerate(groups)] + ([more] if more else [])
        results = run.batch(parts, name=name) if parts else []
        given = results.pop() if more else []
        for i, (g, got) in enumerate(zip(groups, results)):
            if extra and i == 0:
                count = len(extra[2])
                given, got = got[:count], got[count:]
            g.take(got)
        return given

    ffn_sums, keep_out, send_out, keep_in, send_in = run(
        ffn_weights_kernel,
        [hid_own, hid_other, act_own, act_other, normed_ffn, low_ffn],
        [((2, unit), F32), ((1, unit, width), F32), ((1, unit, width), BF16)]
        + [((2, unit // 2, width), F32), ((2, unit // 2, width), BF16)],
        name="ffn_weights",
    )
    by_out = Reduction([keep_out], [send_out], [["row"], [0], [1]])
    by_in = Reduction([keep_in], [send_in], [[0], ["row"], [1]])

    scratch = [pltpu.VMEM((seq, wide), BF16)] * n + [pltpu.VMEM((seq, wide), F32)] * 2
    bias_sum = ((2, wide), F32)

    def saved_of(saved):
        return [s[k] for k in range(4) for s in saved]

    got = run(
        functools.partial(cross_backward_kernel, n),
        [after_cross, *terms, cot, vectors, molecules]
        + saved_of(saved_cross) + [*w_cross_out, *w_cross_q],
        [full, whole] + [local] * (3 * n) + [bias_sum] * n + back + [((3, width), F32)],
        scratch=scratch,
        name="cross_backward",
    )
    grad_cross, low_cross, got = got[0], got[1], got[2:]
    cross_grads, cross_bias_sums, got = got[: 3 * n], got[3 * n : 4 * n], got[4 * n :]
    terms, small_ffn = team_parts(got[:BACK]), got[BACK]
    keep, send, *memory_terms, result = run(
        functools.partial(cross_weights_kernel, n),
        [*cross_grads, *heads_cross, *w_cross_kv]
        + [normed_cross, memory_row, low_cross, after_cross, *out_terms, vectors],
        [((2, 2 * head, width), F32), ((2, 2 * head, width), BF16)] + back + [whole],
        name="cross_weights",
    )
    by_cross = Reduction([keep], [send], [[0], [1], ["row"]] + [[k] for k in range(2, bits)])
    advance("fold_ffn", by_out, by_in)

    group = ((1, 4 * head, width), F32)
    ins = [after_self, *terms, grad_cross, vectors, molecules] + [far(v) for v in saved_self[-1]]
    grad_self, low_self, *last_grads, last_sums, small_cross, first, send = run(
        functools.partial(self_backward_kernel, n),
        ins + [*w_self_out, normed_self, heads_self[-1]],
        [full, whole] + [local] * 3 + [bias_sum, ((3, width), F32), local if n == 2 else group, (group[0], BF16)],
        scratch=scratch[-3:],
        name="self_backward",
    )
    by_self = Reduction([first], [send], [["row"]] + [[k] for k in range(bits)])
    by_ffn = by_out
    by_ffn.keeps, by_ffn.gots = by_out.keeps + by_in.keeps, by_out.gots + by_in.gots
    by_ffn.axes = [[0]] + [[k] for k in range(1, bits)]
    mem_terms = team_parts(memory_terms)
    share = width // mp
    along = share == LANES and team == 2 and dp == 8 and mem_len // dp * LANES == SMALL * width
    blocks = ((16, SMALL, width), BF16)
    extra = (functools.partial(memory_start_kernel, 1), mem_terms, [blocks]) if along else None
    given = advance("ffn_1", by_ffn, extra=extra)
    ins = [*w_qkv, *last_grads]
    if n == 2:
        ins += [molecules] + [far(v) for v in saved_self[0]] + [first, normed_self, heads_self[0], low_self]
    outs = ([bias_sum, group] if n == 2 else []) + back
    got = run(
        functools.partial(self_backward_rest_kernel, n),
        ins,
        outs,
        scratch=[pltpu.VMEM((seq, wide), BF16)] * 3 + scratch[-2:] if n == 2 else [],
        name="self_backward_rest",
    )
    self_bias_sums = [last_sums]
    if n == 2:
        self_bias_sums, by_self.keeps, got = [got[0], last_sums], [got[1]], got[2:]
    terms = team_parts(got)
    sent, more = [blocks, ((1, 8 * SMALL, width), BF16)], None
    if along:
        more = (functools.partial(memory_send_kernel, 1, by_ffn.extra_at, 0), [*given, by_ffn.gots[0]], sent)
    given = advance("cross_1", by_cross, more=more)
    advance("ffn_2", by_ffn)
    advance("self_1", by_self)

    fits = apart and 4 * head == width and unit == width
    if fits:
        shard_rows = [*self_bias_sums, *cross_bias_sums, ffn_sums]
        lines = 2
    else:

        def by_shard(sums):
            return sums if n == 2 else [sums[0][:, :head], sums[0][:, head:]]

        shard_rows = [
            jnp.stack(
                [
                    jnp.concatenate([a.reshape(-1), b.reshape(-1), ffn_sums[i]]).reshape(-1, width)
                    for i, (a, b) in enumerate(zip(by_shard(self_bias_sums), by_shard(cross_bias_sums)))
                ]
            )
        ]
        lines = shard_rows[0].shape[1]
    both, small_own, small_other = run(
        functools.partial(input_backward_kernel, n),
        [x, *terms, grad_self, vectors, result, small_cross, small_ffn, *shard_rows],
        [((2 * seq, width), BF16)] + [((SMALL, width), BF16)] * 2,
        name="input_backward",
    )

    by_cross.carry = [small_other]
    if along:
        more = (functools.partial(memory_send_kernel, 0, 0, "row"), [given[0], data_swap(given[1], 0)], sent)
    given = advance("cross_2", by_cross, more=more)
    by_self.ride, by_self.ride_at = [small_own, by_cross.gots[0]], by_cross.size
    if along:
        memory_state = [given[0], other(given[1])]
    advance("all_1", by_cross, by_self, by_ffn)
    got_both = other(later(both, by_self.keeps[0]))
    advance("all_2", by_self, by_ffn, by_cross)
    if not along:
        mine, theirs = jnp.concatenate(mem_terms[:BACK]), jnp.concatenate(mem_terms[BACK:])
        total = (mine.astype(F32) + theirs.astype(F32)).astype(BF16)
        total = total.reshape(dp, mem_len // dp, rows, team, share)
        blocks = lax.dynamic_index_in_dim(total, seat, 3, keepdims=False).swapaxes(1, 2)
        blocks = blocks.reshape(dp * rows, mem_len // dp, share)
        same_seat = [[d * mp + m for d in range(dp) for m in range(mp) if m % team == s] for s in range(team)]
        grad_memory = lax.all_to_all(
            blocks, ("dp", "mp"), split_axis=0, concat_axis=0, tiled=True, axis_index_groups=same_seat
        ).astype(F32)
    advance("self_cross_3", by_self, by_cross)

    def cross_grads():
        return run(
            functools.partial(cross_grads_kernel, by_cross.halved[0]),
            [by_cross.chunk, by_cross.got],
            [far(((width, head), F32)), far(((2, width, head), F32)), far(((head, width), F32))],
            name="cross_grads",
        )

    cross_results = None
    if by_cross.ready():
        cross_results = cross_grads()
    more = (functools.partial(memory_send_kernel, "row", 0, 2), memory_state, sent) if along else None
    while more or not (by_self.ready() and by_cross.ready() and by_ffn.ready()):
        given = advance("rest", by_self, by_cross, by_ffn, more=more)
        if more:
            memory_state, more = [given[0], data_swap(given[1], 2)], None
    grad_cross_q, grad_cross_kv, grad_cross_out = cross_results or cross_grads()
    mixed, grad_inputs = run(
        place_rows_kernel,
        [both, got_both],
        [far(((rows, seq, width), BF16)), far(((rows, seq, width), F32))],
        name="place_rows",
    )
    grad_ffn_in, grad_ffn_out = run(
        functools.partial(ffn_grads_kernel, by_ffn.halved[0]),
        [by_ffn.chunk, by_ffn.got],
        [far(((width, unit), F32)), far(((unit, width), F32))],
        name="ffn_grads",
    )
    if along:
        (grad_memory,) = run(
            functools.partial(memory_end_kernel, 2, 0),
            memory_state,
            [far(((16, mem_len // dp, share), F32))],
            name="memory_end",
        )
    if fits:
        outs = [((2, head), F32), ((2, head), F32), ((1, unit), F32)]
    else:
        outs = [((lines, width), F32)]
    grad_self_qkv, grad_self_out, grad_gain, grad_shift, grad_out_bias, *rest = run(
        functools.partial(self_grads_kernel, by_self.halved[0]),
        [by_self.chunk, by_self.got],
        [far(((3, width, head), F32)), far(((head, width), F32))] + [far(((3, width), F32))] * 3 + [far(v) for v in outs],
        name="self_grads",
    )
    if fits:
        grad_self_bias, grad_cross_bias, grad_ffn_bias = rest[0], rest[1], rest[2].reshape(-1)
    else:
        own_small = rest[0].reshape(-1)
        grad_self_bias = own_small[: 2 * head].reshape(2, head)
        grad_cross_bias = own_small[2 * head : 4 * head].reshape(2, head)
        grad_ffn_bias = own_small[4 * head :]
    return (
        mixed,
        grad_inputs,
        grad_memory,
        grad_gain,
        grad_shift,
        grad_self_qkv,
        grad_self_bias,
        grad_self_out,
        grad_cross_q,
        grad_cross_kv,
        grad_cross_bias,
        grad_cross_out,
        grad_ffn_in,
        grad_ffn_bias,
        grad_ffn_out,
        grad_out_bias,
    )


def solution(mesh):
    placed = (
        P("dp", None, None),
        P(None, "dp", None),
        P("dp", None),
        P("dp", None),
        P(),
        P(),
        P(),
        P(),
        P(None, None, "mp"),
        P(None, "mp"),
        P("mp", None),
        P(None, "mp"),
        P(None, None, "mp"),
        P(None, "mp"),
        P("mp", None),
        P(None, "mp"),
        P("mp"),
        P("mp", None),
        P(),
        P("dp", None, None),
    )
    return jax.shard_map(
        shards,
        mesh=mesh,
        in_specs=placed,
        out_specs=(
            P("dp", None, None),
            P("dp", None, None),
            P(None, "dp", "mp"),
            P(),
            P(),
            P(None, None, "mp"),
            P(None, "mp"),
            P("mp", None),
            P(None, "mp"),
            P(None, None, "mp"),
            P(None, "mp"),
            P("mp", None),
            P(None, "mp"),
            P("mp"),
            P("mp", None),
            P(),
        ),
        check_vma=False,
    )
```

```python
import functools

import jax
import jax.numpy as jnp
from jax import lax
from jax.experimental import pallas as pl
from jax.experimental.pallas import tpu as pltpu
from jax.sharding import PartitionSpec as P

HDIM = 64
LANES = 128
BLOCK = 128
SMALL = 16
FRONT = 2
BACK = 2
EPSILON = 1e-05
F32 = jnp.float32
BF16 = jnp.bfloat16


def dot(left, right):
    return lax.dot_general(left, right, (((1,), (0,)), ((), ())), preferred_element_type=F32)


def dot_right(left, right):
    return lax.dot_general(left, right, (((1,), (1,)), ((), ())), preferred_element_type=F32)


def dot_left(left, right):
    return lax.dot_general(left, right, (((0,), (0,)), ((), ())), preferred_element_type=F32)


class Far:
    def __init__(self, value, pick=False):
        self.value, self.pick = value, pick


class Raw:
    def __init__(self, value):
        self.value = value


class Scalars:
    def __init__(self, value):
        self.value = value


class Flow:
    def __init__(self):
        self.loads, self.stores, self.sent = {}, {}, []

    def need(self, *refs):
        for ref in refs:
            copy = self.loads.pop(id(ref), None)
            if copy is not None:
                copy.wait()

    def send(self, *refs):
        for ref in refs:
            copy = self.stores.pop(id(ref), None)
            if copy is not None:
                copy.start()
                self.sent.append(copy)


class Steps:
    def __init__(self, where):
        self.where, self.token = where, None

    def batch(self, parts, name=None, cost=0.1):
        def kernel(flow, where, *refs):
            at, to = 0, sum(len(ins) for _, ins, _ in parts)
            for part, ins, outs in parts:
                part(flow, where, *refs[at : at + len(ins)], *refs[to : to + len(outs)])
                at, to = at + len(ins), to + len(outs)

        got = self(
            kernel, [v for _, ins, _ in parts for v in ins], [v for _, _, outs in parts for v in outs], name=name, cost=cost
        )
        results = []
        for _, _, outs in parts:
            results.append(got[: len(outs)])
            got = got[len(outs) :]
        return results

    def __call__(self, kernel, ins, outs, scratch=(), name=None, cost=0.1, hold=()):
        near = pl.BlockSpec(memory_space=pltpu.VMEM)
        far = pl.BlockSpec(memory_space=pltpu.HBM)
        words = pl.BlockSpec(memory_space=pltpu.SMEM)
        values, specs, stages = [], [], []
        for v in ins:
            if isinstance(v, Scalars):
                values.append(v.value)
                specs.append(words)
            elif isinstance(v, Raw):
                values.append(pltpu.with_memory_space_constraint(v.value, pltpu.HBM))
                specs.append(far)
            elif isinstance(v, Far):
                values.append(pltpu.with_memory_space_constraint(v.value, pltpu.HBM))
                specs.append(far)
                stages.append(pltpu.VMEM(v.value.shape[1:] if v.pick else v.value.shape, v.value.dtype))
            else:
                values.append(pltpu.with_memory_space_constraint(v, pltpu.VMEM))
                specs.append(near)
        after = [pltpu.with_memory_space_constraint(v, pltpu.VMEM) for v in hold]
        after_specs = [near] * len(after)
        if self.token is not None:
            after.append(pltpu.with_memory_space_constraint(self.token, pltpu.HBM))
            after_specs.append(far)
        for v in outs:
            if isinstance(v, Far):
                stages.append(pltpu.VMEM(*v.value))
        shapes = [pltpu.HBM(*v.value) if isinstance(v, (Far, Raw)) else pltpu.VMEM(*v) for v in outs]
        count, n_in, n_out, n_after = len(stages), len(ins), len(outs), len(after)

        def body(where_ref, *refs):
            refs = list(refs)
            in_refs, refs = refs[:n_in], refs[n_in + n_after :]
            out_refs, refs = refs[:n_out], refs[n_out + 1 :]
            stage_refs, refs = refs[:count], refs[count:]
            flow = Flow()
            if count:
                sems, refs = refs[0], refs[1:]
            given, k = [], 0
            for v, ref in zip(ins, in_refs):
                if isinstance(v, Far):
                    source = ref.at[where_ref[0]] if v.pick else ref
                    copy = pltpu.make_async_copy(source, stage_refs[k], sems.at[k])
                    copy.start()
                    flow.loads[id(stage_refs[k])] = copy
                    ref, k = stage_refs[k], k + 1
                given.append(ref)
            for v, ref in zip(outs, out_refs):
                if isinstance(v, Far):
                    flow.stores[id(stage_refs[k])] = pltpu.make_async_copy(stage_refs[k], ref, sems.at[k])
                    ref, k = stage_refs[k], k + 1
                given.append(ref)
            kernel(flow, where_ref, *given, *refs)
            for copy in flow.loads.values():
                copy.wait()
            for copy in flow.stores.values():
                copy.start()
            for copy in [*flow.sent, *flow.stores.values()]:
                copy.wait()

        results = pl.pallas_call(
            body,
            in_specs=[words] + specs + after_specs,
            out_specs=[far if isinstance(v, (Far, Raw)) else near for v in outs] + [far],
            out_shape=shapes + [pltpu.HBM((8, LANES), F32)],
            scratch_shapes=stages + ([pltpu.SemaphoreType.DMA((count,))] if count else []) + list(scratch),
            compiler_params=pltpu.CompilerParams(vmem_limit_bytes=24 * 1024 * 1024),
            cost_estimate=pl.CostEstimate(flops=10**6, bytes_accessed=int(cost * 3 * 10**6), transcendentals=0),
            name=name,
        )(self.where, *values, *after)
        self.token = results[-1]
        return list(results[:-1])


def row_blocks(seq):
    return [slice(start, start + BLOCK) for start in range(0, seq, BLOCK)]


def row_of(ref, i):
    return ref[i : i + 1, :].astype(F32)


GAIN, SHIFT, OUT, SCALE, VECTORS = 0, 3, 6, 9, 16


def norm_parts(value):
    centre = value - jnp.mean(value, axis=-1, keepdims=True)
    spread = jnp.mean(centre * centre, axis=-1, keepdims=True)
    scale = lax.rsqrt(spread + EPSILON)
    return centre * scale, scale


def norm_backward(value, gain, incoming):
    xhat, scale = norm_parts(value)
    weighted = incoming * gain
    grad = scale * (
        weighted
        - jnp.mean(weighted, axis=-1, keepdims=True)
        - xhat * jnp.mean(weighted * xhat, axis=-1, keepdims=True)
    )
    return grad, jnp.sum(incoming * xhat, axis=0, keepdims=True), jnp.sum(incoming, axis=0, keepdims=True)


def head_lanes(value, j):
    lane = lax.broadcasted_iota(jnp.int32, value.shape, 1)
    return jnp.where((lane >= HDIM) == bool(j), value, jnp.zeros_like(value))


def span_of(block, seq, banded):
    if not banded:
        return slice(0, seq)
    return slice(max(block.start - BLOCK, 0), block.stop)


def start_all(moves, sems):
    copies = [pltpu.make_async_copy(a, b, sems.at[i]) for i, (a, b) in enumerate(moves)]
    for copy in copies:
        copy.start()
    return copies


def setup_kernel(packing, flow, where, *refs):
    group_tokens, bucket_group, lengths, inputs, cotangent, memory, segments, gains, shifts, biases, refs = *refs[:10], refs[10:]
    if packing:
        query, kv, out, w_in, w_out, cross, ffn, refs = *refs[:7], refs[7:]
    x, cot, memory_part, vectors, molecules, tokens_now, group_now, lengths_now, word_sems, sems = refs
    words = start_all([(group_tokens, tokens_now), (bucket_group, group_now), (lengths, lengths_now)], word_sems)
    moves = [(memory.at[:, where[0]], memory_part), (inputs.at[where[0]], x), (cotangent.at[where[0]], cot)]
    if packing:
        full, wide = query.shape
        half = full // 2
        rows = pl.ds(pl.multiple_of(where[3] * half, half), half)
        moves += [
            (query.at[rows, :], cross.at[0:half, :]),
            (kv.at[0, rows, :], cross.at[half : 2 * half, :]),
            (kv.at[1, rows, :], cross.at[2 * half : 3 * half, :]),
        ]
        count, size = out.shape[1] // wide // 2, out.shape[0]
        for k in range(count):
            lanes = pl.ds(pl.multiple_of((where[3] * count + k) * wide, wide), wide)
            moves.append((out.at[:, lanes], cross.at[3 * half + k * size : 3 * half + (k + 1) * size, :]))
        moves += [(w_in, ffn.at[0]), (w_out, ffn.at[1])]
    copies = start_all(moves, sems)
    for copy in words:
        copy.wait()
    width = vectors.shape[1]
    total, own = 0, 0
    for b in range(bucket_group.shape[0]):
        tokens = tokens_now[group_now[b]]
        total = total + tokens
        own = own + jnp.where(where[2] == b, tokens, 0)
    scaled = jnp.full((1, width), bucket_group.shape[0] * own, jnp.int32).astype(F32)
    scale = scaled / jnp.full((1, width), total, jnp.int32).astype(F32)
    size = molecules.shape[1]
    place = lax.broadcasted_iota(jnp.int32, (1, size), 1)
    count, end = jnp.zeros((1, size), jnp.int32), 0
    for k in range(lengths.shape[1]):
        end = end + lengths_now[where[0], k]
        count = count + (end <= place).astype(jnp.int32)
    molecules[1:2, :] = count
    flow.need(segments, gains, shifts, biases)
    molecules[0:1, :] = segments[pl.ds(where[0], 1), :]
    rows = [r[...].astype(F32) for r in (gains, shifts, biases)] + [scale]
    vectors[...] = jnp.concatenate(rows + [jnp.zeros((VECTORS - 10, width), F32)], axis=0)
    for copy in copies:
        copy.wait()


def key_columns(keys):
    size = keys.shape[1]
    tiles = [jnp.broadcast_to(keys[:, at : at + BLOCK], (LANES, BLOCK)).T for at in range(0, size, BLOCK)]
    return jnp.concatenate(tiles, axis=0)


def allowed_of(own, columns, block, span, banded):
    allowed = columns[span] == own[:, block]
    if banded:
        query = lax.broadcasted_iota(jnp.int32, allowed.shape, 1) + block.start
        key = lax.broadcasted_iota(jnp.int32, allowed.shape, 0) + span.start
        allowed = allowed & (key <= query)
    return allowed


def both_heads(value):
    return jnp.concatenate([head_lanes(value, 0), head_lanes(value, 1)], axis=0)


def own_rows(value):
    half = value.shape[1] // 2
    row = lax.broadcasted_iota(jnp.int32, (value.shape[0], half), 0)
    return jnp.where(row < HDIM, value[:, :half], value[:, half:])


def pair_columns(at):
    return slice(2 * at * BLOCK, 2 * (at + 1) * BLOCK)


def attend_forward(q, k, v, own, keys, heads, totals, raised_all, shares, banded):
    seq, wide = q.shape
    columns = key_columns(keys)
    blocks = row_blocks(seq)
    for pair in range(wide // LANES):
        lanes = slice(pair * LANES, (pair + 1) * LANES)
        for at, block in enumerate(blocks):
            span = span_of(block, k.shape[0], banded)
            allowed = allowed_of(own, columns, block, span, banded)
            allowed = jnp.concatenate([allowed, allowed], axis=1)
            scores = dot_right(k[span, lanes], both_heads(q[block, lanes] * 0.125))
            scores = jnp.where(allowed, scores, -1e30)
            maxima = jnp.max(scores, axis=0, keepdims=True)
            raised = jnp.exp(scores - maxima)
            total = jnp.sum(raised, axis=0, keepdims=True)
            raised_all[span, pair_columns(at)] = raised.astype(BF16)
            shares[:, pair_columns(at)] = 1.0 / total
            logs = maxima + jnp.log(total)
            for j in (0, 1):
                totals[2 * pair + j : 2 * pair + j + 1, block] = logs[:, j * BLOCK : (j + 1) * BLOCK]
        turned = v[:, lanes].T
        if not banded:
            mixed = dot(turned, raised_all[...]) * shares[...]
        for at, block in enumerate(blocks):
            if banded:
                span = span_of(block, k.shape[0], banded)
                part = dot(turned[:, span], raised_all[span, pair_columns(at)]) * shares[:, pair_columns(at)]
            else:
                part = mixed[:, pair_columns(at)]
            heads[block, lanes] = own_rows(part).T.astype(BF16)


def attend_backward(q, k, v, own, keys, totals, grad_heads, dq, dk, dv, work, banded):
    seq, wide = q.shape
    columns = key_columns(keys)
    blocks = row_blocks(seq)
    scores_all, query_all = work[:2]
    for pair in range(wide // LANES):
        lanes = slice(pair * LANES, (pair + 1) * LANES)
        for at, block in enumerate(blocks):
            span = span_of(block, k.shape[0], banded)
            allowed = allowed_of(own, columns, block, span, banded)
            allowed = jnp.concatenate([allowed, allowed], axis=1)
            query, grad = both_heads(q[block, lanes] * 0.125), both_heads(grad_heads[block, lanes])
            query_all[pair_columns(at), :] = query
            logs = jnp.concatenate([totals[2 * pair + j : 2 * pair + j + 1, block] for j in (0, 1)], axis=1)
            scores = jnp.where(allowed, dot_right(k[span, lanes], query), -1e30)
            chances = jnp.exp(scores - logs)
            if banded:
                work[2][span, pair_columns(at)] = chances.astype(BF16)
                work[3][pair_columns(at), :] = grad
            else:
                grad_value = dot(chances.astype(BF16), grad)
                work[2][...] = grad_value if at == 0 else work[2][...] + grad_value
            weighted = chances * dot_right(v[span, lanes], grad)
            mean = jnp.sum(weighted, axis=0, keepdims=True)
            scores_all[span, pair_columns(at)] = (weighted - chances * mean).astype(BF16)
        turned = k[:, lanes].T
        if not banded:
            grad_query = dot(turned, scores_all[...])
            dk[:, lanes] = dot(scores_all[...], query_all[...]).astype(BF16)
            dv[:, lanes] = work[2][...].astype(BF16)
        for at, block in enumerate(blocks):
            if banded:
                span = span_of(block, k.shape[0], banded)
                part = dot(turned[:, span], scores_all[span, pair_columns(at)])
                met = slice(pair_columns(at).start, pair_columns(min(at + 1, len(blocks) - 1)).stop)
                dk[block, lanes] = dot(scores_all[block, met], query_all[met, :]).astype(BF16)
                dv[block, lanes] = dot(work[2][block, met], work[3][met, :]).astype(BF16)
            else:
                part = grad_query[:, pair_columns(at)]
            dq[block, lanes] = (own_rows(part).T * 0.125).astype(BF16)


def team_total(mine, theirs, block):
    half = mine[0].shape[0]
    k, rows = block.start // half, slice(block.start % half, block.start % half + BLOCK)
    return mine[k][rows, :].astype(F32) + theirs[k][rows, :].astype(F32)


def put_half(parts, block, value):
    half = parts[0].shape[0]
    start = block.start % half
    parts[block.start // half][start : start + BLOCK, :] = value.astype(parts[0].dtype)


def self_forward_kernel(n, i, flow, where, *refs):
    last = i == n - 1
    first, vectors, molecules, w, bias, refs = *refs[:5], refs[5:]
    if last:
        w_out, done, refs = refs[:n], refs[n : 2 * n - 1], refs[2 * n - 1 :]
    if i == 0:
        normed, refs = refs[0], refs[1:]
        for block in row_blocks(first.shape[0]):
            norm = norm_parts(first[block, :].astype(F32))[0]
            normed[block, :] = (norm * row_of(vectors, GAIN) + row_of(vectors, SHIFT)).astype(BF16)
    else:
        normed = first
    q, k, v, heads, totals = refs[:5]
    flow.need(w)
    q[...] = (dot(normed[...], w[0]) + row_of(bias, 0)).astype(BF16)
    k[...] = dot(normed[...], w[1]).astype(BF16)
    v[...] = (dot(normed[...], w[2]) + row_of(bias, 1)).astype(BF16)
    own = molecules[0:1, :]
    flow.send(q, k, v)
    attend_forward(q, k, v, own, own, heads, totals, *refs[-2:], True)
    flow.send(totals)
    if last:
        project_out(flow, [*done, heads], w_out, refs[5 : 5 + FRONT])


def project_out(flow, heads, w_out, parts):
    flow.need(*w_out)
    for block in row_blocks(heads[0].shape[0]):
        put_half(parts, block, sum(dot(h[block, :], w[...]) for h, w in zip(heads, w_out)))


def memory_kernel(flow, where, memory, w, bias, k, v):
    flow.need(w)
    k[...] = dot(memory[...], w[0]).astype(BF16)
    v[...] = (dot(memory[...], w[1]) + row_of(bias, 3)).astype(BF16)


def unpack_memory_kernel(flow, where, near, got, memory, bias, query, kv, out, k, v):
    full, wide = query.shape
    half, size = full // 2, out.shape[0]
    count = out.shape[1] // wide // 2
    for packed, bit in ((near, where[3]), (got, 1 - where[3])):
        rows = pl.ds(pl.multiple_of(bit * half, half), half)
        query[rows, :] = packed[:half]
        for i in (0, 1):
            kv[i, rows, :] = packed[(i + 1) * half : (i + 2) * half]
        for i in range(count):
            lanes = pl.ds(pl.multiple_of((bit * count + i) * wide, wide), wide)
            out[:, lanes] = packed[3 * half + i * size : 3 * half + (i + 1) * size]
    memory_kernel(flow, where, memory, kv, bias, k, v)


def cross_forward_kernel(n, i, flow, where, *refs):
    last = i == n - 1
    if i == 0:
        x, mine, theirs, refs = refs[0], refs[1 : 1 + FRONT], refs[1 + FRONT : 1 + 2 * FRONT], refs[1 + 2 * FRONT :]
    else:
        normed, refs = refs[0], refs[1:]
    vectors, molecules, w, bias, k, v, refs = *refs[:6], refs[6:]
    if last:
        w_out, done, refs = refs[:n], refs[n : 2 * n - 1], refs[2 * n - 1 :]
    if i == 0:
        after_self, normed, refs = refs[0], refs[1], refs[2:]
    q, heads, totals = refs[:3]
    if i == 0:
        for block in row_blocks(x.shape[0]):
            value = x[block, :].astype(F32) + team_total(mine, theirs, block) + row_of(vectors, OUT)
            after_self[block, :] = value
            norm = norm_parts(value)[0]
            normed[block, :] = (norm * row_of(vectors, GAIN + 1) + row_of(vectors, SHIFT + 1)).astype(BF16)
    flow.need(w)
    q[...] = (dot(normed[...], w[...]) + row_of(bias, 2)).astype(BF16)
    attend_forward(q, k, v, molecules[0:1, :], molecules[1:2, :], heads, totals, *refs[-2:], False)
    if last:
        project_out(flow, [*done, heads], w_out, refs[3 : 3 + FRONT])


def ffn_kernel(i, flow, where, *refs):
    if i == 0:
        after_self, mine, theirs, refs = refs[0], refs[1 : 1 + FRONT], refs[1 + FRONT : 1 + 2 * FRONT], refs[1 + 2 * FRONT :]
        cotangent, vectors, w_in, bias, w_out, refs = *refs[:5], refs[5:]
        after_cross, normed, low, active, grad_hidden, part, part_grad = refs
    else:
        normed, low, begun, begun_grad, w_in, bias, refs = *refs[:6], refs[6:]
        if len(w_in.shape) == 3:
            w_in, w_out = w_in.at[0], w_in.at[1]
        else:
            w_out, refs = refs[0], refs[1:]
        active, grad_hidden, parts, parts_grad = refs[0], refs[1], refs[2 : 2 + BACK], refs[2 + BACK :]
    if bias.shape[0] == 1:
        row = row_of(bias, 0)
    else:
        row = jnp.concatenate([row_of(bias, k) for k in range(4, bias.shape[0])], axis=1)
    if i == 0:
        for block in row_blocks(normed.shape[0]):
            value = after_self[block, :] + team_total(mine, theirs, block) + row_of(vectors, OUT + 1)
            after_cross[block, :] = value
            norm = norm_parts(value)[0]
            normed[block, :] = (norm * row_of(vectors, GAIN + 2) + row_of(vectors, SHIFT + 2)).astype(BF16)
            low[block, :] = (cotangent[block, :].astype(F32) * row_of(vectors, SCALE)).astype(BF16)
    flow.need(w_in, w_out)
    for block in row_blocks(normed.shape[0]):
        hidden = dot(normed[block, :], w_in[...]) + row
        cdf = 0.5 * (1.0 + lax.erf(hidden * 0.7071067811865476))
        act = (hidden * cdf).astype(BF16)
        active[block, :] = act
        slope = cdf + hidden * (0.3989422804014327 * jnp.exp(-0.5 * hidden * hidden))
        back = (slope * dot_right(low[block, :], w_out[...])).astype(BF16)
        grad_hidden[block, :] = back
        out, out_grad = dot(act, w_out[...]), dot_right(back, w_in[...])
        if i == 0:
            part[block, :], part_grad[block, :] = out, out_grad
        else:
            put_half(parts, block, begun[block, :] + out)
            put_half(parts_grad, block, begun_grad[block, :] + out_grad)


def ffn_weights_kernel(flow, where, *refs):
    hidden, active, normed, low, sums = refs[:2], refs[2:4], refs[4], refs[5], refs[6]
    keep_out, send_out, keep_in, send_in = refs[7:]
    half = keep_in.shape[1]
    for i in (0, 1):
        for target, bit in ((keep_in, where[3]), (send_in, 1 - where[3])):
            lanes = pl.ds(pl.multiple_of(bit * half, half), half)
            target[i] = dot_left(hidden[i][:, lanes], normed[...]).astype(target.dtype)
        sums[i : i + 1, :] = jnp.sum(hidden[i][...].astype(F32), axis=0, keepdims=True)
    keep_out[0] = dot_left(active[0][...], low[...])
    send_out[0] = dot_left(active[1][...], low[...]).astype(BF16)


def spread_grad_heads(low, w_out, grad_heads):
    for piece, target in zip(w_out, grad_heads):
        target[...] = dot_right(low[...], piece[...]).astype(BF16)


def column_sums(sums, values):
    for i, value in enumerate(values):
        sums[i : i + 1, :] = jnp.sum(value[...].astype(F32), axis=0, keepdims=True)


def cross_backward_kernel(n, flow, where, *refs):
    after_cross, mine, theirs, refs = refs[0], refs[1 : 1 + BACK], refs[1 + BACK : 1 + 2 * BACK], refs[1 + 2 * BACK :]
    cotangent, vectors, molecules, refs = *refs[:3], refs[3:]
    (q, k, v, totals, w_out, w), refs = [refs[i * n : (i + 1) * n] for i in range(6)], refs[6 * n :]
    grad_cross, low, refs = refs[0], refs[1], refs[2:]
    (dq, dk, dv, bias_sums), refs = [refs[i * n : (i + 1) * n] for i in range(4)], refs[4 * n :]
    parts_out, sums, refs = refs[:BACK], refs[BACK], refs[BACK + 1 :]
    grad_heads, work = refs[:n], refs[n:]
    seq, width = after_cross.shape
    rows = [jnp.zeros((1, width), F32)] * 3
    for block in row_blocks(seq):
        incoming = team_total(mine, theirs, block)
        grad_result = cotangent[block, :].astype(F32) * row_of(vectors, SCALE)
        back, by_gain, by_shift = norm_backward(after_cross[block, :], row_of(vectors, GAIN + 2), incoming)
        value = grad_result + back
        grad_cross[block, :] = value
        low[block, :] = value.astype(BF16)
        parts = (by_gain, by_shift, jnp.sum(grad_result, axis=0, keepdims=True))
        rows = [a + b for a, b in zip(rows, parts)]
    for i, row in enumerate(rows):
        sums[i : i + 1, :] = row
    flow.need(*w_out)
    spread_grad_heads(low, w_out, grad_heads)
    own, keys = molecules[0:1, :], molecules[1:2, :]
    for i in range(n):
        attend_backward(
            q[i], k[i], v[i], own, keys, totals[i], grad_heads[i], dq[i], dk[i], dv[i], work, False
        )
        column_sums(bias_sums[i], (dq[i], dv[i]))
    flow.need(*w)
    for block in row_blocks(seq):
        put_half(parts_out, block, sum(dot_right(d[block, :], m[...]) for d, m in zip(dq, w)))


def shard_grads(kinds):
    grads = ([], [])
    for kind in kinds:
        if len(kind) == 2:
            for i in (0, 1):
                grads[i].append(dot_left(kind[i][0][...], kind[i][1][...]))
        else:
            left, right = kind[0]
            both, half = dot_left(left[...], right[...]), left.shape[1] // 2
            grads[0].append(both[:half])
            grads[1].append(both[half:])
    return grads


def cross_weights_kernel(n, flow, where, *refs):
    (dq, dk, dv, heads, w), refs = [refs[i * n : (i + 1) * n] for i in range(5)], refs[5 * n :]
    normed, memory, low, after_cross, refs = *refs[:4], refs[4:]
    mine, theirs, vectors, refs = refs[:BACK], refs[BACK : 2 * BACK], refs[2 * BACK], refs[2 * BACK + 1 :]
    keep, send, terms, result = refs[0], refs[1], refs[2 : 2 + BACK], refs[-1]
    flow.need(*w)
    pairs = [[(a, b) for a in left] for left, b in ((dq, normed), (dk, memory), (dv, memory), (heads, low))]
    first = where[3] == 0
    for i, grads in enumerate(shard_grads(pairs)):
        upper, lower = jnp.concatenate(grads[:2], axis=0), jnp.concatenate(grads[2:], axis=0)
        keep[i] = jnp.where(first, upper, lower)
        send[i] = jnp.where(first, lower, upper).astype(BF16)
    for block in row_blocks(memory.shape[0]):
        total = sum(
            dot_right(a[block, :], m[0]) + dot_right(b[block, :], m[1]) for a, b, m in zip(dk, dv, w)
        )
        put_half(terms, block, total)
    for block in row_blocks(after_cross.shape[0]):
        both = team_total(mine, theirs, block)
        result[block, :] = (after_cross[block, :] + both + row_of(vectors, OUT + 2)).astype(BF16)


def put_grads(target, grads):
    size = grads[0].shape[0]
    for k, grad in enumerate(grads):
        target[0, k * size : (k + 1) * size, :] = grad.astype(target.dtype)


def self_backward_kernel(n, flow, where, *refs):
    after_self, mine, theirs, refs = refs[0], refs[1 : 1 + BACK], refs[1 + BACK : 1 + 2 * BACK], refs[1 + 2 * BACK :]
    grad_cross, vectors, molecules, q, k, v, totals, refs = *refs[:7], refs[7:]
    w_out, refs = refs[:n], refs[n:]
    normed, heads, grad_self, low, dq, dk, dv, bias_sums, sums, refs = *refs[:9], refs[9:]
    first, send, grad_heads, work = *refs[:3], refs[3:]
    seq, width = after_self.shape
    rows = [jnp.zeros((1, width), F32)] * 3
    for block in row_blocks(seq):
        incoming = team_total(mine, theirs, block)
        back, by_gain, by_shift = norm_backward(after_self[block, :], row_of(vectors, GAIN + 1), incoming)
        upper = grad_cross[block, :]
        value = upper + back
        grad_self[block, :] = value
        low[block, :] = value.astype(BF16)
        parts = (by_gain, by_shift, jnp.sum(upper, axis=0, keepdims=True))
        rows = [a + b for a, b in zip(rows, parts)]
    for i, row in enumerate(rows):
        sums[i : i + 1, :] = row
    flow.need(*w_out)
    spread_grad_heads(low, w_out, [first, grad_heads] if n == 2 else [grad_heads])
    own = molecules[0:1, :]
    flow.need(q, k, v, totals)
    attend_backward(q, k, v, own, own, totals, grad_heads, dq, dk, dv, work, True)
    column_sums(bias_sums, (dq, dv))
    grads = [dot_left(a[...], b[...]) for a, b in ((dq, normed), (dk, normed), (dv, normed), (heads, low))]
    if n == 2:
        put_grads(send, grads)
    else:
        half = grads[0].shape[0] // 2
        put_grads(first, [g[:half] for g in grads])
        put_grads(send, [g[half:] for g in grads])


def self_backward_rest_kernel(n, flow, where, *refs):
    w, grads_last, refs = refs[:n], refs[n : n + 3], refs[n + 3 :]
    pieces = [grads_last]
    if n == 2:
        molecules, q, k, v, totals, grad_heads, normed, heads, low, refs = *refs[:9], refs[9:]
        bias_sums, keep, parts_out, refs = refs[0], refs[1], refs[2 : 2 + BACK], refs[2 + BACK :]
        dq, dk, dv, work = *refs[:3], refs[3:]
        own = molecules[0:1, :]
        flow.need(q, k, v, totals)
        attend_backward(q, k, v, own, own, totals, grad_heads, dq, dk, dv, work, True)
        column_sums(bias_sums, (dq, dv))
        put_grads(keep, [dot_left(a[...], b[...]) for a, b in ((dq, normed), (dk, normed), (dv, normed), (heads, low))])
        pieces = [(dq, dk, dv), grads_last]
    else:
        parts_out = refs[:BACK]
    flow.need(*w)
    for block in row_blocks(grads_last[0].shape[0]):
        total = 0.0
        for matrices, grads in zip(w, pieces):
            for which, d in enumerate(grads):
                total += dot_right(d[block, :], matrices[which])
        put_half(parts_out, block, total)


def input_backward_kernel(n, flow, where, x, *refs):
    mine, theirs, refs = refs[:BACK], refs[BACK : 2 * BACK], refs[2 * BACK :]
    grad_self, vectors, result, by_cross, by_ffn, refs = *refs[:5], refs[5:]
    shard_rows, (both, small_own, small_other) = refs[:-3], refs[-3:]
    seq = x.shape[0]
    both[:seq, :] = result[...]
    width = x.shape[1]
    rows = [jnp.zeros((1, width), F32)] * 3
    for block in row_blocks(x.shape[0]):
        incoming = team_total(mine, theirs, block)
        back, by_gain, by_shift = norm_backward(x[block, :].astype(F32), row_of(vectors, GAIN), incoming)
        upper = grad_self[block, :]
        both[seq + block.start : seq + block.stop, :] = (upper + back).astype(BF16)
        parts = (by_gain, by_shift, jnp.sum(upper, axis=0, keepdims=True))
        rows = [a + b for a, b in zip(rows, parts)]
    common = [r for k in range(3) for r in (rows[k], by_cross[k : k + 1, :], by_ffn[k : k + 1, :])]
    if len(shard_rows) == 1:
        lines = [shard_rows[0][i] for i in (0, 1)]
    else:
        sums_self, sums_cross, sums_ffn = shard_rows[:n], shard_rows[n : 2 * n], shard_rows[2 * n]
        lines = []
        for i in (0, 1):
            pieces = [r[k : k + 1, :] for r in (sums_self[i], sums_cross[i]) for k in (0, 1)]
            lines.append(jnp.concatenate([jnp.concatenate(pieces, axis=1), sums_ffn[i : i + 1, :]], axis=0))
    rest = jnp.zeros((SMALL - 9 - lines[0].shape[0], width), F32)
    small = [jnp.concatenate([*common, line, rest], axis=0).astype(BF16) for line in lines]
    small_own[...] = small[0]
    small_other[...] = small[1]


def fold_kernel(count, size, ride, mode, bit, flow, where, *refs):
    keeps, gots, refs = refs[:count], refs[count : 2 * count], refs[2 * count :]
    planes = [(k, p) for k in range(count) for p in range(keeps[k].shape[0])]

    def part(at, rows):
        k, p = planes[at]
        return keeps[k][p, rows, :].astype(F32) + gots[k][p, rows, :].astype(F32)

    if mode == "half":
        keep, send = refs
        half = size // 2
        for at in range(len(planes)):
            for target, side in ((keep, where[3 + bit]), (send, 1 - where[3 + bit])):
                rows = pl.ds(pl.multiple_of(side * half, half), half)
                target[at, :half, :] = part(at, rows).astype(target.dtype)
    elif mode == "shard":
        if ride is not None:
            refs[-1][0, size : size + SMALL, :] = refs[0][...]
        for at, target in enumerate(refs[-2:]):
            target[0, :size, :] = part(at, slice(0, size)).astype(target.dtype)
    else:
        out = refs[-1]
        for at in range(len(planes)):
            out[at, :size, :] = part(at, slice(0, size)).astype(out.dtype)
        if ride is not None:
            own, came = refs[:2]
            small = own[...].astype(F32) + came[0, ride : ride + SMALL, :].astype(F32)
            out[0, size : size + SMALL, :] = small.astype(out.dtype)


def memory_pairs(axis):
    step = 1 if axis == "row" else 2 << axis
    return [(k, k | step) for k in range(16) if not k & step]


def memory_bit(where, axis):
    return where[0] if axis == "row" else where[3 + axis]


def send_blocks(where, axis, blocks, send, offset):
    low = memory_bit(where, axis) == 0
    per = 8 // send.shape[0]
    for k, (a, b) in enumerate(memory_pairs(axis)):
        at = offset + k % per * SMALL
        send[k // per, at : at + SMALL, :] = jnp.where(low, blocks[b], blocks[a])


def take_blocks(where, axis, kept, got, offset):
    low = memory_bit(where, axis) == 0
    per = 8 // got.shape[0]
    blocks = {}
    for k, (a, b) in enumerate(memory_pairs(axis)):
        at = offset + k % per * SMALL
        came = got[k // per, at : at + SMALL, :]
        blocks[a] = jnp.where(low, kept[a], came)
        blocks[b] = jnp.where(low, came, kept[b])
    return blocks


def memory_start_kernel(axis, flow, where, *refs, send, offset):
    mine, theirs, kept = refs[:BACK], refs[BACK : 2 * BACK], refs[2 * BACK]
    half, width = mine[0].shape
    tokens = half * BACK // 8
    share = LANES
    blocks = {}
    for r in (0, 1):
        lanes = pl.ds(pl.multiple_of((2 * r + where[1]) * share, share), share)
        for k in range(BACK):
            total = (mine[k][:, lanes].astype(F32) + theirs[k][:, lanes].astype(F32)).astype(BF16)
            for d in range(half // tokens):
                block = total[d * tokens : (d + 1) * tokens]
                parts = [block[q : q + SMALL] for q in range(0, tokens, SMALL)]
                at = 2 * (k * half // tokens + d) + r
                blocks[at] = jnp.concatenate(parts, axis=1)
                kept[at] = blocks[at]
    send_blocks(where, axis, blocks, send, offset)


def memory_send_kernel(before, at, axis, flow, where, old, got, kept, send):
    blocks = take_blocks(where, before, old, got, at)
    for k, block in blocks.items():
        kept[k] = block
    send_blocks(where, axis, blocks, send, 0)


def memory_end_kernel(before, at, flow, where, old, got, out):
    for k, block in take_blocks(where, before, old, got, at).items():
        parts = [block[:, q : q + LANES] for q in range(0, block.shape[1], LANES)]
        out[k] = jnp.concatenate(parts, axis=0).astype(out.dtype)


def join_kernel(ride, pad, bit, flow, where, near, got, out):
    half = near.shape[1] - (SMALL if ride else 0)
    for value, side in ((near, where[3 + bit]), (got, 1 - where[3 + bit])):
        rows = pl.ds(pl.multiple_of(side * half, half), half)
        for p in range(near.shape[0]):
            out[p, rows, :] = value[p, :half]
    if ride:
        out[0, 2 * half :, :] = (near[0, half:].astype(F32) + got[0, half:].astype(F32)).astype(BF16)
    if pad:
        out[:, 2 * half :, :] = jnp.zeros((out.shape[0], pad, out.shape[2]), out.dtype)


def joined(where, bit, near, got, p, ride=0):
    first = where[3 + bit] == 0
    size = near.shape[1] - ride
    a, b = near[p, :size], got[p, :size]
    rows = [jnp.where(first, a, b), jnp.where(first, b, a)]
    return jnp.concatenate(rows, axis=0).astype(F32)


def self_grads_kernel(bit, flow, where, near, got, qkv, out, gains, shifts, biases, *rest):
    size = near.shape[1] - SMALL
    small = near[0, size:].astype(F32) + got[0, size:].astype(F32)
    for k, target in enumerate((gains, shifts, biases)):
        target[...] = small[3 * k : 3 * k + 3]
    if len(rest) == 1:
        rest[0][...] = small[9 : 9 + rest[0].shape[0]]
    else:
        for k, target in enumerate(rest[:2]):
            wide = target.shape[1]
            for i in (0, 1):
                at = (2 * k + i) * wide
                target[i : i + 1, :] = small[9:10, at : at + wide]
        rest[2][...] = small[10:11]
    flow.send(gains, shifts, biases, *rest)
    value = joined(where, bit, near, got, 0, SMALL)
    size = out.shape[0]
    for k in range(3):
        qkv[k] = value[k * size : (k + 1) * size].T
    out[...] = value[3 * size :]


def joined_inside(where, bit, near, got, p, pad):
    half = (near.shape[1] - pad) // 2
    first, parts = where[3 + bit] == 0, []
    for k in (0, 1):
        a, b = near[p, k * half : (k + 1) * half], got[p, k * half : (k + 1) * half]
        parts += [jnp.where(first, a, b), jnp.where(first, b, a)]
    return jnp.concatenate(parts, axis=0).astype(F32)


def cross_grads_kernel(bit, flow, where, near, got, query, kv, out):
    value = joined_inside(where, bit, near, got, 0, 2 * SMALL)
    size = out.shape[0]
    query[...] = value[:size].T
    for k in (0, 1):
        kv[k] = value[(k + 1) * size : (k + 2) * size].T
    out[...] = value[3 * size :]


def ffn_grads_kernel(bit, flow, where, near, got, grad_in, grad_out):
    grad_out[...] = joined(where, bit, near, got, 0)
    flow.send(grad_out)
    grad_in[...] = joined(where, bit, near, got, 1).T


def place_rows_kernel(flow, where, own, got, mixed, grad):
    seq = own.shape[0] // 2
    for k, out in enumerate((mixed, grad)):
        for row, value in ((where[0], own), (1 - where[0], got)):
            out[row] = value[k * seq : (k + 1) * seq, :].astype(out.dtype)
        flow.send(out)


def shards(
    inputs,
    memory,
    segment_ids,
    mem_lengths,
    bucket_group,
    group_tokens,
    norm_gain,
    norm_bias,
    self_qkv,
    self_bias,
    self_out,
    cross_q,
    cross_kv,
    cross_bias,
    cross_out,
    ffn_in,
    ffn_bias,
    ffn_out,
    out_bias,
    cotangent,
):
    dp, mp = lax.axis_size("dp"), lax.axis_size("mp")
    rows, seq, width = inputs.shape
    team = mp // rows
    data, place = lax.axis_index("dp"), lax.axis_index("mp")
    row, seat = place // team, place % team
    bits = dp.bit_length() - 1
    where = jnp.stack([row, seat, data] + [(data >> k) & 1 for k in range(bits)]).astype(jnp.int32)
    run, far = Steps(where), Far

    across = [(i, (i + team) % mp) for i in range(mp)]

    def other(value):
        return lax.ppermute(value, "mp", across)

    def seat_swap(value, step):
        return lax.ppermute(value, "mp", [(i, i ^ step) for i in range(mp)])

    def data_swap(value, k):
        return lax.ppermute(value, "dp", [(i, i ^ (1 << k)) for i in range(dp)])

    def swap(value, axis):
        return other(value) if axis == "row" else data_swap(value, axis)

    def later(value, *after):
        return lax.optimization_barrier((value, *after))[0]

    def team_parts(values):
        step = 1
        while 2 * step < team:
            values = [(v.astype(F32) + seat_swap(v, step).astype(F32)).astype(BF16) for v in values]
            step *= 2
        return [*values, *(seat_swap(v, step) for v in values)]

    head, unit = self_bias.shape[1], ffn_bias.shape[0]
    mem_len = memory.shape[1] * dp
    apart = head % LANES == 0
    n = 2 if apart else 1
    wide = head if apart else 2 * head

    front = [((seq // FRONT, width), BF16)] * FRONT
    back = [((seq // BACK, width), BF16)] * BACK
    whole, full = ((seq, width), BF16), ((seq, width), F32)
    local, totals = ((seq, wide), BF16), ((2 * wide // LANES, seq), F32)
    units = ((seq, unit), BF16)

    other_qkv = other(self_qkv)
    bias_own = jnp.concatenate([self_bias, cross_bias, ffn_bias.reshape(-1, head)])
    bias_other = other(bias_own)
    other_self_out = other(self_out)
    memory_rows = memory.reshape((dp, rows) + memory.shape[1:])
    packing = apart and width % (2 * head) == 0 and ffn_in.shape == ffn_out.shape
    ins = [Raw(group_tokens), Raw(bucket_group), Raw(mem_lengths), Raw(inputs), Raw(cotangent), Raw(memory_rows)]
    ins += [far(segment_ids), far(norm_gain), far(norm_bias), far(out_bias)]
    outs = [whole, whole, ((dp,) + memory.shape[1:], BF16), ((VECTORS, width), F32), ((2, seq), jnp.int32)]
    if packing:
        ins += [Raw(v) for v in (cross_q, cross_kv, cross_out, ffn_in, ffn_out)]
        outs = [((3 * width // 2 + cross_out.size // head // 2, head), BF16), ((2,) + ffn_in.shape, BF16)] + outs
    *packed, x, cot, memory_part, vectors, molecules = run(
        functools.partial(setup_kernel, packing),
        ins,
        outs,
        scratch=[pltpu.SMEM(v.shape, jnp.int32) for v in (group_tokens, bucket_group, mem_lengths)]
        + [pltpu.SemaphoreType.DMA((3,)), pltpu.SemaphoreType.DMA((8 + width // head // 2,))],
        name="setup",
    )
    if packing:
        near_cross = other(packed[0])
        got_cross = data_swap(near_cross, 0)
    memory_row = lax.all_to_all(memory_part, "dp", split_axis=0, concat_axis=0, tiled=True).reshape(mem_len, width)
    def pieces(own, theirs, axis):
        return [far(own), theirs] if apart else [jnp.concatenate([own, theirs], axis=axis)]

    w_qkv = pieces(self_qkv, other_qkv, 2)
    w_self_out = pieces(self_out, other_self_out, 0)
    b_heads = [bias_own, bias_other] if apart else [jnp.concatenate([bias_own, bias_other], axis=1)]
    b_in = b_heads if apart else [b[4:].reshape(1, unit) for b in (bias_own, bias_other)]

    forward_work = [pltpu.VMEM((seq, 2 * seq), BF16), pltpu.VMEM((1, 2 * seq), F32)]
    cross_work = [pltpu.VMEM((mem_len, 2 * seq), BF16), pltpu.VMEM((1, 2 * seq), F32)]
    heads_self, saved_self = [], []
    for i in range(n):
        last = i == n - 1
        ins = [x if i == 0 else normed_self, vectors, molecules, w_qkv[i], b_heads[i]]
        outs = ([whole] if i == 0 else []) + [far(local)] * 3 + [local, far(totals)]
        if last:
            ins += [*w_self_out, *heads_self]
            outs += front
        got = run(functools.partial(self_forward_kernel, n, i), ins, outs, scratch=forward_work, name=f"self_forward_{i}")
        if i == 0:
            normed_self, got = got[0], got[1:]
            early = (normed_self, other_qkv, bias_other, other_self_out)
            if packing:
                other_ffn = other(later(packed[1], *early, near_cross))
            else:
                other_cross = [other(later(w, *early)) for w in (cross_q, cross_kv, cross_out)]
                other_in, other_out = [other(later(w, *other_cross)) for w in (ffn_in, ffn_out)]
        saved_self.append((got[0], got[1], got[2], got[4]))
        heads_self.append(got[3])
    terms = team_parts(got[5:])

    heads_cross, saved_cross = [], []
    if apart:
        w_cross_q, w_cross_kv, w_cross_out = [far(cross_q)], [far(cross_kv)], [far(cross_out)]
    else:
        w_cross_q = pieces(cross_q, other_cross[0], 1)
        w_cross_kv = pieces(cross_kv, other_cross[1], 2)
        w_cross_out = pieces(cross_out, other_cross[2], 0)
    projected = ((mem_len, wide), BF16)
    for i in range(n):
        last = i == n - 1
        if i == 1 and packing:
            query, both, out, *kv = run(
                unpack_memory_kernel,
                [near_cross, got_cross, memory_row, b_heads[1]],
                [(v.shape, BF16) for v in (cross_q, cross_kv, cross_out)] + [projected] * 2,
                name="memory_1",
            )
            for pieces_of, w in ((w_cross_q, query), (w_cross_kv, both), (w_cross_out, out)):
                pieces_of.append(w)
        else:
            if i == 1:
                for pieces_of, w in zip((w_cross_q, w_cross_kv, w_cross_out), other_cross):
                    pieces_of.append(w)
            kv = run(memory_kernel, [memory_row, w_cross_kv[i], b_heads[i]], [projected] * 2, name=f"memory_{i}")
        first = [x, *terms] if i == 0 else [normed_cross]
        ins = first + [vectors, molecules, w_cross_q[i], b_heads[i], *kv]
        outs = ([full, whole] if i == 0 else []) + [local] * 2 + [totals]
        if last:
            ins += [*w_cross_out, *heads_cross]
            outs += front
        got = run(functools.partial(cross_forward_kernel, n, i), ins, outs, scratch=cross_work, name=f"cross_forward_{i}")
        if i == 0:
            after_self, normed_cross, got = got[0], got[1], got[2:]
        saved_cross.append((got[0], *kv, got[2]))
        heads_cross.append(got[1])
    terms = team_parts(got[3:])

    after_cross, normed_ffn, low_ffn, act_own, hid_own, begun, begun_grad = run(
        functools.partial(ffn_kernel, 0),
        [after_self, *terms, cot, vectors, far(ffn_in), b_in[0], far(ffn_out)],
        [full, whole, whole, units, units, full, full],
        name="ffn_0",
    )
    ins = [other_ffn if packing else other_in, b_in[1]] + ([] if packing else [other_out])
    act_other, hid_other, *parts = run(
        functools.partial(ffn_kernel, 1),
        [normed_ffn, low_ffn, begun, begun_grad, *ins],
        [units, units] + back + back,
        name="ffn_1",
    )
    terms = team_parts(parts[BACK:])
    out_terms = team_parts(parts[:BACK])

    class Reduction:
        def __init__(self, keeps, sends, axes, pad=0, turned=False):
            self.pad, self.turned = pad, turned
            self.keeps, self.axes, self.ride, self.carry = keeps, axes, [], []
            self.gots = [swap(s, a) for s, a in zip(sends, axes[0])]
            self.halved = [b for b in axes[0] if b != "row"][:1]
            self.size = sends[0].shape[1]
            self.chunk = None

        def plan(self, extra=None):
            if self.chunk is not None:
                bit, small = self.halved.pop(), SMALL if self.ride else 0
                planes, size, _ = self.chunk.shape
                pad = self.pad if len(self.halved) == 1 else 0
                outs = [((planes, 2 * size - small + pad, width), BF16)]
                return functools.partial(join_kernel, bool(small), pad, bit), [self.chunk, self.got], outs
            axes, keeps, size = self.axes, self.keeps, self.size
            planes = sum(k.shape[0] for k in keeps)
            bit, ride, at, rows = 0, [], None, size
            if len(axes) == 1:
                mode = "last"
            elif axes[1][0] == "row":
                mode, planes = "shard", 1
                if self.carry:
                    ride, at, rows = self.carry, size, size + SMALL
            elif len(axes) == 2:
                mode = "full"
                if self.ride:
                    ride, at, rows = self.ride, self.ride_at, size + SMALL
                    self.size += SMALL
            else:
                mode, bit, rows = "half", axes[1][0], size // 2
                self.size = rows
                self.halved.append(bit)
            more = 8 // planes * SMALL if extra else 0
            outs = [((planes, rows + more, width), BF16)]
            if mode in ("half", "shard"):
                outs = [((planes, self.size, width), F32)] + outs
            ins = [*keeps, *self.gots, *ride]
            kernel = functools.partial(fold_kernel, len(keeps), size, at, mode, bit)
            if not extra:
                return kernel, ins, outs
            second, second_ins, second_outs = extra
            self.extra_at = rows

            def both(flow, where, *refs):
                a, b = len(ins), len(ins) + len(second_ins)
                c = b + len(second_outs)
                kernel(flow, where, *refs[:a], *refs[c:])
                second(flow, where, *refs[a:c], send=refs[-1], offset=rows)

            return both, ins + second_ins, second_outs + outs

        def take(self, got):
            if self.chunk is not None or len(self.axes) == 1:
                if self.chunk is None and self.turned:
                    self.halved[:2] = self.halved[1::-1]
                self.chunk = got[0]
                self.got = swap(self.chunk, self.halved[-1])
            else:
                self.axes = self.axes[1:]
                self.keeps = [got[0]]
                self.gots = [swap(got[-1], self.axes[0][0])]

        def ready(self):
            return self.chunk is not None and len(self.halved) == 1

    def advance(name, *groups, extra=None, more=None):
        groups = [g for g in groups if not g.ready()]
        parts = [g.plan(extra if i == 0 else None) for i, g in enumerate(groups)] + ([more] if more else [])
        results = run.batch(parts, name=name) if parts else []
        given = results.pop() if more else []
        for i, (g, got) in enumerate(zip(groups, results)):
            if extra and i == 0:
                count = len(extra[2])
                given, got = got[:count], got[count:]
            g.take(got)
        return given

    ffn_sums, keep_out, send_out, keep_in, send_in = run(
        ffn_weights_kernel,
        [hid_own, hid_other, act_own, act_other, normed_ffn, low_ffn],
        [((2, unit), F32), ((1, unit, width), F32), ((1, unit, width), BF16)]
        + [((2, unit // 2, width), F32), ((2, unit // 2, width), BF16)],
        name="ffn_weights",
    )
    by_out = Reduction([keep_out], [send_out], [["row"], [0], [1]])
    by_in = Reduction([keep_in], [send_in], [[0], ["row"], [1]])

    all_scores = [pltpu.VMEM((mem_len, 2 * seq), BF16), pltpu.VMEM((2 * seq, LANES), BF16)]
    scratch = [pltpu.VMEM((seq, wide), BF16)] * n + all_scores + [pltpu.VMEM((mem_len, LANES), F32)]
    self_work = [pltpu.VMEM((seq, 2 * seq), BF16), pltpu.VMEM((2 * seq, LANES), BF16)] * 2
    bias_sum = ((2, wide), F32)

    def saved_of(saved):
        return [s[k] for k in range(4) for s in saved]

    got = run(
        functools.partial(cross_backward_kernel, n),
        [after_cross, *terms, cot, vectors, molecules]
        + saved_of(saved_cross) + [*w_cross_out, *w_cross_q],
        [full, whole] + [local] * (3 * n) + [bias_sum] * n + back + [((3, width), F32)],
        scratch=scratch,
        name="cross_backward",
    )
    grad_cross, low_cross, got = got[0], got[1], got[2:]
    cross_grads, cross_bias_sums, got = got[: 3 * n], got[3 * n : 4 * n], got[4 * n :]
    terms, small_ffn = team_parts(got[:BACK]), got[BACK]
    keep, send, *memory_terms, result = run(
        functools.partial(cross_weights_kernel, n),
        [*cross_grads, *heads_cross, *w_cross_kv]
        + [normed_cross, memory_row, low_cross, after_cross, *out_terms, vectors],
        [((2, 2 * head, width), F32), ((2, 2 * head, width), BF16)] + back + [whole],
        name="cross_weights",
    )
    by_cross = Reduction([keep], [send], [[0], [1], ["row"]] + [[k] for k in range(2, bits)], pad=2 * SMALL, turned=True)
    advance("fold_ffn", by_out, by_in)

    group = ((1, 4 * head, width), F32)
    ins = [after_self, *terms, grad_cross, vectors, molecules] + [far(v) for v in saved_self[-1]]
    grad_self, low_self, *last_grads, last_sums, small_cross, first, send = run(
        functools.partial(self_backward_kernel, n),
        ins + [*w_self_out, normed_self, heads_self[-1]],
        [full, whole] + [local] * 3 + [bias_sum, ((3, width), F32), local if n == 2 else group, (group[0], BF16)],
        scratch=[pltpu.VMEM((seq, wide), BF16)] + self_work,
        name="self_backward",
    )
    by_self = Reduction([first], [send], [["row"]] + [[k] for k in range(bits)])
    by_ffn = by_out
    by_ffn.keeps, by_ffn.gots = by_out.keeps + by_in.keeps, by_out.gots + by_in.gots
    by_ffn.axes = [[0]] + [[k] for k in range(1, bits)]
    mem_terms = team_parts(memory_terms)
    share = width // mp
    along = share == LANES and team == 2 and dp == 8 and mem_len // dp * LANES == SMALL * width
    blocks = ((16, SMALL, width), BF16)
    extra = (functools.partial(memory_start_kernel, 1), mem_terms, [blocks]) if along else None
    given = advance("ffn_1", by_ffn, extra=extra)
    ins = [*w_qkv, *last_grads]
    if n == 2:
        ins += [molecules] + [far(v) for v in saved_self[0]] + [first, normed_self, heads_self[0], low_self]
    outs = ([bias_sum, group] if n == 2 else []) + back
    got = run(
        functools.partial(self_backward_rest_kernel, n),
        ins,
        outs,
        scratch=[pltpu.VMEM((seq, wide), BF16)] * 3 + self_work if n == 2 else [],
        name="self_backward_rest",
    )
    self_bias_sums = [last_sums]
    if n == 2:
        self_bias_sums, by_self.keeps, got = [got[0], last_sums], [got[1]], got[2:]
    terms = team_parts(got)
    moved = [*given, by_ffn.gots[0]]
    moved_at = by_ffn.extra_at if along else None
    advance("ffn_2", by_ffn)
    sent, more = [blocks, ((1, 8 * SMALL, width), BF16)], None
    if along:
        more = (functools.partial(memory_send_kernel, 1, moved_at, 0), moved, sent)
    given = advance("cross_1", by_cross, more=more)
    advance("self_1", by_self)

    fits = apart and 4 * head == width and unit == width
    if fits:
        shard_rows = [*self_bias_sums, *cross_bias_sums, ffn_sums]
        lines = 2
    else:

        def by_shard(sums):
            return sums if n == 2 else [sums[0][:, :head], sums[0][:, head:]]

        shard_rows = [
            jnp.stack(
                [
                    jnp.concatenate([a.reshape(-1), b.reshape(-1), ffn_sums[i]]).reshape(-1, width)
                    for i, (a, b) in enumerate(zip(by_shard(self_bias_sums), by_shard(cross_bias_sums)))
                ]
            )
        ]
        lines = shard_rows[0].shape[1]
    both, small_own, small_other = run(
        functools.partial(input_backward_kernel, n),
        [x, *terms, grad_self, vectors, result, small_cross, small_ffn, *shard_rows],
        [((2 * seq, width), BF16)] + [((SMALL, width), BF16)] * 2,
        name="input_backward",
    )

    by_cross.carry = [small_other]
    if along:
        more = (functools.partial(memory_send_kernel, 0, 0, "row"), [given[0], data_swap(given[1], 0)], sent)
    given = advance("cross_2", by_cross, more=more)
    by_self.ride, by_self.ride_at = [small_own, by_cross.gots[0]], by_cross.size
    if along:
        memory_state = [given[0], other(given[1])]
    advance("ffn_3", by_ffn)
    advance("self_cross_2", by_self, by_cross)
    got_both = other(later(both, by_cross.keeps[0]))
    advance("all_3", by_self, by_ffn, by_cross)
    if not along:
        mine, theirs = jnp.concatenate(mem_terms[:BACK]), jnp.concatenate(mem_terms[BACK:])
        total = (mine.astype(F32) + theirs.astype(F32)).astype(BF16)
        total = total.reshape(dp, mem_len // dp, rows, team, share)
        blocks = lax.dynamic_index_in_dim(total, seat, 3, keepdims=False).swapaxes(1, 2)
        blocks = blocks.reshape(dp * rows, mem_len // dp, share)
        same_seat = [[d * mp + m for d in range(dp) for m in range(mp) if m % team == s] for s in range(team)]
        grad_memory = lax.all_to_all(
            blocks, ("dp", "mp"), split_axis=0, concat_axis=0, tiled=True, axis_index_groups=same_seat
        ).astype(F32)
    advance("self_cross_4", by_self, by_cross)

    def cross_grads():
        return run(
            functools.partial(cross_grads_kernel, by_cross.halved[0]),
            [by_cross.chunk, by_cross.got],
            [far(((width, head), F32)), far(((2, width, head), F32)), far(((head, width), F32))],
            name="cross_grads",
        )

    more = (functools.partial(memory_send_kernel, "row", 0, 2), memory_state, sent) if along else None
    while more or not (by_self.ready() and by_cross.ready() and by_ffn.ready()):
        given = advance("rest", by_self, more=more)
        if more:
            memory_state, more = [given[0], data_swap(given[1], 2)], None
        advance("rest_cross", by_ffn, by_cross)
    mixed, grad_inputs = run(
        place_rows_kernel,
        [both, got_both],
        [far(((rows, seq, width), BF16)), far(((rows, seq, width), F32))],
        name="place_rows",
    )
    grad_ffn_in, grad_ffn_out = run(
        functools.partial(ffn_grads_kernel, by_ffn.halved[0]),
        [by_ffn.chunk, by_ffn.got],
        [far(((width, unit), F32)), far(((unit, width), F32))],
        name="ffn_grads",
    )
    grad_cross_q, grad_cross_kv, grad_cross_out = cross_grads()
    if along:
        (grad_memory,) = run(
            functools.partial(memory_end_kernel, 2, 0),
            memory_state,
            [far(((16, mem_len // dp, share), F32))],
            name="memory_end",
        )
    if fits:
        outs = [((2, head), F32), ((2, head), F32), ((1, unit), F32)]
    else:
        outs = [((lines, width), F32)]
    grad_self_qkv, grad_self_out, grad_gain, grad_shift, grad_out_bias, *rest = run(
        functools.partial(self_grads_kernel, by_self.halved[0]),
        [by_self.chunk, by_self.got],
        [far(((3, width, head), F32)), far(((head, width), F32))] + [far(((3, width), F32))] * 3 + [far(v) for v in outs],
        name="self_grads",
    )
    if fits:
        grad_self_bias, grad_cross_bias, grad_ffn_bias = rest[0], rest[1], rest[2].reshape(-1)
    else:
        own_small = rest[0].reshape(-1)
        grad_self_bias = own_small[: 2 * head].reshape(2, head)
        grad_cross_bias = own_small[2 * head : 4 * head].reshape(2, head)
        grad_ffn_bias = own_small[4 * head :]
    return (
        mixed,
        grad_inputs,
        grad_memory,
        grad_gain,
        grad_shift,
        grad_self_qkv,
        grad_self_bias,
        grad_self_out,
        grad_cross_q,
        grad_cross_kv,
        grad_cross_bias,
        grad_cross_out,
        grad_ffn_in,
        grad_ffn_bias,
        grad_ffn_out,
        grad_out_bias,
    )


def solution(mesh):
    placed = (
        P("dp", None, None),
        P(None, "dp", None),
        P("dp", None),
        P("dp", None),
        P(),
        P(),
        P(),
        P(),
        P(None, None, "mp"),
        P(None, "mp"),
        P("mp", None),
        P(None, "mp"),
        P(None, None, "mp"),
        P(None, "mp"),
        P("mp", None),
        P(None, "mp"),
        P("mp"),
        P("mp", None),
        P(),
        P("dp", None, None),
    )
    return jax.shard_map(
        shards,
        mesh=mesh,
        in_specs=placed,
        out_specs=(
            P("dp", None, None),
            P("dp", None, None),
            P(None, "dp", "mp"),
            P(),
            P(),
            P(None, None, "mp"),
            P(None, "mp"),
            P("mp", None),
            P(None, "mp"),
            P(None, None, "mp"),
            P(None, "mp"),
            P("mp", None),
            P(None, "mp"),
            P("mp"),
            P("mp", None),
            P(),
        ),
        check_vma=False,
    )
```

```python
import functools

import jax
import jax.numpy as jnp
from jax import lax
from jax.experimental import pallas as pl
from jax.experimental.pallas import tpu as pltpu
from jax.sharding import PartitionSpec as P

HDIM = 64
LANES = 128
BLOCK = 128
SMALL = 16
FRONT = 2
BACK = 2
EPSILON = 1e-05
F32 = jnp.float32
BF16 = jnp.bfloat16


def dot(left, right):
    return lax.dot_general(left, right, (((1,), (0,)), ((), ())), preferred_element_type=F32)


def dot_right(left, right):
    return lax.dot_general(left, right, (((1,), (1,)), ((), ())), preferred_element_type=F32)


def dot_left(left, right):
    return lax.dot_general(left, right, (((0,), (0,)), ((), ())), preferred_element_type=F32)


class Far:
    def __init__(self, value, pick=False):
        self.value, self.pick = value, pick


class Raw:
    def __init__(self, value):
        self.value = value


class Scalars:
    def __init__(self, value):
        self.value = value


class Flow:
    def __init__(self):
        self.loads, self.stores, self.sent = {}, {}, []

    def need(self, *refs):
        for ref in refs:
            copy = self.loads.pop(id(ref), None)
            if copy is not None:
                copy.wait()

    def send(self, *refs):
        for ref in refs:
            copy = self.stores.pop(id(ref), None)
            if copy is not None:
                copy.start()
                self.sent.append(copy)


class Steps:
    def __init__(self, where):
        self.where, self.token = where, None

    def batch(self, parts, name=None, cost=0.1):
        def kernel(flow, where, *refs):
            at, to = 0, sum(len(ins) for _, ins, _ in parts)
            for part, ins, outs in parts:
                part(flow, where, *refs[at : at + len(ins)], *refs[to : to + len(outs)])
                at, to = at + len(ins), to + len(outs)

        got = self(
            kernel, [v for _, ins, _ in parts for v in ins], [v for _, _, outs in parts for v in outs], name=name, cost=cost
        )
        results = []
        for _, _, outs in parts:
            results.append(got[: len(outs)])
            got = got[len(outs) :]
        return results

    def __call__(self, kernel, ins, outs, scratch=(), name=None, cost=0.1, hold=()):
        near = pl.BlockSpec(memory_space=pltpu.VMEM)
        far = pl.BlockSpec(memory_space=pltpu.HBM)
        words = pl.BlockSpec(memory_space=pltpu.SMEM)
        values, specs, stages = [], [], []
        for v in ins:
            if isinstance(v, Scalars):
                values.append(v.value)
                specs.append(words)
            elif isinstance(v, Raw):
                values.append(pltpu.with_memory_space_constraint(v.value, pltpu.HBM))
                specs.append(far)
            elif isinstance(v, Far):
                values.append(pltpu.with_memory_space_constraint(v.value, pltpu.HBM))
                specs.append(far)
                stages.append(pltpu.VMEM(v.value.shape[1:] if v.pick else v.value.shape, v.value.dtype))
            else:
                values.append(pltpu.with_memory_space_constraint(v, pltpu.VMEM))
                specs.append(near)
        after = [pltpu.with_memory_space_constraint(v, pltpu.VMEM) for v in hold]
        after_specs = [near] * len(after)
        if self.token is not None:
            after.append(pltpu.with_memory_space_constraint(self.token, pltpu.HBM))
            after_specs.append(far)
        for v in outs:
            if isinstance(v, Far):
                stages.append(pltpu.VMEM(*v.value))
        shapes = [pltpu.HBM(*v.value) if isinstance(v, (Far, Raw)) else pltpu.VMEM(*v) for v in outs]
        count, n_in, n_out, n_after = len(stages), len(ins), len(outs), len(after)

        def body(where_ref, *refs):
            refs = list(refs)
            in_refs, refs = refs[:n_in], refs[n_in + n_after :]
            out_refs, refs = refs[:n_out], refs[n_out + 1 :]
            stage_refs, refs = refs[:count], refs[count:]
            flow = Flow()
            if count:
                sems, refs = refs[0], refs[1:]
            given, k = [], 0
            for v, ref in zip(ins, in_refs):
                if isinstance(v, Far):
                    source = ref.at[where_ref[0]] if v.pick else ref
                    copy = pltpu.make_async_copy(source, stage_refs[k], sems.at[k])
                    copy.start()
                    flow.loads[id(stage_refs[k])] = copy
                    ref, k = stage_refs[k], k + 1
                given.append(ref)
            for v, ref in zip(outs, out_refs):
                if isinstance(v, Far):
                    flow.stores[id(stage_refs[k])] = pltpu.make_async_copy(stage_refs[k], ref, sems.at[k])
                    ref, k = stage_refs[k], k + 1
                given.append(ref)
            kernel(flow, where_ref, *given, *refs)
            for copy in flow.loads.values():
                copy.wait()
            for copy in flow.stores.values():
                copy.start()
            for copy in [*flow.sent, *flow.stores.values()]:
                copy.wait()

        results = pl.pallas_call(
            body,
            in_specs=[words] + specs + after_specs,
            out_specs=[far if isinstance(v, (Far, Raw)) else near for v in outs] + [far],
            out_shape=shapes + [pltpu.HBM((8, LANES), F32)],
            scratch_shapes=stages + ([pltpu.SemaphoreType.DMA((count,))] if count else []) + list(scratch),
            compiler_params=pltpu.CompilerParams(vmem_limit_bytes=24 * 1024 * 1024),
            cost_estimate=pl.CostEstimate(flops=10**6, bytes_accessed=int(cost * 3 * 10**6), transcendentals=0),
            name=name,
        )(self.where, *values, *after)
        self.token = results[-1]
        return list(results[:-1])


def row_blocks(seq):
    return [slice(start, start + BLOCK) for start in range(0, seq, BLOCK)]


def row_of(ref, i):
    return ref[i : i + 1, :].astype(F32)


GAIN, SHIFT, OUT, SCALE, VECTORS = 0, 3, 6, 9, 16


def norm_parts(value):
    centre = value - jnp.mean(value, axis=-1, keepdims=True)
    spread = jnp.mean(centre * centre, axis=-1, keepdims=True)
    scale = lax.rsqrt(spread + EPSILON)
    return centre * scale, scale


def norm_backward(value, gain, incoming):
    xhat, scale = norm_parts(value)
    weighted = incoming * gain
    grad = scale * (
        weighted
        - jnp.mean(weighted, axis=-1, keepdims=True)
        - xhat * jnp.mean(weighted * xhat, axis=-1, keepdims=True)
    )
    return grad, jnp.sum(incoming * xhat, axis=0, keepdims=True), jnp.sum(incoming, axis=0, keepdims=True)


def head_lanes(value, j):
    lane = lax.broadcasted_iota(jnp.int32, value.shape, 1)
    return jnp.where((lane >= HDIM) == bool(j), value, jnp.zeros_like(value))


def span_of(block, seq, banded):
    if not banded:
        return slice(0, seq)
    return slice(max(block.start - BLOCK, 0), block.stop)


def start_all(moves, sems):
    copies = [pltpu.make_async_copy(a, b, sems.at[i]) for i, (a, b) in enumerate(moves)]
    for copy in copies:
        copy.start()
    return copies


def setup_kernel(packing, flow, where, *refs):
    group_tokens, bucket_group, lengths, inputs, cotangent, memory, segments, gains, shifts, biases, refs = *refs[:10], refs[10:]
    if packing:
        query, kv, out, w_in, w_out, cross, ffn, own_kv, refs = *refs[:8], refs[8:]
    x, cot, memory_part, vectors, molecules, tokens_now, group_now, lengths_now, word_sems, sems = refs
    words = start_all([(group_tokens, tokens_now), (bucket_group, group_now), (lengths, lengths_now)], word_sems)
    moves = [(memory.at[:, where[0]], memory_part), (inputs.at[where[0]], x), (cotangent.at[where[0]], cot)]
    if packing:
        full, wide = query.shape
        half = full // 2
        rows = pl.ds(pl.multiple_of(where[3] * half, half), half)
        moves += [
            (query.at[rows, :], cross.at[0:half, :]),
            (kv.at[0, rows, :], cross.at[half : 2 * half, :]),
            (kv.at[1, rows, :], cross.at[2 * half : 3 * half, :]),
        ]
        count, size = out.shape[1] // wide // 2, out.shape[0]
        for k in range(count):
            lanes = pl.ds(pl.multiple_of((where[3] * count + k) * wide, wide), wide)
            moves.append((out.at[:, lanes], cross.at[3 * half + k * size : 3 * half + (k + 1) * size, :]))
        moves += [(w_in, ffn.at[0]), (w_out, ffn.at[1]), (kv, own_kv)]
    copies = start_all(moves, sems)
    for copy in words:
        copy.wait()
    width = vectors.shape[1]
    total, own = 0, 0
    for b in range(bucket_group.shape[0]):
        tokens = tokens_now[group_now[b]]
        total = total + tokens
        own = own + jnp.where(where[2] == b, tokens, 0)
    scaled = jnp.full((1, width), bucket_group.shape[0] * own, jnp.int32).astype(F32)
    scale = scaled / jnp.full((1, width), total, jnp.int32).astype(F32)
    size = molecules.shape[1]
    place = lax.broadcasted_iota(jnp.int32, (1, size), 1)
    count, end = jnp.zeros((1, size), jnp.int32), 0
    for k in range(lengths.shape[1]):
        end = end + lengths_now[where[0], k]
        count = count + (end <= place).astype(jnp.int32)
    molecules[1:2, :] = count
    flow.need(segments, gains, shifts, biases)
    molecules[0:1, :] = segments[pl.ds(where[0], 1), :]
    rows = [r[...].astype(F32) for r in (gains, shifts, biases)] + [scale]
    vectors[...] = jnp.concatenate(rows + [jnp.zeros((VECTORS - 10, width), F32)], axis=0)
    for copy in copies:
        copy.wait()


def key_columns(keys):
    size = keys.shape[1]
    tiles = [jnp.broadcast_to(keys[:, at : at + BLOCK], (LANES, BLOCK)).T for at in range(0, size, BLOCK)]
    return jnp.concatenate(tiles, axis=0)


def allowed_of(own, columns, block, span, banded):
    allowed = columns[span] == own[:, block]
    if banded:
        query = lax.broadcasted_iota(jnp.int32, allowed.shape, 1) + block.start
        key = lax.broadcasted_iota(jnp.int32, allowed.shape, 0) + span.start
        allowed = allowed & (key <= query)
    return allowed


def both_heads(value):
    return jnp.concatenate([head_lanes(value, 0), head_lanes(value, 1)], axis=0)


def own_rows(value):
    half = value.shape[1] // 2
    row = lax.broadcasted_iota(jnp.int32, (value.shape[0], half), 0)
    return jnp.where(row < HDIM, value[:, :half], value[:, half:])


def pair_columns(at):
    return slice(2 * at * BLOCK, 2 * (at + 1) * BLOCK)


def attend_forward(q, k, v, own, keys, heads, totals, raised_all, shares, banded):
    seq, wide = q.shape
    columns = key_columns(keys)
    blocks = row_blocks(seq)
    for pair in range(wide // LANES):
        lanes = slice(pair * LANES, (pair + 1) * LANES)
        for at, block in enumerate(blocks):
            span = span_of(block, k.shape[0], banded)
            allowed = allowed_of(own, columns, block, span, banded)
            allowed = jnp.concatenate([allowed, allowed], axis=1)
            scores = dot_right(k[span, lanes], both_heads(q[block, lanes] * 0.125))
            scores = jnp.where(allowed, scores, -1e30)
            maxima = jnp.max(scores, axis=0, keepdims=True)
            raised = jnp.exp(scores - maxima)
            total = jnp.sum(raised, axis=0, keepdims=True)
            raised_all[span, pair_columns(at)] = raised.astype(BF16)
            shares[:, pair_columns(at)] = 1.0 / total
            logs = maxima + jnp.log(total)
            for j in (0, 1):
                totals[2 * pair + j : 2 * pair + j + 1, block] = logs[:, j * BLOCK : (j + 1) * BLOCK]
        turned = v[:, lanes].T
        if not banded:
            mixed = dot(turned, raised_all[...]) * shares[...]
        for at, block in enumerate(blocks):
            if banded:
                span = span_of(block, k.shape[0], banded)
                part = dot(turned[:, span], raised_all[span, pair_columns(at)]) * shares[:, pair_columns(at)]
            else:
                part = mixed[:, pair_columns(at)]
            heads[block, lanes] = own_rows(part).T.astype(BF16)


def attend_backward(q, k, v, own, keys, totals, grad_heads, dq, dk, dv, work, banded):
    seq, wide = q.shape
    columns = key_columns(keys)
    blocks = row_blocks(seq)
    scores_all, query_all = work[:2]
    for pair in range(wide // LANES):
        lanes = slice(pair * LANES, (pair + 1) * LANES)
        for at, block in enumerate(blocks):
            span = span_of(block, k.shape[0], banded)
            allowed = allowed_of(own, columns, block, span, banded)
            allowed = jnp.concatenate([allowed, allowed], axis=1)
            query, grad = both_heads(q[block, lanes] * 0.125), both_heads(grad_heads[block, lanes])
            query_all[pair_columns(at), :] = query
            logs = jnp.concatenate([totals[2 * pair + j : 2 * pair + j + 1, block] for j in (0, 1)], axis=1)
            scores = jnp.where(allowed, dot_right(k[span, lanes], query), -1e30)
            chances = jnp.exp(scores - logs)
            if banded:
                work[2][span, pair_columns(at)] = chances.astype(BF16)
                work[3][pair_columns(at), :] = grad
            else:
                grad_value = dot(chances.astype(BF16), grad)
                work[2][...] = grad_value if at == 0 else work[2][...] + grad_value
            weighted = chances * dot_right(v[span, lanes], grad)
            mean = jnp.sum(weighted, axis=0, keepdims=True)
            scores_all[span, pair_columns(at)] = (weighted - chances * mean).astype(BF16)
        turned = k[:, lanes].T
        if not banded:
            grad_query = dot(turned, scores_all[...])
            dk[:, lanes] = dot(scores_all[...], query_all[...]).astype(BF16)
            dv[:, lanes] = work[2][...].astype(BF16)
        for at, block in enumerate(blocks):
            if banded:
                span = span_of(block, k.shape[0], banded)
                part = dot(turned[:, span], scores_all[span, pair_columns(at)])
                met = slice(pair_columns(at).start, pair_columns(min(at + 1, len(blocks) - 1)).stop)
                dk[block, lanes] = dot(scores_all[block, met], query_all[met, :]).astype(BF16)
                dv[block, lanes] = dot(work[2][block, met], work[3][met, :]).astype(BF16)
            else:
                part = grad_query[:, pair_columns(at)]
            dq[block, lanes] = (own_rows(part).T * 0.125).astype(BF16)


def team_total(mine, theirs, block):
    half = mine[0].shape[0]
    k, rows = block.start // half, slice(block.start % half, block.start % half + BLOCK)
    return mine[k][rows, :].astype(F32) + theirs[k][rows, :].astype(F32)


def put_half(parts, block, value):
    half = parts[0].shape[0]
    start = block.start % half
    parts[block.start // half][start : start + BLOCK, :] = value.astype(parts[0].dtype)


def self_forward_kernel(n, i, flow, where, *refs):
    last = i == n - 1
    first, vectors, molecules, w, bias, refs = *refs[:5], refs[5:]
    if last:
        w_out, done, refs = refs[:n], refs[n : 2 * n - 1], refs[2 * n - 1 :]
    if i == 0:
        normed, refs = refs[0], refs[1:]
        for block in row_blocks(first.shape[0]):
            norm = norm_parts(first[block, :].astype(F32))[0]
            normed[block, :] = (norm * row_of(vectors, GAIN) + row_of(vectors, SHIFT)).astype(BF16)
    else:
        normed = first
    q, k, v, heads, totals = refs[:5]
    flow.need(w)
    q[...] = (dot(normed[...], w[0]) + row_of(bias, 0)).astype(BF16)
    k[...] = dot(normed[...], w[1]).astype(BF16)
    v[...] = (dot(normed[...], w[2]) + row_of(bias, 1)).astype(BF16)
    own = molecules[0:1, :]
    flow.send(q, k, v)
    attend_forward(q, k, v, own, own, heads, totals, *refs[-2:], True)
    flow.send(totals)
    if last:
        project_out(flow, [*done, heads], w_out, refs[5 : 5 + FRONT])


def project_out(flow, heads, w_out, parts):
    flow.need(*w_out)
    for block in row_blocks(heads[0].shape[0]):
        put_half(parts, block, sum(dot(h[block, :], w[...]) for h, w in zip(heads, w_out)))


def memory_kernel(flow, where, memory, w, bias, k, v):
    flow.need(w)
    k[...] = dot(memory[...], w[0]).astype(BF16)
    v[...] = (dot(memory[...], w[1]) + row_of(bias, 3)).astype(BF16)


def unpack_memory_kernel(flow, where, near, got, memory, bias, query, kv, out, k, v):
    full, wide = query.shape
    half, size = full // 2, out.shape[0]
    count = out.shape[1] // wide // 2
    for packed, bit in ((near, where[3]), (got, 1 - where[3])):
        rows = pl.ds(pl.multiple_of(bit * half, half), half)
        query[rows, :] = packed[:half]
        for i in (0, 1):
            kv[i, rows, :] = packed[(i + 1) * half : (i + 2) * half]
        for i in range(count):
            lanes = pl.ds(pl.multiple_of((bit * count + i) * wide, wide), wide)
            out[:, lanes] = packed[3 * half + i * size : 3 * half + (i + 1) * size]
    memory_kernel(flow, where, memory, kv, bias, k, v)


def cross_forward_kernel(n, i, flow, where, *refs):
    last = i == n - 1
    if i == 0:
        x, mine, theirs, refs = refs[0], refs[1 : 1 + FRONT], refs[1 + FRONT : 1 + 2 * FRONT], refs[1 + 2 * FRONT :]
    else:
        normed, refs = refs[0], refs[1:]
    vectors, molecules, w, bias, k, v, refs = *refs[:6], refs[6:]
    if last:
        w_out, done, refs = refs[:n], refs[n : 2 * n - 1], refs[2 * n - 1 :]
    if i == 0:
        after_self, normed, refs = refs[0], refs[1], refs[2:]
    q, heads, totals = refs[:3]
    if i == 0:
        for block in row_blocks(x.shape[0]):
            value = x[block, :].astype(F32) + team_total(mine, theirs, block) + row_of(vectors, OUT)
            after_self[block, :] = value
            norm = norm_parts(value)[0]
            normed[block, :] = (norm * row_of(vectors, GAIN + 1) + row_of(vectors, SHIFT + 1)).astype(BF16)
    flow.need(w)
    q[...] = (dot(normed[...], w[...]) + row_of(bias, 2)).astype(BF16)
    attend_forward(q, k, v, molecules[0:1, :], molecules[1:2, :], heads, totals, *refs[-2:], False)
    if last:
        project_out(flow, [*done, heads], w_out, refs[3 : 3 + FRONT])


def ffn_kernel(i, flow, where, *refs):
    if i == 0:
        after_self, mine, theirs, refs = refs[0], refs[1 : 1 + FRONT], refs[1 + FRONT : 1 + 2 * FRONT], refs[1 + 2 * FRONT :]
        cotangent, vectors, w_in, bias, w_out, refs = *refs[:5], refs[5:]
        after_cross, normed, low, active, grad_hidden, part, part_grad = refs
    else:
        normed, low, begun, begun_grad, w_in, bias, refs = *refs[:6], refs[6:]
        if len(w_in.shape) == 3:
            w_in, w_out = w_in.at[0], w_in.at[1]
        else:
            w_out, refs = refs[0], refs[1:]
        active, grad_hidden, parts, parts_grad = refs[0], refs[1], refs[2 : 2 + BACK], refs[2 + BACK :]
    if bias.shape[0] == 1:
        row = row_of(bias, 0)
    else:
        row = jnp.concatenate([row_of(bias, k) for k in range(4, bias.shape[0])], axis=1)
    if i == 0:
        for block in row_blocks(normed.shape[0]):
            value = after_self[block, :] + team_total(mine, theirs, block) + row_of(vectors, OUT + 1)
            after_cross[block, :] = value
            norm = norm_parts(value)[0]
            normed[block, :] = (norm * row_of(vectors, GAIN + 2) + row_of(vectors, SHIFT + 2)).astype(BF16)
            low[block, :] = (cotangent[block, :].astype(F32) * row_of(vectors, SCALE)).astype(BF16)
    flow.need(w_in, w_out)
    for block in row_blocks(normed.shape[0]):
        hidden = dot(normed[block, :], w_in[...]) + row
        cdf = 0.5 * (1.0 + lax.erf(hidden * 0.7071067811865476))
        act = (hidden * cdf).astype(BF16)
        active[block, :] = act
        slope = cdf + hidden * (0.3989422804014327 * jnp.exp(-0.5 * hidden * hidden))
        back = (slope * dot_right(low[block, :], w_out[...])).astype(BF16)
        grad_hidden[block, :] = back
        out, out_grad = dot(act, w_out[...]), dot_right(back, w_in[...])
        if i == 0:
            part[block, :], part_grad[block, :] = out, out_grad
        else:
            put_half(parts, block, begun[block, :] + out)
            put_half(parts_grad, block, begun_grad[block, :] + out_grad)


def ffn_weights_kernel(flow, where, *refs):
    hidden, active, normed, low, sums = refs[:2], refs[2:4], refs[4], refs[5], refs[6]
    keep_out, send_out, keep_in, send_in = refs[7:]
    half = keep_in.shape[1]
    for i in (0, 1):
        for target, bit in ((keep_in, where[3]), (send_in, 1 - where[3])):
            lanes = pl.ds(pl.multiple_of(bit * half, half), half)
            target[i] = dot_left(hidden[i][:, lanes], normed[...]).astype(target.dtype)
        sums[i : i + 1, :] = jnp.sum(hidden[i][...].astype(F32), axis=0, keepdims=True)
    keep_out[0] = dot_left(active[0][...], low[...])
    send_out[0] = dot_left(active[1][...], low[...]).astype(BF16)


def spread_grad_heads(low, w_out, grad_heads):
    for piece, target in zip(w_out, grad_heads):
        target[...] = dot_right(low[...], piece[...]).astype(BF16)


def column_sums(sums, values):
    for i, value in enumerate(values):
        sums[i : i + 1, :] = jnp.sum(value[...].astype(F32), axis=0, keepdims=True)


def cross_backward_kernel(n, flow, where, *refs):
    after_cross, mine, theirs, refs = refs[0], refs[1 : 1 + BACK], refs[1 + BACK : 1 + 2 * BACK], refs[1 + 2 * BACK :]
    cotangent, vectors, molecules, refs = *refs[:3], refs[3:]
    (q, k, v, totals, w_out, w), refs = [refs[i * n : (i + 1) * n] for i in range(6)], refs[6 * n :]
    grad_cross, low, refs = refs[0], refs[1], refs[2:]
    (dq, dk, dv, bias_sums), refs = [refs[i * n : (i + 1) * n] for i in range(4)], refs[4 * n :]
    parts_out, sums, refs = refs[:BACK], refs[BACK], refs[BACK + 1 :]
    grad_heads, work = refs[:n], refs[n:]
    seq, width = after_cross.shape
    rows = [jnp.zeros((1, width), F32)] * 3
    for block in row_blocks(seq):
        incoming = team_total(mine, theirs, block)
        grad_result = cotangent[block, :].astype(F32) * row_of(vectors, SCALE)
        back, by_gain, by_shift = norm_backward(after_cross[block, :], row_of(vectors, GAIN + 2), incoming)
        value = grad_result + back
        grad_cross[block, :] = value
        low[block, :] = value.astype(BF16)
        parts = (by_gain, by_shift, jnp.sum(grad_result, axis=0, keepdims=True))
        rows = [a + b for a, b in zip(rows, parts)]
    for i, row in enumerate(rows):
        sums[i : i + 1, :] = row
    flow.need(*w_out)
    spread_grad_heads(low, w_out, grad_heads)
    own, keys = molecules[0:1, :], molecules[1:2, :]
    for i in range(n):
        attend_backward(
            q[i], k[i], v[i], own, keys, totals[i], grad_heads[i], dq[i], dk[i], dv[i], work, False
        )
        column_sums(bias_sums[i], (dq[i], dv[i]))
    flow.need(*w)
    for block in row_blocks(seq):
        put_half(parts_out, block, sum(dot_right(d[block, :], m[...]) for d, m in zip(dq, w)))


def shard_grads(kinds):
    grads = ([], [])
    for kind in kinds:
        if len(kind) == 2:
            for i in (0, 1):
                grads[i].append(dot_left(kind[i][0][...], kind[i][1][...]))
        else:
            left, right = kind[0]
            both, half = dot_left(left[...], right[...]), left.shape[1] // 2
            grads[0].append(both[:half])
            grads[1].append(both[half:])
    return grads


def cross_weights_kernel(n, flow, where, *refs):
    (dq, dk, dv, heads, w), refs = [refs[i * n : (i + 1) * n] for i in range(5)], refs[5 * n :]
    normed, memory, low, after_cross, refs = *refs[:4], refs[4:]
    mine, theirs, vectors, refs = refs[:BACK], refs[BACK : 2 * BACK], refs[2 * BACK], refs[2 * BACK + 1 :]
    keep, send, terms, result = refs[0], refs[1], refs[2 : 2 + BACK], refs[-1]
    flow.need(*w)
    pairs = [[(a, b) for a in left] for left, b in ((dq, normed), (dk, memory), (dv, memory), (heads, low))]
    first = where[3] == 0
    for i, grads in enumerate(shard_grads(pairs)):
        upper, lower = jnp.concatenate(grads[:2], axis=0), jnp.concatenate(grads[2:], axis=0)
        keep[i] = jnp.where(first, upper, lower)
        send[i] = jnp.where(first, lower, upper).astype(BF16)
    for block in row_blocks(memory.shape[0]):
        total = sum(
            dot_right(a[block, :], m[0]) + dot_right(b[block, :], m[1]) for a, b, m in zip(dk, dv, w)
        )
        put_half(terms, block, total)
    for block in row_blocks(after_cross.shape[0]):
        both = team_total(mine, theirs, block)
        result[block, :] = (after_cross[block, :] + both + row_of(vectors, OUT + 2)).astype(BF16)


def put_grads(target, grads):
    size = grads[0].shape[0]
    for k, grad in enumerate(grads):
        target[0, k * size : (k + 1) * size, :] = grad.astype(target.dtype)


def self_backward_kernel(n, flow, where, *refs):
    after_self, mine, theirs, refs = refs[0], refs[1 : 1 + BACK], refs[1 + BACK : 1 + 2 * BACK], refs[1 + 2 * BACK :]
    grad_cross, vectors, molecules, q, k, v, totals, refs = *refs[:7], refs[7:]
    w_out, refs = refs[:n], refs[n:]
    normed, heads, grad_self, low, dq, dk, dv, bias_sums, sums, refs = *refs[:9], refs[9:]
    first, send, grad_heads, work = *refs[:3], refs[3:]
    seq, width = after_self.shape
    rows = [jnp.zeros((1, width), F32)] * 3
    for block in row_blocks(seq):
        incoming = team_total(mine, theirs, block)
        back, by_gain, by_shift = norm_backward(after_self[block, :], row_of(vectors, GAIN + 1), incoming)
        upper = grad_cross[block, :]
        value = upper + back
        grad_self[block, :] = value
        low[block, :] = value.astype(BF16)
        parts = (by_gain, by_shift, jnp.sum(upper, axis=0, keepdims=True))
        rows = [a + b for a, b in zip(rows, parts)]
    for i, row in enumerate(rows):
        sums[i : i + 1, :] = row
    flow.need(*w_out)
    spread_grad_heads(low, w_out, [first, grad_heads] if n == 2 else [grad_heads])
    own = molecules[0:1, :]
    flow.need(q, k, v, totals)
    attend_backward(q, k, v, own, own, totals, grad_heads, dq, dk, dv, work, True)
    column_sums(bias_sums, (dq, dv))
    grads = [dot_left(a[...], b[...]) for a, b in ((dq, normed), (dk, normed), (dv, normed), (heads, low))]
    if n == 2:
        put_grads(send, grads)
    else:
        half = grads[0].shape[0] // 2
        put_grads(first, [g[:half] for g in grads])
        put_grads(send, [g[half:] for g in grads])


def self_backward_rest_kernel(n, flow, where, *refs):
    w, grads_last, refs = refs[:n], refs[n : n + 3], refs[n + 3 :]
    pieces = [grads_last]
    if n == 2:
        molecules, q, k, v, totals, grad_heads, normed, heads, low, refs = *refs[:9], refs[9:]
        bias_sums, keep, parts_out, refs = refs[0], refs[1], refs[2 : 2 + BACK], refs[2 + BACK :]
        dq, dk, dv, work = *refs[:3], refs[3:]
        own = molecules[0:1, :]
        flow.need(q, k, v, totals)
        attend_backward(q, k, v, own, own, totals, grad_heads, dq, dk, dv, work, True)
        column_sums(bias_sums, (dq, dv))
        put_grads(keep, [dot_left(a[...], b[...]) for a, b in ((dq, normed), (dk, normed), (dv, normed), (heads, low))])
        pieces = [(dq, dk, dv), grads_last]
    else:
        parts_out = refs[:BACK]
    flow.need(*w)
    for block in row_blocks(grads_last[0].shape[0]):
        total = 0.0
        for matrices, grads in zip(w, pieces):
            for which, d in enumerate(grads):
                total += dot_right(d[block, :], matrices[which])
        put_half(parts_out, block, total)


def input_backward_kernel(n, flow, where, x, *refs):
    mine, theirs, refs = refs[:BACK], refs[BACK : 2 * BACK], refs[2 * BACK :]
    grad_self, vectors, result, by_cross, by_ffn, refs = *refs[:5], refs[5:]
    shard_rows, (both, small_own, small_other) = refs[:-3], refs[-3:]
    seq = x.shape[0]
    both[:seq, :] = result[...]
    width = x.shape[1]
    rows = [jnp.zeros((1, width), F32)] * 3
    for block in row_blocks(x.shape[0]):
        incoming = team_total(mine, theirs, block)
        back, by_gain, by_shift = norm_backward(x[block, :].astype(F32), row_of(vectors, GAIN), incoming)
        upper = grad_self[block, :]
        both[seq + block.start : seq + block.stop, :] = (upper + back).astype(BF16)
        parts = (by_gain, by_shift, jnp.sum(upper, axis=0, keepdims=True))
        rows = [a + b for a, b in zip(rows, parts)]
    common = [r for k in range(3) for r in (rows[k], by_cross[k : k + 1, :], by_ffn[k : k + 1, :])]
    if len(shard_rows) == 1:
        lines = [shard_rows[0][i] for i in (0, 1)]
    else:
        sums_self, sums_cross, sums_ffn = shard_rows[:n], shard_rows[n : 2 * n], shard_rows[2 * n]
        lines = []
        for i in (0, 1):
            pieces = [r[k : k + 1, :] for r in (sums_self[i], sums_cross[i]) for k in (0, 1)]
            lines.append(jnp.concatenate([jnp.concatenate(pieces, axis=1), sums_ffn[i : i + 1, :]], axis=0))
    rest = jnp.zeros((SMALL - 9 - lines[0].shape[0], width), F32)
    small = [jnp.concatenate([*common, line, rest], axis=0).astype(BF16) for line in lines]
    small_own[...] = small[0]
    small_other[...] = small[1]


def fold_kernel(count, size, ride, mode, bit, flow, where, *refs):
    keeps, gots, refs = refs[:count], refs[count : 2 * count], refs[2 * count :]
    planes = [(k, p) for k in range(count) for p in range(keeps[k].shape[0])]

    def part(at, rows):
        k, p = planes[at]
        return keeps[k][p, rows, :].astype(F32) + gots[k][p, rows, :].astype(F32)

    if mode == "half":
        keep, send = refs
        half = size // 2
        for at in range(len(planes)):
            for target, side in ((keep, where[3 + bit]), (send, 1 - where[3 + bit])):
                rows = pl.ds(pl.multiple_of(side * half, half), half)
                target[at, :half, :] = part(at, rows).astype(target.dtype)
    elif mode == "shard":
        if ride is not None:
            refs[-1][0, size : size + SMALL, :] = refs[0][...]
        for at, target in enumerate(refs[-2:]):
            target[0, :size, :] = part(at, slice(0, size)).astype(target.dtype)
    else:
        out = refs[-1]
        for at in range(len(planes)):
            out[at, :size, :] = part(at, slice(0, size)).astype(out.dtype)
        if ride is not None:
            own, came = refs[:2]
            small = own[...].astype(F32) + came[0, ride : ride + SMALL, :].astype(F32)
            out[0, size : size + SMALL, :] = small.astype(out.dtype)


def memory_pairs(axis):
    step = 1 if axis == "row" else 2 << axis
    return [(k, k | step) for k in range(16) if not k & step]


def memory_bit(where, axis):
    return where[0] if axis == "row" else where[3 + axis]


def send_blocks(where, axis, blocks, send, offset):
    low = memory_bit(where, axis) == 0
    per = 8 // send.shape[0]
    for k, (a, b) in enumerate(memory_pairs(axis)):
        at = offset + k % per * SMALL
        send[k // per, at : at + SMALL, :] = jnp.where(low, blocks[b], blocks[a])


def take_blocks(where, axis, kept, got, offset):
    low = memory_bit(where, axis) == 0
    per = 8 // got.shape[0]
    blocks = {}
    for k, (a, b) in enumerate(memory_pairs(axis)):
        at = offset + k % per * SMALL
        came = got[k // per, at : at + SMALL, :]
        blocks[a] = jnp.where(low, kept[a], came)
        blocks[b] = jnp.where(low, came, kept[b])
    return blocks


def memory_start_kernel(axis, flow, where, *refs, send, offset):
    mine, theirs, kept = refs[:BACK], refs[BACK : 2 * BACK], refs[2 * BACK]
    half, width = mine[0].shape
    tokens = half * BACK // 8
    share = LANES
    blocks = {}
    for r in (0, 1):
        lanes = pl.ds(pl.multiple_of((2 * r + where[1]) * share, share), share)
        for k in range(BACK):
            total = (mine[k][:, lanes].astype(F32) + theirs[k][:, lanes].astype(F32)).astype(BF16)
            for d in range(half // tokens):
                block = total[d * tokens : (d + 1) * tokens]
                parts = [block[q : q + SMALL] for q in range(0, tokens, SMALL)]
                at = 2 * (k * half // tokens + d) + r
                blocks[at] = jnp.concatenate(parts, axis=1)
                kept[at] = blocks[at]
    send_blocks(where, axis, blocks, send, offset)


def memory_send_kernel(before, at, axis, flow, where, old, got, kept, send):
    blocks = take_blocks(where, before, old, got, at)
    for k, block in blocks.items():
        kept[k] = block
    send_blocks(where, axis, blocks, send, 0)


def memory_end_kernel(before, at, flow, where, old, got, out):
    for k, block in take_blocks(where, before, old, got, at).items():
        parts = [block[:, q : q + LANES] for q in range(0, block.shape[1], LANES)]
        out[k] = jnp.concatenate(parts, axis=0).astype(out.dtype)


def join_kernel(ride, pad, bit, flow, where, near, got, out):
    half = near.shape[1] - (SMALL if ride else 0)
    for value, side in ((near, where[3 + bit]), (got, 1 - where[3 + bit])):
        rows = pl.ds(pl.multiple_of(side * half, half), half)
        for p in range(near.shape[0]):
            out[p, rows, :] = value[p, :half]
    if ride:
        out[0, 2 * half :, :] = (near[0, half:].astype(F32) + got[0, half:].astype(F32)).astype(BF16)
    if pad:
        out[:, 2 * half :, :] = jnp.zeros((out.shape[0], pad, out.shape[2]), out.dtype)


def joined(where, bit, near, got, p, ride=0):
    first = where[3 + bit] == 0
    size = near.shape[1] - ride
    a, b = near[p, :size], got[p, :size]
    rows = [jnp.where(first, a, b), jnp.where(first, b, a)]
    return jnp.concatenate(rows, axis=0).astype(F32)


def self_grads_kernel(bit, flow, where, near, got, qkv, out, gains, shifts, biases, *rest):
    size = near.shape[1] - SMALL
    small = near[0, size:].astype(F32) + got[0, size:].astype(F32)
    for k, target in enumerate((gains, shifts, biases)):
        target[...] = small[3 * k : 3 * k + 3]
    if len(rest) == 1:
        rest[0][...] = small[9 : 9 + rest[0].shape[0]]
    else:
        for k, target in enumerate(rest[:2]):
            wide = target.shape[1]
            for i in (0, 1):
                at = (2 * k + i) * wide
                target[i : i + 1, :] = small[9:10, at : at + wide]
        rest[2][...] = small[10:11]
    flow.send(gains, shifts, biases, *rest)
    value = joined_inside(where, bit, near, got, 0, SMALL)
    size = out.shape[0]
    for k in range(3):
        qkv[k] = value[k * size : (k + 1) * size].T
    out[...] = value[3 * size :]


def joined_inside(where, bit, near, got, p, pad=0):
    half = (near.shape[1] - pad) // 2
    first, parts = where[3 + bit] == 0, []
    for k in (0, 1):
        a, b = near[p, k * half : (k + 1) * half], got[p, k * half : (k + 1) * half]
        parts += [jnp.where(first, a, b), jnp.where(first, b, a)]
    return jnp.concatenate(parts, axis=0).astype(F32)


def cross_grads_kernel(bit, flow, where, near, got, query, kv, out):
    value = joined(where, bit, near, got, 0, 2 * SMALL)
    size = out.shape[0]
    query[...] = value[:size].T
    for k in (0, 1):
        kv[k] = value[(k + 1) * size : (k + 2) * size].T
    out[...] = value[3 * size :]


def ffn_grads_kernel(bit, flow, where, near, got, grad_in, grad_out):
    grad_out[...] = joined_inside(where, bit, near, got, 0)
    flow.send(grad_out)
    grad_in[...] = joined_inside(where, bit, near, got, 1).T


def place_rows_kernel(flow, where, own, got, mixed, grad):
    seq = own.shape[0] // 2
    for k, out in enumerate((mixed, grad)):
        for row, value in ((where[0], own), (1 - where[0], got)):
            out[row] = value[k * seq : (k + 1) * seq, :].astype(out.dtype)
        flow.send(out)


def shards(
    inputs,
    memory,
    segment_ids,
    mem_lengths,
    bucket_group,
    group_tokens,
    norm_gain,
    norm_bias,
    self_qkv,
    self_bias,
    self_out,
    cross_q,
    cross_kv,
    cross_bias,
    cross_out,
    ffn_in,
    ffn_bias,
    ffn_out,
    out_bias,
    cotangent,
):
    dp, mp = lax.axis_size("dp"), lax.axis_size("mp")
    rows, seq, width = inputs.shape
    team = mp // rows
    data, place = lax.axis_index("dp"), lax.axis_index("mp")
    row, seat = place // team, place % team
    bits = dp.bit_length() - 1
    where = jnp.stack([row, seat, data] + [(data >> k) & 1 for k in range(bits)]).astype(jnp.int32)
    run, far = Steps(where), Far

    across = [(i, (i + team) % mp) for i in range(mp)]

    def other(value):
        return lax.ppermute(value, "mp", across)

    def seat_swap(value, step):
        return lax.ppermute(value, "mp", [(i, i ^ step) for i in range(mp)])

    def data_swap(value, k):
        return lax.ppermute(value, "dp", [(i, i ^ (1 << k)) for i in range(dp)])

    def swap(value, axis):
        return other(value) if axis == "row" else data_swap(value, axis)

    def later(value, *after):
        return lax.optimization_barrier((value, *after))[0]

    def team_parts(values):
        step = 1
        while 2 * step < team:
            values = [(v.astype(F32) + seat_swap(v, step).astype(F32)).astype(BF16) for v in values]
            step *= 2
        return [*values, *(seat_swap(v, step) for v in values)]

    head, unit = self_bias.shape[1], ffn_bias.shape[0]
    mem_len = memory.shape[1] * dp
    apart = head % LANES == 0
    n = 2 if apart else 1
    wide = head if apart else 2 * head

    front = [((seq // FRONT, width), BF16)] * FRONT
    back = [((seq // BACK, width), BF16)] * BACK
    whole, full = ((seq, width), BF16), ((seq, width), F32)
    local, totals = ((seq, wide), BF16), ((2 * wide // LANES, seq), F32)
    units = ((seq, unit), BF16)

    other_qkv = other(self_qkv)
    bias_own = jnp.concatenate([self_bias, cross_bias, ffn_bias.reshape(-1, head)])
    bias_other = other(bias_own)
    other_self_out = other(self_out)
    memory_rows = memory.reshape((dp, rows) + memory.shape[1:])
    packing = apart and width % (2 * head) == 0 and ffn_in.shape == ffn_out.shape
    ins = [Raw(group_tokens), Raw(bucket_group), Raw(mem_lengths), Raw(inputs), Raw(cotangent), Raw(memory_rows)]
    ins += [far(segment_ids), far(norm_gain), far(norm_bias), far(out_bias)]
    outs = [whole, whole, ((dp,) + memory.shape[1:], BF16), ((VECTORS, width), F32), ((2, seq), jnp.int32)]
    if packing:
        ins += [Raw(v) for v in (cross_q, cross_kv, cross_out, ffn_in, ffn_out)]
        packs = [((3 * width // 2 + cross_out.size // head // 2, head), BF16), ((2,) + ffn_in.shape, BF16)]
        outs = packs + [(cross_kv.shape, BF16)] + outs
    *packed, x, cot, memory_part, vectors, molecules = run(
        functools.partial(setup_kernel, packing),
        ins,
        outs,
        scratch=[pltpu.SMEM(v.shape, jnp.int32) for v in (group_tokens, bucket_group, mem_lengths)]
        + [pltpu.SemaphoreType.DMA((3,)), pltpu.SemaphoreType.DMA((9 + width // head // 2,))],
        name="setup",
    )
    if packing:
        near_cross = other(packed[0])
        got_cross = data_swap(near_cross, 0)
    memory_row = lax.all_to_all(memory_part, "dp", split_axis=0, concat_axis=0, tiled=True).reshape(mem_len, width)
    def pieces(own, theirs, axis):
        return [far(own), theirs] if apart else [jnp.concatenate([own, theirs], axis=axis)]

    w_qkv = pieces(self_qkv, other_qkv, 2)
    w_self_out = pieces(self_out, other_self_out, 0)
    b_heads = [bias_own, bias_other] if apart else [jnp.concatenate([bias_own, bias_other], axis=1)]
    b_in = b_heads if apart else [b[4:].reshape(1, unit) for b in (bias_own, bias_other)]

    forward_work = [pltpu.VMEM((seq, 2 * seq), BF16), pltpu.VMEM((1, 2 * seq), F32)]
    cross_work = [pltpu.VMEM((mem_len, 2 * seq), BF16), pltpu.VMEM((1, 2 * seq), F32)]
    heads_self, saved_self = [], []
    for i in range(n):
        last = i == n - 1
        ins = [x if i == 0 else normed_self, vectors, molecules, w_qkv[i], b_heads[i]]
        outs = ([whole] if i == 0 else []) + [far(local)] * 3 + [local, far(totals)]
        if last:
            ins += [*w_self_out, *heads_self]
            outs += front
        got = run(functools.partial(self_forward_kernel, n, i), ins, outs, scratch=forward_work, name=f"self_forward_{i}")
        if i == 0:
            normed_self, got = got[0], got[1:]
            early = (normed_self, other_qkv, bias_other, other_self_out)
            if packing:
                other_ffn = other(later(packed[1], *early, near_cross))
            else:
                other_cross = [other(later(w, *early)) for w in (cross_q, cross_kv, cross_out)]
                other_in, other_out = [other(later(w, *other_cross)) for w in (ffn_in, ffn_out)]
        saved_self.append((got[0], got[1], got[2], got[4]))
        heads_self.append(got[3])
    terms = team_parts(got[5:])

    heads_cross, saved_cross = [], []
    if apart:
        w_cross_q, w_cross_out = [far(cross_q)], [far(cross_out)]
        w_cross_kv = [packed[2] if packing else far(cross_kv)]
    else:
        w_cross_q = pieces(cross_q, other_cross[0], 1)
        w_cross_kv = pieces(cross_kv, other_cross[1], 2)
        w_cross_out = pieces(cross_out, other_cross[2], 0)
    projected = ((mem_len, wide), BF16)
    for i in range(n):
        last = i == n - 1
        if i == 1 and packing:
            query, both, out, *kv = run(
                unpack_memory_kernel,
                [near_cross, got_cross, memory_row, b_heads[1]],
                [(v.shape, BF16) for v in (cross_q, cross_kv, cross_out)] + [projected] * 2,
                name="memory_1",
            )
            for pieces_of, w in ((w_cross_q, query), (w_cross_kv, both), (w_cross_out, out)):
                pieces_of.append(w)
        else:
            if i == 1:
                for pieces_of, w in zip((w_cross_q, w_cross_kv, w_cross_out), other_cross):
                    pieces_of.append(w)
            kv = run(memory_kernel, [memory_row, w_cross_kv[i], b_heads[i]], [projected] * 2, name=f"memory_{i}")
        first = [x, *terms] if i == 0 else [normed_cross]
        ins = first + [vectors, molecules, w_cross_q[i], b_heads[i], *kv]
        outs = ([full, whole] if i == 0 else []) + [local] * 2 + [totals]
        if last:
            ins += [*w_cross_out, *heads_cross]
            outs += front
        got = run(functools.partial(cross_forward_kernel, n, i), ins, outs, scratch=cross_work, name=f"cross_forward_{i}")
        if i == 0:
            after_self, normed_cross, got = got[0], got[1], got[2:]
        saved_cross.append((got[0], *kv, got[2]))
        heads_cross.append(got[1])
    terms = team_parts(got[3:])

    after_cross, normed_ffn, low_ffn, act_own, hid_own, begun, begun_grad = run(
        functools.partial(ffn_kernel, 0),
        [after_self, *terms, cot, vectors, far(ffn_in), b_in[0], far(ffn_out)],
        [full, whole, whole, units, units, full, full],
        name="ffn_0",
    )
    ins = [other_ffn if packing else other_in, b_in[1]] + ([] if packing else [other_out])
    act_other, hid_other, *parts = run(
        functools.partial(ffn_kernel, 1),
        [normed_ffn, low_ffn, begun, begun_grad, *ins],
        [units, units] + back + back,
        name="ffn_1",
    )
    terms = team_parts(parts[BACK:])
    out_terms = team_parts(parts[:BACK])

    class Reduction:
        def __init__(self, keeps, sends, axes, pad=0, turned=False):
            self.pad, self.turned = pad, turned
            self.keeps, self.axes, self.ride, self.carry = keeps, axes, [], []
            self.gots = [swap(s, a) for s, a in zip(sends, axes[0])]
            self.halved = [b for b in axes[0] if b != "row"][:1]
            self.size = sends[0].shape[1]
            self.chunk = None

        def plan(self, extra=None):
            if self.chunk is not None:
                bit, small = self.halved.pop(), SMALL if self.ride else 0
                planes, size, _ = self.chunk.shape
                pad = self.pad if len(self.halved) == 1 else 0
                outs = [((planes, 2 * size - small + pad, width), BF16)]
                return functools.partial(join_kernel, bool(small), pad, bit), [self.chunk, self.got], outs
            axes, keeps, size = self.axes, self.keeps, self.size
            planes = sum(k.shape[0] for k in keeps)
            bit, ride, at, rows = 0, [], None, size
            if len(axes) == 1:
                mode = "last"
            elif axes[1][0] == "row":
                mode, planes = "shard", 1
                if self.carry:
                    ride, at, rows = self.carry, size, size + SMALL
            elif len(axes) == 2:
                mode = "full"
                if self.ride:
                    ride, at, rows = self.ride, self.ride_at, size + SMALL
                    self.size += SMALL
            else:
                mode, bit, rows = "half", axes[1][0], size // 2
                self.size = rows
                self.halved.append(bit)
            more = 8 // planes * SMALL if extra else 0
            outs = [((planes, rows + more, width), BF16)]
            if mode in ("half", "shard"):
                outs = [((planes, self.size, width), F32)] + outs
            ins = [*keeps, *self.gots, *ride]
            kernel = functools.partial(fold_kernel, len(keeps), size, at, mode, bit)
            if not extra:
                return kernel, ins, outs
            second, second_ins, second_outs = extra
            self.extra_at = rows

            def both(flow, where, *refs):
                a, b = len(ins), len(ins) + len(second_ins)
                c = b + len(second_outs)
                kernel(flow, where, *refs[:a], *refs[c:])
                second(flow, where, *refs[a:c], send=refs[-1], offset=rows)

            return both, ins + second_ins, second_outs + outs

        def take(self, got):
            if self.chunk is not None or len(self.axes) == 1:
                if self.chunk is None and self.turned:
                    self.halved[:2] = self.halved[1::-1]
                self.chunk = got[0]
                self.got = swap(self.chunk, self.halved[-1])
            else:
                self.axes = self.axes[1:]
                self.keeps = [got[0]]
                self.gots = [swap(got[-1], self.axes[0][0])]

        def ready(self):
            return self.chunk is not None and len(self.halved) == 1

    def advance(name, *groups, extra=None, more=None):
        groups = [g for g in groups if not g.ready()]
        parts = [g.plan(extra if i == 0 else None) for i, g in enumerate(groups)] + ([more] if more else [])
        results = run.batch(parts, name=name) if parts else []
        given = results.pop() if more else []
        for i, (g, got) in enumerate(zip(groups, results)):
            if extra and i == 0:
                count = len(extra[2])
                given, got = got[:count], got[count:]
            g.take(got)
        return given

    ffn_sums, keep_out, send_out, keep_in, send_in = run(
        ffn_weights_kernel,
        [hid_own, hid_other, act_own, act_other, normed_ffn, low_ffn],
        [((2, unit), F32), ((1, unit, width), F32), ((1, unit, width), BF16)]
        + [((2, unit // 2, width), F32), ((2, unit // 2, width), BF16)],
        name="ffn_weights",
    )
    by_out = Reduction([keep_out], [send_out], [["row"], [0], [1]])
    by_in = Reduction([keep_in], [send_in], [[0], ["row"], [1]])

    all_scores = [pltpu.VMEM((mem_len, 2 * seq), BF16), pltpu.VMEM((2 * seq, LANES), BF16)]
    scratch = [pltpu.VMEM((seq, wide), BF16)] * n + all_scores + [pltpu.VMEM((mem_len, LANES), F32)]
    self_work = [pltpu.VMEM((seq, 2 * seq), BF16), pltpu.VMEM((2 * seq, LANES), BF16)] * 2
    bias_sum = ((2, wide), F32)

    def saved_of(saved):
        return [s[k] for k in range(4) for s in saved]

    got = run(
        functools.partial(cross_backward_kernel, n),
        [after_cross, *terms, cot, vectors, molecules]
        + saved_of(saved_cross) + [*w_cross_out, *w_cross_q],
        [full, whole] + [local] * (3 * n) + [bias_sum] * n + back + [((3, width), F32)],
        scratch=scratch,
        name="cross_backward",
    )
    grad_cross, low_cross, got = got[0], got[1], got[2:]
    cross_grads, cross_bias_sums, got = got[: 3 * n], got[3 * n : 4 * n], got[4 * n :]
    terms, small_ffn = team_parts(got[:BACK]), got[BACK]
    keep, send, *memory_terms, result = run(
        functools.partial(cross_weights_kernel, n),
        [*cross_grads, *heads_cross, *w_cross_kv]
        + [normed_cross, memory_row, low_cross, after_cross, *out_terms, vectors],
        [((2, 2 * head, width), F32), ((2, 2 * head, width), BF16)] + back + [whole],
        name="cross_weights",
    )
    by_cross = Reduction([keep], [send], [[0], [1], ["row"]] + [[k] for k in range(2, bits)], pad=2 * SMALL)
    advance("fold_ffn", by_out, by_in)

    group = ((1, 4 * head, width), F32)
    ins = [after_self, *terms, grad_cross, vectors, molecules] + [far(v) for v in saved_self[-1]]
    grad_self, low_self, *last_grads, last_sums, small_cross, first, send = run(
        functools.partial(self_backward_kernel, n),
        ins + [*w_self_out, normed_self, heads_self[-1]],
        [full, whole] + [local] * 3 + [bias_sum, ((3, width), F32), local if n == 2 else group, (group[0], BF16)],
        scratch=[pltpu.VMEM((seq, wide), BF16)] + self_work,
        name="self_backward",
    )
    by_self = Reduction([first], [send], [["row"]] + [[k] for k in range(bits)], turned=True)
    by_ffn = by_out
    by_ffn.keeps, by_ffn.gots = by_out.keeps + by_in.keeps, by_out.gots + by_in.gots
    by_ffn.turned = True
    by_ffn.axes = [[0]] + [[k] for k in range(1, bits)]
    mem_terms = team_parts(memory_terms)
    share = width // mp
    along = share == LANES and team == 2 and dp == 8 and mem_len // dp * LANES == SMALL * width
    blocks = ((16, SMALL, width), BF16)
    extra = (functools.partial(memory_start_kernel, 1), mem_terms, [blocks]) if along else None
    given = advance("ffn_1", by_ffn, extra=extra)
    ins = [*w_qkv, *last_grads]
    if n == 2:
        ins += [molecules] + [far(v) for v in saved_self[0]] + [first, normed_self, heads_self[0], low_self]
    outs = ([bias_sum, group] if n == 2 else []) + back
    got = run(
        functools.partial(self_backward_rest_kernel, n),
        ins,
        outs,
        scratch=[pltpu.VMEM((seq, wide), BF16)] * 3 + self_work if n == 2 else [],
        name="self_backward_rest",
    )
    self_bias_sums = [last_sums]
    if n == 2:
        self_bias_sums, by_self.keeps, got = [got[0], last_sums], [got[1]], got[2:]
    terms = team_parts(got)
    moved = [*given, by_ffn.gots[0]]
    moved_at = by_ffn.extra_at if along else None
    advance("ffn_2", by_ffn)
    sent, more = [blocks, ((1, 8 * SMALL, width), BF16)], None
    if along:
        more = (functools.partial(memory_send_kernel, 1, moved_at, 0), moved, sent)
    given = advance("cross_1", by_cross, more=more)
    advance("self_1", by_self)

    fits = apart and 4 * head == width and unit == width
    if fits:
        shard_rows = [*self_bias_sums, *cross_bias_sums, ffn_sums]
        lines = 2
    else:

        def by_shard(sums):
            return sums if n == 2 else [sums[0][:, :head], sums[0][:, head:]]

        shard_rows = [
            jnp.stack(
                [
                    jnp.concatenate([a.reshape(-1), b.reshape(-1), ffn_sums[i]]).reshape(-1, width)
                    for i, (a, b) in enumerate(zip(by_shard(self_bias_sums), by_shard(cross_bias_sums)))
                ]
            )
        ]
        lines = shard_rows[0].shape[1]
    both, small_own, small_other = run(
        functools.partial(input_backward_kernel, n),
        [x, *terms, grad_self, vectors, result, small_cross, small_ffn, *shard_rows],
        [((2 * seq, width), BF16)] + [((SMALL, width), BF16)] * 2,
        name="input_backward",
    )

    by_cross.carry = [small_other]
    if along:
        more = (functools.partial(memory_send_kernel, 0, 0, "row"), [given[0], data_swap(given[1], 0)], sent)
    given = advance("cross_2", by_cross, more=more)
    by_self.ride, by_self.ride_at = [small_own, by_cross.gots[0]], by_cross.size
    if along:
        memory_state = [given[0], other(given[1])]
    advance("ffn_3", by_ffn)
    advance("self_cross_2", by_self, by_cross)
    got_both = other(later(both, by_cross.keeps[0]))
    advance("all_3", by_self, by_ffn, by_cross)
    if not along:
        mine, theirs = jnp.concatenate(mem_terms[:BACK]), jnp.concatenate(mem_terms[BACK:])
        total = (mine.astype(F32) + theirs.astype(F32)).astype(BF16)
        total = total.reshape(dp, mem_len // dp, rows, team, share)
        blocks = lax.dynamic_index_in_dim(total, seat, 3, keepdims=False).swapaxes(1, 2)
        blocks = blocks.reshape(dp * rows, mem_len // dp, share)
        same_seat = [[d * mp + m for d in range(dp) for m in range(mp) if m % team == s] for s in range(team)]
        grad_memory = lax.all_to_all(
            blocks, ("dp", "mp"), split_axis=0, concat_axis=0, tiled=True, axis_index_groups=same_seat
        ).astype(F32)
    advance("self_cross_4", by_self, by_cross)

    more = (functools.partial(memory_send_kernel, "row", 0, 2), memory_state, sent) if along else None
    while more or not (by_self.ready() and by_cross.ready() and by_ffn.ready()):
        given = advance("rest", by_self, more=more)
        if more:
            memory_state, more = [given[0], data_swap(given[1], 2)], None
        advance("rest_cross", by_ffn, by_cross)
    (mixed, grad_inputs), (grad_ffn_in, grad_ffn_out) = run.batch(
        [
            (
                place_rows_kernel,
                [both, got_both],
                [far(((rows, seq, width), BF16)), far(((rows, seq, width), F32))],
            ),
            (
                functools.partial(ffn_grads_kernel, by_ffn.halved[0]),
                [by_ffn.chunk, by_ffn.got],
                [far(((width, unit), F32)), far(((unit, width), F32))],
            ),
        ],
        name="rows_and_ffn_grads",
    )
    grad_cross_q, grad_cross_kv, grad_cross_out = run(
        functools.partial(cross_grads_kernel, by_cross.halved[0]),
        [by_cross.chunk, by_cross.got],
        [far(((width, head), F32)), far(((2, width, head), F32)), far(((head, width), F32))],
        name="cross_grads",
    )
    parts = []
    if along:
        end = functools.partial(memory_end_kernel, 2, 0)
        parts = [(end, memory_state, [far(((16, mem_len // dp, share), F32))])]
    if fits:
        outs = [((2, head), F32), ((2, head), F32), ((1, unit), F32)]
    else:
        outs = [((lines, width), F32)]
    outs = [((3, width, head), F32), ((head, width), F32)] + [((3, width), F32)] * 3 + outs
    parts.append(
        (
            functools.partial(self_grads_kernel, by_self.halved[0]),
            [by_self.chunk, by_self.got],
            [far(v) for v in outs],
        )
    )
    *got, (grad_self_qkv, grad_self_out, grad_gain, grad_shift, grad_out_bias, *rest) = run.batch(parts, name="last_grads")
    if along:
        grad_memory = got[0][0]
    if fits:
        grad_self_bias, grad_cross_bias, grad_ffn_bias = rest[0], rest[1], rest[2].reshape(-1)
    else:
        own_small = rest[0].reshape(-1)
        grad_self_bias = own_small[: 2 * head].reshape(2, head)
        grad_cross_bias = own_small[2 * head : 4 * head].reshape(2, head)
        grad_ffn_bias = own_small[4 * head :]
    return (
        mixed,
        grad_inputs,
        grad_memory,
        grad_gain,
        grad_shift,
        grad_self_qkv,
        grad_self_bias,
        grad_self_out,
        grad_cross_q,
        grad_cross_kv,
        grad_cross_bias,
        grad_cross_out,
        grad_ffn_in,
        grad_ffn_bias,
        grad_ffn_out,
        grad_out_bias,
    )


def solution(mesh):
    placed = (
        P("dp", None, None),
        P(None, "dp", None),
        P("dp", None),
        P("dp", None),
        P(),
        P(),
        P(),
        P(),
        P(None, None, "mp"),
        P(None, "mp"),
        P("mp", None),
        P(None, "mp"),
        P(None, None, "mp"),
        P(None, "mp"),
        P("mp", None),
        P(None, "mp"),
        P("mp"),
        P("mp", None),
        P(),
        P("dp", None, None),
    )
    return jax.shard_map(
        shards,
        mesh=mesh,
        in_specs=placed,
        out_specs=(
            P("dp", None, None),
            P("dp", None, None),
            P(None, "dp", "mp"),
            P(),
            P(),
            P(None, None, "mp"),
            P(None, "mp"),
            P("mp", None),
            P(None, "mp"),
            P(None, None, "mp"),
            P(None, "mp"),
            P("mp", None),
            P(None, "mp"),
            P("mp"),
            P("mp", None),
            P(),
        ),
        check_vma=False,
    )
```

```python
import functools

import jax
import jax.numpy as jnp
from jax import lax
from jax.experimental import pallas as pl
from jax.experimental.pallas import tpu as pltpu
from jax.sharding import PartitionSpec as P

HDIM = 64
LANES = 128
BLOCK = 128
SMALL = 16
FRONT = 2
BACK = 2
EPSILON = 1e-05
F32 = jnp.float32
BF16 = jnp.bfloat16


def dot(left, right):
    return lax.dot_general(left, right, (((1,), (0,)), ((), ())), preferred_element_type=F32)


def dot_right(left, right):
    return lax.dot_general(left, right, (((1,), (1,)), ((), ())), preferred_element_type=F32)


def dot_left(left, right):
    return lax.dot_general(left, right, (((0,), (0,)), ((), ())), preferred_element_type=F32)


class Far:
    def __init__(self, value, pick=False):
        self.value, self.pick = value, pick


class Raw:
    def __init__(self, value):
        self.value = value


class Scalars:
    def __init__(self, value):
        self.value = value


class Flow:
    def __init__(self):
        self.loads, self.stores, self.sent = {}, {}, []

    def need(self, *refs):
        for ref in refs:
            copy = self.loads.pop(id(ref), None)
            if copy is not None:
                copy.wait()

    def send(self, *refs):
        for ref in refs:
            copy = self.stores.pop(id(ref), None)
            if copy is not None:
                copy.start()
                self.sent.append(copy)


class Steps:
    def __init__(self, where):
        self.where, self.token = where, None

    def batch(self, parts, name=None, cost=0.1):
        def kernel(flow, where, *refs):
            at, to = 0, sum(len(ins) for _, ins, _ in parts)
            for part, ins, outs in parts:
                part(flow, where, *refs[at : at + len(ins)], *refs[to : to + len(outs)])
                at, to = at + len(ins), to + len(outs)

        got = self(
            kernel, [v for _, ins, _ in parts for v in ins], [v for _, _, outs in parts for v in outs], name=name, cost=cost
        )
        results = []
        for _, _, outs in parts:
            results.append(got[: len(outs)])
            got = got[len(outs) :]
        return results

    def __call__(self, kernel, ins, outs, scratch=(), name=None, cost=0.1, hold=()):
        near = pl.BlockSpec(memory_space=pltpu.VMEM)
        far = pl.BlockSpec(memory_space=pltpu.HBM)
        words = pl.BlockSpec(memory_space=pltpu.SMEM)
        values, specs, stages = [], [], []
        for v in ins:
            if isinstance(v, Scalars):
                values.append(v.value)
                specs.append(words)
            elif isinstance(v, Raw):
                values.append(pltpu.with_memory_space_constraint(v.value, pltpu.HBM))
                specs.append(far)
            elif isinstance(v, Far):
                values.append(pltpu.with_memory_space_constraint(v.value, pltpu.HBM))
                specs.append(far)
                stages.append(pltpu.VMEM(v.value.shape[1:] if v.pick else v.value.shape, v.value.dtype))
            else:
                values.append(pltpu.with_memory_space_constraint(v, pltpu.VMEM))
                specs.append(near)
        after = [pltpu.with_memory_space_constraint(v, pltpu.VMEM) for v in hold]
        after_specs = [near] * len(after)
        if self.token is not None:
            after.append(pltpu.with_memory_space_constraint(self.token, pltpu.HBM))
            after_specs.append(far)
        for v in outs:
            if isinstance(v, Far):
                stages.append(pltpu.VMEM(*v.value))
        shapes = [pltpu.HBM(*v.value) if isinstance(v, (Far, Raw)) else pltpu.VMEM(*v) for v in outs]
        count, n_in, n_out, n_after = len(stages), len(ins), len(outs), len(after)

        def body(where_ref, *refs):
            refs = list(refs)
            in_refs, refs = refs[:n_in], refs[n_in + n_after :]
            out_refs, refs = refs[:n_out], refs[n_out + 1 :]
            stage_refs, refs = refs[:count], refs[count:]
            flow = Flow()
            if count:
                sems, refs = refs[0], refs[1:]
            given, k = [], 0
            for v, ref in zip(ins, in_refs):
                if isinstance(v, Far):
                    source = ref.at[where_ref[0]] if v.pick else ref
                    copy = pltpu.make_async_copy(source, stage_refs[k], sems.at[k])
                    copy.start()
                    flow.loads[id(stage_refs[k])] = copy
                    ref, k = stage_refs[k], k + 1
                given.append(ref)
            for v, ref in zip(outs, out_refs):
                if isinstance(v, Far):
                    flow.stores[id(stage_refs[k])] = pltpu.make_async_copy(stage_refs[k], ref, sems.at[k])
                    ref, k = stage_refs[k], k + 1
                given.append(ref)
            kernel(flow, where_ref, *given, *refs)
            for copy in flow.loads.values():
                copy.wait()
            for copy in flow.stores.values():
                copy.start()
            for copy in [*flow.sent, *flow.stores.values()]:
                copy.wait()

        results = pl.pallas_call(
            body,
            in_specs=[words] + specs + after_specs,
            out_specs=[far if isinstance(v, (Far, Raw)) else near for v in outs] + [far],
            out_shape=shapes + [pltpu.HBM((8, LANES), F32)],
            scratch_shapes=stages + ([pltpu.SemaphoreType.DMA((count,))] if count else []) + list(scratch),
            compiler_params=pltpu.CompilerParams(vmem_limit_bytes=24 * 1024 * 1024),
            cost_estimate=pl.CostEstimate(flops=10**6, bytes_accessed=int(cost * 3 * 10**6), transcendentals=0),
            name=name,
        )(self.where, *values, *after)
        self.token = results[-1]
        return list(results[:-1])


def row_blocks(seq):
    return [slice(start, start + BLOCK) for start in range(0, seq, BLOCK)]


def row_of(ref, i):
    return ref[i : i + 1, :].astype(F32)


GAIN, SHIFT, OUT, SCALE, VECTORS = 0, 3, 6, 9, 16


def norm_parts(value):
    centre = value - jnp.mean(value, axis=-1, keepdims=True)
    spread = jnp.mean(centre * centre, axis=-1, keepdims=True)
    scale = lax.rsqrt(spread + EPSILON)
    return centre * scale, scale


def norm_backward(value, gain, incoming):
    xhat, scale = norm_parts(value)
    weighted = incoming * gain
    grad = scale * (
        weighted
        - jnp.mean(weighted, axis=-1, keepdims=True)
        - xhat * jnp.mean(weighted * xhat, axis=-1, keepdims=True)
    )
    return grad, jnp.sum(incoming * xhat, axis=0, keepdims=True), jnp.sum(incoming, axis=0, keepdims=True)


def head_lanes(value, j):
    lane = lax.broadcasted_iota(jnp.int32, value.shape, 1)
    return jnp.where((lane >= HDIM) == bool(j), value, jnp.zeros_like(value))


def span_of(block, seq, banded):
    if not banded:
        return slice(0, seq)
    return slice(max(block.start - BLOCK, 0), block.stop)


def start_all(moves, sems):
    copies = [pltpu.make_async_copy(a, b, sems.at[i]) for i, (a, b) in enumerate(moves)]
    for copy in copies:
        copy.start()
    return copies


def setup_kernel(packing, flow, where, *refs):
    group_tokens, bucket_group, lengths, inputs, cotangent, memory, segments, gains, shifts, biases, refs = *refs[:10], refs[10:]
    if packing:
        query, kv, out, w_in, w_out, cross, ffn, own_kv, refs = *refs[:8], refs[8:]
    x, cot, memory_part, vectors, molecules, tokens_now, group_now, lengths_now, word_sems, sems = refs
    words = start_all([(group_tokens, tokens_now), (bucket_group, group_now), (lengths, lengths_now)], word_sems)
    moves = [(memory.at[:, where[0]], memory_part), (inputs.at[where[0]], x), (cotangent.at[where[0]], cot)]
    if packing:
        full, wide = query.shape
        half = full // 2
        rows = pl.ds(pl.multiple_of(where[3] * half, half), half)
        moves += [
            (query.at[rows, :], cross.at[0:half, :]),
            (kv.at[0, rows, :], cross.at[half : 2 * half, :]),
            (kv.at[1, rows, :], cross.at[2 * half : 3 * half, :]),
        ]
        count, size = out.shape[1] // wide // 2, out.shape[0]
        for k in range(count):
            lanes = pl.ds(pl.multiple_of((where[3] * count + k) * wide, wide), wide)
            moves.append((out.at[:, lanes], cross.at[3 * half + k * size : 3 * half + (k + 1) * size, :]))
        moves += [(w_in, ffn.at[0]), (w_out, ffn.at[1]), (kv, own_kv)]
    copies = start_all(moves, sems)
    for copy in words:
        copy.wait()
    width = vectors.shape[1]
    total, own = 0, 0
    for b in range(bucket_group.shape[0]):
        tokens = tokens_now[group_now[b]]
        total = total + tokens
        own = own + jnp.where(where[2] == b, tokens, 0)
    scaled = jnp.full((1, width), bucket_group.shape[0] * own, jnp.int32).astype(F32)
    scale = scaled / jnp.full((1, width), total, jnp.int32).astype(F32)
    size = molecules.shape[1]
    place = lax.broadcasted_iota(jnp.int32, (1, size), 1)
    count, end = jnp.zeros((1, size), jnp.int32), 0
    for k in range(lengths.shape[1]):
        end = end + lengths_now[where[0], k]
        count = count + (end <= place).astype(jnp.int32)
    molecules[1:2, :] = count
    flow.need(segments, gains, shifts, biases)
    molecules[0:1, :] = segments[pl.ds(where[0], 1), :]
    rows = [r[...].astype(F32) for r in (gains, shifts, biases)] + [scale]
    vectors[...] = jnp.concatenate(rows + [jnp.zeros((VECTORS - 10, width), F32)], axis=0)
    for copy in copies:
        copy.wait()


def key_columns(keys):
    size = keys.shape[1]
    tiles = [jnp.broadcast_to(keys[:, at : at + BLOCK], (LANES, BLOCK)).T for at in range(0, size, BLOCK)]
    return jnp.concatenate(tiles, axis=0)


def allowed_of(own, columns, block, span, banded):
    allowed = columns[span] == own[:, block]
    if banded:
        query = lax.broadcasted_iota(jnp.int32, allowed.shape, 1) + block.start
        key = lax.broadcasted_iota(jnp.int32, allowed.shape, 0) + span.start
        allowed = allowed & (key <= query)
    return allowed


def both_heads(value):
    return jnp.concatenate([head_lanes(value, 0), head_lanes(value, 1)], axis=0)


def own_rows(value):
    half = value.shape[1] // 2
    row = lax.broadcasted_iota(jnp.int32, (value.shape[0], half), 0)
    return jnp.where(row < HDIM, value[:, :half], value[:, half:])


def pair_columns(at):
    return slice(2 * at * BLOCK, 2 * (at + 1) * BLOCK)


def attend_forward(q, k, v, own, keys, heads, totals, raised_all, shares, banded):
    seq, wide = q.shape
    columns = key_columns(keys)
    blocks = row_blocks(seq)
    for pair in range(wide // LANES):
        lanes = slice(pair * LANES, (pair + 1) * LANES)
        for at, block in enumerate(blocks):
            span = span_of(block, k.shape[0], banded)
            allowed = allowed_of(own, columns, block, span, banded)
            allowed = jnp.concatenate([allowed, allowed], axis=1)
            scores = dot_right(k[span, lanes], both_heads(q[block, lanes] * 0.125))
            scores = jnp.where(allowed, scores, -1e30)
            maxima = jnp.max(scores, axis=0, keepdims=True)
            raised = jnp.exp(scores - maxima)
            total = jnp.sum(raised, axis=0, keepdims=True)
            raised_all[span, pair_columns(at)] = raised.astype(BF16)
            shares[:, pair_columns(at)] = 1.0 / total
            logs = maxima + jnp.log(total)
            for j in (0, 1):
                totals[2 * pair + j : 2 * pair + j + 1, block] = logs[:, j * BLOCK : (j + 1) * BLOCK]
        turned = v[:, lanes].T
        if not banded:
            mixed = dot(turned, raised_all[...]) * shares[...]
        for at, block in enumerate(blocks):
            if banded:
                span = span_of(block, k.shape[0], banded)
                part = dot(turned[:, span], raised_all[span, pair_columns(at)]) * shares[:, pair_columns(at)]
            else:
                part = mixed[:, pair_columns(at)]
            heads[block, lanes] = own_rows(part).T.astype(BF16)


def attend_backward(q, k, v, own, keys, totals, grad_heads, dq, dk, dv, work, banded):
    seq, wide = q.shape
    columns = key_columns(keys)
    blocks = row_blocks(seq)
    scores_all, query_all = work[:2]
    for pair in range(wide // LANES):
        lanes = slice(pair * LANES, (pair + 1) * LANES)
        for at, block in enumerate(blocks):
            span = span_of(block, k.shape[0], banded)
            allowed = allowed_of(own, columns, block, span, banded)
            allowed = jnp.concatenate([allowed, allowed], axis=1)
            query, grad = both_heads(q[block, lanes] * 0.125), both_heads(grad_heads[block, lanes])
            query_all[pair_columns(at), :] = query
            logs = jnp.concatenate([totals[2 * pair + j : 2 * pair + j + 1, block] for j in (0, 1)], axis=1)
            scores = jnp.where(allowed, dot_right(k[span, lanes], query), -1e30)
            chances = jnp.exp(scores - logs)
            if banded:
                work[2][span, pair_columns(at)] = chances.astype(BF16)
                work[3][pair_columns(at), :] = grad
            else:
                grad_value = dot(chances.astype(BF16), grad)
                work[2][...] = grad_value if at == 0 else work[2][...] + grad_value
            weighted = chances * dot_right(v[span, lanes], grad)
            mean = jnp.sum(weighted, axis=0, keepdims=True)
            scores_all[span, pair_columns(at)] = (weighted - chances * mean).astype(BF16)
        turned = k[:, lanes].T
        if not banded:
            grad_query = dot(turned, scores_all[...])
            dk[:, lanes] = dot(scores_all[...], query_all[...]).astype(BF16)
            dv[:, lanes] = work[2][...].astype(BF16)
        for at, block in enumerate(blocks):
            if banded:
                span = span_of(block, k.shape[0], banded)
                part = dot(turned[:, span], scores_all[span, pair_columns(at)])
                met = slice(pair_columns(at).start, pair_columns(min(at + 1, len(blocks) - 1)).stop)
                dk[block, lanes] = dot(scores_all[block, met], query_all[met, :]).astype(BF16)
                dv[block, lanes] = dot(work[2][block, met], work[3][met, :]).astype(BF16)
            else:
                part = grad_query[:, pair_columns(at)]
            dq[block, lanes] = (own_rows(part).T * 0.125).astype(BF16)


def team_total(mine, theirs, block):
    half = mine[0].shape[0]
    k, rows = block.start // half, slice(block.start % half, block.start % half + BLOCK)
    return mine[k][rows, :].astype(F32) + theirs[k][rows, :].astype(F32)


def put_half(parts, block, value):
    half = parts[0].shape[0]
    start = block.start % half
    parts[block.start // half][start : start + BLOCK, :] = value.astype(parts[0].dtype)


def self_forward_kernel(n, i, flow, where, *refs):
    last = i == n - 1
    first, vectors, molecules, w, bias, refs = *refs[:5], refs[5:]
    if last:
        w_out, done, refs = refs[:n], refs[n : 2 * n - 1], refs[2 * n - 1 :]
    if i == 0:
        normed, refs = refs[0], refs[1:]
        for block in row_blocks(first.shape[0]):
            norm = norm_parts(first[block, :].astype(F32))[0]
            normed[block, :] = (norm * row_of(vectors, GAIN) + row_of(vectors, SHIFT)).astype(BF16)
    else:
        normed = first
    q, k, v, heads, totals = refs[:5]
    flow.need(w)
    q[...] = (dot(normed[...], w[0]) + row_of(bias, 0)).astype(BF16)
    k[...] = dot(normed[...], w[1]).astype(BF16)
    v[...] = (dot(normed[...], w[2]) + row_of(bias, 1)).astype(BF16)
    own = molecules[0:1, :]
    flow.send(q, k, v)
    attend_forward(q, k, v, own, own, heads, totals, *refs[-2:], True)
    flow.send(totals)
    if last:
        project_out(flow, [*done, heads], w_out, refs[5 : 5 + FRONT])


def project_out(flow, heads, w_out, parts):
    flow.need(*w_out)
    for block in row_blocks(heads[0].shape[0]):
        put_half(parts, block, sum(dot(h[block, :], w[...]) for h, w in zip(heads, w_out)))


def memory_kernel(flow, where, memory, w, bias, k, v):
    flow.need(w)
    k[...] = dot(memory[...], w[0]).astype(BF16)
    v[...] = (dot(memory[...], w[1]) + row_of(bias, 3)).astype(BF16)


def unpack_memory_kernel(flow, where, near, got, memory, bias, query, kv, out, k, v):
    full, wide = query.shape
    half, size = full // 2, out.shape[0]
    count = out.shape[1] // wide // 2
    for packed, bit in ((near, where[3]), (got, 1 - where[3])):
        rows = pl.ds(pl.multiple_of(bit * half, half), half)
        query[rows, :] = packed[:half]
        for i in (0, 1):
            kv[i, rows, :] = packed[(i + 1) * half : (i + 2) * half]
        for i in range(count):
            lanes = pl.ds(pl.multiple_of((bit * count + i) * wide, wide), wide)
            out[:, lanes] = packed[3 * half + i * size : 3 * half + (i + 1) * size]
    memory_kernel(flow, where, memory, kv, bias, k, v)


def cross_forward_kernel(n, i, flow, where, *refs):
    last = i == n - 1
    if i == 0:
        x, mine, theirs, refs = refs[0], refs[1 : 1 + FRONT], refs[1 + FRONT : 1 + 2 * FRONT], refs[1 + 2 * FRONT :]
    else:
        normed, refs = refs[0], refs[1:]
    vectors, molecules, w, bias, k, v, refs = *refs[:6], refs[6:]
    if last:
        w_out, done, refs = refs[:n], refs[n : 2 * n - 1], refs[2 * n - 1 :]
    if i == 0:
        after_self, normed, refs = refs[0], refs[1], refs[2:]
    q, heads, totals = refs[:3]
    if i == 0:
        for block in row_blocks(x.shape[0]):
            value = x[block, :].astype(F32) + team_total(mine, theirs, block) + row_of(vectors, OUT)
            after_self[block, :] = value
            norm = norm_parts(value)[0]
            normed[block, :] = (norm * row_of(vectors, GAIN + 1) + row_of(vectors, SHIFT + 1)).astype(BF16)
    flow.need(w)
    q[...] = (dot(normed[...], w[...]) + row_of(bias, 2)).astype(BF16)
    attend_forward(q, k, v, molecules[0:1, :], molecules[1:2, :], heads, totals, *refs[-2:], False)
    if last:
        project_out(flow, [*done, heads], w_out, refs[3 : 3 + FRONT])


def ffn_kernel(i, flow, where, *refs):
    if i == 0:
        after_self, mine, theirs, refs = refs[0], refs[1 : 1 + FRONT], refs[1 + FRONT : 1 + 2 * FRONT], refs[1 + 2 * FRONT :]
        cotangent, vectors, w_in, bias, w_out, refs = *refs[:5], refs[5:]
        after_cross, normed, low, active, grad_hidden, part, part_grad = refs
    else:
        normed, low, begun, begun_grad, w_in, bias, refs = *refs[:6], refs[6:]
        if len(w_in.shape) == 3:
            w_in, w_out = w_in.at[0], w_in.at[1]
        else:
            w_out, refs = refs[0], refs[1:]
        active, grad_hidden, parts, parts_grad = refs[0], refs[1], refs[2 : 2 + BACK], refs[2 + BACK :]
    if bias.shape[0] == 1:
        row = row_of(bias, 0)
    else:
        row = jnp.concatenate([row_of(bias, k) for k in range(4, bias.shape[0])], axis=1)
    if i == 0:
        for block in row_blocks(normed.shape[0]):
            value = after_self[block, :] + team_total(mine, theirs, block) + row_of(vectors, OUT + 1)
            after_cross[block, :] = value
            norm = norm_parts(value)[0]
            normed[block, :] = (norm * row_of(vectors, GAIN + 2) + row_of(vectors, SHIFT + 2)).astype(BF16)
            low[block, :] = (cotangent[block, :].astype(F32) * row_of(vectors, SCALE)).astype(BF16)
    flow.need(w_in, w_out)
    for block in row_blocks(normed.shape[0]):
        hidden = dot(normed[block, :], w_in[...]) + row
        cdf = 0.5 * (1.0 + lax.erf(hidden * 0.7071067811865476))
        act = (hidden * cdf).astype(BF16)
        active[block, :] = act
        slope = cdf + hidden * (0.3989422804014327 * jnp.exp(-0.5 * hidden * hidden))
        back = (slope * dot_right(low[block, :], w_out[...])).astype(BF16)
        grad_hidden[block, :] = back
        out, out_grad = dot(act, w_out[...]), dot_right(back, w_in[...])
        if i == 0:
            part[block, :], part_grad[block, :] = out, out_grad
        else:
            put_half(parts, block, begun[block, :] + out)
            put_half(parts_grad, block, begun_grad[block, :] + out_grad)


def ffn_weights_kernel(flow, where, *refs):
    hidden, active, normed, low, sums = refs[:2], refs[2:4], refs[4], refs[5], refs[6]
    keep_out, send_out, keep_in, send_in = refs[7:]
    half = keep_in.shape[1]
    for i in (0, 1):
        for target, bit in ((keep_in, where[3]), (send_in, 1 - where[3])):
            lanes = pl.ds(pl.multiple_of(bit * half, half), half)
            target[i] = dot_left(hidden[i][:, lanes], normed[...]).astype(target.dtype)
        sums[i : i + 1, :] = jnp.sum(hidden[i][...].astype(F32), axis=0, keepdims=True)
    keep_out[0] = dot_left(active[0][...], low[...])
    send_out[0] = dot_left(active[1][...], low[...]).astype(BF16)


def spread_grad_heads(low, w_out, grad_heads):
    for piece, target in zip(w_out, grad_heads):
        target[...] = dot_right(low[...], piece[...]).astype(BF16)


def column_sums(sums, values):
    for i, value in enumerate(values):
        sums[i : i + 1, :] = jnp.sum(value[...].astype(F32), axis=0, keepdims=True)


def cross_backward_kernel(n, flow, where, *refs):
    after_cross, mine, theirs, refs = refs[0], refs[1 : 1 + BACK], refs[1 + BACK : 1 + 2 * BACK], refs[1 + 2 * BACK :]
    cotangent, vectors, molecules, refs = *refs[:3], refs[3:]
    (q, k, v, totals, w_out, w), refs = [refs[i * n : (i + 1) * n] for i in range(6)], refs[6 * n :]
    grad_cross, low, refs = refs[0], refs[1], refs[2:]
    (dq, dk, dv, bias_sums), refs = [refs[i * n : (i + 1) * n] for i in range(4)], refs[4 * n :]
    parts_out, sums, refs = refs[:BACK], refs[BACK], refs[BACK + 1 :]
    grad_heads, work = refs[:n], refs[n:]
    seq, width = after_cross.shape
    rows = [jnp.zeros((1, width), F32)] * 3
    for block in row_blocks(seq):
        incoming = team_total(mine, theirs, block)
        grad_result = cotangent[block, :].astype(F32) * row_of(vectors, SCALE)
        back, by_gain, by_shift = norm_backward(after_cross[block, :], row_of(vectors, GAIN + 2), incoming)
        value = grad_result + back
        grad_cross[block, :] = value
        low[block, :] = value.astype(BF16)
        parts = (by_gain, by_shift, jnp.sum(grad_result, axis=0, keepdims=True))
        rows = [a + b for a, b in zip(rows, parts)]
    for i, row in enumerate(rows):
        sums[i : i + 1, :] = row
    flow.need(*w_out)
    spread_grad_heads(low, w_out, grad_heads)
    own, keys = molecules[0:1, :], molecules[1:2, :]
    for i in range(n):
        attend_backward(
            q[i], k[i], v[i], own, keys, totals[i], grad_heads[i], dq[i], dk[i], dv[i], work, False
        )
        column_sums(bias_sums[i], (dq[i], dv[i]))
    flow.need(*w)
    for block in row_blocks(seq):
        put_half(parts_out, block, sum(dot_right(d[block, :], m[...]) for d, m in zip(dq, w)))


def shard_grads(kinds):
    grads = ([], [])
    for kind in kinds:
        if len(kind) == 2:
            for i in (0, 1):
                grads[i].append(dot_left(kind[i][0][...], kind[i][1][...]))
        else:
            left, right = kind[0]
            both, half = dot_left(left[...], right[...]), left.shape[1] // 2
            grads[0].append(both[:half])
            grads[1].append(both[half:])
    return grads


def cross_weights_kernel(n, flow, where, *refs):
    (dq, dk, dv, heads, w), refs = [refs[i * n : (i + 1) * n] for i in range(5)], refs[5 * n :]
    normed, memory, low, after_cross, refs = *refs[:4], refs[4:]
    mine, theirs, vectors, refs = refs[:BACK], refs[BACK : 2 * BACK], refs[2 * BACK], refs[2 * BACK + 1 :]
    keep, send, terms, result = refs[0], refs[1], refs[2 : 2 + BACK], refs[-1]
    flow.need(*w)
    pairs = [[(a, b) for a in left] for left, b in ((dq, normed), (dk, memory), (dv, memory), (heads, low))]
    first = where[3] == 0
    for i, grads in enumerate(shard_grads(pairs)):
        upper, lower = jnp.concatenate(grads[:2], axis=0), jnp.concatenate(grads[2:], axis=0)
        keep[i] = jnp.where(first, upper, lower)
        send[i] = jnp.where(first, lower, upper).astype(BF16)
    for block in row_blocks(memory.shape[0]):
        total = sum(
            dot_right(a[block, :], m[0]) + dot_right(b[block, :], m[1]) for a, b, m in zip(dk, dv, w)
        )
        put_half(terms, block, total)
    for block in row_blocks(after_cross.shape[0]):
        both = team_total(mine, theirs, block)
        result[block, :] = (after_cross[block, :] + both + row_of(vectors, OUT + 2)).astype(BF16)


def put_grads(target, grads):
    size = grads[0].shape[0]
    for k, grad in enumerate(grads):
        target[0, k * size : (k + 1) * size, :] = grad.astype(target.dtype)


def self_backward_kernel(n, flow, where, *refs):
    after_self, mine, theirs, refs = refs[0], refs[1 : 1 + BACK], refs[1 + BACK : 1 + 2 * BACK], refs[1 + 2 * BACK :]
    grad_cross, vectors, molecules, q, k, v, totals, refs = *refs[:7], refs[7:]
    w_out, refs = refs[:n], refs[n:]
    normed, heads, grad_self, low, dq, dk, dv, bias_sums, sums, refs = *refs[:9], refs[9:]
    first, send, grad_heads, work = *refs[:3], refs[3:]
    seq, width = after_self.shape
    rows = [jnp.zeros((1, width), F32)] * 3
    for block in row_blocks(seq):
        incoming = team_total(mine, theirs, block)
        back, by_gain, by_shift = norm_backward(after_self[block, :], row_of(vectors, GAIN + 1), incoming)
        upper = grad_cross[block, :]
        value = upper + back
        grad_self[block, :] = value
        low[block, :] = value.astype(BF16)
        parts = (by_gain, by_shift, jnp.sum(upper, axis=0, keepdims=True))
        rows = [a + b for a, b in zip(rows, parts)]
    for i, row in enumerate(rows):
        sums[i : i + 1, :] = row
    flow.need(*w_out)
    spread_grad_heads(low, w_out, [first, grad_heads] if n == 2 else [grad_heads])
    own = molecules[0:1, :]
    flow.need(q, k, v, totals)
    attend_backward(q, k, v, own, own, totals, grad_heads, dq, dk, dv, work, True)
    column_sums(bias_sums, (dq, dv))
    grads = [dot_left(a[...], b[...]) for a, b in ((dq, normed), (dk, normed), (dv, normed), (heads, low))]
    if n == 2:
        put_grads(send, grads)
    else:
        half = grads[0].shape[0] // 2
        put_grads(first, [g[:half] for g in grads])
        put_grads(send, [g[half:] for g in grads])


def self_backward_rest_kernel(n, flow, where, *refs):
    w, grads_last, refs = refs[:n], refs[n : n + 3], refs[n + 3 :]
    pieces = [grads_last]
    if n == 2:
        molecules, q, k, v, totals, grad_heads, normed, heads, low, refs = *refs[:9], refs[9:]
        bias_sums, keep, parts_out, refs = refs[0], refs[1], refs[2 : 2 + BACK], refs[2 + BACK :]
        dq, dk, dv, work = *refs[:3], refs[3:]
        own = molecules[0:1, :]
        flow.need(q, k, v, totals)
        attend_backward(q, k, v, own, own, totals, grad_heads, dq, dk, dv, work, True)
        column_sums(bias_sums, (dq, dv))
        put_grads(keep, [dot_left(a[...], b[...]) for a, b in ((dq, normed), (dk, normed), (dv, normed), (heads, low))])
        pieces = [(dq, dk, dv), grads_last]
    else:
        parts_out = refs[:BACK]
    flow.need(*w)
    for block in row_blocks(grads_last[0].shape[0]):
        total = 0.0
        for matrices, grads in zip(w, pieces):
            for which, d in enumerate(grads):
                total += dot_right(d[block, :], matrices[which])
        put_half(parts_out, block, total)


def input_backward_kernel(n, flow, where, x, *refs):
    mine, theirs, refs = refs[:BACK], refs[BACK : 2 * BACK], refs[2 * BACK :]
    grad_self, vectors, result, by_cross, by_ffn, refs = *refs[:5], refs[5:]
    shard_rows, (both, small_own, small_other) = refs[:-3], refs[-3:]
    seq = x.shape[0]
    both[:seq, :] = result[...]
    width = x.shape[1]
    rows = [jnp.zeros((1, width), F32)] * 3
    for block in row_blocks(x.shape[0]):
        incoming = team_total(mine, theirs, block)
        back, by_gain, by_shift = norm_backward(x[block, :].astype(F32), row_of(vectors, GAIN), incoming)
        upper = grad_self[block, :]
        both[seq + block.start : seq + block.stop, :] = (upper + back).astype(BF16)
        parts = (by_gain, by_shift, jnp.sum(upper, axis=0, keepdims=True))
        rows = [a + b for a, b in zip(rows, parts)]
    common = [r for k in range(3) for r in (rows[k], by_cross[k : k + 1, :], by_ffn[k : k + 1, :])]
    if len(shard_rows) == 1:
        lines = [shard_rows[0][i] for i in (0, 1)]
    else:
        sums_self, sums_cross, sums_ffn = shard_rows[:n], shard_rows[n : 2 * n], shard_rows[2 * n]
        lines = []
        for i in (0, 1):
            pieces = [r[k : k + 1, :] for r in (sums_self[i], sums_cross[i]) for k in (0, 1)]
            lines.append(jnp.concatenate([jnp.concatenate(pieces, axis=1), sums_ffn[i : i + 1, :]], axis=0))
    rest = jnp.zeros((SMALL - 9 - lines[0].shape[0], width), F32)
    small = [jnp.concatenate([*common, line, rest], axis=0).astype(BF16) for line in lines]
    small_own[...] = small[0]
    small_other[...] = small[1]


def fold_kernel(count, size, ride, mode, bit, flow, where, *refs):
    keeps, gots, refs = refs[:count], refs[count : 2 * count], refs[2 * count :]
    planes = [(k, p) for k in range(count) for p in range(keeps[k].shape[0])]

    def part(at, rows):
        k, p = planes[at]
        return keeps[k][p, rows, :].astype(F32) + gots[k][p, rows, :].astype(F32)

    if mode == "half":
        keep, send = refs
        half = size // 2
        for at in range(len(planes)):
            for target, side in ((keep, where[3 + bit]), (send, 1 - where[3 + bit])):
                rows = pl.ds(pl.multiple_of(side * half, half), half)
                target[at, :half, :] = part(at, rows).astype(target.dtype)
    elif mode == "shard":
        if ride is not None:
            refs[-1][0, size : size + SMALL, :] = refs[0][...]
        for at, target in enumerate(refs[-2:]):
            target[0, :size, :] = part(at, slice(0, size)).astype(target.dtype)
    else:
        out = refs[-1]
        for at in range(len(planes)):
            out[at, :size, :] = part(at, slice(0, size)).astype(out.dtype)
        if ride is not None:
            own, came = refs[:2]
            small = own[...].astype(F32) + came[0, ride : ride + SMALL, :].astype(F32)
            out[0, size : size + SMALL, :] = small.astype(out.dtype)


def memory_pairs(axis):
    step = 1 if axis == "row" else 2 << axis
    return [(k, k | step) for k in range(16) if not k & step]


def memory_bit(where, axis):
    return where[0] if axis == "row" else where[3 + axis]


def send_blocks(where, axis, blocks, send, offset):
    low = memory_bit(where, axis) == 0
    per = 8 // send.shape[0]
    for k, (a, b) in enumerate(memory_pairs(axis)):
        at = offset + k % per * SMALL
        send[k // per, at : at + SMALL, :] = jnp.where(low, blocks[b], blocks[a])


def take_blocks(where, axis, kept, got, offset):
    low = memory_bit(where, axis) == 0
    per = 8 // got.shape[0]
    blocks = {}
    for k, (a, b) in enumerate(memory_pairs(axis)):
        at = offset + k % per * SMALL
        came = got[k // per, at : at + SMALL, :]
        blocks[a] = jnp.where(low, kept[a], came)
        blocks[b] = jnp.where(low, came, kept[b])
    return blocks


def memory_start_kernel(axis, flow, where, *refs, send, offset):
    mine, theirs, kept = refs[:BACK], refs[BACK : 2 * BACK], refs[2 * BACK]
    half, width = mine[0].shape
    tokens = half * BACK // 8
    share = LANES
    blocks = {}
    for r in (0, 1):
        lanes = pl.ds(pl.multiple_of((2 * r + where[1]) * share, share), share)
        for k in range(BACK):
            total = (mine[k][:, lanes].astype(F32) + theirs[k][:, lanes].astype(F32)).astype(BF16)
            for d in range(half // tokens):
                block = total[d * tokens : (d + 1) * tokens]
                parts = [block[q : q + SMALL] for q in range(0, tokens, SMALL)]
                at = 2 * (k * half // tokens + d) + r
                blocks[at] = jnp.concatenate(parts, axis=1)
                kept[at] = blocks[at]
    send_blocks(where, axis, blocks, send, offset)


def memory_send_kernel(before, at, axis, flow, where, old, got, kept, send):
    blocks = take_blocks(where, before, old, got, at)
    for k, block in blocks.items():
        kept[k] = block
    send_blocks(where, axis, blocks, send, 0)


def memory_end_kernel(before, at, flow, where, old, got, out):
    for k, block in take_blocks(where, before, old, got, at).items():
        parts = [block[:, q : q + LANES] for q in range(0, block.shape[1], LANES)]
        out[k] = jnp.concatenate(parts, axis=0).astype(out.dtype)


def join_kernel(ride, pad, bit, flow, where, near, got, out):
    half = near.shape[1] - (SMALL if ride else 0)
    for value, side in ((near, where[3 + bit]), (got, 1 - where[3 + bit])):
        rows = pl.ds(pl.multiple_of(side * half, half), half)
        for p in range(near.shape[0]):
            out[p, rows, :] = value[p, :half]
    if ride:
        out[0, 2 * half :, :] = (near[0, half:].astype(F32) + got[0, half:].astype(F32)).astype(BF16)
    if pad:
        out[:, 2 * half :, :] = jnp.zeros((out.shape[0], pad, out.shape[2]), out.dtype)


def joined(where, bit, near, got, p, ride=0):
    first = where[3 + bit] == 0
    size = near.shape[1] - ride
    a, b = near[p, :size], got[p, :size]
    rows = [jnp.where(first, a, b), jnp.where(first, b, a)]
    return jnp.concatenate(rows, axis=0).astype(F32)


def self_grads_kernel(bit, flow, where, near, got, qkv, out, gains, shifts, biases, *rest):
    size = near.shape[1] - SMALL
    small = near[0, size:].astype(F32) + got[0, size:].astype(F32)
    for k, target in enumerate((gains, shifts, biases)):
        target[...] = small[3 * k : 3 * k + 3]
    if len(rest) == 1:
        rest[0][...] = small[9 : 9 + rest[0].shape[0]]
    else:
        for k, target in enumerate(rest[:2]):
            wide = target.shape[1]
            for i in (0, 1):
                at = (2 * k + i) * wide
                target[i : i + 1, :] = small[9:10, at : at + wide]
        rest[2][...] = small[10:11]
    flow.send(gains, shifts, biases, *rest)
    value = joined_inside(where, bit, near, got, 0, SMALL)
    size = out.shape[0]
    for k in range(3):
        qkv[k] = value[k * size : (k + 1) * size].T
    out[...] = value[3 * size :]


def joined_inside(where, bit, near, got, p, pad=0):
    half = (near.shape[1] - pad) // 2
    first, parts = where[3 + bit] == 0, []
    for k in (0, 1):
        a, b = near[p, k * half : (k + 1) * half], got[p, k * half : (k + 1) * half]
        parts += [jnp.where(first, a, b), jnp.where(first, b, a)]
    return jnp.concatenate(parts, axis=0).astype(F32)


def cross_grads_kernel(bit, flow, where, near, got, query, kv, out):
    value = joined(where, bit, near, got, 0, 2 * SMALL)
    size = out.shape[0]
    query[...] = value[:size].T
    for k in (0, 1):
        kv[k] = value[(k + 1) * size : (k + 2) * size].T
    out[...] = value[3 * size :]


def ffn_grads_kernel(bit, flow, where, near, got, grad_in, grad_out):
    grad_out[...] = joined_inside(where, bit, near, got, 0)
    flow.send(grad_out)
    grad_in[...] = joined_inside(where, bit, near, got, 1).T


def place_rows_kernel(flow, where, own, got, mixed, grad):
    seq = own.shape[0] // 2
    for k, out in enumerate((mixed, grad)):
        for row, value in ((where[0], own), (1 - where[0], got)):
            out[row] = value[k * seq : (k + 1) * seq, :].astype(out.dtype)
        flow.send(out)


def shards(
    inputs,
    memory,
    segment_ids,
    mem_lengths,
    bucket_group,
    group_tokens,
    norm_gain,
    norm_bias,
    self_qkv,
    self_bias,
    self_out,
    cross_q,
    cross_kv,
    cross_bias,
    cross_out,
    ffn_in,
    ffn_bias,
    ffn_out,
    out_bias,
    cotangent,
):
    dp, mp = lax.axis_size("dp"), lax.axis_size("mp")
    rows, seq, width = inputs.shape
    team = mp // rows
    data, place = lax.axis_index("dp"), lax.axis_index("mp")
    row, seat = place // team, place % team
    bits = dp.bit_length() - 1
    where = jnp.stack([row, seat, data] + [(data >> k) & 1 for k in range(bits)]).astype(jnp.int32)
    run, far = Steps(where), Far

    across = [(i, (i + team) % mp) for i in range(mp)]

    def other(value):
        return lax.ppermute(value, "mp", across)

    def seat_swap(value, step):
        return lax.ppermute(value, "mp", [(i, i ^ step) for i in range(mp)])

    def data_swap(value, k):
        return lax.ppermute(value, "dp", [(i, i ^ (1 << k)) for i in range(dp)])

    def swap(value, axis):
        return other(value) if axis == "row" else data_swap(value, axis)

    def later(value, *after):
        return lax.optimization_barrier((value, *after))[0]

    def team_parts(values):
        step = 1
        while 2 * step < team:
            values = [(v.astype(F32) + seat_swap(v, step).astype(F32)).astype(BF16) for v in values]
            step *= 2
        return [*values, *(seat_swap(v, step) for v in values)]

    head, unit = self_bias.shape[1], ffn_bias.shape[0]
    mem_len = memory.shape[1] * dp
    apart = head % LANES == 0
    n = 2 if apart else 1
    wide = head if apart else 2 * head

    front = [((seq // FRONT, width), BF16)] * FRONT
    back = [((seq // BACK, width), BF16)] * BACK
    whole, full = ((seq, width), BF16), ((seq, width), F32)
    local, totals = ((seq, wide), BF16), ((2 * wide // LANES, seq), F32)
    units = ((seq, unit), BF16)

    other_qkv = other(self_qkv)
    bias_own = jnp.concatenate([self_bias, cross_bias, ffn_bias.reshape(-1, head)])
    bias_other = other(bias_own)
    other_self_out = other(self_out)
    memory_rows = memory.reshape((dp, rows) + memory.shape[1:])
    packing = apart and width % (2 * head) == 0 and ffn_in.shape == ffn_out.shape
    ins = [Raw(group_tokens), Raw(bucket_group), Raw(mem_lengths), Raw(inputs), Raw(cotangent), Raw(memory_rows)]
    ins += [far(segment_ids), far(norm_gain), far(norm_bias), far(out_bias)]
    outs = [whole, whole, ((dp,) + memory.shape[1:], BF16), ((VECTORS, width), F32), ((2, seq), jnp.int32)]
    if packing:
        ins += [Raw(v) for v in (cross_q, cross_kv, cross_out, ffn_in, ffn_out)]
        packs = [((3 * width // 2 + cross_out.size // head // 2, head), BF16), ((2,) + ffn_in.shape, BF16)]
        outs = packs + [(cross_kv.shape, BF16)] + outs
    *packed, x, cot, memory_part, vectors, molecules = run(
        functools.partial(setup_kernel, packing),
        ins,
        outs,
        scratch=[pltpu.SMEM(v.shape, jnp.int32) for v in (group_tokens, bucket_group, mem_lengths)]
        + [pltpu.SemaphoreType.DMA((3,)), pltpu.SemaphoreType.DMA((9 + width // head // 2,))],
        name="setup",
    )
    if packing:
        near_cross = other(packed[0])
        got_cross = data_swap(near_cross, 0)
    memory_row = lax.all_to_all(memory_part, "dp", split_axis=0, concat_axis=0, tiled=True).reshape(mem_len, width)
    def pieces(own, theirs, axis):
        return [far(own), theirs] if apart else [jnp.concatenate([own, theirs], axis=axis)]

    w_qkv = pieces(self_qkv, other_qkv, 2)
    w_self_out = pieces(self_out, other_self_out, 0)
    b_heads = [bias_own, bias_other] if apart else [jnp.concatenate([bias_own, bias_other], axis=1)]
    b_in = b_heads if apart else [b[4:].reshape(1, unit) for b in (bias_own, bias_other)]

    forward_work = [pltpu.VMEM((seq, 2 * seq), BF16), pltpu.VMEM((1, 2 * seq), F32)]
    cross_work = [pltpu.VMEM((mem_len, 2 * seq), BF16), pltpu.VMEM((1, 2 * seq), F32)]
    heads_self, saved_self = [], []
    for i in range(n):
        last = i == n - 1
        ins = [x if i == 0 else normed_self, vectors, molecules, w_qkv[i], b_heads[i]]
        outs = ([whole] if i == 0 else []) + [far(local)] * 3 + [local, far(totals)]
        if last:
            ins += [*w_self_out, *heads_self]
            outs += front
        got = run(functools.partial(self_forward_kernel, n, i), ins, outs, scratch=forward_work, name=f"self_forward_{i}")
        if i == 0:
            normed_self, got = got[0], got[1:]
            early = (normed_self, other_qkv, bias_other, other_self_out)
            if packing:
                other_ffn = other(later(packed[1], *early, near_cross))
            else:
                other_cross = [other(later(w, *early)) for w in (cross_q, cross_kv, cross_out)]
                other_in, other_out = [other(later(w, *other_cross)) for w in (ffn_in, ffn_out)]
        saved_self.append((got[0], got[1], got[2], got[4]))
        heads_self.append(got[3])
    terms = team_parts(got[5:])

    heads_cross, saved_cross = [], []
    if apart:
        w_cross_q, w_cross_out = [far(cross_q)], [far(cross_out)]
        w_cross_kv = [packed[2] if packing else far(cross_kv)]
    else:
        w_cross_q = pieces(cross_q, other_cross[0], 1)
        w_cross_kv = pieces(cross_kv, other_cross[1], 2)
        w_cross_out = pieces(cross_out, other_cross[2], 0)
    projected = ((mem_len, wide), BF16)
    for i in range(n):
        last = i == n - 1
        if i == 1 and packing:
            query, both, out, *kv = run(
                unpack_memory_kernel,
                [near_cross, got_cross, memory_row, b_heads[1]],
                [(v.shape, BF16) for v in (cross_q, cross_kv, cross_out)] + [projected] * 2,
                name="memory_1",
            )
            for pieces_of, w in ((w_cross_q, query), (w_cross_kv, both), (w_cross_out, out)):
                pieces_of.append(w)
        else:
            if i == 1:
                for pieces_of, w in zip((w_cross_q, w_cross_kv, w_cross_out), other_cross):
                    pieces_of.append(w)
            kv = run(memory_kernel, [memory_row, w_cross_kv[i], b_heads[i]], [projected] * 2, name=f"memory_{i}")
        first = [x, *terms] if i == 0 else [normed_cross]
        ins = first + [vectors, molecules, w_cross_q[i], b_heads[i], *kv]
        outs = ([full, whole] if i == 0 else []) + [local] * 2 + [totals]
        if last:
            ins += [*w_cross_out, *heads_cross]
            outs += front
        got = run(functools.partial(cross_forward_kernel, n, i), ins, outs, scratch=cross_work, name=f"cross_forward_{i}")
        if i == 0:
            after_self, normed_cross, got = got[0], got[1], got[2:]
        saved_cross.append((got[0], *kv, got[2]))
        heads_cross.append(got[1])
    terms = team_parts(got[3:])

    after_cross, normed_ffn, low_ffn, act_own, hid_own, begun, begun_grad = run(
        functools.partial(ffn_kernel, 0),
        [after_self, *terms, cot, vectors, far(ffn_in), b_in[0], far(ffn_out)],
        [full, whole, whole, units, units, full, full],
        name="ffn_0",
    )
    ins = [other_ffn if packing else other_in, b_in[1]] + ([] if packing else [other_out])
    act_other, hid_other, *parts = run(
        functools.partial(ffn_kernel, 1),
        [normed_ffn, low_ffn, begun, begun_grad, *ins],
        [units, units] + back + back,
        name="ffn_1",
    )
    terms = team_parts(parts[BACK:])
    out_terms = team_parts(parts[:BACK])

    class Reduction:
        def __init__(self, keeps, sends, axes, pad=0, turned=False):
            self.pad, self.turned = pad, turned
            self.keeps, self.axes, self.ride, self.carry = keeps, axes, [], []
            self.gots = [swap(s, a) for s, a in zip(sends, axes[0])]
            self.halved = [b for b in axes[0] if b != "row"][:1]
            self.size = sends[0].shape[1]
            self.chunk = None

        def plan(self, extra=None):
            if self.chunk is not None:
                bit, small = self.halved.pop(), SMALL if self.ride else 0
                planes, size, _ = self.chunk.shape
                pad = self.pad if len(self.halved) == 1 else 0
                outs = [((planes, 2 * size - small + pad, width), BF16)]
                return functools.partial(join_kernel, bool(small), pad, bit), [self.chunk, self.got], outs
            axes, keeps, size = self.axes, self.keeps, self.size
            planes = sum(k.shape[0] for k in keeps)
            bit, ride, at, rows = 0, [], None, size
            if len(axes) == 1:
                mode = "last"
            elif axes[1][0] == "row":
                mode, planes = "shard", 1
                if self.carry:
                    ride, at, rows = self.carry, size, size + SMALL
            elif len(axes) == 2:
                mode = "full"
                if self.ride:
                    ride, at, rows = self.ride, self.ride_at, size + SMALL
                    self.size += SMALL
            else:
                mode, bit, rows = "half", axes[1][0], size // 2
                self.size = rows
                self.halved.append(bit)
            more = 8 // planes * SMALL if extra else 0
            outs = [((planes, rows + more, width), BF16)]
            if mode in ("half", "shard"):
                outs = [((planes, self.size, width), F32)] + outs
            ins = [*keeps, *self.gots, *ride]
            kernel = functools.partial(fold_kernel, len(keeps), size, at, mode, bit)
            if not extra:
                return kernel, ins, outs
            second, second_ins, second_outs = extra
            self.extra_at = rows

            def both(flow, where, *refs):
                a, b = len(ins), len(ins) + len(second_ins)
                c = b + len(second_outs)
                kernel(flow, where, *refs[:a], *refs[c:])
                second(flow, where, *refs[a:c], send=refs[-1], offset=rows)

            return both, ins + second_ins, second_outs + outs

        def take(self, got):
            if self.chunk is not None or len(self.axes) == 1:
                if self.chunk is None and self.turned:
                    self.halved[:2] = self.halved[1::-1]
                self.chunk = got[0]
                self.got = swap(self.chunk, self.halved[-1])
            else:
                self.axes = self.axes[1:]
                self.keeps = [got[0]]
                self.gots = [swap(got[-1], self.axes[0][0])]

        def ready(self):
            return self.chunk is not None and len(self.halved) == 1

    def advance(name, *groups, extra=None, more=None):
        groups = [g for g in groups if not g.ready()]
        parts = [g.plan(extra if i == 0 else None) for i, g in enumerate(groups)] + ([more] if more else [])
        results = run.batch(parts, name=name) if parts else []
        given = results.pop() if more else []
        for i, (g, got) in enumerate(zip(groups, results)):
            if extra and i == 0:
                count = len(extra[2])
                given, got = got[:count], got[count:]
            g.take(got)
        return given

    ffn_sums, keep_out, send_out, keep_in, send_in = run(
        ffn_weights_kernel,
        [hid_own, hid_other, act_own, act_other, normed_ffn, low_ffn],
        [((2, unit), F32), ((1, unit, width), F32), ((1, unit, width), BF16)]
        + [((2, unit // 2, width), F32), ((2, unit // 2, width), BF16)],
        name="ffn_weights",
    )
    by_out = Reduction([keep_out], [send_out], [["row"], [0], [1]])
    by_in = Reduction([keep_in], [send_in], [[0], ["row"], [1]])

    all_scores = [pltpu.VMEM((mem_len, 2 * seq), BF16), pltpu.VMEM((2 * seq, LANES), BF16)]
    scratch = [pltpu.VMEM((seq, wide), BF16)] * n + all_scores + [pltpu.VMEM((mem_len, LANES), F32)]
    self_work = [pltpu.VMEM((seq, 2 * seq), BF16), pltpu.VMEM((2 * seq, LANES), BF16)] * 2
    bias_sum = ((2, wide), F32)

    def saved_of(saved):
        return [s[k] for k in range(4) for s in saved]

    got = run(
        functools.partial(cross_backward_kernel, n),
        [after_cross, *terms, cot, vectors, molecules]
        + saved_of(saved_cross) + [*w_cross_out, *w_cross_q],
        [full, whole] + [local] * (3 * n) + [bias_sum] * n + back + [((3, width), F32)],
        scratch=scratch,
        name="cross_backward",
    )
    grad_cross, low_cross, got = got[0], got[1], got[2:]
    cross_grads, cross_bias_sums, got = got[: 3 * n], got[3 * n : 4 * n], got[4 * n :]
    terms, small_ffn = team_parts(got[:BACK]), got[BACK]
    keep, send, *memory_terms, result = run(
        functools.partial(cross_weights_kernel, n),
        [*cross_grads, *heads_cross, *w_cross_kv]
        + [normed_cross, memory_row, low_cross, after_cross, *out_terms, vectors],
        [((2, 2 * head, width), F32), ((2, 2 * head, width), BF16)] + back + [whole],
        name="cross_weights",
    )
    by_cross = Reduction([keep], [send], [[0], [1], ["row"]] + [[k] for k in range(2, bits)], pad=2 * SMALL)
    advance("fold_ffn", by_out, by_in)

    group = ((1, 4 * head, width), F32)
    ins = [after_self, *terms, grad_cross, vectors, molecules] + [far(v) for v in saved_self[-1]]
    grad_self, low_self, *last_grads, last_sums, small_cross, first, send = run(
        functools.partial(self_backward_kernel, n),
        ins + [*w_self_out, normed_self, heads_self[-1]],
        [full, whole] + [local] * 3 + [bias_sum, ((3, width), F32), local if n == 2 else group, (group[0], BF16)],
        scratch=[pltpu.VMEM((seq, wide), BF16)] + self_work,
        name="self_backward",
    )
    by_self = Reduction([first], [send], [["row"]] + [[k] for k in range(bits)], turned=True)
    by_ffn = by_out
    by_ffn.keeps, by_ffn.gots = by_out.keeps + by_in.keeps, by_out.gots + by_in.gots
    by_ffn.turned = True
    by_ffn.axes = [[0]] + [[k] for k in range(1, bits)]
    mem_terms = team_parts(memory_terms)
    share = width // mp
    along = share == LANES and team == 2 and dp == 8 and mem_len // dp * LANES == SMALL * width
    blocks = ((16, SMALL, width), BF16)
    extra = (functools.partial(memory_start_kernel, 1), mem_terms, [blocks]) if along else None
    given = advance("ffn_1", by_ffn, extra=extra)
    ins = [*w_qkv, *last_grads]
    if n == 2:
        ins += [molecules] + [far(v) for v in saved_self[0]] + [first, normed_self, heads_self[0], low_self]
    outs = ([bias_sum, group] if n == 2 else []) + back
    got = run(
        functools.partial(self_backward_rest_kernel, n),
        ins,
        outs,
        scratch=[pltpu.VMEM((seq, wide), BF16)] * 3 + self_work if n == 2 else [],
        name="self_backward_rest",
    )
    self_bias_sums = [last_sums]
    if n == 2:
        self_bias_sums, by_self.keeps, got = [got[0], last_sums], [got[1]], got[2:]
    terms = team_parts(got)
    moved = [*given, by_ffn.gots[0]]
    moved_at = by_ffn.extra_at if along else None
    advance("ffn_2", by_ffn)
    sent, more = [blocks, ((1, 8 * SMALL, width), BF16)], None
    if along:
        more = (functools.partial(memory_send_kernel, 1, moved_at, 0), moved, sent)
    given = advance("cross_1", by_cross, more=more)
    advance("self_1", by_self)

    fits = apart and 4 * head == width and unit == width
    if fits:
        shard_rows = [*self_bias_sums, *cross_bias_sums, ffn_sums]
        lines = 2
    else:

        def by_shard(sums):
            return sums if n == 2 else [sums[0][:, :head], sums[0][:, head:]]

        shard_rows = [
            jnp.stack(
                [
                    jnp.concatenate([a.reshape(-1), b.reshape(-1), ffn_sums[i]]).reshape(-1, width)
                    for i, (a, b) in enumerate(zip(by_shard(self_bias_sums), by_shard(cross_bias_sums)))
                ]
            )
        ]
        lines = shard_rows[0].shape[1]
    both, small_own, small_other = run(
        functools.partial(input_backward_kernel, n),
        [x, *terms, grad_self, vectors, result, small_cross, small_ffn, *shard_rows],
        [((2 * seq, width), BF16)] + [((SMALL, width), BF16)] * 2,
        name="input_backward",
    )

    by_cross.carry = [small_other]
    if along:
        more = (functools.partial(memory_send_kernel, 0, 0, "row"), [given[0], data_swap(given[1], 0)], sent)
    given = advance("cross_2", by_cross, more=more)
    by_self.ride, by_self.ride_at = [small_own, by_cross.gots[0]], by_cross.size
    if along:
        memory_state = [given[0], other(given[1])]
    advance("ffn_3", by_ffn)
    advance("self_cross_2", by_self, by_cross)
    got_both = other(later(both, by_cross.keeps[0]))
    advance("all_3", by_self, by_ffn, by_cross)
    if not along:
        mine, theirs = jnp.concatenate(mem_terms[:BACK]), jnp.concatenate(mem_terms[BACK:])
        total = (mine.astype(F32) + theirs.astype(F32)).astype(BF16)
        total = total.reshape(dp, mem_len // dp, rows, team, share)
        blocks = lax.dynamic_index_in_dim(total, seat, 3, keepdims=False).swapaxes(1, 2)
        blocks = blocks.reshape(dp * rows, mem_len // dp, share)
        same_seat = [[d * mp + m for d in range(dp) for m in range(mp) if m % team == s] for s in range(team)]
        grad_memory = lax.all_to_all(
            blocks, ("dp", "mp"), split_axis=0, concat_axis=0, tiled=True, axis_index_groups=same_seat
        ).astype(F32)
    advance("self_cross_4", by_self, by_cross)

    mixed, grad_inputs = run(
        place_rows_kernel,
        [both, got_both],
        [far(((rows, seq, width), BF16)), far(((rows, seq, width), F32))],
        name="place_rows",
    )
    more = (functools.partial(memory_send_kernel, "row", 0, 2), memory_state, sent) if along else None
    while more or not (by_self.ready() and by_cross.ready() and by_ffn.ready()):
        given = advance("rest", by_self, more=more)
        if more:
            memory_state, more = [given[0], data_swap(given[1], 2)], None
        advance("rest_cross", by_ffn, by_cross)
    (grad_ffn_in, grad_ffn_out), (grad_cross_q, grad_cross_kv, grad_cross_out) = run.batch(
        [
            (
                functools.partial(ffn_grads_kernel, by_ffn.halved[0]),
                [by_ffn.chunk, by_ffn.got],
                [far(((width, unit), F32)), far(((unit, width), F32))],
            ),
            (
                functools.partial(cross_grads_kernel, by_cross.halved[0]),
                [by_cross.chunk, by_cross.got],
                [far(((width, head), F32)), far(((2, width, head), F32)), far(((head, width), F32))],
            ),
        ],
        name="ffn_and_cross_grads",
    )
    parts = []
    if along:
        end = functools.partial(memory_end_kernel, 2, 0)
        parts = [(end, memory_state, [far(((16, mem_len // dp, share), F32))])]
    if fits:
        outs = [((2, head), F32), ((2, head), F32), ((1, unit), F32)]
    else:
        outs = [((lines, width), F32)]
    outs = [((3, width, head), F32), ((head, width), F32)] + [((3, width), F32)] * 3 + outs
    parts.append(
        (
            functools.partial(self_grads_kernel, by_self.halved[0]),
            [by_self.chunk, by_self.got],
            [far(v) for v in outs],
        )
    )
    *got, (grad_self_qkv, grad_self_out, grad_gain, grad_shift, grad_out_bias, *rest) = run.batch(parts, name="last_grads")
    if along:
        grad_memory = got[0][0]
    if fits:
        grad_self_bias, grad_cross_bias, grad_ffn_bias = rest[0], rest[1], rest[2].reshape(-1)
    else:
        own_small = rest[0].reshape(-1)
        grad_self_bias = own_small[: 2 * head].reshape(2, head)
        grad_cross_bias = own_small[2 * head : 4 * head].reshape(2, head)
        grad_ffn_bias = own_small[4 * head :]
    return (
        mixed,
        grad_inputs,
        grad_memory,
        grad_gain,
        grad_shift,
        grad_self_qkv,
        grad_self_bias,
        grad_self_out,
        grad_cross_q,
        grad_cross_kv,
        grad_cross_bias,
        grad_cross_out,
        grad_ffn_in,
        grad_ffn_bias,
        grad_ffn_out,
        grad_out_bias,
    )


def solution(mesh):
    placed = (
        P("dp", None, None),
        P(None, "dp", None),
        P("dp", None),
        P("dp", None),
        P(),
        P(),
        P(),
        P(),
        P(None, None, "mp"),
        P(None, "mp"),
        P("mp", None),
        P(None, "mp"),
        P(None, None, "mp"),
        P(None, "mp"),
        P("mp", None),
        P(None, "mp"),
        P("mp"),
        P("mp", None),
        P(),
        P("dp", None, None),
    )
    return jax.shard_map(
        shards,
        mesh=mesh,
        in_specs=placed,
        out_specs=(
            P("dp", None, None),
            P("dp", None, None),
            P(None, "dp", "mp"),
            P(),
            P(),
            P(None, None, "mp"),
            P(None, "mp"),
            P("mp", None),
            P(None, "mp"),
            P(None, None, "mp"),
            P(None, "mp"),
            P("mp", None),
            P(None, "mp"),
            P("mp"),
            P("mp", None),
            P(),
        ),
        check_vma=False,
    )
```

```python
import functools

import jax
import jax.numpy as jnp
from jax import lax
from jax.experimental import pallas as pl
from jax.experimental.pallas import tpu as pltpu
from jax.sharding import PartitionSpec as P

HDIM = 64
LANES = 128
BLOCK = 128
SMALL = 16
FRONT = 2
BACK = 2
EPSILON = 1e-05
F32 = jnp.float32
BF16 = jnp.bfloat16


def dot(left, right):
    return lax.dot_general(left, right, (((1,), (0,)), ((), ())), preferred_element_type=F32)


def dot_right(left, right):
    return lax.dot_general(left, right, (((1,), (1,)), ((), ())), preferred_element_type=F32)


def dot_left(left, right):
    return lax.dot_general(left, right, (((0,), (0,)), ((), ())), preferred_element_type=F32)


class Far:
    def __init__(self, value, pick=False):
        self.value, self.pick = value, pick


class Raw:
    def __init__(self, value):
        self.value = value


class Scalars:
    def __init__(self, value):
        self.value = value


class Flow:
    def __init__(self):
        self.loads, self.stores, self.sent = {}, {}, []

    def need(self, *refs):
        for ref in refs:
            copy = self.loads.pop(id(ref), None)
            if copy is not None:
                copy.wait()

    def send(self, *refs):
        for ref in refs:
            copy = self.stores.pop(id(ref), None)
            if copy is not None:
                copy.start()
                self.sent.append(copy)


class Steps:
    def __init__(self, where):
        self.where, self.token = where, None

    def batch(self, parts, name=None, cost=0.1):
        def kernel(flow, where, *refs):
            at, to = 0, sum(len(ins) for _, ins, _ in parts)
            for part, ins, outs in parts:
                part(flow, where, *refs[at : at + len(ins)], *refs[to : to + len(outs)])
                at, to = at + len(ins), to + len(outs)

        got = self(
            kernel, [v for _, ins, _ in parts for v in ins], [v for _, _, outs in parts for v in outs], name=name, cost=cost
        )
        results = []
        for _, _, outs in parts:
            results.append(got[: len(outs)])
            got = got[len(outs) :]
        return results

    def __call__(self, kernel, ins, outs, scratch=(), name=None, cost=0.1, hold=()):
        near = pl.BlockSpec(memory_space=pltpu.VMEM)
        far = pl.BlockSpec(memory_space=pltpu.HBM)
        words = pl.BlockSpec(memory_space=pltpu.SMEM)
        values, specs, stages = [], [], []
        for v in ins:
            if isinstance(v, Scalars):
                values.append(v.value)
                specs.append(words)
            elif isinstance(v, Raw):
                values.append(pltpu.with_memory_space_constraint(v.value, pltpu.HBM))
                specs.append(far)
            elif isinstance(v, Far):
                values.append(pltpu.with_memory_space_constraint(v.value, pltpu.HBM))
                specs.append(far)
                stages.append(pltpu.VMEM(v.value.shape[1:] if v.pick else v.value.shape, v.value.dtype))
            else:
                values.append(pltpu.with_memory_space_constraint(v, pltpu.VMEM))
                specs.append(near)
        after = [pltpu.with_memory_space_constraint(v, pltpu.VMEM) for v in hold]
        after_specs = [near] * len(after)
        if self.token is not None:
            after.append(pltpu.with_memory_space_constraint(self.token, pltpu.HBM))
            after_specs.append(far)
        for v in outs:
            if isinstance(v, Far):
                stages.append(pltpu.VMEM(*v.value))
        shapes = [pltpu.HBM(*v.value) if isinstance(v, (Far, Raw)) else pltpu.VMEM(*v) for v in outs]
        count, n_in, n_out, n_after = len(stages), len(ins), len(outs), len(after)

        def body(where_ref, *refs):
            refs = list(refs)
            in_refs, refs = refs[:n_in], refs[n_in + n_after :]
            out_refs, refs = refs[:n_out], refs[n_out + 1 :]
            stage_refs, refs = refs[:count], refs[count:]
            flow = Flow()
            if count:
                sems, refs = refs[0], refs[1:]
            given, k = [], 0
            for v, ref in zip(ins, in_refs):
                if isinstance(v, Far):
                    source = ref.at[where_ref[0]] if v.pick else ref
                    copy = pltpu.make_async_copy(source, stage_refs[k], sems.at[k])
                    copy.start()
                    flow.loads[id(stage_refs[k])] = copy
                    ref, k = stage_refs[k], k + 1
                given.append(ref)
            for v, ref in zip(outs, out_refs):
                if isinstance(v, Far):
                    flow.stores[id(stage_refs[k])] = pltpu.make_async_copy(stage_refs[k], ref, sems.at[k])
                    ref, k = stage_refs[k], k + 1
                given.append(ref)
            kernel(flow, where_ref, *given, *refs)
            for copy in flow.loads.values():
                copy.wait()
            for copy in flow.stores.values():
                copy.start()
            for copy in [*flow.sent, *flow.stores.values()]:
                copy.wait()

        results = pl.pallas_call(
            body,
            in_specs=[words] + specs + after_specs,
            out_specs=[far if isinstance(v, (Far, Raw)) else near for v in outs] + [far],
            out_shape=shapes + [pltpu.HBM((8, LANES), F32)],
            scratch_shapes=stages + ([pltpu.SemaphoreType.DMA((count,))] if count else []) + list(scratch),
            compiler_params=pltpu.CompilerParams(vmem_limit_bytes=24 * 1024 * 1024),
            cost_estimate=pl.CostEstimate(flops=10**6, bytes_accessed=int(cost * 3 * 10**6), transcendentals=0),
            name=name,
        )(self.where, *values, *after)
        self.token = results[-1]
        return list(results[:-1])


def row_blocks(seq):
    return [slice(start, start + BLOCK) for start in range(0, seq, BLOCK)]


def row_of(ref, i):
    return ref[i : i + 1, :].astype(F32)


GAIN, SHIFT, OUT, SCALE, VECTORS = 0, 3, 6, 9, 16


def norm_parts(value):
    centre = value - jnp.mean(value, axis=-1, keepdims=True)
    spread = jnp.mean(centre * centre, axis=-1, keepdims=True)
    scale = lax.rsqrt(spread + EPSILON)
    return centre * scale, scale


def norm_backward(value, gain, incoming):
    xhat, scale = norm_parts(value)
    weighted = incoming * gain
    grad = scale * (
        weighted
        - jnp.mean(weighted, axis=-1, keepdims=True)
        - xhat * jnp.mean(weighted * xhat, axis=-1, keepdims=True)
    )
    return grad, jnp.sum(incoming * xhat, axis=0, keepdims=True), jnp.sum(incoming, axis=0, keepdims=True)


def head_lanes(value, j):
    lane = lax.broadcasted_iota(jnp.int32, value.shape, 1)
    return jnp.where((lane >= HDIM) == bool(j), value, jnp.zeros_like(value))


def span_of(block, seq, banded):
    if not banded:
        return slice(0, seq)
    return slice(max(block.start - BLOCK, 0), block.stop)


def start_all(moves, sems):
    copies = [pltpu.make_async_copy(a, b, sems.at[i]) for i, (a, b) in enumerate(moves)]
    for copy in copies:
        copy.start()
    return copies


def setup_kernel(packing, flow, where, *refs):
    group_tokens, bucket_group, lengths, inputs, cotangent, memory, segments, gains, shifts, biases, refs = *refs[:10], refs[10:]
    if packing:
        query, kv, out, w_in, w_out, cross, ffn, own_kv, refs = *refs[:8], refs[8:]
    x, cot, memory_part, vectors, molecules, tokens_now, group_now, lengths_now, word_sems, sems = refs
    words = start_all([(group_tokens, tokens_now), (bucket_group, group_now), (lengths, lengths_now)], word_sems)
    moves = [(memory.at[:, where[0]], memory_part), (inputs.at[where[0]], x), (cotangent.at[where[0]], cot)]
    if packing:
        full, wide = query.shape
        half = full // 2
        rows = pl.ds(pl.multiple_of(where[3] * half, half), half)
        moves += [
            (query.at[rows, :], cross.at[0:half, :]),
            (kv.at[0, rows, :], cross.at[half : 2 * half, :]),
            (kv.at[1, rows, :], cross.at[2 * half : 3 * half, :]),
        ]
        count, size = out.shape[1] // wide // 2, out.shape[0]
        for k in range(count):
            lanes = pl.ds(pl.multiple_of((where[3] * count + k) * wide, wide), wide)
            moves.append((out.at[:, lanes], cross.at[3 * half + k * size : 3 * half + (k + 1) * size, :]))
        moves += [(w_in, ffn.at[0]), (w_out, ffn.at[1]), (kv, own_kv)]
    copies = start_all(moves, sems)
    for copy in words:
        copy.wait()
    width = vectors.shape[1]
    total, own = 0, 0
    for b in range(bucket_group.shape[0]):
        tokens = tokens_now[group_now[b]]
        total = total + tokens
        own = own + jnp.where(where[2] == b, tokens, 0)
    scaled = jnp.full((1, width), bucket_group.shape[0] * own, jnp.int32).astype(F32)
    scale = scaled / jnp.full((1, width), total, jnp.int32).astype(F32)
    size = molecules.shape[1]
    place = lax.broadcasted_iota(jnp.int32, (1, size), 1)
    count, end = jnp.zeros((1, size), jnp.int32), 0
    for k in range(lengths.shape[1]):
        end = end + lengths_now[where[0], k]
        count = count + (end <= place).astype(jnp.int32)
    molecules[1:2, :] = count
    flow.need(segments, gains, shifts, biases)
    molecules[0:1, :] = segments[pl.ds(where[0], 1), :]
    rows = [r[...].astype(F32) for r in (gains, shifts, biases)] + [scale]
    vectors[...] = jnp.concatenate(rows + [jnp.zeros((VECTORS - 10, width), F32)], axis=0)
    for copy in copies:
        copy.wait()


def key_columns(keys):
    size = keys.shape[1]
    tiles = [jnp.broadcast_to(keys[:, at : at + BLOCK], (LANES, BLOCK)).T for at in range(0, size, BLOCK)]
    return jnp.concatenate(tiles, axis=0)


def allowed_of(own, columns, block, span, banded):
    allowed = columns[span] == own[:, block]
    if banded:
        query = lax.broadcasted_iota(jnp.int32, allowed.shape, 1) + block.start
        key = lax.broadcasted_iota(jnp.int32, allowed.shape, 0) + span.start
        allowed = allowed & (key <= query)
    return allowed


def both_heads(value):
    return jnp.concatenate([head_lanes(value, 0), head_lanes(value, 1)], axis=0)


def own_rows(value):
    half = value.shape[1] // 2
    row = lax.broadcasted_iota(jnp.int32, (value.shape[0], half), 0)
    return jnp.where(row < HDIM, value[:, :half], value[:, half:])


def pair_columns(at):
    return slice(2 * at * BLOCK, 2 * (at + 1) * BLOCK)


def attend_forward(q, k, v, own, keys, heads, totals, raised_all, shares, banded):
    seq, wide = q.shape
    columns = key_columns(keys)
    blocks = row_blocks(seq)
    for pair in range(wide // LANES):
        lanes = slice(pair * LANES, (pair + 1) * LANES)
        for at, block in enumerate(blocks):
            span = span_of(block, k.shape[0], banded)
            allowed = allowed_of(own, columns, block, span, banded)
            allowed = jnp.concatenate([allowed, allowed], axis=1)
            scores = dot_right(k[span, lanes], both_heads(q[block, lanes] * 0.125))
            scores = jnp.where(allowed, scores, -1e30)
            maxima = jnp.max(scores, axis=0, keepdims=True)
            raised = jnp.exp(scores - maxima)
            total = jnp.sum(raised, axis=0, keepdims=True)
            raised_all[span, pair_columns(at)] = raised.astype(BF16)
            shares[:, pair_columns(at)] = 1.0 / total
            logs = maxima + jnp.log(total)
            for j in (0, 1):
                totals[2 * pair + j : 2 * pair + j + 1, block] = logs[:, j * BLOCK : (j + 1) * BLOCK]
        turned = v[:, lanes].T
        if not banded:
            mixed = dot(turned, raised_all[...]) * shares[...]
        for at, block in enumerate(blocks):
            if banded:
                span = span_of(block, k.shape[0], banded)
                part = dot(turned[:, span], raised_all[span, pair_columns(at)]) * shares[:, pair_columns(at)]
            else:
                part = mixed[:, pair_columns(at)]
            heads[block, lanes] = own_rows(part).T.astype(BF16)


def attend_backward(q, k, v, own, keys, totals, grad_heads, dq, dk, dv, work, banded):
    seq, wide = q.shape
    columns = key_columns(keys)
    blocks = row_blocks(seq)
    scores_all, query_all = work[:2]
    for pair in range(wide // LANES):
        lanes = slice(pair * LANES, (pair + 1) * LANES)
        for at, block in enumerate(blocks):
            span = span_of(block, k.shape[0], banded)
            allowed = allowed_of(own, columns, block, span, banded)
            allowed = jnp.concatenate([allowed, allowed], axis=1)
            query, grad = both_heads(q[block, lanes] * 0.125), both_heads(grad_heads[block, lanes])
            query_all[pair_columns(at), :] = query
            logs = jnp.concatenate([totals[2 * pair + j : 2 * pair + j + 1, block] for j in (0, 1)], axis=1)
            scores = jnp.where(allowed, dot_right(k[span, lanes], query), -1e30)
            chances = jnp.exp(scores - logs)
            if banded:
                work[2][span, pair_columns(at)] = chances.astype(BF16)
                work[3][pair_columns(at), :] = grad
            else:
                grad_value = dot(chances.astype(BF16), grad)
                work[2][...] = grad_value if at == 0 else work[2][...] + grad_value
            weighted = chances * dot_right(v[span, lanes], grad)
            mean = jnp.sum(weighted, axis=0, keepdims=True)
            scores_all[span, pair_columns(at)] = (weighted - chances * mean).astype(BF16)
        turned = k[:, lanes].T
        if not banded:
            grad_query = dot(turned, scores_all[...])
            dk[:, lanes] = dot(scores_all[...], query_all[...]).astype(BF16)
            dv[:, lanes] = work[2][...].astype(BF16)
        for at, block in enumerate(blocks):
            if banded:
                span = span_of(block, k.shape[0], banded)
                part = dot(turned[:, span], scores_all[span, pair_columns(at)])
                met = slice(pair_columns(at).start, pair_columns(min(at + 1, len(blocks) - 1)).stop)
                dk[block, lanes] = dot(scores_all[block, met], query_all[met, :]).astype(BF16)
                dv[block, lanes] = dot(work[2][block, met], work[3][met, :]).astype(BF16)
            else:
                part = grad_query[:, pair_columns(at)]
            dq[block, lanes] = (own_rows(part).T * 0.125).astype(BF16)


def team_total(mine, theirs, block):
    half = mine[0].shape[0]
    k, rows = block.start // half, slice(block.start % half, block.start % half + BLOCK)
    return mine[k][rows, :].astype(F32) + theirs[k][rows, :].astype(F32)


def put_half(parts, block, value):
    half = parts[0].shape[0]
    start = block.start % half
    parts[block.start // half][start : start + BLOCK, :] = value.astype(parts[0].dtype)


def self_forward_kernel(n, i, flow, where, *refs):
    last = i == n - 1
    first, vectors, molecules, w, bias, refs = *refs[:5], refs[5:]
    if last:
        w_out, done, refs = refs[:n], refs[n : 2 * n - 1], refs[2 * n - 1 :]
    if i == 0:
        normed, refs = refs[0], refs[1:]
        for block in row_blocks(first.shape[0]):
            norm = norm_parts(first[block, :].astype(F32))[0]
            normed[block, :] = (norm * row_of(vectors, GAIN) + row_of(vectors, SHIFT)).astype(BF16)
    else:
        normed = first
    q, k, v, heads, totals = refs[:5]
    flow.need(w)
    q[...] = (dot(normed[...], w[0]) + row_of(bias, 0)).astype(BF16)
    k[...] = dot(normed[...], w[1]).astype(BF16)
    v[...] = (dot(normed[...], w[2]) + row_of(bias, 1)).astype(BF16)
    own = molecules[0:1, :]
    flow.send(q, k, v)
    attend_forward(q, k, v, own, own, heads, totals, *refs[-2:], True)
    flow.send(totals)
    if last:
        project_out(flow, [*done, heads], w_out, refs[5 : 5 + FRONT])


def project_out(flow, heads, w_out, parts):
    flow.need(*w_out)
    for block in row_blocks(heads[0].shape[0]):
        put_half(parts, block, sum(dot(h[block, :], w[...]) for h, w in zip(heads, w_out)))


def memory_kernel(flow, where, memory, w, bias, k, v):
    flow.need(w)
    k[...] = dot(memory[...], w[0]).astype(BF16)
    v[...] = (dot(memory[...], w[1]) + row_of(bias, 3)).astype(BF16)


def unpack_memory_kernel(flow, where, near, got, memory, bias, query, kv, out, k, v):
    full, wide = query.shape
    half, size = full // 2, out.shape[0]
    count = out.shape[1] // wide // 2
    for packed, bit in ((near, where[3]), (got, 1 - where[3])):
        rows = pl.ds(pl.multiple_of(bit * half, half), half)
        query[rows, :] = packed[:half]
        for i in (0, 1):
            kv[i, rows, :] = packed[(i + 1) * half : (i + 2) * half]
        for i in range(count):
            lanes = pl.ds(pl.multiple_of((bit * count + i) * wide, wide), wide)
            out[:, lanes] = packed[3 * half + i * size : 3 * half + (i + 1) * size]
    memory_kernel(flow, where, memory, kv, bias, k, v)


def cross_forward_kernel(n, i, flow, where, *refs):
    last = i == n - 1
    if i == 0:
        x, mine, theirs, refs = refs[0], refs[1 : 1 + FRONT], refs[1 + FRONT : 1 + 2 * FRONT], refs[1 + 2 * FRONT :]
    else:
        normed, refs = refs[0], refs[1:]
    vectors, molecules, w, bias, k, v, refs = *refs[:6], refs[6:]
    if last:
        w_out, done, refs = refs[:n], refs[n : 2 * n - 1], refs[2 * n - 1 :]
    if i == 0:
        after_self, normed, refs = refs[0], refs[1], refs[2:]
    q, heads, totals = refs[:3]
    if i == 0:
        for block in row_blocks(x.shape[0]):
            value = x[block, :].astype(F32) + team_total(mine, theirs, block) + row_of(vectors, OUT)
            after_self[block, :] = value
            norm = norm_parts(value)[0]
            normed[block, :] = (norm * row_of(vectors, GAIN + 1) + row_of(vectors, SHIFT + 1)).astype(BF16)
    flow.need(w)
    q[...] = (dot(normed[...], w[...]) + row_of(bias, 2)).astype(BF16)
    attend_forward(q, k, v, molecules[0:1, :], molecules[1:2, :], heads, totals, *refs[-2:], False)
    if last:
        project_out(flow, [*done, heads], w_out, refs[3 : 3 + FRONT])


def ffn_kernel(i, flow, where, *refs):
    if i == 0:
        after_self, mine, theirs, refs = refs[0], refs[1 : 1 + FRONT], refs[1 + FRONT : 1 + 2 * FRONT], refs[1 + 2 * FRONT :]
        cotangent, vectors, w_in, bias, w_out, refs = *refs[:5], refs[5:]
        after_cross, normed, low, active, grad_hidden, part, part_grad = refs
    else:
        normed, low, begun, begun_grad, w_in, bias, refs = *refs[:6], refs[6:]
        if len(w_in.shape) == 3:
            w_in, w_out = w_in.at[0], w_in.at[1]
        else:
            w_out, refs = refs[0], refs[1:]
        active, grad_hidden, parts, parts_grad = refs[0], refs[1], refs[2 : 2 + BACK], refs[2 + BACK :]
    if bias.shape[0] == 1:
        row = row_of(bias, 0)
    else:
        row = jnp.concatenate([row_of(bias, k) for k in range(4, bias.shape[0])], axis=1)
    if i == 0:
        for block in row_blocks(normed.shape[0]):
            value = after_self[block, :] + team_total(mine, theirs, block) + row_of(vectors, OUT + 1)
            after_cross[block, :] = value
            norm = norm_parts(value)[0]
            normed[block, :] = (norm * row_of(vectors, GAIN + 2) + row_of(vectors, SHIFT + 2)).astype(BF16)
            low[block, :] = (cotangent[block, :].astype(F32) * row_of(vectors, SCALE)).astype(BF16)
    flow.need(w_in, w_out)
    for block in row_blocks(normed.shape[0]):
        hidden = dot(normed[block, :], w_in[...]) + row
        cdf = 0.5 * (1.0 + lax.erf(hidden * 0.7071067811865476))
        act = (hidden * cdf).astype(BF16)
        active[block, :] = act
        slope = cdf + hidden * (0.3989422804014327 * jnp.exp(-0.5 * hidden * hidden))
        back = (slope * dot_right(low[block, :], w_out[...])).astype(BF16)
        grad_hidden[block, :] = back
        out, out_grad = dot(act, w_out[...]), dot_right(back, w_in[...])
        if i == 0:
            part[block, :], part_grad[block, :] = out, out_grad
        else:
            put_half(parts, block, begun[block, :] + out)
            put_half(parts_grad, block, begun_grad[block, :] + out_grad)


def ffn_weights_kernel(flow, where, *refs):
    hidden, active, normed, low, sums = refs[:2], refs[2:4], refs[4], refs[5], refs[6]
    keep_out, send_out, keep_in, send_in = refs[7:]
    half = keep_in.shape[1]
    for i in (0, 1):
        for target, bit in ((keep_in, where[3]), (send_in, 1 - where[3])):
            lanes = pl.ds(pl.multiple_of(bit * half, half), half)
            target[i] = dot_left(hidden[i][:, lanes], normed[...]).astype(target.dtype)
        sums[i : i + 1, :] = jnp.sum(hidden[i][...].astype(F32), axis=0, keepdims=True)
    keep_out[0] = dot_left(active[0][...], low[...])
    send_out[0] = dot_left(active[1][...], low[...]).astype(BF16)


def spread_grad_heads(low, w_out, grad_heads):
    for piece, target in zip(w_out, grad_heads):
        target[...] = dot_right(low[...], piece[...]).astype(BF16)


def column_sums(sums, values):
    for i, value in enumerate(values):
        sums[i : i + 1, :] = jnp.sum(value[...].astype(F32), axis=0, keepdims=True)


def cross_backward_kernel(n, flow, where, *refs):
    after_cross, mine, theirs, refs = refs[0], refs[1 : 1 + BACK], refs[1 + BACK : 1 + 2 * BACK], refs[1 + 2 * BACK :]
    cotangent, vectors, molecules, refs = *refs[:3], refs[3:]
    (q, k, v, totals, w_out, w), refs = [refs[i * n : (i + 1) * n] for i in range(6)], refs[6 * n :]
    grad_cross, low, refs = refs[0], refs[1], refs[2:]
    (dq, dk, dv, bias_sums), refs = [refs[i * n : (i + 1) * n] for i in range(4)], refs[4 * n :]
    parts_out, sums, refs = refs[:BACK], refs[BACK], refs[BACK + 1 :]
    grad_heads, work = refs[:n], refs[n:]
    seq, width = after_cross.shape
    rows = [jnp.zeros((1, width), F32)] * 3
    for block in row_blocks(seq):
        incoming = team_total(mine, theirs, block)
        grad_result = cotangent[block, :].astype(F32) * row_of(vectors, SCALE)
        back, by_gain, by_shift = norm_backward(after_cross[block, :], row_of(vectors, GAIN + 2), incoming)
        value = grad_result + back
        grad_cross[block, :] = value
        low[block, :] = value.astype(BF16)
        parts = (by_gain, by_shift, jnp.sum(grad_result, axis=0, keepdims=True))
        rows = [a + b for a, b in zip(rows, parts)]
    for i, row in enumerate(rows):
        sums[i : i + 1, :] = row
    flow.need(*w_out)
    spread_grad_heads(low, w_out, grad_heads)
    own, keys = molecules[0:1, :], molecules[1:2, :]
    for i in range(n):
        attend_backward(
            q[i], k[i], v[i], own, keys, totals[i], grad_heads[i], dq[i], dk[i], dv[i], work, False
        )
        column_sums(bias_sums[i], (dq[i], dv[i]))
    flow.need(*w)
    for block in row_blocks(seq):
        put_half(parts_out, block, sum(dot_right(d[block, :], m[...]) for d, m in zip(dq, w)))


def shard_grads(kinds):
    grads = ([], [])
    for kind in kinds:
        if len(kind) == 2:
            for i in (0, 1):
                grads[i].append(dot_left(kind[i][0][...], kind[i][1][...]))
        else:
            left, right = kind[0]
            both, half = dot_left(left[...], right[...]), left.shape[1] // 2
            grads[0].append(both[:half])
            grads[1].append(both[half:])
    return grads


def cross_weights_kernel(n, flow, where, *refs):
    (dq, dk, dv, heads, w), refs = [refs[i * n : (i + 1) * n] for i in range(5)], refs[5 * n :]
    normed, memory, low, after_cross, refs = *refs[:4], refs[4:]
    mine, theirs, vectors, refs = refs[:BACK], refs[BACK : 2 * BACK], refs[2 * BACK], refs[2 * BACK + 1 :]
    keep, send, terms, result = refs[0], refs[1], refs[2 : 2 + BACK], refs[-1]
    flow.need(*w)
    pairs = [[(a, b) for a in left] for left, b in ((dq, normed), (dk, memory), (dv, memory), (heads, low))]
    first = where[3] == 0
    for i, grads in enumerate(shard_grads(pairs)):
        upper, lower = jnp.concatenate(grads[:2], axis=0), jnp.concatenate(grads[2:], axis=0)
        keep[i] = jnp.where(first, upper, lower)
        send[i] = jnp.where(first, lower, upper).astype(BF16)
    for block in row_blocks(memory.shape[0]):
        total = sum(
            dot_right(a[block, :], m[0]) + dot_right(b[block, :], m[1]) for a, b, m in zip(dk, dv, w)
        )
        put_half(terms, block, total)
    for block in row_blocks(after_cross.shape[0]):
        both = team_total(mine, theirs, block)
        result[block, :] = (after_cross[block, :] + both + row_of(vectors, OUT + 2)).astype(BF16)


def put_grads(target, grads):
    size = grads[0].shape[0]
    for k, grad in enumerate(grads):
        target[0, k * size : (k + 1) * size, :] = grad.astype(target.dtype)


def self_backward_kernel(n, flow, where, *refs):
    after_self, mine, theirs, refs = refs[0], refs[1 : 1 + BACK], refs[1 + BACK : 1 + 2 * BACK], refs[1 + 2 * BACK :]
    grad_cross, vectors, molecules, q, k, v, totals, refs = *refs[:7], refs[7:]
    w_out, refs = refs[:n], refs[n:]
    normed, heads, grad_self, low, dq, dk, dv, bias_sums, sums, refs = *refs[:9], refs[9:]
    first, send, grad_heads, work = *refs[:3], refs[3:]
    seq, width = after_self.shape
    rows = [jnp.zeros((1, width), F32)] * 3
    for block in row_blocks(seq):
        incoming = team_total(mine, theirs, block)
        back, by_gain, by_shift = norm_backward(after_self[block, :], row_of(vectors, GAIN + 1), incoming)
        upper = grad_cross[block, :]
        value = upper + back
        grad_self[block, :] = value
        low[block, :] = value.astype(BF16)
        parts = (by_gain, by_shift, jnp.sum(upper, axis=0, keepdims=True))
        rows = [a + b for a, b in zip(rows, parts)]
    for i, row in enumerate(rows):
        sums[i : i + 1, :] = row
    flow.need(*w_out)
    spread_grad_heads(low, w_out, [first, grad_heads] if n == 2 else [grad_heads])
    own = molecules[0:1, :]
    flow.need(q, k, v, totals)
    attend_backward(q, k, v, own, own, totals, grad_heads, dq, dk, dv, work, True)
    column_sums(bias_sums, (dq, dv))
    grads = [dot_left(a[...], b[...]) for a, b in ((dq, normed), (dk, normed), (dv, normed), (heads, low))]
    if n == 2:
        put_grads(send, grads)
    else:
        half = grads[0].shape[0] // 2
        put_grads(first, [g[:half] for g in grads])
        put_grads(send, [g[half:] for g in grads])


def self_backward_rest_kernel(n, flow, where, *refs):
    w, grads_last, refs = refs[:n], refs[n : n + 3], refs[n + 3 :]
    pieces = [grads_last]
    if n == 2:
        molecules, q, k, v, totals, grad_heads, normed, heads, low, refs = *refs[:9], refs[9:]
        bias_sums, keep, parts_out, refs = refs[0], refs[1], refs[2 : 2 + BACK], refs[2 + BACK :]
        dq, dk, dv, work = *refs[:3], refs[3:]
        own = molecules[0:1, :]
        flow.need(q, k, v, totals)
        attend_backward(q, k, v, own, own, totals, grad_heads, dq, dk, dv, work, True)
        column_sums(bias_sums, (dq, dv))
        put_grads(keep, [dot_left(a[...], b[...]) for a, b in ((dq, normed), (dk, normed), (dv, normed), (heads, low))])
        pieces = [(dq, dk, dv), grads_last]
    else:
        parts_out = refs[:BACK]
    flow.need(*w)
    for block in row_blocks(grads_last[0].shape[0]):
        total = 0.0
        for matrices, grads in zip(w, pieces):
            for which, d in enumerate(grads):
                total += dot_right(d[block, :], matrices[which])
        put_half(parts_out, block, total)


def input_backward_kernel(n, flow, where, x, *refs):
    mine, theirs, refs = refs[:BACK], refs[BACK : 2 * BACK], refs[2 * BACK :]
    grad_self, vectors, result, by_cross, by_ffn, refs = *refs[:5], refs[5:]
    shard_rows, (both, small_own, small_other) = refs[:-3], refs[-3:]
    seq = x.shape[0]
    both[:seq, :] = result[...]
    width = x.shape[1]
    rows = [jnp.zeros((1, width), F32)] * 3
    for block in row_blocks(x.shape[0]):
        incoming = team_total(mine, theirs, block)
        back, by_gain, by_shift = norm_backward(x[block, :].astype(F32), row_of(vectors, GAIN), incoming)
        upper = grad_self[block, :]
        both[seq + block.start : seq + block.stop, :] = (upper + back).astype(BF16)
        parts = (by_gain, by_shift, jnp.sum(upper, axis=0, keepdims=True))
        rows = [a + b for a, b in zip(rows, parts)]
    common = [r for k in range(3) for r in (rows[k], by_cross[k : k + 1, :], by_ffn[k : k + 1, :])]
    if len(shard_rows) == 1:
        lines = [shard_rows[0][i] for i in (0, 1)]
    else:
        sums_self, sums_cross, sums_ffn = shard_rows[:n], shard_rows[n : 2 * n], shard_rows[2 * n]
        lines = []
        for i in (0, 1):
            pieces = [r[k : k + 1, :] for r in (sums_self[i], sums_cross[i]) for k in (0, 1)]
            lines.append(jnp.concatenate([jnp.concatenate(pieces, axis=1), sums_ffn[i : i + 1, :]], axis=0))
    rest = jnp.zeros((SMALL - 9 - lines[0].shape[0], width), F32)
    small = [jnp.concatenate([*common, line, rest], axis=0).astype(BF16) for line in lines]
    small_own[...] = small[0]
    small_other[...] = small[1]


def fold_kernel(count, size, ride, mode, bit, flow, where, *refs):
    keeps, gots, refs = refs[:count], refs[count : 2 * count], refs[2 * count :]
    planes = [(k, p) for k in range(count) for p in range(keeps[k].shape[0])]

    def part(at, rows):
        k, p = planes[at]
        return keeps[k][p, rows, :].astype(F32) + gots[k][p, rows, :].astype(F32)

    if mode == "half":
        keep, send = refs
        half = size // 2
        for at in range(len(planes)):
            for target, side in ((keep, where[3 + bit]), (send, 1 - where[3 + bit])):
                rows = pl.ds(pl.multiple_of(side * half, half), half)
                target[at, :half, :] = part(at, rows).astype(target.dtype)
    elif mode == "shard":
        if ride is not None:
            refs[-1][0, size : size + SMALL, :] = refs[0][...]
        for at, target in enumerate(refs[-2:]):
            target[0, :size, :] = part(at, slice(0, size)).astype(target.dtype)
    else:
        out = refs[-1]
        for at in range(len(planes)):
            out[at, :size, :] = part(at, slice(0, size)).astype(out.dtype)
        if ride is not None:
            own, came = refs[:2]
            small = own[...].astype(F32) + came[0, ride : ride + SMALL, :].astype(F32)
            out[0, size : size + SMALL, :] = small.astype(out.dtype)


def memory_pairs(axis):
    step = 1 if axis == "row" else 2 << axis
    return [(k, k | step) for k in range(16) if not k & step]


def memory_bit(where, axis):
    return where[0] if axis == "row" else where[3 + axis]


def send_blocks(where, axis, blocks, send, offset):
    low = memory_bit(where, axis) == 0
    per = 8 // send.shape[0]
    for k, (a, b) in enumerate(memory_pairs(axis)):
        at = offset + k % per * SMALL
        send[k // per, at : at + SMALL, :] = jnp.where(low, blocks[b], blocks[a])


def take_blocks(where, axis, kept, got, offset):
    low = memory_bit(where, axis) == 0
    per = 8 // got.shape[0]
    blocks = {}
    for k, (a, b) in enumerate(memory_pairs(axis)):
        at = offset + k % per * SMALL
        came = got[k // per, at : at + SMALL, :]
        blocks[a] = jnp.where(low, kept[a], came)
        blocks[b] = jnp.where(low, came, kept[b])
    return blocks


def memory_start_kernel(axis, flow, where, *refs, send, offset):
    mine, theirs, kept = refs[:BACK], refs[BACK : 2 * BACK], refs[2 * BACK]
    half, width = mine[0].shape
    tokens = half * BACK // 8
    share = LANES
    blocks = {}
    for r in (0, 1):
        lanes = pl.ds(pl.multiple_of((2 * r + where[1]) * share, share), share)
        for k in range(BACK):
            total = (mine[k][:, lanes].astype(F32) + theirs[k][:, lanes].astype(F32)).astype(BF16)
            for d in range(half // tokens):
                block = total[d * tokens : (d + 1) * tokens]
                parts = [block[q : q + SMALL] for q in range(0, tokens, SMALL)]
                at = 2 * (k * half // tokens + d) + r
                blocks[at] = jnp.concatenate(parts, axis=1)
                kept[at] = blocks[at]
    send_blocks(where, axis, blocks, send, offset)


def memory_send_kernel(before, at, axis, flow, where, old, got, kept, send):
    blocks = take_blocks(where, before, old, got, at)
    for k, block in blocks.items():
        kept[k] = block
    send_blocks(where, axis, blocks, send, 0)


def memory_end_kernel(before, at, flow, where, old, got, out):
    for k, block in take_blocks(where, before, old, got, at).items():
        parts = [block[:, q : q + LANES] for q in range(0, block.shape[1], LANES)]
        out[k] = jnp.concatenate(parts, axis=0).astype(out.dtype)


def join_kernel(ride, pad, bit, flow, where, near, got, out):
    half = near.shape[1] - (SMALL if ride else 0)
    for value, side in ((near, where[3 + bit]), (got, 1 - where[3 + bit])):
        rows = pl.ds(pl.multiple_of(side * half, half), half)
        for p in range(near.shape[0]):
            out[p, rows, :] = value[p, :half]
    if ride:
        out[0, 2 * half :, :] = (near[0, half:].astype(F32) + got[0, half:].astype(F32)).astype(BF16)
    if pad:
        out[:, 2 * half :, :] = jnp.zeros((out.shape[0], pad, out.shape[2]), out.dtype)


def joined(where, bit, near, got, p, ride=0):
    first = where[3 + bit] == 0
    size = near.shape[1] - ride
    a, b = near[p, :size], got[p, :size]
    rows = [jnp.where(first, a, b), jnp.where(first, b, a)]
    return jnp.concatenate(rows, axis=0).astype(F32)


def self_grads_kernel(bit, flow, where, near, got, qkv, out, gains, shifts, biases, *rest):
    size = near.shape[1] - SMALL
    small = near[0, size:].astype(F32) + got[0, size:].astype(F32)
    for k, target in enumerate((gains, shifts, biases)):
        target[...] = small[3 * k : 3 * k + 3]
    if len(rest) == 1:
        rest[0][...] = small[9 : 9 + rest[0].shape[0]]
    else:
        for k, target in enumerate(rest[:2]):
            wide = target.shape[1]
            for i in (0, 1):
                at = (2 * k + i) * wide
                target[i : i + 1, :] = small[9:10, at : at + wide]
        rest[2][...] = small[10:11]
    flow.send(gains, shifts, biases, *rest)
    value = joined_inside(where, bit, near, got, 0, SMALL)
    size = out.shape[0]
    for k in range(3):
        qkv[k] = value[k * size : (k + 1) * size].T
    out[...] = value[3 * size :]


def joined_inside(where, bit, near, got, p, pad=0):
    half = (near.shape[1] - pad) // 2
    first, parts = where[3 + bit] == 0, []
    for k in (0, 1):
        a, b = near[p, k * half : (k + 1) * half], got[p, k * half : (k + 1) * half]
        parts += [jnp.where(first, a, b), jnp.where(first, b, a)]
    return jnp.concatenate(parts, axis=0).astype(F32)


def cross_grads_kernel(bit, flow, where, near, got, query, kv, out):
    value = joined(where, bit, near, got, 0, 2 * SMALL)
    size = out.shape[0]
    query[...] = value[:size].T
    for k in (0, 1):
        kv[k] = value[(k + 1) * size : (k + 2) * size].T
    out[...] = value[3 * size :]


def ffn_grads_kernel(bit, flow, where, near, got, grad_in, grad_out):
    grad_out[...] = joined_inside(where, bit, near, got, 0)
    flow.send(grad_out)
    grad_in[...] = joined_inside(where, bit, near, got, 1).T


def place_rows_kernel(flow, where, own, got, mixed, grad):
    seq = own.shape[0] // 2
    for k, out in enumerate((mixed, grad)):
        for row, value in ((where[0], own), (1 - where[0], got)):
            out[row] = value[k * seq : (k + 1) * seq, :].astype(out.dtype)
        flow.send(out)


def shards(
    inputs,
    memory,
    segment_ids,
    mem_lengths,
    bucket_group,
    group_tokens,
    norm_gain,
    norm_bias,
    self_qkv,
    self_bias,
    self_out,
    cross_q,
    cross_kv,
    cross_bias,
    cross_out,
    ffn_in,
    ffn_bias,
    ffn_out,
    out_bias,
    cotangent,
):
    dp, mp = lax.axis_size("dp"), lax.axis_size("mp")
    rows, seq, width = inputs.shape
    team = mp // rows
    data, place = lax.axis_index("dp"), lax.axis_index("mp")
    row, seat = place // team, place % team
    bits = dp.bit_length() - 1
    where = jnp.stack([row, seat, data] + [(data >> k) & 1 for k in range(bits)]).astype(jnp.int32)
    run, far = Steps(where), Far

    across = [(i, (i + team) % mp) for i in range(mp)]

    def other(value):
        return lax.ppermute(value, "mp", across)

    def seat_swap(value, step):
        return lax.ppermute(value, "mp", [(i, i ^ step) for i in range(mp)])

    def data_swap(value, k):
        return lax.ppermute(value, "dp", [(i, i ^ (1 << k)) for i in range(dp)])

    def swap(value, axis):
        return other(value) if axis == "row" else data_swap(value, axis)

    def later(value, *after):
        return lax.optimization_barrier((value, *after))[0]

    def team_parts(values):
        step = 1
        while 2 * step < team:
            values = [(v.astype(F32) + seat_swap(v, step).astype(F32)).astype(BF16) for v in values]
            step *= 2
        return [*values, *(seat_swap(v, step) for v in values)]

    head, unit = self_bias.shape[1], ffn_bias.shape[0]
    mem_len = memory.shape[1] * dp
    apart = head % LANES == 0
    n = 2 if apart else 1
    wide = head if apart else 2 * head

    front = [((seq // FRONT, width), BF16)] * FRONT
    back = [((seq // BACK, width), BF16)] * BACK
    whole, full = ((seq, width), BF16), ((seq, width), F32)
    local, totals = ((seq, wide), BF16), ((2 * wide // LANES, seq), F32)
    units = ((seq, unit), BF16)

    other_qkv = other(self_qkv)
    bias_own = jnp.concatenate([self_bias, cross_bias, ffn_bias.reshape(-1, head)])
    bias_other = other(bias_own)
    other_self_out = other(self_out)
    memory_rows = memory.reshape((dp, rows) + memory.shape[1:])
    packing = apart and width % (2 * head) == 0 and ffn_in.shape == ffn_out.shape
    ins = [Raw(group_tokens), Raw(bucket_group), Raw(mem_lengths), Raw(inputs), Raw(cotangent), Raw(memory_rows)]
    ins += [far(segment_ids), far(norm_gain), far(norm_bias), far(out_bias)]
    outs = [whole, whole, ((dp,) + memory.shape[1:], BF16), ((VECTORS, width), F32), ((2, seq), jnp.int32)]
    if packing:
        ins += [Raw(v) for v in (cross_q, cross_kv, cross_out, ffn_in, ffn_out)]
        packs = [((3 * width // 2 + cross_out.size // head // 2, head), BF16), ((2,) + ffn_in.shape, BF16)]
        outs = packs + [(cross_kv.shape, BF16)] + outs
    *packed, x, cot, memory_part, vectors, molecules = run(
        functools.partial(setup_kernel, packing),
        ins,
        outs,
        scratch=[pltpu.SMEM(v.shape, jnp.int32) for v in (group_tokens, bucket_group, mem_lengths)]
        + [pltpu.SemaphoreType.DMA((3,)), pltpu.SemaphoreType.DMA((9 + width // head // 2,))],
        name="setup",
    )
    if packing:
        near_cross = other(packed[0])
        got_cross = data_swap(near_cross, 0)
    memory_row = lax.all_to_all(memory_part, "dp", split_axis=0, concat_axis=0, tiled=True).reshape(mem_len, width)
    def pieces(own, theirs, axis):
        return [far(own), theirs] if apart else [jnp.concatenate([own, theirs], axis=axis)]

    w_qkv = pieces(self_qkv, other_qkv, 2)
    w_self_out = pieces(self_out, other_self_out, 0)
    b_heads = [bias_own, bias_other] if apart else [jnp.concatenate([bias_own, bias_other], axis=1)]
    b_in = b_heads if apart else [b[4:].reshape(1, unit) for b in (bias_own, bias_other)]

    forward_work = [pltpu.VMEM((seq, 2 * seq), BF16), pltpu.VMEM((1, 2 * seq), F32)]
    cross_work = [pltpu.VMEM((mem_len, 2 * seq), BF16), pltpu.VMEM((1, 2 * seq), F32)]
    heads_self, saved_self = [], []
    for i in range(n):
        last = i == n - 1
        ins = [x if i == 0 else normed_self, vectors, molecules, w_qkv[i], b_heads[i]]
        outs = ([whole] if i == 0 else []) + [far(local)] * 3 + [local, far(totals)]
        if last:
            ins += [*w_self_out, *heads_self]
            outs += front
        got = run(functools.partial(self_forward_kernel, n, i), ins, outs, scratch=forward_work, name=f"self_forward_{i}")
        if i == 0:
            normed_self, got = got[0], got[1:]
            early = (normed_self, other_qkv, bias_other, other_self_out)
            if packing:
                other_ffn = other(later(packed[1], *early, near_cross))
            else:
                other_cross = [other(later(w, *early)) for w in (cross_q, cross_kv, cross_out)]
                other_in, other_out = [other(later(w, *other_cross)) for w in (ffn_in, ffn_out)]
        saved_self.append((got[0], got[1], got[2], got[4]))
        heads_self.append(got[3])
    terms = team_parts(got[5:])

    heads_cross, saved_cross = [], []
    if apart:
        w_cross_q, w_cross_out = [far(cross_q)], [far(cross_out)]
        w_cross_kv = [packed[2] if packing else far(cross_kv)]
    else:
        w_cross_q = pieces(cross_q, other_cross[0], 1)
        w_cross_kv = pieces(cross_kv, other_cross[1], 2)
        w_cross_out = pieces(cross_out, other_cross[2], 0)
    projected = ((mem_len, wide), BF16)
    for i in range(n):
        last = i == n - 1
        if i == 1 and packing:
            query, both, out, *kv = run(
                unpack_memory_kernel,
                [near_cross, got_cross, memory_row, b_heads[1]],
                [(v.shape, BF16) for v in (cross_q, cross_kv, cross_out)] + [projected] * 2,
                name="memory_1",
            )
            for pieces_of, w in ((w_cross_q, query), (w_cross_kv, both), (w_cross_out, out)):
                pieces_of.append(w)
        else:
            if i == 1:
                for pieces_of, w in zip((w_cross_q, w_cross_kv, w_cross_out), other_cross):
                    pieces_of.append(w)
            kv = run(memory_kernel, [memory_row, w_cross_kv[i], b_heads[i]], [projected] * 2, name=f"memory_{i}")
        first = [x, *terms] if i == 0 else [normed_cross]
        ins = first + [vectors, molecules, w_cross_q[i], b_heads[i], *kv]
        outs = ([full, whole] if i == 0 else []) + [local] * 2 + [totals]
        if last:
            ins += [*w_cross_out, *heads_cross]
            outs += front
        got = run(functools.partial(cross_forward_kernel, n, i), ins, outs, scratch=cross_work, name=f"cross_forward_{i}")
        if i == 0:
            after_self, normed_cross, got = got[0], got[1], got[2:]
        saved_cross.append((got[0], *kv, got[2]))
        heads_cross.append(got[1])
    terms = team_parts(got[3:])

    after_cross, normed_ffn, low_ffn, act_own, hid_own, begun, begun_grad = run(
        functools.partial(ffn_kernel, 0),
        [after_self, *terms, cot, vectors, far(ffn_in), b_in[0], far(ffn_out)],
        [full, whole, whole, units, units, full, full],
        name="ffn_0",
    )
    ins = [other_ffn if packing else other_in, b_in[1]] + ([] if packing else [other_out])
    act_other, hid_other, *parts = run(
        functools.partial(ffn_kernel, 1),
        [normed_ffn, low_ffn, begun, begun_grad, *ins],
        [units, units] + back + back,
        name="ffn_1",
    )
    terms = team_parts(parts[BACK:])
    out_terms = team_parts(parts[:BACK])

    class Reduction:
        def __init__(self, keeps, sends, axes, pad=0, turned=False):
            self.pad, self.turned = pad, turned
            self.keeps, self.axes, self.ride, self.carry = keeps, axes, [], []
            self.gots = [swap(s, a) for s, a in zip(sends, axes[0])]
            self.halved = [b for b in axes[0] if b != "row"][:1]
            self.size = sends[0].shape[1]
            self.chunk = None

        def plan(self, extra=None):
            if self.chunk is not None:
                bit, small = self.halved.pop(), SMALL if self.ride else 0
                planes, size, _ = self.chunk.shape
                pad = self.pad if len(self.halved) == 1 else 0
                outs = [((planes, 2 * size - small + pad, width), BF16)]
                return functools.partial(join_kernel, bool(small), pad, bit), [self.chunk, self.got], outs
            axes, keeps, size = self.axes, self.keeps, self.size
            planes = sum(k.shape[0] for k in keeps)
            bit, ride, at, rows = 0, [], None, size
            if len(axes) == 1:
                mode = "last"
            elif axes[1][0] == "row":
                mode, planes = "shard", 1
                if self.carry:
                    ride, at, rows = self.carry, size, size + SMALL
            elif len(axes) == 2:
                mode = "full"
                if self.ride:
                    ride, at, rows = self.ride, self.ride_at, size + SMALL
                    self.size += SMALL
            else:
                mode, bit, rows = "half", axes[1][0], size // 2
                self.size = rows
                self.halved.append(bit)
            more = 8 // planes * SMALL if extra else 0
            outs = [((planes, rows + more, width), BF16)]
            if mode in ("half", "shard"):
                outs = [((planes, self.size, width), F32)] + outs
            ins = [*keeps, *self.gots, *ride]
            kernel = functools.partial(fold_kernel, len(keeps), size, at, mode, bit)
            if not extra:
                return kernel, ins, outs
            second, second_ins, second_outs = extra
            self.extra_at = rows

            def both(flow, where, *refs):
                a, b = len(ins), len(ins) + len(second_ins)
                c = b + len(second_outs)
                kernel(flow, where, *refs[:a], *refs[c:])
                second(flow, where, *refs[a:c], send=refs[-1], offset=rows)

            return both, ins + second_ins, second_outs + outs

        def take(self, got):
            if self.chunk is not None or len(self.axes) == 1:
                if self.chunk is None and self.turned:
                    self.halved[:2] = self.halved[1::-1]
                self.chunk = got[0]
                self.got = swap(self.chunk, self.halved[-1])
            else:
                self.axes = self.axes[1:]
                self.keeps = [got[0]]
                self.gots = [swap(got[-1], self.axes[0][0])]

        def ready(self):
            return self.chunk is not None and len(self.halved) == 1

    def advance(name, *groups, extra=None, more=None):
        groups = [g for g in groups if not g.ready()]
        parts = [g.plan(extra if i == 0 else None) for i, g in enumerate(groups)] + ([more] if more else [])
        results = run.batch(parts, name=name) if parts else []
        given = results.pop() if more else []
        for i, (g, got) in enumerate(zip(groups, results)):
            if extra and i == 0:
                count = len(extra[2])
                given, got = got[:count], got[count:]
            g.take(got)
        return given

    ffn_sums, keep_out, send_out, keep_in, send_in = run(
        ffn_weights_kernel,
        [hid_own, hid_other, act_own, act_other, normed_ffn, low_ffn],
        [((2, unit), F32), ((1, unit, width), F32), ((1, unit, width), BF16)]
        + [((2, unit // 2, width), F32), ((2, unit // 2, width), BF16)],
        name="ffn_weights",
    )
    by_out = Reduction([keep_out], [send_out], [["row"], [0], [1]])
    by_in = Reduction([keep_in], [send_in], [[0], ["row"], [1]])

    all_scores = [pltpu.VMEM((mem_len, 2 * seq), BF16), pltpu.VMEM((2 * seq, LANES), BF16)]
    scratch = [pltpu.VMEM((seq, wide), BF16)] * n + all_scores + [pltpu.VMEM((mem_len, LANES), F32)]
    self_work = [pltpu.VMEM((seq, 2 * seq), BF16), pltpu.VMEM((2 * seq, LANES), BF16)] * 2
    bias_sum = ((2, wide), F32)

    def saved_of(saved):
        return [s[k] for k in range(4) for s in saved]

    got = run(
        functools.partial(cross_backward_kernel, n),
        [after_cross, *terms, cot, vectors, molecules]
        + saved_of(saved_cross) + [*w_cross_out, *w_cross_q],
        [full, whole] + [local] * (3 * n) + [bias_sum] * n + back + [((3, width), F32)],
        scratch=scratch,
        name="cross_backward",
    )
    grad_cross, low_cross, got = got[0], got[1], got[2:]
    cross_grads, cross_bias_sums, got = got[: 3 * n], got[3 * n : 4 * n], got[4 * n :]
    terms, small_ffn = team_parts(got[:BACK]), got[BACK]
    keep, send, *memory_terms, result = run(
        functools.partial(cross_weights_kernel, n),
        [*cross_grads, *heads_cross, *w_cross_kv]
        + [normed_cross, memory_row, low_cross, after_cross, *out_terms, vectors],
        [((2, 2 * head, width), F32), ((2, 2 * head, width), BF16)] + back + [whole],
        name="cross_weights",
    )
    by_cross = Reduction([keep], [send], [[0], [1], ["row"]] + [[k] for k in range(2, bits)], pad=2 * SMALL)
    advance("fold_ffn", by_out, by_in)

    group = ((1, 4 * head, width), F32)
    ins = [after_self, *terms, grad_cross, vectors, molecules] + [far(v) for v in saved_self[-1]]
    grad_self, low_self, *last_grads, last_sums, small_cross, first, send = run(
        functools.partial(self_backward_kernel, n),
        ins + [*w_self_out, normed_self, heads_self[-1]],
        [full, whole] + [local] * 3 + [bias_sum, ((3, width), F32), local if n == 2 else group, (group[0], BF16)],
        scratch=[pltpu.VMEM((seq, wide), BF16)] + self_work,
        name="self_backward",
    )
    by_self = Reduction([first], [send], [["row"]] + [[k] for k in range(bits)], turned=True)
    by_ffn = by_out
    by_ffn.keeps, by_ffn.gots = by_out.keeps + by_in.keeps, by_out.gots + by_in.gots
    by_ffn.turned = True
    by_ffn.axes = [[0]] + [[k] for k in range(1, bits)]
    mem_terms = team_parts(memory_terms)
    share = width // mp
    along = share == LANES and team == 2 and dp == 8 and mem_len // dp * LANES == SMALL * width
    blocks = ((16, SMALL, width), BF16)
    extra = (functools.partial(memory_start_kernel, 1), mem_terms, [blocks]) if along else None
    given = advance("ffn_1", by_ffn, extra=extra)
    ins = [*w_qkv, *last_grads]
    if n == 2:
        ins += [molecules] + [far(v) for v in saved_self[0]] + [first, normed_self, heads_self[0], low_self]
    outs = ([bias_sum, group] if n == 2 else []) + back
    got = run(
        functools.partial(self_backward_rest_kernel, n),
        ins,
        outs,
        scratch=[pltpu.VMEM((seq, wide), BF16)] * 3 + self_work if n == 2 else [],
        name="self_backward_rest",
    )
    self_bias_sums = [last_sums]
    if n == 2:
        self_bias_sums, by_self.keeps, got = [got[0], last_sums], [got[1]], got[2:]
    terms = team_parts(got)
    moved = [*given, by_ffn.gots[0]]
    moved_at = by_ffn.extra_at if along else None
    advance("ffn_2", by_ffn)
    sent, more = [blocks, ((1, 8 * SMALL, width), BF16)], None
    if along:
        more = (functools.partial(memory_send_kernel, 1, moved_at, 0), moved, sent)
    given = advance("cross_1", by_cross, more=more)
    advance("self_1", by_self)

    fits = apart and 4 * head == width and unit == width
    if fits:
        shard_rows = [*self_bias_sums, *cross_bias_sums, ffn_sums]
        lines = 2
    else:

        def by_shard(sums):
            return sums if n == 2 else [sums[0][:, :head], sums[0][:, head:]]

        shard_rows = [
            jnp.stack(
                [
                    jnp.concatenate([a.reshape(-1), b.reshape(-1), ffn_sums[i]]).reshape(-1, width)
                    for i, (a, b) in enumerate(zip(by_shard(self_bias_sums), by_shard(cross_bias_sums)))
                ]
            )
        ]
        lines = shard_rows[0].shape[1]
    both, small_own, small_other = run(
        functools.partial(input_backward_kernel, n),
        [x, *terms, grad_self, vectors, result, small_cross, small_ffn, *shard_rows],
        [((2 * seq, width), BF16)] + [((SMALL, width), BF16)] * 2,
        name="input_backward",
    )

    by_cross.carry = [small_other]
    if along:
        more = (functools.partial(memory_send_kernel, 0, 0, "row"), [given[0], data_swap(given[1], 0)], sent)
    given = advance("cross_2", by_cross, more=more)
    by_self.ride, by_self.ride_at = [small_own, by_cross.gots[0]], by_cross.size
    if along:
        memory_state = [given[0], other(given[1])]
    advance("ffn_3", by_ffn)
    advance("self_cross_2", by_self, by_cross)
    got_both = other(later(both, by_cross.keeps[0]))
    advance("all_3", by_self, by_ffn, by_cross)
    if not along:
        mine, theirs = jnp.concatenate(mem_terms[:BACK]), jnp.concatenate(mem_terms[BACK:])
        total = (mine.astype(F32) + theirs.astype(F32)).astype(BF16)
        total = total.reshape(dp, mem_len // dp, rows, team, share)
        blocks = lax.dynamic_index_in_dim(total, seat, 3, keepdims=False).swapaxes(1, 2)
        blocks = blocks.reshape(dp * rows, mem_len // dp, share)
        same_seat = [[d * mp + m for d in range(dp) for m in range(mp) if m % team == s] for s in range(team)]
        grad_memory = lax.all_to_all(
            blocks, ("dp", "mp"), split_axis=0, concat_axis=0, tiled=True, axis_index_groups=same_seat
        ).astype(F32)
    advance("self_cross_4", by_self, by_cross)
    if by_ffn.ready():
        by_ffn.got = swap(later(by_ffn.chunk, by_cross.chunk), by_ffn.halved[0])

    mixed, grad_inputs = run(
        place_rows_kernel,
        [both, got_both],
        [far(((rows, seq, width), BF16)), far(((rows, seq, width), F32))],
        name="place_rows",
    )
    more = (functools.partial(memory_send_kernel, "row", 0, 2), memory_state, sent) if along else None
    while more or not (by_self.ready() and by_cross.ready() and by_ffn.ready()):
        given = advance("rest", by_self, more=more)
        if more:
            memory_state, more = [given[0], data_swap(given[1], 2)], None
        advance("rest_cross", by_ffn, by_cross)
    (grad_ffn_in, grad_ffn_out), (grad_cross_q, grad_cross_kv, grad_cross_out) = run.batch(
        [
            (
                functools.partial(ffn_grads_kernel, by_ffn.halved[0]),
                [by_ffn.chunk, by_ffn.got],
                [far(((width, unit), F32)), far(((unit, width), F32))],
            ),
            (
                functools.partial(cross_grads_kernel, by_cross.halved[0]),
                [by_cross.chunk, by_cross.got],
                [far(((width, head), F32)), far(((2, width, head), F32)), far(((head, width), F32))],
            ),
        ],
        name="ffn_and_cross_grads",
    )
    parts = []
    if along:
        end = functools.partial(memory_end_kernel, 2, 0)
        parts = [(end, memory_state, [far(((16, mem_len // dp, share), F32))])]
    if fits:
        outs = [((2, head), F32), ((2, head), F32), ((1, unit), F32)]
    else:
        outs = [((lines, width), F32)]
    outs = [((3, width, head), F32), ((head, width), F32)] + [((3, width), F32)] * 3 + outs
    parts.append(
        (
            functools.partial(self_grads_kernel, by_self.halved[0]),
            [by_self.chunk, by_self.got],
            [far(v) for v in outs],
        )
    )
    *got, (grad_self_qkv, grad_self_out, grad_gain, grad_shift, grad_out_bias, *rest) = run.batch(parts, name="last_grads")
    if along:
        grad_memory = got[0][0]
    if fits:
        grad_self_bias, grad_cross_bias, grad_ffn_bias = rest[0], rest[1], rest[2].reshape(-1)
    else:
        own_small = rest[0].reshape(-1)
        grad_self_bias = own_small[: 2 * head].reshape(2, head)
        grad_cross_bias = own_small[2 * head : 4 * head].reshape(2, head)
        grad_ffn_bias = own_small[4 * head :]
    return (
        mixed,
        grad_inputs,
        grad_memory,
        grad_gain,
        grad_shift,
        grad_self_qkv,
        grad_self_bias,
        grad_self_out,
        grad_cross_q,
        grad_cross_kv,
        grad_cross_bias,
        grad_cross_out,
        grad_ffn_in,
        grad_ffn_bias,
        grad_ffn_out,
        grad_out_bias,
    )


def solution(mesh):
    placed = (
        P("dp", None, None),
        P(None, "dp", None),
        P("dp", None),
        P("dp", None),
        P(),
        P(),
        P(),
        P(),
        P(None, None, "mp"),
        P(None, "mp"),
        P("mp", None),
        P(None, "mp"),
        P(None, None, "mp"),
        P(None, "mp"),
        P("mp", None),
        P(None, "mp"),
        P("mp"),
        P("mp", None),
        P(),
        P("dp", None, None),
    )
    return jax.shard_map(
        shards,
        mesh=mesh,
        in_specs=placed,
        out_specs=(
            P("dp", None, None),
            P("dp", None, None),
            P(None, "dp", "mp"),
            P(),
            P(),
            P(None, None, "mp"),
            P(None, "mp"),
            P("mp", None),
            P(None, "mp"),
            P(None, None, "mp"),
            P(None, "mp"),
            P("mp", None),
            P(None, "mp"),
            P("mp"),
            P("mp", None),
            P(),
        ),
        check_vma=False,
    )
```
